32 devices in a mesh: grp: 4 (over y, x), dp: 8 (over z, core).
Axes of the slice: x: 2, y: 2, z: 4, core: 2. Of those that a mesh axis runs over, the one named last changes fastest.
Arguments:
- source_ids: int32 [2, 32, 512], P(None, ('grp', 'dp')), may hold values from 0 to 32127
- target_inputs: int32 [2, 32, 256], P(None, ('grp', 'dp')), may hold values from 0 to 32127
- lengths: int32 [2, 32, 2], P(None, ('grp', 'dp')), may hold values from 64 to 512, as said below
- positions: int32 [2, 32, 256], P(None, ('grp', 'dp')), may hold values from 0 to 255, as said below
- target_ids: int32 [2, 32, 256], P(None, ('grp', 'dp')), may hold values from 0 to 32127
- target_mask: int32 [2, 32, 256], P(None, ('grp', 'dp')), may hold values from 0 to 1, as said below
- table: bfloat16 [32128, 512], P('dp')
- backbone_attn: bfloat16 [3, 512, 2048], replicated, may hold values from -0.25 to 0.25
- backbone_ffn_in: bfloat16 [2, 512, 2048], replicated, may hold values from -0.25 to 0.25
- backbone_ffn_out: bfloat16 [2, 2048, 512], replicated, may hold values from -0.125 to 0.125
- backbone_gains: float32 [6, 512], replicated, may hold values from 0.5 to 1.5
- inner_weights: float32 [4, 279104], P('grp')
- first_moment: float32 [4, 279104], P('grp'), may hold values from -3.0517578e-05 to 3.0517578e-05
- second_moment: float32 [4, 279104], P('grp'), may hold values from 3.6187227e-12 to 1.4474891e-11
- anchor: float32 [279104], replicated
- outer_momentum: float32 [279104], replicated, may hold values from -0.75 to 0.75
Outputs:
- loss_sum: float32 [4], P('grp')
- target_count: float32 [4], P('grp')
- grad_norm: float32 [4], P('grp')
- new_first: float32 [4, 279104], P('grp')
- new_second: float32 [4, 279104], P('grp')
- new_inner: float32 [4, 279104], P('grp')
- outer_delta: float32 [279104], replicated
- new_momentum: float32 [279104], replicated
- new_anchor: float32 [279104], replicated
The draws below stay inside these ranges and needn't reach their ends.
Inputs may be any that keep to these rules, and one draw needn't show every extreme that they name: lengths[m, b, 0] is a source length of at least 128 and lengths[m, b, 1] a target length from 64 to 256; pair 0 of micro-batch 0 has both at 512 and 256. `positions`: each position is below its pair's target length. `target_mask`: the first entry of every pair's mask is 1.
All inputs are finite; a program needn't handle non-finite values.
Results may differ from the reference program's by a relative error of at most 0.0079.
Values may be sent and summed in bfloat16 or wider, within the bound.
No kernel may reach another device: no remote copies, remote signals or barrier semaphores. Data moves between devices by JAX's collectives and lax.ppermute only.
A program may use at most 320 MiB of HBM per device.

```python
import math
import jax
import jax.numpy as jnp
import numpy as np
from jax import lax

D = 512
HEADS = 8
HEAD_DIM = 64
FF = 2048
VOCAB = 32128
SIDE = 64
SIDE_HEADS = 8
SIDE_FF = 256
SRC = 512
TGT = 256
LOSS_POS = 256
MICRO = 2
STEP = 5
GROUPS = 4
GROUP_ROWS = 8
BATCH = 32
PARAMS = 279104


def length_table(key):
    source = jax.random.randint(jax.random.fold_in(key, 11), (MICRO, BATCH), SRC // 4, SRC + 1)
    target = jax.random.randint(jax.random.fold_in(key, 12), (MICRO, BATCH), TGT // 4, TGT + 1)
    source = source.at[0, 0].set(SRC)
    target = target.at[0, 0].set(TGT)
    return jnp.stack([source, target], axis=-1).astype(jnp.int32)


def draw_lengths(key, part):
    return length_table(key)


def draw_positions(key, part):
    target = length_table(key)[..., 1]
    key = jax.random.fold_in(key, 2)
    picks = jax.random.randint(key, (MICRO, BATCH, LOSS_POS), 0, target[..., None])
    return picks.at[0, 0, LOSS_POS - 1].set(TGT - 1).astype(jnp.int32)


def draw_target_mask(key, part):
    key = jax.random.fold_in(key, 3)
    rows = jnp.arange(BATCH, dtype=jnp.int32)
    inner_span = max(GROUP_ROWS - 1, 1)
    outer_span = max(GROUPS - 1, 1)
    threshold = (inner_span + 2 * (rows % GROUP_ROWS)) * (outer_span + 2 * (rows // GROUP_ROWS))
    bits = jax.random.randint(key, (MICRO, BATCH, LOSS_POS), 0, 9 * inner_span * outer_span)
    mask = (bits < threshold[None, :, None]).astype(jnp.int32)
    return mask.at[:, :, 0].set(1)


def draw_table(key, part):
    key = jax.random.fold_in(key, 4)
    rows = jnp.arange(VOCAB, dtype=jnp.float32) / (VOCAB - 1)
    values = jax.random.normal(key, (VOCAB, D), jnp.float32)
    scale = 1.0 + 2.0 * rows
    return (values * scale[:, None]).astype(jnp.bfloat16)


def side_values(key, rows):
    spans = [(4 * D * SIDE, D ** (-0.5)), (9 * SIDE * SIDE, SIDE ** (-0.5)), (3 * SIDE * SIDE, (SRC / SIDE) ** 0.5 / 4.0), (2 * SIDE * SIDE_FF, SIDE ** (-0.5)), (2 * SIDE_FF * SIDE, SIDE_FF ** (-0.5)), (SIDE * D, SIDE ** (-0.5))]
    scales = jnp.concatenate([jnp.full((count,), scale, jnp.float32) for count, scale in spans])
    normal = jax.random.normal(jax.random.fold_in(key, 1), (rows, scales.shape[0]), jnp.float32)
    gains = jax.random.uniform(jax.random.fold_in(key, 2), (rows, 7 * SIDE), jnp.float32, 0.6, 1.4)
    gates = jax.random.uniform(jax.random.fold_in(key, 3), (rows, 2 * SIDE), jnp.float32, -1.5, 1.5)
    return jnp.concatenate([normal * scales[None, :], gains, gates], axis=1)


def draw_inner_weights(key, part):
    key = jax.random.fold_in(key, 5)
    return side_values(key, GROUPS)


def draw_anchor(key, part):
    key = jax.random.fold_in(key, 6)
    return side_values(key, 1)[0]


def plant(result, own_key, low, top_value):
    longest = result.shape.index(max(result.shape))
    spots = []
    for shift in (0, 1):
        where = [jax.random.randint(jax.random.fold_in(own_key, axis), (), 0, length) for axis, length in enumerate(result.shape)]
        where[longest] = (where[longest] + shift) % result.shape[longest]
        spots.append(tuple(where))
    return result.at[spots[0]].set(low).at[spots[1]].set(top_value)


def level_of(rng, dims, cuts, least, largest):
    level = 1.0
    for position, blocks in cuts:
        steps = jax.random.uniform(jax.random.fold_in(jax.random.fold_in(rng, 6), position), (blocks,), jnp.float32, least / len(cuts), largest / len(cuts))
        level = level * jnp.repeat(jnp.exp(steps), dims[position] // blocks).reshape((-1,) + (1,) * (len(dims) - 1 - position))
    return level


def rank_table(count, slope):
    weights = [(1 << 20) // math.isqrt(standing ** slope) + 1 for standing in range(1, count + 1)]
    width = 1 + sum(weights) // (1 << 30)
    return np.cumsum(np.array([max(1, weight // width) for weight in weights]))


def ranked(own_key, shape, amount, slope):
    listing = rank_table(amount, slope)
    lot = jax.random.randint(jax.random.fold_in(own_key, 1), shape, 0, int(listing[amount - 1]))
    standing = jnp.searchsorted(jnp.asarray(listing, jnp.int32), lot, side="right")
    return jax.random.permutation(jax.random.fold_in(own_key, 2), amount)[standing].astype(jnp.int32)


def scatter_about(rng, shape, spread, reach, cuts=(), held_as=jnp.bfloat16):
    drawn = jax.random.normal(rng, shape, jnp.float32) * spread
    if len(cuts) > 0:
        drawn = level_of(rng, shape, cuts, -0.22, 0.18) * drawn
    return jnp.clip(drawn, min=-reach, max=reach).astype(held_as)


def setup_inputs(seed: int = 0) -> dict:
    seeds = jax.random.split(jax.random.key(seed), 17)
    source_ids = plant(ranked(seeds[0], (MICRO, BATCH, SRC), VOCAB, 2), jax.random.fold_in(seeds[0], 3), 0, VOCAB - 1).astype(jnp.int32)
    target_inputs = plant(ranked(seeds[1], (MICRO, BATCH, TGT), VOCAB, 2), jax.random.fold_in(seeds[1], 3), 0, VOCAB - 1).astype(jnp.int32)
    lengths = draw_lengths(jax.random.fold_in(seeds[16], 71), 0)
    positions = draw_positions(jax.random.fold_in(seeds[16], 71), 0)
    target_ids = plant(ranked(seeds[4], (MICRO, BATCH, LOSS_POS), VOCAB, 2), jax.random.fold_in(seeds[4], 3), 0, VOCAB - 1).astype(jnp.int32)
    target_mask = draw_target_mask(jax.random.fold_in(seeds[16], 71), 0)
    table = draw_table(jax.random.fold_in(seeds[16], 71), 0)
    backbone_attn = scatter_about(seeds[7], (3, D, 4 * D), D ** -0.5, 0.25)
    backbone_ffn_in = scatter_about(seeds[8], (2, D, FF), D ** -0.5, 0.25)
    backbone_ffn_out = scatter_about(seeds[9], (2, FF, D), FF ** -0.5, 0.125)
    backbone_gains = jnp.clip(1.0 + 0.1 * jax.random.normal(seeds[10], (6, D), jnp.float32), 0.5, 1.5)
    inner_weights = draw_inner_weights(jax.random.fold_in(seeds[16], 71), 0)
    first_moment = scatter_about(seeds[12], (GROUPS, PARAMS), (0.111 * 0.01 / PARAMS ** 0.5), 3.0517578125e-05, ((0, 4),), jnp.float32)
    second_moment = jnp.clip(jnp.exp(math.log(1.4474890903948268e-11) - 1.3862944 * jax.random.uniform(seeds[13], (GROUPS, PARAMS), jnp.float32) ** level_of(seeds[13], (GROUPS, PARAMS), ((0, 4),), -0.2, 0.2)), 3.618722725987067e-12, 1.4474890903948268e-11)
    anchor = draw_anchor(jax.random.fold_in(seeds[16], 71), 0)
    outer_momentum = scatter_about(seeds[15], (PARAMS,), 0.05, 0.75, (), jnp.float32)
    return {"source_ids": source_ids, "target_inputs": target_inputs, "lengths": lengths, "positions": positions, "target_ids": target_ids, "target_mask": target_mask, "table": table, "backbone_attn": backbone_attn, "backbone_ffn_in": backbone_ffn_in, "backbone_ffn_out": backbone_ffn_out, "backbone_gains": backbone_gains, "inner_weights": inner_weights, "first_moment": first_moment, "second_moment": second_moment, "anchor": anchor, "outer_momentum": outer_momentum}


highest = lax.Precision.HIGHEST
norm_eps = 1e-06
negative = -1000000000.0
beta_first = 0.9
beta_second = 0.99
adam_eps = 1e-08
learn_rate = 0.03
decay_rate = 0.01
clip_norm = 0.01
outer_rate = 0.7
outer_beta = 0.9

@jax.custom_vjp
def low(v):
    return lax.optimization_barrier(v.astype(jnp.bfloat16)).astype(jnp.float32)

@jax.custom_vjp
def low_back(v):
    return v

def low_keep(v):
    return (low(v), None)

def low_pass(kept, grad):
    return (grad,)

def back_keep(v):
    return (v, None)

def back_low(kept, grad):
    return (low(grad),)
low.defvjp(low_keep, low_pass)
low_back.defvjp(back_keep, back_low)

def matmul(left, right):
    return jnp.dot(left, right, precision=highest, preferred_element_type=jnp.float32)

def linear(inputs, weight):
    return matmul(low(inputs), low(weight))

def rmsnorm(values, gain):
    return values * lax.rsqrt(lax.optimization_barrier(jnp.mean(values * values, axis=-1, keepdims=True)) + norm_eps) * gain

def layout():
    return [('down', (4, D, SIDE)), ('attn_in', (3, SIDE, 3 * SIDE)), ('attn_out', (3, SIDE, SIDE)), ('ffn_in', (2, SIDE, SIDE_FF)), ('ffn_out', (2, SIDE_FF, SIDE)), ('upsample', (SIDE, D)), ('small', (9, SIDE))]

def unpack(flat):
    parts = {}
    offset = 0
    for label, shape in layout():
        count = 1
        for extent in shape:
            count = count * extent
        parts[label] = flat[offset:offset + count].reshape(shape)
        offset = offset + count
    return parts

def key_mask(queries, keys, valid, causal):
    key_pos = jnp.arange(keys)
    allowed = jnp.broadcast_to(key_pos[None, :] < valid, (queries, keys))
    if causal:
        allowed = allowed & (key_pos[None, :] <= jnp.arange(queries)[:, None])
    return allowed

def frozen_attention(normed, source, weight, mask):
    query = low(matmul(low(normed), weight[:, :D])).reshape(-1, HEADS, HEAD_DIM)
    keyval = low(matmul(low(source), weight[:, D:3 * D]))
    key_heads = keyval[:, :D].reshape(-1, HEADS, HEAD_DIM)
    value_heads = keyval[:, D:].reshape(-1, HEADS, HEAD_DIM)
    scores = jnp.einsum('qhd,khd->hqk', query, key_heads, precision=highest) * HEAD_DIM ** (-0.5)
    scores = jnp.where(mask[None], scores, negative)
    mixing = low(jax.nn.softmax(scores, axis=-1))
    mixed = jnp.einsum('hqk,khd->qhd', mixing, value_heads, precision=highest).reshape(-1, D)
    return matmul(low(mixed), weight[:, 3 * D:])

def frozen_ffn(normed, weight_in, weight_out):
    hidden = low(jax.nn.gelu(matmul(low(normed), weight_in), approximate=True))
    return matmul(hidden, weight_out)

def backbone(embed_src, embed_tgt, src_len, tgt_len, attn, ffn_in, ffn_out, gains):
    enc_mask = key_mask(SRC, SRC, src_len, False)
    self_mask = key_mask(TGT, TGT, tgt_len, True)
    cross_mask = key_mask(TGT, SRC, src_len, False)
    normed = rmsnorm(embed_src, gains[0])
    state = embed_src + frozen_attention(normed, normed, attn[0], enc_mask)
    state = state + frozen_ffn(rmsnorm(state, gains[1]), ffn_in[0], ffn_out[0])
    encoded = low(rmsnorm(state, gains[2]))
    normed = rmsnorm(embed_tgt, gains[3])
    flow = embed_tgt + frozen_attention(normed, normed, attn[1], self_mask)
    flow = flow + frozen_attention(rmsnorm(flow, gains[4]), encoded, attn[2], cross_mask)
    flow = flow + frozen_ffn(rmsnorm(flow, gains[5]), ffn_in[1], ffn_out[1])
    return (encoded, low(flow))

def side_attention(normed, source, weight_in, weight_out, mask):
    size = SIDE // SIDE_HEADS
    query = low(low_back(linear(normed, weight_in[:, :SIDE]))).reshape(-1, SIDE_HEADS, size)
    keyval = low(low_back(linear(source, weight_in[:, SIDE:])))
    key_heads = keyval[:, :SIDE].reshape(-1, SIDE_HEADS, size)
    value_heads = keyval[:, SIDE:].reshape(-1, SIDE_HEADS, size)
    scores = low_back(jnp.einsum('qhd,khd->hqk', query, key_heads, precision=highest) * size ** (-0.5))
    scores = jnp.where(mask[None], scores, negative)
    mixing = low(low_back(jax.nn.softmax(scores, axis=-1)))
    mixed = low_back(jnp.einsum('hqk,khd->qhd', mixing, value_heads, precision=highest).reshape(-1, SIDE))
    return low_back(linear(mixed, weight_out))

def side_ffn(normed, weight_in, weight_out):
    hidden = low_back(linear(normed, weight_in))
    return low_back(linear(jax.nn.gelu(hidden, approximate=True), weight_out))

def side_loss(flat, embed_src, encoded, embed_tgt, decoded, src_len, tgt_len, picks, target_row, weights, table32):
    parts = unpack(flat)
    small = parts['small']
    down = parts['down']
    enc_mask = key_mask(SRC, SRC, src_len, False)
    self_mask = key_mask(TGT, TGT, tgt_len, True)
    cross_mask = key_mask(TGT, SRC, src_len, False)
    state = low_back(matmul(embed_src, low(down[0])))
    normed = rmsnorm(state, small[0])
    state = state + side_attention(normed, normed, parts['attn_in'][0], parts['attn_out'][0], enc_mask)
    state = state + side_ffn(rmsnorm(state, small[1]), parts['ffn_in'][0], parts['ffn_out'][0])
    gate = jax.nn.sigmoid(small[7])
    state = gate * low_back(matmul(encoded, low(down[1]))) + (1.0 - gate) * state
    memory = rmsnorm(state, small[2])
    flow = low_back(matmul(embed_tgt, low(down[2])))
    normed = rmsnorm(flow, small[3])
    flow = flow + side_attention(normed, normed, parts['attn_in'][1], parts['attn_out'][1], self_mask)
    flow = flow + side_attention(rmsnorm(flow, small[4]), memory, parts['attn_in'][2], parts['attn_out'][2], cross_mask)
    flow = flow + side_ffn(rmsnorm(flow, small[5]), parts['ffn_in'][1], parts['ffn_out'][1])
    gate = jax.nn.sigmoid(small[8])
    flow = gate * low_back(matmul(decoded, low(down[3]))) + (1.0 - gate) * flow
    top = rmsnorm(flow, small[6])
    picked = jnp.take(top, picks, axis=0)
    lifted = low_back(linear(picked, parts['upsample']))
    head_in = low(lifted * D ** (-0.5))
    logits = low_back(matmul(head_in, table32.T))
    losses = jax.nn.logsumexp(logits, axis=-1) - jnp.take_along_axis(logits, target_row[:, None], axis=1)[:, 0]
    return jnp.sum(weights * losses)

def reference(source_ids, target_inputs, lengths, positions, target_ids, target_mask, table, backbone_attn, backbone_ffn_in, backbone_ffn_out, backbone_gains, inner_weights, first_moment, second_moment, anchor, outer_momentum):
    table32 = table.astype(jnp.float32)
    attn = backbone_attn.astype(jnp.float32)
    ffn_in = backbone_ffn_in.astype(jnp.float32)
    ffn_out = backbone_ffn_out.astype(jnp.float32)
    items = (source_ids.reshape(MICRO * BATCH, SRC), target_inputs.reshape(MICRO * BATCH, TGT), lengths.reshape(MICRO * BATCH, 2), positions.reshape(MICRO * BATCH, LOSS_POS), target_ids.reshape(MICRO * BATCH, LOSS_POS), target_mask.reshape(MICRO * BATCH, LOSS_POS), jnp.tile(jnp.arange(BATCH, dtype=jnp.int32) // GROUP_ROWS, MICRO))

    def one_pair(carry, item):
        gradients, loss_sums, counts = carry
        src_row, tgt_row, lens, picks, target_row, mask_row, group = item
        embed_src = jnp.take(table32, src_row, axis=0)
        embed_tgt = jnp.take(table32, tgt_row, axis=0)
        encoded, decoded = backbone(embed_src, embed_tgt, lens[0], lens[1], attn, ffn_in, ffn_out, backbone_gains)
        weights = mask_row.astype(jnp.float32)

        def loss_of(flat):
            return side_loss(flat, embed_src, encoded, embed_tgt, decoded, lens[0], lens[1], picks, target_row, weights, table32)
        loss, pullback = jax.vjp(loss_of, inner_weights[group])
        gradient, = pullback(jnp.ones((), jnp.float32))
        selector = (jnp.arange(GROUPS) == group).astype(jnp.float32)
        return ((gradients + selector[:, None] * gradient[None], loss_sums + selector * loss, counts + selector * jnp.sum(weights)), None)
    start = (jnp.zeros((GROUPS, PARAMS), jnp.float32), jnp.zeros((GROUPS,), jnp.float32), jnp.zeros((GROUPS,), jnp.float32))
    (gradients, loss_sums, counts), _ = lax.scan(one_pair, start, items)
    mean_grad = gradients / counts[:, None]
    norms = jnp.sqrt(lax.optimization_barrier(jnp.sum(mean_grad * mean_grad, axis=1)))
    clipped = mean_grad * jnp.minimum(1.0, clip_norm / norms)[:, None]
    moment_one = beta_first * first_moment + (1.0 - beta_first) * clipped
    moment_two = beta_second * second_moment + (1.0 - beta_second) * clipped * clipped
    fixed_one = moment_one / (1.0 - beta_first ** STEP)
    fixed_two = moment_two / (1.0 - beta_second ** STEP)
    new_inner = inner_weights - learn_rate * (fixed_one / (jnp.sqrt(fixed_two) + adam_eps) + decay_rate * inner_weights)
    delta = lax.optimization_barrier(jnp.mean(anchor[None] - new_inner, axis=0))
    momentum = outer_beta * outer_momentum + delta
    new_anchor = anchor - outer_rate * (delta + outer_beta * momentum)
    return (loss_sums, counts, norms, moment_one, moment_two, new_inner, delta, momentum, new_anchor)
```

```python
import functools

import jax
import jax.numpy as jnp
from jax import lax
from jax.experimental import pallas as pl
from jax.experimental.pallas import tpu as pltpu
from jax.sharding import PartitionSpec as P

D = 512
HEADS = 8
SIDE = 64
SIDE_HEADS = 8
SIDE_FF = 256
STEP = 5


norm_eps = 1e-06
negative = -1000000000.0
beta_first = 0.9
beta_second = 0.99
adam_eps = 1e-08
learn_rate = 0.03
decay_rate = 0.01
clip_norm = 0.01
outer_rate = 0.7
outer_beta = 0.9


def layout():
    return [
        ("down", (4, D, SIDE)),
        ("attn_in", (3, SIDE, 3 * SIDE)),
        ("attn_out", (3, SIDE, SIDE)),
        ("ffn_in", (2, SIDE, SIDE_FF)),
        ("ffn_out", (2, SIDE_FF, SIDE)),
        ("upsample", (SIDE, D)),
        ("small", (9, SIDE)),
    ]


def unpack(flat):
    parts = {}
    offset = 0
    for label, shape in layout():
        count = 1
        for extent in shape:
            count = count * extent
        parts[label] = flat[offset : offset + count].reshape(shape)
        offset = offset + count
    return parts


LOG2E = 1.4426950408889634
masked = -1e30

def dot(left, right):
    return jnp.dot(left, right, preferred_element_type=jnp.float32)

def dot_t(left, right):
    return lax.dot_general(left, right, (((1,), (1,)), ((), ())), preferred_element_type=jnp.float32)

def rms_rows(values, gain):
    return values * lax.rsqrt(jnp.mean(values * values, axis=1, keepdims=True) + norm_eps) * gain

def gelu(values):
    inner = values * (0.7978845608028654 + 0.035677408136300125 * (values * values))
    return (0.5 * values) * (1.0 + jnp.tanh(inner))

def lane_heads(query, keys, values, key_bias, causal_bias):
    lane = lax.broadcasted_iota(jnp.int32, (1, 128), 1)
    scale = 0.125 * LOG2E
    mixed = []
    for pair in range(4):
        span = slice(128 * pair, 128 * pair + 128)
        q_pair, k_pair, v_pair = query[:, span], keys[:, span], values[:, span]
        halves = []
        for side in range(2):
            own = (lane < 64) if side == 0 else (lane >= 64)
            spare = lane == (64 if side == 0 else 0)
            q_head = jnp.where(own, q_pair, spare.astype(jnp.bfloat16))
            k_head = jnp.where(own, k_pair, jnp.where(spare, key_bias, jnp.bfloat16(0)))
            scores = dot_t(q_head, k_head)
            if causal_bias is not None:
                scores = scores + causal_bias
            peak = jnp.max(scores, axis=1, keepdims=True)
            weight = jnp.exp2((scores - peak) * scale)
            total = jnp.sum(weight, axis=1, keepdims=True)
            halves.append(dot(weight.astype(jnp.bfloat16), v_pair) / total)
        mixed.append(jnp.where(lane < 64, halves[0], halves[1]).astype(jnp.bfloat16))
    return jnp.concatenate(mixed, axis=1)

def bias_column(count, valid):
    place = lax.broadcasted_iota(jnp.int32, (count, 1), 0)
    return jnp.where(place < valid, 0.0, masked).astype(jnp.bfloat16)

def frozen_ffn(state_ref, out_ref, gain, win_ref, wout_ref, finish):
    tokens = state_ref.shape[0]
    tile = 256
    def step(i, carry):
        at = pl.ds(i * tile, tile)
        state = state_ref[at]
        normed = rms_rows(state, gain).astype(jnp.bfloat16)
        total = state
        for start in range(0, win_ref.shape[1], 512):
            hidden = gelu(dot(normed, win_ref[:, start:start + 512])).astype(jnp.bfloat16)
            total = total + dot(hidden, wout_ref[start:start + 512])
        out_ref[at] = finish(total).astype(out_ref.dtype)
        return carry
    lax.fori_loop(0, tokens // tile, step, 0)

def fetch(pairs, sems):
    copies = [pltpu.make_async_copy(src, dst, sems.at[i]) for i, (src, dst) in enumerate(pairs)]
    for copy in copies:
        copy.start()
    return copies

def encoder_kernel(len_ref, x_ref, gains_ref, attn_hbm, win_hbm, wout_hbm, out_ref, attn_ref, win_ref, wout_ref, qkv_ref, state_ref, sems):
    first, second, third, fourth = fetch([(attn_hbm.at[0, :, :3 * D], attn_ref.at[:, :3 * D]), (attn_hbm.at[0, :, 3 * D:], attn_ref.at[:, 3 * D:]), (win_hbm.at[0], win_ref), (wout_hbm.at[0], wout_ref)], sems)
    tokens = x_ref.shape[0]
    x = x_ref[...].astype(jnp.float32)
    normed = rms_rows(x, gains_ref[0:1]).astype(jnp.bfloat16)
    first.wait()
    qkv_ref[...] = dot(normed, attn_ref[:, :3 * D]).astype(jnp.bfloat16)
    bias = bias_column(tokens, len_ref[0])
    second.wait()
    def step(i, carry):
        at = pl.ds(i * 256, 256)
        mixed = lane_heads(qkv_ref[at, :D], qkv_ref[:, D:2 * D], qkv_ref[:, 2 * D:], bias, None)
        state_ref[at] = x_ref[at].astype(jnp.float32) + dot(mixed, attn_ref[:, 3 * D:])
        return carry
    lax.fori_loop(0, tokens // 256, step, 0)
    third.wait()
    fourth.wait()
    frozen_ffn(state_ref, out_ref, gains_ref[1:2], win_ref, wout_ref, lambda v: rms_rows(v, gains_ref[2:3]))

def decoder_kernel(len_ref, x_ref, encoded_ref, gains_ref, attn_hbm, win_hbm, wout_hbm, out_ref, attn_ref, cross_ref, win_ref, wout_ref, kv_ref, state_ref, sems):
    first, second, third, fourth = fetch([(attn_hbm.at[1], attn_ref), (attn_hbm.at[2], cross_ref), (win_hbm.at[1], win_ref), (wout_hbm.at[1], wout_ref)], sems)
    tokens = x_ref.shape[0]
    sources = encoded_ref.shape[0]
    x = x_ref[...].astype(jnp.float32)
    normed = rms_rows(x, gains_ref[3:4]).astype(jnp.bfloat16)
    row = lax.broadcasted_iota(jnp.int32, (tokens, tokens), 0)
    column = lax.broadcasted_iota(jnp.int32, (tokens, tokens), 1)
    causal = jnp.where(column <= row, 0.0, masked)
    first.wait()
    qkv = dot(normed, attn_ref[:, :3 * D]).astype(jnp.bfloat16)
    mixed = lane_heads(qkv[:, :D], qkv[:, D:2 * D], qkv[:, 2 * D:], bias_column(tokens, len_ref[1]), causal)
    state = x + dot(mixed, attn_ref[:, 3 * D:])
    second.wait()
    kv_ref[...] = dot(encoded_ref[...], cross_ref[:, D:3 * D]).astype(jnp.bfloat16)
    normed = rms_rows(state, gains_ref[4:5]).astype(jnp.bfloat16)
    query = dot(normed, cross_ref[:, :D]).astype(jnp.bfloat16)
    mixed = lane_heads(query, kv_ref[:, :D], kv_ref[:, D:], bias_column(sources, len_ref[0]), None)
    state_ref[...] = state + dot(mixed, cross_ref[:, 3 * D:])
    third.wait()
    fourth.wait()
    frozen_ffn(state_ref, out_ref, gains_ref[5:6], win_ref, wout_ref, lambda v: v)

smem = pl.BlockSpec(memory_space=pltpu.SMEM)
vmem = pl.BlockSpec(memory_space=pltpu.VMEM)
hbm = pl.BlockSpec(memory_space=pl.ANY)
LIMIT = pltpu.CompilerParams(vmem_limit_bytes=56 * 2**20)

def encode(lens, x, attn, ffn_in, ffn_out, gains):
    tokens = x.shape[0]
    return pl.pallas_call(
        encoder_kernel,
        out_shape=jax.ShapeDtypeStruct((tokens, D), jnp.bfloat16),
        in_specs=[smem, vmem, vmem, hbm, hbm, hbm],
        out_specs=vmem,
        scratch_shapes=[pltpu.VMEM((D, 4 * D), jnp.bfloat16), pltpu.VMEM((D, 4 * D), jnp.bfloat16), pltpu.VMEM((4 * D, D), jnp.bfloat16),
            pltpu.VMEM((tokens, 3 * D), jnp.bfloat16), pltpu.VMEM((tokens, D), jnp.float32), pltpu.SemaphoreType.DMA((4,))],
        compiler_params=LIMIT,
        name="encoder",
    )(lens, x, gains, attn, ffn_in, ffn_out)

def decode(lens, x, encoded, attn, ffn_in, ffn_out, gains):
    tokens = x.shape[0]
    sources = encoded.shape[0]
    return pl.pallas_call(
        decoder_kernel,
        out_shape=jax.ShapeDtypeStruct((tokens, D), jnp.bfloat16),
        in_specs=[smem, vmem, vmem, vmem, hbm, hbm, hbm],
        out_specs=vmem,
        scratch_shapes=[pltpu.VMEM((D, 4 * D), jnp.bfloat16), pltpu.VMEM((D, 4 * D), jnp.bfloat16), pltpu.VMEM((D, 4 * D), jnp.bfloat16), pltpu.VMEM((4 * D, D), jnp.bfloat16),
            pltpu.VMEM((sources, 2 * D), jnp.bfloat16), pltpu.VMEM((tokens, D), jnp.float32), pltpu.SemaphoreType.DMA((4,))],
        compiler_params=LIMIT,
        name="decoder",
    )(lens, x, encoded, gains, attn, ffn_in, ffn_out)

def dot_l(left, right):
    return lax.dot_general(left, right, (((0,), (0,)), ((), ())), preferred_element_type=jnp.float32)

def rms_columns(values, gain):
    return values * lax.rsqrt(jnp.mean(values * values, axis=0, keepdims=True) + norm_eps) * gain

def rms_columns_back(values, gain, grad):
    inverse = lax.rsqrt(jnp.mean(values * values, axis=0, keepdims=True) + norm_eps)
    gained = grad * gain
    along = jnp.mean(values * gained, axis=0, keepdims=True)
    gain_grad = jnp.sum(grad * (values * inverse), axis=1, keepdims=True)
    return inverse * gained - values * (inverse * inverse * inverse * along), gain_grad

def gelu_back(values, grad):
    square = values * values
    tanh = jnp.tanh(values * (0.7978845608028654 + 0.035677408136300125 * square))
    slope = 0.5 * (1.0 + tanh) + (0.5 * values) * (1.0 - tanh * tanh) * (0.7978845608028654 + 0.107032224408900375 * square)
    return grad * slope

side_scale = (SIDE // SIDE_HEADS) ** -0.5

def keys_with_bias(keys_t, valid):
    count = keys_t.shape[1]
    place = lax.broadcasted_iota(jnp.int32, (64, count), 1)
    line = lax.broadcasted_iota(jnp.int32, (64, count), 0)
    bias = jnp.where((line == 0) & (place >= valid), masked, 0.0)
    return jnp.concatenate([keys_t.astype(jnp.float32), bias], axis=0).T.astype(jnp.bfloat16)

def head_query(query_t, head):
    line = lax.broadcasted_iota(jnp.int32, (64, 1), 0)
    own = jnp.where(line // 8 == head, query_t, 0.0)
    ones = jnp.broadcast_to(jnp.where(line == 0, 1.0, 0.0), own.shape)
    return jnp.concatenate([own, ones], axis=0).astype(jnp.bfloat16)

def rounded(values):
    return values.astype(jnp.bfloat16).astype(jnp.float32)

def causal_columns(count):
    key = lax.broadcasted_iota(jnp.int32, (count, count), 0)
    query = lax.broadcasted_iota(jnp.int32, (count, count), 1)
    return jnp.where(key <= query, 0.0, masked)

def side_heads(query_t, keys_t, values_t, valid, causal):
    keys = keys_with_bias(keys_t, valid)
    outs, sums = [], []
    for head in range(SIDE_HEADS):
        scores = dot(keys, head_query(query_t, head))
        if causal is not None:
            scores = scores + causal
        peak = jnp.max(scores, axis=0, keepdims=True)
        weight = jnp.exp2((scores - peak) * (side_scale * LOG2E))
        total = jnp.sum(weight, axis=0, keepdims=True)
        span = slice(8 * head, 8 * head + 8)
        outs.append(dot(values_t[span].astype(jnp.bfloat16), weight.astype(jnp.bfloat16)) / total)
        sums.append(peak * (side_scale * LOG2E) + jnp.log2(total))
    return jnp.concatenate(outs, axis=0), jnp.concatenate(sums, axis=0)

def side_heads_back(query_t, keys_t, values_t, sums, grad_t, valid, causal):
    keys = keys_with_bias(keys_t, valid)
    values = values_t.T.astype(jnp.bfloat16)
    line = lax.broadcasted_iota(jnp.int32, (64, 1), 0)
    grad_q, grad_k, grad_v = [], [], []
    for head in range(SIDE_HEADS):
        span = slice(8 * head, 8 * head + 8)
        scores = dot(keys, head_query(query_t, head))
        if causal is not None:
            scores = scores + causal
        weight = jnp.exp2(scores * (side_scale * LOG2E) - sums[head:head + 1])
        own_grad = jnp.where(line // 8 == head, grad_t, 0.0).astype(jnp.bfloat16)
        grad_w = rounded(dot(values, own_grad))
        along = jnp.sum(grad_w * weight, axis=0, keepdims=True)
        grad_s = (weight * (grad_w - along)).astype(jnp.bfloat16)
        grad_q.append(dot(keys_t[span].astype(jnp.bfloat16), grad_s))
        grad_k.append(dot_t(query_t[span].astype(jnp.bfloat16), grad_s))
        grad_v.append(dot_t(grad_t[span].astype(jnp.bfloat16), weight.astype(jnp.bfloat16)))
    return (jnp.concatenate(grad_q, axis=0) * side_scale, jnp.concatenate(grad_k, axis=0) * side_scale,
            jnp.concatenate(grad_v, axis=0))

def chosen_columns(tokens, positions_ref):
    token = lax.broadcasted_iota(jnp.int32, (tokens, positions_ref.shape[1]), 0)
    return jnp.where(token == positions_ref[...], 1.0, 0.0).astype(jnp.bfloat16)

def side_kernel(len_ref, src_ref, encoded_ref, tgt_ref, decoded_ref, positions_ref, down_ref, attn_in_ref, attn_out_ref, ffn_in_ref, ffn_out_ref, small_ref,
                picked_ref, enc_ref, dec_ref, enc_mixed_ref, self_mixed_ref, cross_mixed_ref, enc_sums_ref, self_sums_ref, cross_sums_ref):
    def gain(i):
        return small_ref[:, i:i + 1]

    def attend(which, query_n, key_n, valid, causal, mixed_ref, sums_ref):
        query = rounded(dot(attn_in_ref[which, :64], query_n))
        keyval = rounded(dot(attn_in_ref[which, 64:], key_n))
        mixed, sums = side_heads(query, keyval[:64], keyval[64:], valid, causal)
        mixed_b = mixed.astype(jnp.bfloat16)
        mixed_ref[...] = mixed_b
        sums_ref[...] = sums
        return dot(attn_out_ref[which], mixed_b)

    def ffn(which, normed):
        active = gelu(dot(ffn_in_ref[which], normed)).astype(jnp.bfloat16)
        return dot(ffn_out_ref[which], active)

    def norm(values, i):
        return rms_columns(values, gain(i)).astype(jnp.bfloat16)

    source_valid, target_valid = len_ref[0], len_ref[1]
    state = dot_t(down_ref[0], src_ref[...])
    enc_ref[0] = state
    normed = norm(state, 0)
    state = state + attend(0, normed, normed, source_valid, None, enc_mixed_ref, enc_sums_ref)
    enc_ref[1] = state
    state = state + ffn(0, norm(state, 1))
    enc_ref[2] = state
    joined = dot_t(down_ref[1], encoded_ref[...])
    enc_ref[3] = joined
    gate = jax.nn.sigmoid(gain(7))
    memory = norm(gate * joined + (1.0 - gate) * state, 2)
    flow = dot_t(down_ref[2], tgt_ref[...])
    dec_ref[0] = flow
    normed = norm(flow, 3)
    causal = causal_columns(flow.shape[1])
    flow = flow + attend(1, normed, normed, target_valid, causal, self_mixed_ref, self_sums_ref)
    dec_ref[1] = flow
    flow = flow + attend(2, norm(flow, 4), memory, source_valid, None, cross_mixed_ref, cross_sums_ref)
    dec_ref[2] = flow
    flow = flow + ffn(1, norm(flow, 5))
    dec_ref[3] = flow
    joined = dot_t(down_ref[3], decoded_ref[...])
    dec_ref[4] = joined
    gate = jax.nn.sigmoid(gain(8))
    top = norm(gate * joined + (1.0 - gate) * flow, 6)
    picked = dot(top, chosen_columns(flow.shape[1], positions_ref)).astype(jnp.bfloat16)
    picked_ref[...] = picked

def side(lens, src, encoded, tgt, decoded, positions, weights):
    s, t, p = src.shape[0], tgt.shape[0], positions.shape[1]
    f32, bf16 = jnp.float32, jnp.bfloat16
    shapes = [((64, p), bf16), ((4, 64, s), f32), ((5, 64, t), f32), ((64, s), bf16), ((64, t), bf16), ((64, t), bf16), ((8, s), f32), ((8, t), f32), ((8, t), f32)]
    return pl.pallas_call(
        side_kernel,
        out_shape=[jax.ShapeDtypeStruct(*item) for item in shapes],
        in_specs=[smem] + [vmem] * 11,
        out_specs=[vmem] * 9,
        compiler_params=LIMIT,
        name="side",
    )(lens, src, encoded, tgt, decoded, positions, *weights)

def back_kernel(*refs, started):
    (len_ref, src_ref, encoded_ref, tgt_ref, decoded_ref, positions_ref, attn_in_t_ref, ffn_in_t_ref, attn_in_ref, attn_out_ref, ffn_in_ref, ffn_out_ref, small_ref,
     enc_ref, dec_ref, enc_mixed_ref, self_mixed_ref, cross_mixed_ref, enc_sums_ref, self_sums_ref, cross_sums_ref, parts_ref) = refs[:22]
    before = refs[22:28] if started else (None,) * 6
    down_out, attn_in_out, attn_out_out, ffn_in_out, ffn_out_out, small_out = refs[-6:]

    def put(which, index, values):
        refs_of = {"down": 0, "attn_in": 1, "attn_out": 2, "ffn_in": 3, "ffn_out": 4}
        at = refs_of[which]
        out = (down_out, attn_in_out, attn_out_out, ffn_in_out, ffn_out_out)[at]
        out[index] = values if before[at] is None else before[at][index] + values

    smalls = {}

    def gain(i):
        return small_ref[:, i:i + 1]

    def norm(values, i):
        return rms_columns(values, gain(i)).astype(jnp.bfloat16)

    def norm_back(values, i, grad):
        result, smalls[i] = rms_columns_back(values, gain(i), grad)
        return result

    def blend_back(i, joined, late, grad):
        gate = jax.nn.sigmoid(gain(i))
        smalls[i] = jnp.sum(grad * (joined - late), axis=1, keepdims=True) * (gate * (1.0 - gate))
        return gate * grad, (1.0 - gate) * grad

    def ffn_back(which, normed, grad):
        grad_b = grad.astype(jnp.bfloat16)
        hidden = dot(ffn_in_t_ref[which], normed)
        active = gelu(hidden).astype(jnp.bfloat16)
        put("ffn_out", which, dot_t(active, grad_b))
        grad_hidden = gelu_back(hidden, dot(ffn_out_ref[which], grad_b)).astype(jnp.bfloat16)
        put("ffn_in", which, dot_t(normed, grad_hidden))
        return dot(ffn_in_ref[which], grad_hidden)

    def attend_back(which, query_n, key_n, mixed_ref, sums_ref, grad, valid, causal):
        grad_b = grad.astype(jnp.bfloat16)
        put("attn_out", which, dot_t(mixed_ref[...], grad_b))
        grad_mixed = rounded(dot(attn_out_ref[which], grad_b))
        query = rounded(dot(attn_in_t_ref[which, :64], query_n))
        keyval = rounded(dot(attn_in_t_ref[which, 64:], key_n))
        grad_q, grad_k, grad_v = side_heads_back(query, keyval[:64], keyval[64:], sums_ref, grad_mixed, valid, causal)
        return grad_q.astype(jnp.bfloat16), jnp.concatenate([grad_k, grad_v], axis=0).astype(jnp.bfloat16)

    source_valid, target_valid = len_ref[0], len_ref[1]
    tokens = tgt_ref.shape[0]
    grad_picked = parts_ref[0].astype(jnp.float32)
    for i in range(1, parts_ref.shape[0]):
        grad_picked = grad_picked + parts_ref[i].astype(jnp.float32)
    chosen = chosen_columns(tokens, positions_ref)
    high = grad_picked.astype(jnp.bfloat16)
    low = (grad_picked - high.astype(jnp.float32)).astype(jnp.bfloat16)
    grad = dot_t(high, chosen) + dot_t(low, chosen)
    gate = jax.nn.sigmoid(gain(8))
    final = gate * dec_ref[4] + (1.0 - gate) * dec_ref[3]
    grad = norm_back(final, 6, grad)
    grad_joined, grad = blend_back(8, dec_ref[4], dec_ref[3], grad)
    put("down", 3, dot(grad_joined.astype(jnp.bfloat16), decoded_ref[...]))
    grad = grad + norm_back(dec_ref[2], 5, ffn_back(1, norm(dec_ref[2], 5), grad))
    gate = jax.nn.sigmoid(gain(7))
    final = gate * enc_ref[3] + (1.0 - gate) * enc_ref[2]
    memory = norm(final, 2)
    normed = norm(dec_ref[1], 4)
    grad_q, grad_kv = attend_back(2, normed, memory, cross_mixed_ref, cross_sums_ref, grad, source_valid, None)
    zero_q = jnp.zeros((128, tokens), jnp.bfloat16)
    zero_kv = jnp.zeros((64, src_ref.shape[0]), jnp.bfloat16)
    put("attn_in", 2, dot_t(normed, jnp.concatenate([grad_q, zero_q], axis=0)) + dot_t(memory, jnp.concatenate([zero_kv, grad_kv], axis=0)))
    weight = attn_in_ref[2]
    grad_memory = dot(weight, jnp.concatenate([zero_kv, grad_kv], axis=0))
    grad = grad + norm_back(dec_ref[1], 4, dot(weight, jnp.concatenate([grad_q, zero_q], axis=0)))
    normed = norm(dec_ref[0], 3)
    grad_q, grad_kv = attend_back(1, normed, normed, self_mixed_ref, self_sums_ref, grad, target_valid, causal_columns(tokens))
    grad_qkv = jnp.concatenate([grad_q, grad_kv], axis=0)
    put("attn_in", 1, dot_t(normed, grad_qkv))
    grad = grad + norm_back(dec_ref[0], 3, dot(attn_in_ref[1], grad_qkv))
    put("down", 2, dot(grad.astype(jnp.bfloat16), tgt_ref[...]))
    grad = norm_back(final, 2, grad_memory)
    grad_joined, grad = blend_back(7, enc_ref[3], enc_ref[2], grad)
    put("down", 1, dot(grad_joined.astype(jnp.bfloat16), encoded_ref[...]))
    grad = grad + norm_back(enc_ref[1], 1, ffn_back(0, norm(enc_ref[1], 1), grad))
    normed = norm(enc_ref[0], 0)
    grad_q, grad_kv = attend_back(0, normed, normed, enc_mixed_ref, enc_sums_ref, grad, source_valid, None)
    grad_qkv = jnp.concatenate([grad_q, grad_kv], axis=0)
    put("attn_in", 0, dot_t(normed, grad_qkv))
    grad = grad + norm_back(enc_ref[0], 0, dot(attn_in_ref[0], grad_qkv))
    put("down", 0, dot(grad.astype(jnp.bfloat16), src_ref[...]))
    lane = lax.broadcasted_iota(jnp.int32, (1, 128), 1)
    total = jnp.zeros((64, 128), jnp.float32) if before[5] is None else before[5][...]
    for i in range(9):
        total = total + jnp.where(lane == i, smalls[i], 0.0)
    small_out[...] = total

def side_back(lens, src, encoded, tgt, decoded, positions, weights, kept, parts, before):
    f32 = jnp.float32
    shapes = [(4, 64, 512), (3, 64, 192), (3, 64, 64), (2, 64, 256), (2, 256, 64), (64, 128)]
    extra = list(before) if before is not None else []
    return pl.pallas_call(
        functools.partial(back_kernel, started=before is not None),
        out_shape=[jax.ShapeDtypeStruct(shape, f32) for shape in shapes],
        in_specs=[smem] + [vmem] * (21 + len(extra)),
        out_specs=[vmem] * 6,
        compiler_params=LIMIT,
        name="side_back",
    )(lens, src, encoded, tgt, decoded, positions, *weights, *kept, parts, *extra)


def swap(values, axis, distance):
    size = lax.axis_size(axis)
    return lax.ppermute(values, axis, [(i, i ^ distance) for i in range(size)])


def gather_peers(values, axis):
    return [values] + [swap(values, axis, s) for s in range(1, lax.axis_size(axis))]


def exchange(pieces, axis):
    return [pieces[0]] + [swap(pieces[s], axis, s) for s in range(1, lax.axis_size(axis))]


def tree_sum(terms):
    while len(terms) > 1:
        terms = [terms[i] + terms[i + 1] for i in range(0, len(terms), 2)]
    return terms[0]


def round_bf16(values):
    return lax.reduce_precision(values, 8, 7)


def split_bf16(values):
    high = round_bf16(values)
    return high.astype(jnp.bfloat16), (values - high).astype(jnp.bfloat16)


def embed_rows(ids, table, rows):
    size = lax.axis_size("dp")
    count = ids.shape[0]
    me = lax.axis_index("dp")
    cap = -(-(count * 5 // (size * 6)) // 32) * 32
    total = size * cap
    place = jnp.arange(count)
    same = ids[:, None] == ids[None, :]
    first_at = jnp.min(jnp.where(same, place[None, :], count), axis=1)
    first = first_at == place
    owner = (ids // rows) ^ me
    ahead = (
        first[None, :] & (owner[None, :] == owner[:, None]) & (place[None, :] < first_at[:, None])
    )
    rank = jnp.sum(ahead.astype(jnp.int32), axis=1)
    local = ids % rows
    busiest = jnp.max(jnp.where(first, rank, 0)) + 1
    slot_owner = jnp.arange(total) // cap
    slot_rank = jnp.arange(total) % cap

    def one_round(start):
        hit = (
            first[None, :]
            & (owner[None, :] == slot_owner[:, None])
            & (rank[None, :] == slot_rank[:, None] + start)
        )
        wanted = jnp.sum(jnp.where(hit, local[None, :], 0), axis=1).reshape(size, cap)
        asked = jnp.stack(exchange([wanted[s] for s in range(size)], "dp"))
        found = jnp.take(table, asked.reshape(-1), axis=0, mode="clip").reshape(size, cap, -1)
        came = jnp.concatenate(exchange([found[s] for s in range(size)], "dp"))
        mine = (owner * cap + rank - start)[:, None] == jnp.arange(total)[None, :]
        mine = mine & (rank >= start)[:, None] & (rank < start + cap)[:, None]
        return jnp.dot(
            mine.astype(jnp.bfloat16), came, preferred_element_type=jnp.bfloat16
        )

    most = jnp.full((8, 128), busiest, jnp.int32)
    for axis in ("dp", "grp"):
        peers = gather_peers(most, axis)
        for peer in peers:
            most = jnp.maximum(most, peer)
    most = most[0, 0]
    result = one_round(0)
    return lax.while_loop(
        lambda carry: carry[0] < most,
        lambda carry: (carry[0] + cap, carry[1] + one_round(carry[0])),
        (jnp.int32(cap), result),
    )[1]


CHUNK = 512
TILE = 256


def stats_kernel(rows, weight_ref, picked_ref, target_ref, out_ref):
    picked = picked_ref[...]
    target = target_ref[...]
    peak = jnp.full((1, TILE), -jnp.inf, jnp.float32)
    total = jnp.zeros((1, TILE), jnp.float32)
    aim = jnp.zeros((1, TILE), jnp.float32)
    padded = weight_ref.shape[0]
    chunk = min(CHUNK, padded)
    for start in range(0, padded, chunk):
        logits = jnp.dot(
            weight_ref[start : start + chunk], picked, preferred_element_type=jnp.float32
        )
        place = lax.broadcasted_iota(jnp.int32, (chunk, TILE), 0) + start
        aim = aim + jnp.sum(jnp.where(place == target, logits, 0.0), axis=0, keepdims=True)
        if start + chunk > rows:
            logits = jnp.where(place < rows, logits, -jnp.inf)
        above = jnp.maximum(peak, jnp.max(logits, axis=0, keepdims=True))
        total = total * jnp.exp(peak - above) + jnp.sum(
            jnp.exp(logits - above), axis=0, keepdims=True
        )
        peak = above
    out_ref[...] = jnp.concatenate([peak, total, aim, jnp.zeros((5, TILE), jnp.float32)], axis=0)


def head_stats(weight, picked, target, rows):
    padded = weight.shape[0]
    many = picked.shape[1]

    def kernel(*refs):
        stats_kernel(rows, *refs)

    return pl.pallas_call(
        kernel,
        out_shape=jax.ShapeDtypeStruct((8, many), jnp.float32),
        grid=(many // TILE,),
        in_specs=[
            pl.BlockSpec((padded, 128), lambda i: (0, 0)),
            pl.BlockSpec((128, TILE), lambda i: (0, i)),
            pl.BlockSpec((1, TILE), lambda i: (0, i)),
        ],
        out_specs=pl.BlockSpec((8, TILE), lambda i: (0, i)),
        compiler_params=pltpu.CompilerParams(vmem_limit_bytes=48 * 2**20),
    )(weight, picked, target)


def grad_kernel(
    rows, weight_ref, table_ref, up_ref, picked_ref, target_ref, lse_ref, mask_ref, top_ref, up_grad_ref
):
    picked = picked_ref[...]
    target = target_ref[...]
    lse = lse_ref[...]
    mask = mask_ref[...]
    padded = weight_ref.shape[0]
    chunk = min(CHUNK, padded)
    lifted = jnp.zeros((table_ref.shape[0], TILE), jnp.float32)
    for start in range(0, padded, chunk):
        logits = jnp.dot(
            weight_ref[start : start + chunk], picked, preferred_element_type=jnp.float32
        )
        place = lax.broadcasted_iota(jnp.int32, (chunk, TILE), 0) + start
        share = jnp.exp(logits - lse)
        grad = mask * jnp.where(place == target, share - 1.0, share)
        if start + chunk > rows:
            grad = jnp.where(place < rows, grad, 0.0)
        lifted = lifted + jnp.dot(
            table_ref[:, start : start + chunk],
            grad.astype(jnp.bfloat16),
            preferred_element_type=jnp.float32,
        )
    lifted_b = (lifted * D ** (-0.5)).astype(jnp.bfloat16)
    top_ref[...] = jnp.dot(up_ref[...], lifted_b, preferred_element_type=jnp.float32).astype(
        top_ref.dtype
    )

    @pl.when(pl.program_id(0) == 0)
    def _():
        up_grad_ref[...] = jnp.zeros_like(up_grad_ref)

    up_grad_ref[...] += dot_t(picked[: up_grad_ref.shape[0]], lifted_b)


def head_grad(weight, table_t, up_b, picked, target, lse, mask, rows):
    padded = weight.shape[0]
    many = picked.shape[1]
    width = table_t.shape[0]

    def kernel(*refs):
        grad_kernel(rows, *refs)

    row_spec = pl.BlockSpec((1, TILE), lambda i: (0, i))
    return pl.pallas_call(
        kernel,
        out_shape=(
            jax.ShapeDtypeStruct((SIDE, many), jnp.bfloat16),
            jax.ShapeDtypeStruct((SIDE, width), jnp.float32),
        ),
        grid=(many // TILE,),
        in_specs=[
            pl.BlockSpec((padded, 128), lambda i: (0, 0)),
            pl.BlockSpec((width, padded), lambda i: (0, 0)),
            pl.BlockSpec((SIDE, width), lambda i: (0, 0)),
            pl.BlockSpec((128, TILE), lambda i: (0, i)),
            row_spec,
            row_spec,
            row_spec,
        ],
        out_specs=(
            pl.BlockSpec((SIDE, TILE), lambda i: (0, i)),
            pl.BlockSpec((SIDE, width), lambda i: (0, 0)),
        ),
        compiler_params=pltpu.CompilerParams(vmem_limit_bytes=48 * 2**20),
    )(weight, table_t, up_b, picked, target, lse, mask)


def per_device(
    source_ids,
    target_inputs,
    lengths,
    positions,
    target_ids,
    target_mask,
    table,
    backbone_attn,
    backbone_ffn_in,
    backbone_ffn_out,
    backbone_gains,
    inner_weights,
    first_moment,
    second_moment,
    anchor,
    outer_momentum,
):
    micro = source_ids.shape[0]
    src_tokens = source_ids.shape[2]
    tgt_tokens = target_inputs.shape[2]
    size = lax.axis_size("dp")
    me = lax.axis_index("dp")
    core = me & 1
    rows = table.shape[0]
    padded = -(-rows // 512) * 512
    id_list = jnp.concatenate([source_ids.reshape(-1), target_inputs.reshape(-1)])
    embedded = embed_rows(id_list, table, rows)
    parts = unpack(inner_weights[0])
    up_b = parts["upsample"].astype(jnp.bfloat16)
    table_pad = jnp.pad(table, ((0, padded - rows), (0, 0)))
    table_t = table_pad.T
    lifted_table = dot_t(table_pad, up_b) * D ** (-0.5)
    weight = jnp.concatenate(split_bf16(lifted_table), axis=1)
    goals = jnp.concatenate([target_ids[:, 0], target_mask[:, 0]])
    goal_peers = jnp.stack(gather_peers(goals, "dp"), axis=1)
    all_targets = goal_peers[:micro].reshape(micro, 1, -1) - me * rows
    all_masks = goal_peers[micro:].reshape(micro, 1, -1).astype(jnp.float32)
    count_total = tree_sum(
        [jnp.sum(goal_peers[micro:, s].astype(jnp.float32)) for s in range(size)]
    )
    low = {label: values.astype(jnp.bfloat16) for label, values in parts.items()}
    turned = {label: jnp.swapaxes(low[label], -1, -2) for label in ("down", "attn_in", "attn_out", "ffn_in", "ffn_out")}
    small = jnp.pad(parts["small"].T, ((0, 0), (0, 128 - 9)))
    ahead = [turned["down"], turned["attn_in"], turned["attn_out"], turned["ffn_in"], turned["ffn_out"], small]
    behind = [turned["attn_in"], turned["ffn_in"], low["attn_in"], low["attn_out"], low["ffn_in"], low["ffn_out"], small]
    states = []
    for index in range(micro):
        embed_src = embedded[index * src_tokens : (index + 1) * src_tokens]
        base = micro * src_tokens + index * tgt_tokens
        embed_tgt = embedded[base : base + tgt_tokens]
        lens = lengths[index, 0]
        encoded = encode(lens, embed_src, backbone_attn, backbone_ffn_in, backbone_ffn_out, backbone_gains)
        decoded = decode(lens, embed_tgt, encoded, backbone_attn, backbone_ffn_in, backbone_ffn_out, backbone_gains)
        picked_t, *kept = side(lens, embed_src, encoded, embed_tgt, decoded, positions[index], ahead)
        picked_all = jnp.concatenate(gather_peers(picked_t, "dp"), axis=1)
        picked_all = jnp.concatenate([picked_all, picked_all], axis=0)
        states.append((lens, embed_src, encoded, embed_tgt, decoded, kept, picked_all))
    heads = []
    loss_total = jnp.zeros((), jnp.float32)
    for index in range(micro):
        stats = head_stats(weight, states[index][6], all_targets[index], rows)
        spots = stats.shape[1] // size
        peers = [
            jnp.concatenate(
                [peer[:, (j ^ s) * spots : ((j ^ s) + 1) * spots] for j in range(size)], axis=1
            )
            for s, peer in enumerate(gather_peers(stats[:3], "dp"))
        ]
        peak = peers[0][0]
        for peer in peers[1:]:
            peak = jnp.maximum(peak, peer[0])
        total = tree_sum([peer[1] * jnp.exp(peer[0] - peak) for peer in peers])
        aim = tree_sum([peer[2] for peer in peers])
        lse = peak + jnp.log(total)
        losses = (all_masks[index, 0] * (lse - aim)).reshape(size, -1)
        loss_total = loss_total + tree_sum([jnp.sum(losses[s]) for s in range(size)])
        heads.append(lse[None])
    grads, grad_up = None, 0.0
    for index in range(micro):
        lens, embed_src, encoded, embed_tgt, decoded, kept, picked_all = states[index]
        top_parts, up_part = head_grad(
            weight,
            table_t,
            up_b,
            picked_all,
            all_targets[index],
            heads[index],
            all_masks[index],
            rows,
        )
        grad_up = grad_up + up_part
        spots = top_parts.shape[1] // size
        back = jnp.stack(
            exchange([top_parts[:, s * spots : (s + 1) * spots] for s in range(size)], "dp")
        )
        grads = side_back(
            lens, embed_src, encoded, embed_tgt, decoded, positions[index], behind, kept, back, grads
        )
    pieces = [jnp.swapaxes(grads[0], 1, 2), *grads[1:5], grad_up, grads[5][:, :9].T]
    grad_total = jnp.concatenate([piece.reshape(-1) for piece in pieces])
    length = grad_total.shape[0]
    half = -(-length // 2048) * 1024
    wide = jnp.pad(grad_total, (0, 2 * half - length)).reshape(2, half)
    mine = lax.dynamic_index_in_dim(wide, core, 0, keepdims=False)
    other = lax.dynamic_index_in_dim(wide, 1 - core, 0, keepdims=False)
    mine = mine + swap(other, "dp", 1)
    sent = mine.astype(jnp.bfloat16)
    terms = [sent] + [swap(sent, "dp", s) for s in range(2, size, 2)]
    summed = tree_sum([term.astype(jnp.float32) for term in terms])
    both = swap(summed, "dp", 1)
    grad_total = jnp.where(core == 0, jnp.stack([summed, both]), jnp.stack([both, summed]))
    grad_total = grad_total.reshape(-1)[:length]
    mean_grad = grad_total / count_total
    norm = jnp.sqrt(jnp.sum(mean_grad * mean_grad))
    clipped = mean_grad * jnp.minimum(1.0, clip_norm / norm)
    moment_one = beta_first * first_moment[0] + (1.0 - beta_first) * clipped
    moment_two = beta_second * second_moment[0] + (1.0 - beta_second) * clipped * clipped
    fixed_one = moment_one / (1.0 - beta_first**STEP)
    fixed_two = moment_two / (1.0 - beta_second**STEP)
    old_weights = inner_weights[0]
    new_inner = old_weights - learn_rate * (
        fixed_one / (jnp.sqrt(fixed_two) + adam_eps) + decay_rate * old_weights
    )
    gap = jnp.pad(anchor - new_inner, (0, 2 * half - length)).reshape(2, half)
    sent = lax.dynamic_index_in_dim(gap, core, 0, keepdims=False).astype(jnp.bfloat16)
    terms = gather_peers(sent, "grp")
    summed = tree_sum([term.astype(jnp.float32) for term in terms]) / lax.axis_size("grp")
    both = swap(summed, "dp", 1)
    delta = jnp.where(core == 0, jnp.stack([summed, both]), jnp.stack([both, summed]))
    delta = delta.reshape(-1)[:length]
    momentum = outer_beta * outer_momentum + delta
    new_anchor = anchor - outer_rate * (delta + outer_beta * momentum)
    return (
        loss_total[None],
        count_total[None],
        norm[None],
        moment_one[None],
        moment_two[None],
        new_inner[None],
        delta,
        momentum,
        new_anchor,
    )


def solution(mesh):
    return jax.shard_map(
        per_device,
        mesh=mesh,
        in_specs=(
            P(None, ("grp", "dp"), None),
            P(None, ("grp", "dp"), None),
            P(None, ("grp", "dp"), None),
            P(None, ("grp", "dp"), None),
            P(None, ("grp", "dp"), None),
            P(None, ("grp", "dp"), None),
            P("dp", None),
            P(),
            P(),
            P(),
            P(),
            P("grp", None),
            P("grp", None),
            P("grp", None),
            P(),
            P(),
        ),
        out_specs=(
            P("grp"),
            P("grp"),
            P("grp"),
            P("grp", None),
            P("grp", None),
            P("grp", None),
            P(),
            P(),
            P(),
        ),
        check_vma=False,
    )
```

```python
import functools

import jax
import jax.numpy as jnp
from jax import lax
from jax.experimental import pallas as pl
from jax.experimental.pallas import tpu as pltpu
from jax.sharding import PartitionSpec as P

D = 512
HEADS = 8
SIDE = 64
SIDE_HEADS = 8
SIDE_FF = 256
STEP = 5


norm_eps = 1e-06
negative = -1000000000.0
beta_first = 0.9
beta_second = 0.99
adam_eps = 1e-08
learn_rate = 0.03
decay_rate = 0.01
clip_norm = 0.01
outer_rate = 0.7
outer_beta = 0.9


LOG2E = 1.4426950408889634
masked = -1e30

def dot(left, right):
    return jnp.dot(left, right, preferred_element_type=jnp.float32)

def dot_t(left, right):
    return lax.dot_general(left, right, (((1,), (1,)), ((), ())), preferred_element_type=jnp.float32)

def rms_rows(values, gain):
    return values * lax.rsqrt(jnp.mean(values * values, axis=1, keepdims=True) + norm_eps) * gain

def gelu(values):
    inner = values * (0.7978845608028654 + 0.035677408136300125 * (values * values))
    return (0.5 * values) * (1.0 + jnp.tanh(inner))

def lane_heads(query, keys, values, key_bias, causal_bias):
    lane = lax.broadcasted_iota(jnp.int32, (1, 128), 1)
    scale = 0.125 * LOG2E
    mixed = []
    for pair in range(4):
        span = slice(128 * pair, 128 * pair + 128)
        q_pair, k_pair, v_pair = query[:, span], keys[:, span], values[:, span]
        halves = []
        for side in range(2):
            own = (lane < 64) if side == 0 else (lane >= 64)
            spare = lane == (64 if side == 0 else 0)
            q_head = jnp.where(own, q_pair, spare.astype(jnp.bfloat16))
            k_head = jnp.where(own, k_pair, jnp.where(spare, key_bias, jnp.bfloat16(0)))
            scores = dot_t(q_head, k_head)
            if causal_bias is not None:
                scores = scores + causal_bias
            peak = jnp.max(scores, axis=1, keepdims=True)
            weight = jnp.exp2((scores - peak) * scale)
            total = jnp.sum(weight, axis=1, keepdims=True)
            halves.append(dot(weight.astype(jnp.bfloat16), v_pair) / total)
        mixed.append(jnp.where(lane < 64, halves[0], halves[1]).astype(jnp.bfloat16))
    return jnp.concatenate(mixed, axis=1)

def bias_column(count, valid):
    place = lax.broadcasted_iota(jnp.int32, (count, 1), 0)
    return jnp.where(place < valid, 0.0, masked).astype(jnp.bfloat16)

def frozen_ffn(state_ref, out_ref, gain, win_ref, wout_ref, finish):
    tokens = state_ref.shape[0]
    tile = 256
    def step(i, carry):
        at = pl.ds(i * tile, tile)
        state = state_ref[at]
        normed = rms_rows(state, gain).astype(jnp.bfloat16)
        total = state
        for start in range(0, win_ref.shape[1], 512):
            hidden = gelu(dot(normed, win_ref[:, start:start + 512])).astype(jnp.bfloat16)
            total = total + dot(hidden, wout_ref[start:start + 512])
        out_ref[at] = finish(total).astype(out_ref.dtype)
        return carry
    lax.fori_loop(0, tokens // tile, step, 0)

def fetch(pairs, sems):
    copies = [pltpu.make_async_copy(src, dst, sems.at[i]) for i, (src, dst) in enumerate(pairs)]
    for copy in copies:
        copy.start()
    return copies

def encoder_kernel(len_ref, x_ref, gains_ref, attn_hbm, win_hbm, wout_hbm, out_ref, attn_ref, win_ref, wout_ref, qkv_ref, state_ref, sems):
    first, second, third, fourth = fetch([(attn_hbm.at[0, :, :3 * D], attn_ref.at[:, :3 * D]), (attn_hbm.at[0, :, 3 * D:], attn_ref.at[:, 3 * D:]), (win_hbm.at[0], win_ref), (wout_hbm.at[0], wout_ref)], sems)
    tokens = x_ref.shape[0]
    x = x_ref[...].astype(jnp.float32)
    normed = rms_rows(x, gains_ref[0:1]).astype(jnp.bfloat16)
    first.wait()
    qkv_ref[...] = dot(normed, attn_ref[:, :3 * D]).astype(jnp.bfloat16)
    bias = bias_column(tokens, len_ref[0])
    second.wait()
    def step(i, carry):
        at = pl.ds(i * 256, 256)
        mixed = lane_heads(qkv_ref[at, :D], qkv_ref[:, D:2 * D], qkv_ref[:, 2 * D:], bias, None)
        state_ref[at] = x_ref[at].astype(jnp.float32) + dot(mixed, attn_ref[:, 3 * D:])
        return carry
    lax.fori_loop(0, tokens // 256, step, 0)
    third.wait()
    fourth.wait()
    frozen_ffn(state_ref, out_ref, gains_ref[1:2], win_ref, wout_ref, lambda v: rms_rows(v, gains_ref[2:3]))

def decoder_kernel(len_ref, x_ref, encoded_ref, gains_ref, attn_hbm, win_hbm, wout_hbm, out_ref, attn_ref, cross_ref, win_ref, wout_ref, kv_ref, state_ref, sems):
    first, second, third, fourth = fetch([(attn_hbm.at[1], attn_ref), (attn_hbm.at[2], cross_ref), (win_hbm.at[1], win_ref), (wout_hbm.at[1], wout_ref)], sems)
    tokens = x_ref.shape[0]
    sources = encoded_ref.shape[0]
    x = x_ref[...].astype(jnp.float32)
    normed = rms_rows(x, gains_ref[3:4]).astype(jnp.bfloat16)
    row = lax.broadcasted_iota(jnp.int32, (tokens, tokens), 0)
    column = lax.broadcasted_iota(jnp.int32, (tokens, tokens), 1)
    causal = jnp.where(column <= row, 0.0, masked)
    first.wait()
    qkv = dot(normed, attn_ref[:, :3 * D]).astype(jnp.bfloat16)
    mixed = lane_heads(qkv[:, :D], qkv[:, D:2 * D], qkv[:, 2 * D:], bias_column(tokens, len_ref[1]), causal)
    state = x + dot(mixed, attn_ref[:, 3 * D:])
    second.wait()
    kv_ref[...] = dot(encoded_ref[...], cross_ref[:, D:3 * D]).astype(jnp.bfloat16)
    normed = rms_rows(state, gains_ref[4:5]).astype(jnp.bfloat16)
    query = dot(normed, cross_ref[:, :D]).astype(jnp.bfloat16)
    mixed = lane_heads(query, kv_ref[:, :D], kv_ref[:, D:], bias_column(sources, len_ref[0]), None)
    state_ref[...] = state + dot(mixed, cross_ref[:, 3 * D:])
    third.wait()
    fourth.wait()
    frozen_ffn(state_ref, out_ref, gains_ref[5:6], win_ref, wout_ref, lambda v: v)

def cost(micros):
    return pl.CostEstimate(
        flops=int(micros * 8e8), bytes_accessed=int(micros * 3e6), transcendentals=0
    )


smem = pl.BlockSpec(memory_space=pltpu.SMEM)
vmem = pl.BlockSpec(memory_space=pltpu.VMEM)
hbm = pl.BlockSpec(memory_space=pl.ANY)
LIMIT = pltpu.CompilerParams(vmem_limit_bytes=56 * 2**20)

def encode(lens, x, attn, ffn_in, ffn_out, gains):
    tokens = x.shape[0]
    return pl.pallas_call(
        encoder_kernel,
        out_shape=jax.ShapeDtypeStruct((tokens, D), jnp.bfloat16),
        in_specs=[smem, vmem, vmem, hbm, hbm, hbm],
        out_specs=vmem,
        scratch_shapes=[pltpu.VMEM((D, 4 * D), jnp.bfloat16), pltpu.VMEM((D, 4 * D), jnp.bfloat16), pltpu.VMEM((4 * D, D), jnp.bfloat16),
            pltpu.VMEM((tokens, 3 * D), jnp.bfloat16), pltpu.VMEM((tokens, D), jnp.float32), pltpu.SemaphoreType.DMA((4,))],
        compiler_params=LIMIT,
        name="encoder",
        cost_estimate=cost(14),
    )(lens, x, gains, attn, ffn_in, ffn_out)

def decode(lens, x, encoded, attn, ffn_in, ffn_out, gains):
    tokens = x.shape[0]
    sources = encoded.shape[0]
    return pl.pallas_call(
        decoder_kernel,
        out_shape=jax.ShapeDtypeStruct((tokens, D), jnp.bfloat16),
        in_specs=[smem, vmem, vmem, vmem, hbm, hbm, hbm],
        out_specs=vmem,
        scratch_shapes=[pltpu.VMEM((D, 4 * D), jnp.bfloat16), pltpu.VMEM((D, 4 * D), jnp.bfloat16), pltpu.VMEM((D, 4 * D), jnp.bfloat16), pltpu.VMEM((4 * D, D), jnp.bfloat16),
            pltpu.VMEM((sources, 2 * D), jnp.bfloat16), pltpu.VMEM((tokens, D), jnp.float32), pltpu.SemaphoreType.DMA((4,))],
        compiler_params=LIMIT,
        name="decoder",
        cost_estimate=cost(10.5),
    )(lens, x, encoded, gains, attn, ffn_in, ffn_out)

def dot_l(left, right):
    return lax.dot_general(left, right, (((0,), (0,)), ((), ())), preferred_element_type=jnp.float32)

def rms_columns(values, gain):
    return values * lax.rsqrt(jnp.mean(values * values, axis=0, keepdims=True) + norm_eps) * gain

def rms_columns_back(values, gain, grad):
    inverse = lax.rsqrt(jnp.mean(values * values, axis=0, keepdims=True) + norm_eps)
    gained = grad * gain
    along = jnp.mean(values * gained, axis=0, keepdims=True)
    gain_grad = jnp.sum(grad * (values * inverse), axis=1, keepdims=True)
    return inverse * gained - values * (inverse * inverse * inverse * along), gain_grad

def gelu_back(values, grad):
    square = values * values
    tanh = jnp.tanh(values * (0.7978845608028654 + 0.035677408136300125 * square))
    slope = 0.5 * (1.0 + tanh) + (0.5 * values) * (1.0 - tanh * tanh) * (0.7978845608028654 + 0.107032224408900375 * square)
    return grad * slope

side_scale = (SIDE // SIDE_HEADS) ** -0.5

def keys_with_bias(keys_t, valid):
    count = keys_t.shape[1]
    place = lax.broadcasted_iota(jnp.int32, (64, count), 1)
    line = lax.broadcasted_iota(jnp.int32, (64, count), 0)
    bias = jnp.where((line == 0) & (place >= valid), masked, 0.0)
    return jnp.concatenate([keys_t.astype(jnp.float32), bias], axis=0).T.astype(jnp.bfloat16)

def head_query(query_t, head):
    line = lax.broadcasted_iota(jnp.int32, (64, 1), 0)
    own = jnp.where(line // 8 == head, query_t, 0.0)
    ones = jnp.broadcast_to(jnp.where(line == 0, 1.0, 0.0), own.shape)
    return jnp.concatenate([own, ones], axis=0).astype(jnp.bfloat16)

def rounded(values):
    return values.astype(jnp.bfloat16).astype(jnp.float32)

def causal_columns(count):
    key = lax.broadcasted_iota(jnp.int32, (count, count), 0)
    query = lax.broadcasted_iota(jnp.int32, (count, count), 1)
    return jnp.where(key <= query, 0.0, masked)

def side_heads(query_t, keys_t, values_t, valid, causal):
    keys = keys_with_bias(keys_t, valid)
    outs, sums = [], []
    for head in range(SIDE_HEADS):
        scores = dot(keys, head_query(query_t, head))
        if causal is not None:
            scores = scores + causal
        peak = jnp.max(scores, axis=0, keepdims=True)
        weight = jnp.exp2((scores - peak) * (side_scale * LOG2E))
        total = jnp.sum(weight, axis=0, keepdims=True)
        span = slice(8 * head, 8 * head + 8)
        outs.append(dot(values_t[span].astype(jnp.bfloat16), weight.astype(jnp.bfloat16)) / total)
        sums.append(peak * (side_scale * LOG2E) + jnp.log2(total))
    return jnp.concatenate(outs, axis=0), jnp.concatenate(sums, axis=0)

def side_heads_back(query_t, keys_t, values_t, sums, grad_t, valid, causal):
    keys = keys_with_bias(keys_t, valid)
    values = values_t.T.astype(jnp.bfloat16)
    line = lax.broadcasted_iota(jnp.int32, (64, 1), 0)
    grad_q, grad_k, grad_v = [], [], []
    for head in range(SIDE_HEADS):
        span = slice(8 * head, 8 * head + 8)
        scores = dot(keys, head_query(query_t, head))
        if causal is not None:
            scores = scores + causal
        weight = jnp.exp2(scores * (side_scale * LOG2E) - sums[head:head + 1])
        own_grad = jnp.where(line // 8 == head, grad_t, 0.0).astype(jnp.bfloat16)
        grad_w = rounded(dot(values, own_grad))
        along = jnp.sum(grad_w * weight, axis=0, keepdims=True)
        grad_s = (weight * (grad_w - along)).astype(jnp.bfloat16)
        grad_q.append(dot(keys_t[span].astype(jnp.bfloat16), grad_s))
        grad_k.append(dot_t(query_t[span].astype(jnp.bfloat16), grad_s))
        grad_v.append(dot_t(grad_t[span].astype(jnp.bfloat16), weight.astype(jnp.bfloat16)))
    return (jnp.concatenate(grad_q, axis=0) * side_scale, jnp.concatenate(grad_k, axis=0) * side_scale,
            jnp.concatenate(grad_v, axis=0))

def chosen_columns(tokens, positions_ref):
    token = lax.broadcasted_iota(jnp.int32, (tokens, positions_ref.shape[1]), 0)
    return jnp.where(token == positions_ref[...], 1.0, 0.0).astype(jnp.bfloat16)

def side_kernel(len_ref, src_ref, encoded_ref, tgt_ref, decoded_ref, positions_ref, down_ref, attn_in_ref, attn_out_ref, ffn_in_ref, ffn_out_ref, small_ref,
                picked_ref, enc_ref, dec_ref, enc_mixed_ref, self_mixed_ref, cross_mixed_ref, enc_sums_ref, self_sums_ref, cross_sums_ref):
    def gain(i):
        return small_ref[:, i:i + 1]

    def attend(which, query_n, key_n, valid, causal, mixed_ref, sums_ref):
        query = rounded(dot(attn_in_ref[which, :64], query_n))
        keyval = rounded(dot(attn_in_ref[which, 64:], key_n))
        mixed, sums = side_heads(query, keyval[:64], keyval[64:], valid, causal)
        mixed_b = mixed.astype(jnp.bfloat16)
        mixed_ref[...] = mixed_b
        sums_ref[...] = sums
        return dot(attn_out_ref[which], mixed_b)

    def ffn(which, normed):
        active = gelu(dot(ffn_in_ref[which], normed)).astype(jnp.bfloat16)
        return dot(ffn_out_ref[which], active)

    def norm(values, i):
        return rms_columns(values, gain(i)).astype(jnp.bfloat16)

    source_valid, target_valid = len_ref[0], len_ref[1]
    state = dot_t(down_ref[0], src_ref[...])
    enc_ref[0] = state
    normed = norm(state, 0)
    state = state + attend(0, normed, normed, source_valid, None, enc_mixed_ref, enc_sums_ref)
    enc_ref[1] = state
    state = state + ffn(0, norm(state, 1))
    enc_ref[2] = state
    joined = dot_t(down_ref[1], encoded_ref[...])
    enc_ref[3] = joined
    gate = jax.nn.sigmoid(gain(7))
    memory = norm(gate * joined + (1.0 - gate) * state, 2)
    flow = dot_t(down_ref[2], tgt_ref[...])
    dec_ref[0] = flow
    normed = norm(flow, 3)
    causal = causal_columns(flow.shape[1])
    flow = flow + attend(1, normed, normed, target_valid, causal, self_mixed_ref, self_sums_ref)
    dec_ref[1] = flow
    flow = flow + attend(2, norm(flow, 4), memory, source_valid, None, cross_mixed_ref, cross_sums_ref)
    dec_ref[2] = flow
    flow = flow + ffn(1, norm(flow, 5))
    dec_ref[3] = flow
    joined = dot_t(down_ref[3], decoded_ref[...])
    dec_ref[4] = joined
    gate = jax.nn.sigmoid(gain(8))
    top = norm(gate * joined + (1.0 - gate) * flow, 6)
    picked = dot(top, chosen_columns(flow.shape[1], positions_ref)).astype(jnp.bfloat16)
    picked_ref[...] = picked

def side(lens, src, encoded, tgt, decoded, positions, weights):
    s, t, p = src.shape[0], tgt.shape[0], positions.shape[1]
    f32, bf16 = jnp.float32, jnp.bfloat16
    shapes = [((64, p), bf16), ((4, 64, s), f32), ((5, 64, t), f32), ((64, s), bf16), ((64, t), bf16), ((64, t), bf16), ((8, s), f32), ((8, t), f32), ((8, t), f32)]
    return pl.pallas_call(
        side_kernel,
        out_shape=[jax.ShapeDtypeStruct(*item) for item in shapes],
        in_specs=[smem] + [vmem] * 11,
        out_specs=[vmem] * 9,
        compiler_params=LIMIT,
        name="side",
        cost_estimate=cost(14),
    )(lens, src, encoded, tgt, decoded, positions, *weights)

def back_kernel(*refs, started):
    (len_ref, src_ref, encoded_ref, tgt_ref, decoded_ref, positions_ref, attn_in_t_ref, ffn_in_t_ref, attn_in_ref, attn_out_ref, ffn_in_ref, ffn_out_ref, small_ref,
     enc_ref, dec_ref, enc_mixed_ref, self_mixed_ref, cross_mixed_ref, enc_sums_ref, self_sums_ref, cross_sums_ref, parts_ref) = refs[:22]
    before = refs[22:29] if started else (None,) * 7
    down_out, attn_in_out, in_rest_out, attn_out_out, ffn_in_out, ffn_out_out, small_out = refs[-7:]

    outs = {
        "down": (down_out, before[0]),
        "attn_in": (attn_in_out, before[1]),
        "in_rest": (in_rest_out, before[2]),
        "attn_out": (attn_out_out, before[3]),
        "ffn_in": (ffn_in_out, before[4]),
        "ffn_out": (ffn_out_out, before[5]),
    }

    def put(which, index, values):
        if values.shape[1] == 3 * SIDE:
            put("in_rest", index, values[:, 128:])
            values = values[:, :128]
        out, old = outs[which]
        out[index] = values if old is None else old[index] + values

    smalls = {}

    def gain(i):
        return small_ref[:, i:i + 1]

    def norm(values, i):
        return rms_columns(values, gain(i)).astype(jnp.bfloat16)

    def norm_back(values, i, grad):
        result, smalls[i] = rms_columns_back(values, gain(i), grad)
        return result

    def blend_back(i, joined, late, grad):
        gate = jax.nn.sigmoid(gain(i))
        smalls[i] = jnp.sum(grad * (joined - late), axis=1, keepdims=True) * (gate * (1.0 - gate))
        return gate * grad, (1.0 - gate) * grad

    def ffn_back(which, normed, grad):
        grad_b = grad.astype(jnp.bfloat16)
        hidden = dot(ffn_in_t_ref[which], normed)
        active = gelu(hidden).astype(jnp.bfloat16)
        put("ffn_out", which, dot_t(active, grad_b))
        grad_hidden = gelu_back(hidden, dot(ffn_out_ref[which], grad_b)).astype(jnp.bfloat16)
        put("ffn_in", which, dot_t(normed, grad_hidden))
        return dot(ffn_in_ref[which], grad_hidden)

    def attend_back(which, query_n, key_n, mixed_ref, sums_ref, grad, valid, causal):
        grad_b = grad.astype(jnp.bfloat16)
        put("attn_out", which, dot_t(mixed_ref[...], grad_b))
        grad_mixed = rounded(dot(attn_out_ref[which], grad_b))
        query = rounded(dot(attn_in_t_ref[which, :64], query_n))
        keyval = rounded(dot(attn_in_t_ref[which, 64:], key_n))
        grad_q, grad_k, grad_v = side_heads_back(query, keyval[:64], keyval[64:], sums_ref, grad_mixed, valid, causal)
        return grad_q.astype(jnp.bfloat16), jnp.concatenate([grad_k, grad_v], axis=0).astype(jnp.bfloat16)

    source_valid, target_valid = len_ref[0], len_ref[1]
    tokens = tgt_ref.shape[0]
    grad_picked = parts_ref[0].astype(jnp.float32)
    for i in range(1, parts_ref.shape[0]):
        grad_picked = grad_picked + parts_ref[i].astype(jnp.float32)
    chosen = chosen_columns(tokens, positions_ref)
    high = grad_picked.astype(jnp.bfloat16)
    low = (grad_picked - high.astype(jnp.float32)).astype(jnp.bfloat16)
    grad = dot_t(high, chosen) + dot_t(low, chosen)
    gate = jax.nn.sigmoid(gain(8))
    final = gate * dec_ref[4] + (1.0 - gate) * dec_ref[3]
    grad = norm_back(final, 6, grad)
    grad_joined, grad = blend_back(8, dec_ref[4], dec_ref[3], grad)
    put("down", 3, dot(grad_joined.astype(jnp.bfloat16), decoded_ref[...]))
    grad = grad + norm_back(dec_ref[2], 5, ffn_back(1, norm(dec_ref[2], 5), grad))
    gate = jax.nn.sigmoid(gain(7))
    final = gate * enc_ref[3] + (1.0 - gate) * enc_ref[2]
    memory = norm(final, 2)
    normed = norm(dec_ref[1], 4)
    grad_q, grad_kv = attend_back(2, normed, memory, cross_mixed_ref, cross_sums_ref, grad, source_valid, None)
    zero_q = jnp.zeros((128, tokens), jnp.bfloat16)
    zero_kv = jnp.zeros((64, src_ref.shape[0]), jnp.bfloat16)
    put("attn_in", 2, dot_t(normed, jnp.concatenate([grad_q, zero_q], axis=0)) + dot_t(memory, jnp.concatenate([zero_kv, grad_kv], axis=0)))
    weight = attn_in_ref[2]
    grad_memory = dot(weight, jnp.concatenate([zero_kv, grad_kv], axis=0))
    grad = grad + norm_back(dec_ref[1], 4, dot(weight, jnp.concatenate([grad_q, zero_q], axis=0)))
    normed = norm(dec_ref[0], 3)
    grad_q, grad_kv = attend_back(1, normed, normed, self_mixed_ref, self_sums_ref, grad, target_valid, causal_columns(tokens))
    grad_qkv = jnp.concatenate([grad_q, grad_kv], axis=0)
    put("attn_in", 1, dot_t(normed, grad_qkv))
    grad = grad + norm_back(dec_ref[0], 3, dot(attn_in_ref[1], grad_qkv))
    put("down", 2, dot(grad.astype(jnp.bfloat16), tgt_ref[...]))
    grad = norm_back(final, 2, grad_memory)
    grad_joined, grad = blend_back(7, enc_ref[3], enc_ref[2], grad)
    put("down", 1, dot(grad_joined.astype(jnp.bfloat16), encoded_ref[...]))
    grad = grad + norm_back(enc_ref[1], 1, ffn_back(0, norm(enc_ref[1], 1), grad))
    normed = norm(enc_ref[0], 0)
    grad_q, grad_kv = attend_back(0, normed, normed, enc_mixed_ref, enc_sums_ref, grad, source_valid, None)
    grad_qkv = jnp.concatenate([grad_q, grad_kv], axis=0)
    put("attn_in", 0, dot_t(normed, grad_qkv))
    grad = grad + norm_back(enc_ref[0], 0, dot(attn_in_ref[0], grad_qkv))
    put("down", 0, dot(grad.astype(jnp.bfloat16), src_ref[...]))
    lane = lax.broadcasted_iota(jnp.int32, (1, 128), 1)
    total = jnp.zeros((64, 128), jnp.float32) if before[6] is None else before[6][...]
    for i in range(9):
        total = total + jnp.where(lane == i, smalls[i], 0.0)
    small_out[...] = total

def side_back(lens, src, encoded, tgt, decoded, positions, weights, kept, parts, before):
    f32 = jnp.float32
    shapes = [(4, 64, 512), (3, 64, 128), (3, 64, 64), (3, 64, 64), (2, 64, 256), (2, 256, 64), (64, 128)]
    extra = list(before) if before is not None else []
    return pl.pallas_call(
        functools.partial(back_kernel, started=before is not None),
        out_shape=[jax.ShapeDtypeStruct(shape, f32) for shape in shapes],
        in_specs=[smem] + [vmem] * (21 + len(extra)),
        out_specs=[vmem] * 7,
        compiler_params=LIMIT,
        name="side_back",
        cost_estimate=cost(19),
    )(lens, src, encoded, tgt, decoded, positions, *weights, *kept, parts, *extra)


def swap(values, axis, distance):
    size = lax.axis_size(axis)
    return lax.ppermute(values, axis, [(i, i ^ distance) for i in range(size)])


def gather_peers(values, axis):
    return [values] + [swap(values, axis, s) for s in range(1, lax.axis_size(axis))]


def exchange(pieces, axis):
    return [pieces[0]] + [swap(pieces[s], axis, s) for s in range(1, lax.axis_size(axis))]


def tree_sum(terms):
    while len(terms) > 1:
        terms = [terms[i] + terms[i + 1] for i in range(0, len(terms), 2)]
    return terms[0]


def plan_kernel(rows, peers, cap, at_ref, ids_ref, slots_ref, column_ref, busy_ref):
    count = ids_ref.shape[1]
    ids = ids_ref[...].astype(jnp.float32)
    column = jnp.broadcast_to(ids, (8, count)).T[:, :1]
    column_ref[...] = column
    first_at = jnp.full((1, count), float(count), jnp.float32)
    for start in range(0, count, 256):
        place = (lax.broadcasted_iota(jnp.int32, (256, 1), 0) + start).astype(jnp.float32)
        same = column[start : start + 256] == ids
        first_at = jnp.minimum(
            first_at, jnp.min(jnp.where(same, place, float(count)), axis=0, keepdims=True)
        )
    first = first_at == lax.broadcasted_iota(jnp.int32, (1, count), 1).astype(jnp.float32)
    owner = jnp.zeros((1, count), jnp.int32)
    for peer in range(1, peers):
        owner = owner + jnp.where(ids_ref[...] >= peer * rows, 1, 0)
    owner = owner ^ at_ref[0]
    line = lax.broadcasted_iota(jnp.int32, (peers, count), 0)
    own = jnp.where((line == owner) & first, 1.0, 0.0)
    own_b = own.astype(jnp.bfloat16)
    before = jnp.where(
        lax.broadcasted_iota(jnp.int32, (128, 128), 0)
        < lax.broadcasted_iota(jnp.int32, (128, 128), 1),
        1.0,
        0.0,
    ).astype(jnp.bfloat16)
    seen = jnp.zeros((peers, 1), jnp.float32)
    ranks = []
    for start in range(0, count, 128):
        block = slice(start, start + 128)
        inside = dot(own_b[:, block], before) + seen
        ranks.append(jnp.sum(own[:, block] * (inside + 1.0), axis=0, keepdims=True) - 1.0)
        seen = seen + jnp.sum(own[:, block], axis=1, keepdims=True)
    busy_ref[...] = jnp.broadcast_to(jnp.max(seen, axis=0, keepdims=True), (8, 128)).astype(
        jnp.int32
    )
    rank = jnp.concatenate(ranks, axis=1) - at_ref[1].astype(jnp.float32)
    rank_column = jnp.broadcast_to(rank, (8, count)).T[:, :1]
    width = -(-cap // 128) * 128
    spot = lax.broadcasted_iota(jnp.int32, (1, width), 1).astype(jnp.float32)
    hit = jnp.where(rank_column == spot, 1.0, 0.0).astype(jnp.bfloat16)
    high = jnp.floor(ids * (1.0 / 256.0))
    low = ids - 256.0 * high
    filled = dot(own_b, hit)
    found = 256.0 * dot((own * high).astype(jnp.bfloat16), hit) + dot(
        (own * low).astype(jnp.bfloat16), hit
    )
    slots_ref[...] = jnp.where(filled > 0.5, found, -1.0).astype(jnp.int32)[:, :cap]


def plan(at, ids, rows, peers, cap):
    count = ids.shape[1]
    return pl.pallas_call(
        functools.partial(plan_kernel, rows, peers, cap),
        out_shape=[
            jax.ShapeDtypeStruct((peers, cap), jnp.int32),
            jax.ShapeDtypeStruct((count, 1), jnp.float32),
            jax.ShapeDtypeStruct((8, 128), jnp.int32),
        ],
        in_specs=[smem, vmem],
        out_specs=[vmem] * 3,
        compiler_params=LIMIT,
        name="plan",
        cost_estimate=cost(3.5),
    )(at, ids)


def expand_kernel(slots_ref, column_ref, came_ref, *out_refs):
    slots = slots_ref[...].astype(jnp.float32)
    base = 0
    for out in out_refs:
        for start in range(0, out.shape[0], 256):
            at = base + start
            pick = jnp.where(column_ref[at : at + 256] == slots, 1.0, 0.0).astype(jnp.bfloat16)
            out[start : start + 256] = dot(pick, came_ref[...]).astype(jnp.bfloat16)
        base = base + out.shape[0]


def expand(slots, column, came, sizes):
    width = came.shape[1]
    return pl.pallas_call(
        expand_kernel,
        out_shape=[jax.ShapeDtypeStruct((size, width), jnp.bfloat16) for size in sizes],
        in_specs=[vmem] * 3,
        out_specs=[vmem] * len(sizes),
        compiler_params=LIMIT,
        name="expand",
        cost_estimate=cost(3.8),
    )(slots, column, came)


def ask(pieces):
    size = pieces.shape[0]
    near = swap(pieces[1::2], "dp", 1)
    pairs = jnp.stack([pieces[0::2], near], axis=1)
    far = [pairs[:1]] + [swap(pairs[i : i + 1], "dp", 2 * i) for i in range(1, size // 2)]
    return jnp.concatenate(far).reshape(pieces.shape)


def answer(pieces):
    size = pieces.shape[0]
    pairs = pieces.reshape((size // 2, 2) + pieces.shape[1:])
    far = [pairs[:1]] + [swap(pairs[i : i + 1], "dp", 2 * i) for i in range(1, size // 2)]
    far = jnp.concatenate(far)
    near = swap(far[:, 1], "dp", 1)
    return jnp.stack([far[:, 0], near], axis=1).reshape(pieces.shape)


def embed_rows(ids, table, sizes, notes):
    size = lax.axis_size("dp")
    me = lax.axis_index("dp")
    rows = table.shape[0]
    count = ids.shape[1]
    cap = -(-(count * 5 // (size * 6)) // 16) * 16
    owners = jnp.arange(size, dtype=jnp.int32)[:, None] ^ me

    def one_round(start, extra):
        slots, column, busy = plan(jnp.stack([me, start]), ids, rows, size, cap)
        letter = jnp.maximum(slots - owners * rows, 0)
        if extra is not None:
            extra = jnp.concatenate([busy[0, :1], extra])
            extra = jnp.broadcast_to(extra[None], (size, extra.shape[0]))
            letter = jnp.concatenate([letter, extra], axis=1)
        asked = ask(letter)
        found = jnp.take(table, asked[:, :cap].reshape(-1), axis=0, mode="clip")
        came = answer(found.reshape(size, cap, -1)).reshape(size * cap, -1)
        result = expand(slots.reshape(1, -1), column, came, sizes)
        return tuple(result), asked[:, cap:], slots, found

    result, told, slots, found = one_round(jnp.int32(0), notes)
    most = jnp.full((8, 128), jnp.max(told[:, 0]), jnp.int32)
    distance = 1
    while distance < lax.axis_size("grp"):
        most = jnp.maximum(most, swap(most, "grp", distance))
        distance = 2 * distance

    def more(carry):
        extra = one_round(carry[0], None)[0]
        return (carry[0] + cap, tuple(old + new for old, new in zip(carry[1], extra)))

    result = lax.while_loop(lambda carry: carry[0] < most[0, 0], more, (jnp.int32(cap), result))[1]
    return result, told[:, 1:], slots, found


def gather_all(values):
    pair = jnp.stack([values, swap(values, "dp", 1)])
    far = [pair] + [swap(pair, "dp", s) for s in range(2, lax.axis_size("dp"), 2)]
    return jnp.concatenate(far)


def table_kernel(rows, table_ref, up_ref, turned_ref, weight_ref):
    block = table_ref.shape[0]
    place = lax.broadcasted_iota(jnp.int32, (block, 1), 0) + pl.program_id(0) * block
    table = jnp.where(place < rows, table_ref[...], jnp.bfloat16(0))
    line = lax.broadcasted_iota(jnp.int32, (table.shape[1], table.shape[1]), 0)
    column = lax.broadcasted_iota(jnp.int32, (table.shape[1], table.shape[1]), 1)
    unit = jnp.where(line == column, 1.0, 0.0).astype(jnp.bfloat16)
    turned_ref[...] = dot_t(unit, table).astype(jnp.bfloat16)
    lifted = dot_t(table, up_ref[...]) * (D ** (-0.5) * LOG2E)
    high = lifted.astype(jnp.bfloat16)
    weight_ref[:, :SIDE] = high
    weight_ref[:, SIDE:] = (lifted - high.astype(jnp.float32)).astype(jnp.bfloat16)


def table_parts(table, up_b):
    rows, width = table.shape
    padded = -(-rows // VOCAB_BLOCK) * VOCAB_BLOCK
    return pl.pallas_call(
        functools.partial(table_kernel, rows),
        out_shape=[
            jax.ShapeDtypeStruct((width, padded), jnp.bfloat16),
            jax.ShapeDtypeStruct((padded, 2 * SIDE), jnp.bfloat16),
        ],
        grid=(padded // VOCAB_BLOCK,),
        in_specs=[
            pl.BlockSpec((VOCAB_BLOCK, width), lambda i: (i, 0)),
            pl.BlockSpec((SIDE, width), lambda i: (0, 0)),
        ],
        out_specs=[
            pl.BlockSpec((width, VOCAB_BLOCK), lambda i: (0, i)),
            pl.BlockSpec((VOCAB_BLOCK, 2 * SIDE), lambda i: (i, 0)),
        ],
        compiler_params=LIMIT,
        name="table_parts",
        cost_estimate=cost(9),
    )(table, up_b)


VOCAB_BLOCK = 512
TILE = 256


def target_kernel(rows, turned_ref, target_ref, out_ref):
    target = target_ref[...]
    width, padded = turned_ref.shape
    chunk = min(1024, padded)
    total = jnp.zeros((width, target.shape[1]), jnp.float32)
    for start in range(0, padded, chunk):
        place = lax.broadcasted_iota(jnp.int32, (chunk, target.shape[1]), 0)
        hit = jnp.where(place == target - start, 1.0, 0.0).astype(jnp.bfloat16)
        total = total + dot(turned_ref[:, start : start + chunk], hit)
    out_ref[...] = total.astype(jnp.bfloat16)


def target_rows(turned, target, rows):
    width, padded = turned.shape
    many = target.shape[1]
    return pl.pallas_call(
        functools.partial(target_kernel, rows),
        out_shape=jax.ShapeDtypeStruct((width, many), jnp.bfloat16),
        grid=(many // TILE,),
        in_specs=[
            pl.BlockSpec((width, padded), lambda i: (0, 0)),
            pl.BlockSpec((1, TILE), lambda i: (0, i)),
        ],
        out_specs=pl.BlockSpec((width, TILE), lambda i: (0, i)),
        compiler_params=LIMIT,
        name="target_rows",
        cost_estimate=cost(13),
    )(turned, target)


def softmax_kernel(rows, weight_ref, turned_ref, picked_ref, mix_ref, stats_ref):
    padded = weight_ref.shape[0]
    chunk = min(1024, padded)
    picked = jnp.concatenate([picked_ref[...], picked_ref[...]], axis=0)
    tile = picked.shape[1]
    peak = total = mix = None
    for start in range(0, padded, chunk):
        logits = dot(weight_ref[start : start + chunk], picked)
        if start + chunk > rows:
            place = lax.broadcasted_iota(jnp.int32, (chunk, 1), 0)
            logits = jnp.where(place < rows - start, logits, -jnp.inf)
        above = jnp.max(logits, axis=0, keepdims=True)
        if peak is not None:
            above = jnp.maximum(peak, above)
        share = jnp.exp2(logits - above)
        part = dot(turned_ref[:, start : start + chunk], share.astype(jnp.bfloat16))
        amount = jnp.sum(share, axis=0, keepdims=True)
        if peak is None:
            total, mix = amount, part
        else:
            fade = jnp.exp2(peak - above)
            total = total * fade + amount
            mix = mix * fade + part
        peak = above
    mix_ref[...] = mix
    stats_ref[...] = jnp.concatenate([peak, total, jnp.zeros((6, tile), jnp.float32)], axis=0)


def softmax_part(weight, turned, picked, rows):
    padded = weight.shape[0]
    width = turned.shape[0]
    size, side_width, spots = picked.shape
    steps = spots // TILE
    return pl.pallas_call(
        functools.partial(softmax_kernel, rows),
        out_shape=[
            jax.ShapeDtypeStruct((width, size * spots), jnp.float32),
            jax.ShapeDtypeStruct((8, size * spots), jnp.float32),
        ],
        grid=(size * steps,),
        in_specs=[
            pl.BlockSpec((padded, 2 * SIDE), lambda i: (0, 0)),
            pl.BlockSpec((width, padded), lambda i: (0, 0)),
            pl.BlockSpec((None, side_width, TILE), lambda i: (i // steps, 0, i % steps)),
        ],
        out_specs=[
            pl.BlockSpec((width, TILE), lambda i: (0, i)),
            pl.BlockSpec((8, TILE), lambda i: (0, i)),
        ],
        compiler_params=LIMIT,
        name="softmax_part",
        cost_estimate=cost(22),
    )(weight, turned, picked)


def peer_block(distance, block):
    return (distance, 0, block ^ distance)


def finish_kernel(*refs):
    peers_refs = refs[:-8]
    mix_ref, goal_ref, mask_ref, up_ref, picked_ref, top_ref, up_grad_ref, loss_ref = refs[-8:]
    peaks = [ref[0:1] for ref in peers_refs]
    peak = functools.reduce(jnp.maximum, peaks)
    total = tree_sum([ref[1:2] * jnp.exp2(top - peak) for ref, top in zip(peers_refs, peaks)])
    lse = peak + jnp.log2(total)
    mask = mask_ref[...].astype(jnp.float32)
    goal = goal_ref[...]
    lifted = (mix_ref[...] * (jnp.exp2(peaks[0] - lse) * mask) - goal.astype(jnp.float32) * mask) * D ** (-0.5)
    lifted_b = lifted.astype(jnp.bfloat16)
    top_ref[...] = dot(up_ref[...], lifted_b).astype(jnp.bfloat16)
    picked = picked_ref[...]
    aim = jnp.sum(dot(up_ref[...], goal) * picked.astype(jnp.float32), axis=0, keepdims=True)
    here = jnp.where(pl.program_id(0) == 0, lse * (1.0 / LOG2E), 0.0)
    loss = mask * (here - aim * D ** (-0.5))

    @pl.when(pl.program_id(0) == 0)
    def _():
        up_grad_ref[...] = jnp.zeros_like(up_grad_ref)
        loss_ref[...] = jnp.zeros_like(loss_ref)

    up_grad_ref[...] += dot_t(picked, lifted_b)
    loss_ref[...] += jnp.broadcast_to(jnp.sum(loss, axis=1, keepdims=True), loss_ref.shape)


def head_finish(peers, mix, goal, mask, up_b, picked):
    size, side_width, spots = picked.shape
    width = mix.shape[0]
    return pl.pallas_call(
        finish_kernel,
        out_shape=[
            jax.ShapeDtypeStruct((size, side_width, spots), jnp.bfloat16),
            jax.ShapeDtypeStruct((side_width, width), jnp.float32),
            jax.ShapeDtypeStruct((8, 128), jnp.float32),
        ],
        grid=(size,),
        in_specs=[
            *[pl.BlockSpec((None, 2, spots), functools.partial(peer_block, s)) for s in range(size)],
            pl.BlockSpec((width, spots), lambda i: (0, i)),
            pl.BlockSpec((width, spots), lambda i: (0, i)),
            pl.BlockSpec((1, spots), lambda i: (0, i)),
            pl.BlockSpec((side_width, width), lambda i: (0, 0)),
            pl.BlockSpec((None, side_width, spots), lambda i: (i, 0, 0)),
        ],
        out_specs=[
            pl.BlockSpec((None, side_width, spots), lambda i: (i, 0, 0)),
            pl.BlockSpec((side_width, width), lambda i: (0, 0)),
            pl.BlockSpec((8, 128), lambda i: (0, 0)),
        ],
        compiler_params=LIMIT,
        name="head_finish",
        cost_estimate=cost(8),
    )(*[peers] * size, mix, goal, mask, up_b, picked)


def after(values, *others):
    return lax.optimization_barrier((values, others))[0]


def pair_lanes(even, odd):
    return jnp.concatenate([even, odd], axis=1)


def flatten_kernel(down_ref, in_ref, in_rest_ref, attn_out_ref, ffn_in_ref, ffn_out_ref, up_ref, small_ref, out_ref, turn_ref):
    at = 0
    for i in range(4):
        turn_ref[...] = down_ref[i].T
        out_ref[at : at + 256] = pair_lanes(
            turn_ref[pl.ds(0, 256, stride=2)], turn_ref[pl.ds(1, 256, stride=2)]
        )
        at += 256
    half = SIDE // 2
    for i in range(3):
        even = in_ref.at[i][pl.ds(0, half, stride=2)]
        odd = in_ref.at[i][pl.ds(1, half, stride=2)]
        even_rest = in_rest_ref.at[i][pl.ds(0, half, stride=2)]
        odd_rest = in_rest_ref.at[i][pl.ds(1, half, stride=2)]
        out_ref[pl.ds(at, half, stride=3)] = even
        out_ref[pl.ds(at + 1, half, stride=3)] = pair_lanes(even_rest, odd[:, :SIDE])
        out_ref[pl.ds(at + 2, half, stride=3)] = pair_lanes(odd[:, SIDE:], odd_rest)
        at += 3 * half
    for i in range(3):
        out_ref[at : at + half] = pair_lanes(
            attn_out_ref.at[i][pl.ds(0, half, stride=2)], attn_out_ref.at[i][pl.ds(1, half, stride=2)]
        )
        at += half
    for i in range(2):
        for j in range(2):
            out_ref[pl.ds(at + j, SIDE, stride=2)] = ffn_in_ref[i, :, 128 * j : 128 * j + 128]
        at += 2 * SIDE
    for i in range(2):
        out_ref[at : at + 128] = pair_lanes(
            ffn_out_ref.at[i][pl.ds(0, 128, stride=2)], ffn_out_ref.at[i][pl.ds(1, 128, stride=2)]
        )
        at += 128
    for j in range(4):
        out_ref[pl.ds(at + j, SIDE, stride=4)] = up_ref[:, 128 * j : 128 * j + 128]
    at += 4 * SIDE
    turn_ref[:128] = small_ref[...].T
    out_ref[at : at + 8] = pair_lanes(
        turn_ref[pl.ds(0, 8, stride=2)], turn_ref[pl.ds(1, 8, stride=2)]
    )
    at += 8
    out_ref[at:] = jnp.zeros((out_ref.shape[0] - at, 128), jnp.float32)


FLAT_ROWS = 2208


def flatten(pieces):
    return pl.pallas_call(
        flatten_kernel,
        out_shape=jax.ShapeDtypeStruct((FLAT_ROWS, 128), jnp.float32),
        in_specs=[vmem] * 8,
        out_specs=vmem,
        scratch_shapes=[pltpu.VMEM((512, 64), jnp.float32)],
        compiler_params=LIMIT,
        name="flatten",
        cost_estimate=cost(4),
    )(*pieces)


MAIN_ROWS = 2176


def rows_of(ref):
    main = 128 * MAIN_ROWS
    one = len(ref.shape) == 2
    load = (lambda a, b: ref[:, a:b]) if one else (lambda a, b: ref[a:b])
    rest = load(main, main + 512).reshape(4, 128)
    last = load(main + 512, main + 576).reshape(1, 64)
    return load(0, main).reshape(MAIN_ROWS, 128), jnp.concatenate(
        [rest, jnp.concatenate([last, jnp.zeros((1, 64), jnp.float32)], axis=1)], axis=0
    )


def put_rows(ref, main_values, rest_values):
    main = 128 * MAIN_ROWS
    if len(ref.shape) == 2:
        ref[:, :main] = main_values.reshape(1, main)
        ref[:, main : main + 512] = rest_values[:4].reshape(1, 512)
        ref[:, main + 512 : main + 576] = rest_values[4:5, :64]
    else:
        ref[:main] = main_values.reshape(main)
        ref[main : main + 512] = rest_values[:4].reshape(512)
        ref[main + 512 : main + 576] = rest_values[4:5, :64].reshape(64)


def adam_kernel(core_ref, count_ref, mine_ref, other_ref, first_ref, second_ref, inner_ref, anchor_ref, new_first_ref, new_second_ref, new_inner_ref, gap_ref, norm_ref, grad_ref):
    half = mine_ref.shape[0]
    core = core_ref[0]
    grad_ref[pl.ds(pl.multiple_of(core * half, 8), half)] = mine_ref[...]
    grad_ref[pl.ds(pl.multiple_of((1 - core) * half, 8), half)] = other_ref[...]
    mean = grad_ref[...] * (1.0 / count_ref[...][:1, :1])
    norm = jnp.sqrt(jnp.sum(jnp.sum(mean * mean, axis=0, keepdims=True), axis=1, keepdims=True))
    norm_ref[...] = jnp.broadcast_to(norm, norm_ref.shape)
    clipped = mean * jnp.minimum(1.0, clip_norm / norm)
    spans = ((0, MAIN_ROWS), (MAIN_ROWS, MAIN_ROWS + 5))
    news = []
    for span, first, second, inner, anchor in zip(
        spans, rows_of(first_ref), rows_of(second_ref), rows_of(inner_ref), rows_of(anchor_ref)
    ):
        part = clipped[span[0] : span[1]]
        new_first = beta_first * first + (1.0 - beta_first) * part
        new_second = beta_second * second + (1.0 - beta_second) * part * part
        fixed_one = new_first / (1.0 - beta_first**STEP)
        fixed_two = new_second / (1.0 - beta_second**STEP)
        new_inner = inner - learn_rate * (
            fixed_one / (jnp.sqrt(fixed_two) + adam_eps) + decay_rate * inner
        )
        news.append((new_first, new_second, new_inner))
        grad_ref[span[0] : span[1]] = anchor - new_inner
    for ref, main, rest in zip((new_first_ref, new_second_ref, new_inner_ref), news[0], news[1]):
        put_rows(ref, main, rest)
    gap_ref[...] = grad_ref[pl.ds(pl.multiple_of(core * half, 8), half)].astype(jnp.bfloat16)


def adam(core, count, mine, other, first, second, inner, anchor):
    flat = jax.ShapeDtypeStruct(first.shape, jnp.float32)
    return pl.pallas_call(
        adam_kernel,
        out_shape=[
            flat,
            flat,
            flat,
            jax.ShapeDtypeStruct(mine.shape, jnp.bfloat16),
            jax.ShapeDtypeStruct((8, 128), jnp.float32),
        ],
        in_specs=[smem] + [vmem] * 7,
        out_specs=[vmem] * 5,
        scratch_shapes=[pltpu.VMEM((FLAT_ROWS, 128), jnp.float32)],
        compiler_params=LIMIT,
        name="adam",
        cost_estimate=cost(7),
    )(core, count, mine, other, first, second, inner, anchor)


def outer_kernel(core_ref, mine_ref, other_ref, anchor_ref, momentum_ref, delta_ref, new_momentum_ref, new_anchor_ref, full_ref):
    half = mine_ref.shape[0]
    core = core_ref[0]
    full_ref[pl.ds(pl.multiple_of(core * half, 8), half)] = mine_ref[...]
    full_ref[pl.ds(pl.multiple_of((1 - core) * half, 8), half)] = other_ref[...]
    news = []
    for span, anchor, momentum in zip(
        ((0, MAIN_ROWS), (MAIN_ROWS, MAIN_ROWS + 5)), rows_of(anchor_ref), rows_of(momentum_ref)
    ):
        delta = full_ref[span[0] : span[1]]
        new_momentum = outer_beta * momentum + delta
        news.append((delta, new_momentum, anchor - outer_rate * (delta + outer_beta * new_momentum)))
    for ref, main, rest in zip((delta_ref, new_momentum_ref, new_anchor_ref), news[0], news[1]):
        put_rows(ref, main, rest)


def outer(core, mine, other, anchor, momentum):
    flat = jax.ShapeDtypeStruct(anchor.shape, jnp.float32)
    return pl.pallas_call(
        outer_kernel,
        out_shape=[flat] * 3,
        in_specs=[smem] + [vmem] * 4,
        out_specs=[vmem] * 3,
        scratch_shapes=[pltpu.VMEM((FLAT_ROWS, 128), jnp.float32)],
        compiler_params=LIMIT,
        name="outer",
        cost_estimate=cost(5),
    )(core, mine, other, anchor, momentum)


def unpack_kernel(flat_ref, down_ref, in_t_ref, out_t_ref, ffn_in_t_ref, ffn_out_t_ref, in_ref, out_ref, ffn_in_ref, ffn_out_ref, up_ref, small_ref, rows_ref, tall_ref):
    main, rest = rows_of(flat_ref)
    rows_ref[:MAIN_ROWS] = main
    rows_ref[MAIN_ROWS : MAIN_ROWS + 8] = jnp.concatenate([rest, jnp.zeros((3, 128), jnp.float32)], axis=0)

    def natural(at, count):
        packed = rows_ref[at : at + count // 2]
        tall_ref[pl.ds(0, count // 2, stride=2)] = packed[:, :SIDE]
        tall_ref[pl.ds(1, count // 2, stride=2)] = packed[:, SIDE:]
        return tall_ref[:count]

    at = 0
    for i in range(4):
        down_ref[i] = natural(at, 512).T.astype(jnp.bfloat16)
        at += 256
    half = SIDE // 2
    for i in range(3):
        one, two, three = [rows_ref[pl.ds(at + j, half, stride=3)] for j in range(3)]
        tall_ref[pl.ds(0, half, stride=2)] = one[:, :SIDE]
        tall_ref[pl.ds(1, half, stride=2)] = two[:, SIDE:]
        tall_ref[pl.ds(64, half, stride=2)] = one[:, SIDE:]
        tall_ref[pl.ds(65, half, stride=2)] = three[:, :SIDE]
        tall_ref[pl.ds(128, half, stride=2)] = two[:, :SIDE]
        tall_ref[pl.ds(129, half, stride=2)] = three[:, SIDE:]
        columns = [tall_ref[64 * j : 64 * j + 64] for j in range(3)]
        in_ref[i] = jnp.concatenate(columns, axis=1).astype(jnp.bfloat16)
        in_t_ref[i] = jnp.concatenate([column.T for column in columns], axis=0).astype(jnp.bfloat16)
        at += 3 * half
    for i in range(3):
        square = natural(at, SIDE)
        out_ref[i] = square.astype(jnp.bfloat16)
        out_t_ref[i] = square.T.astype(jnp.bfloat16)
        at += half
    for i in range(2):
        wide = jnp.concatenate([rows_ref[pl.ds(at + j, SIDE, stride=2)] for j in range(2)], axis=1)
        ffn_in_ref[i] = wide.astype(jnp.bfloat16)
        ffn_in_t_ref[i] = wide.T.astype(jnp.bfloat16)
        at += 2 * SIDE
    for i in range(2):
        tall = natural(at, 256)
        ffn_out_ref[i] = tall.astype(jnp.bfloat16)
        ffn_out_t_ref[i] = tall.T.astype(jnp.bfloat16)
        at += 128
    up_ref[...] = jnp.concatenate(
        [rows_ref[pl.ds(at + j, SIDE, stride=4)] for j in range(4)], axis=1
    ).astype(jnp.bfloat16)
    at += 4 * SIDE
    tall_ref[:128] = jnp.zeros((128, SIDE), jnp.float32)
    tall = natural(at, 16)
    tall_ref[16:128] = jnp.zeros((112, SIDE), jnp.float32)
    small_ref[...] = tall_ref[:128].T


def unpack_weights(flat):
    bf16 = jnp.bfloat16
    shapes = [
        (4, SIDE, D),
        (3, 3 * SIDE, SIDE),
        (3, SIDE, SIDE),
        (2, SIDE_FF, SIDE),
        (2, SIDE, SIDE_FF),
        (3, SIDE, 3 * SIDE),
        (3, SIDE, SIDE),
        (2, SIDE, SIDE_FF),
        (2, SIDE_FF, SIDE),
        (SIDE, D),
    ]
    return pl.pallas_call(
        unpack_kernel,
        out_shape=[jax.ShapeDtypeStruct(shape, bf16) for shape in shapes]
        + [jax.ShapeDtypeStruct((SIDE, 128), jnp.float32)],
        in_specs=[vmem],
        out_specs=[vmem] * 11,
        scratch_shapes=[
            pltpu.VMEM((MAIN_ROWS + 8, 128), jnp.float32),
            pltpu.VMEM((512, SIDE), jnp.float32),
        ],
        compiler_params=LIMIT,
        name="unpack",
        cost_estimate=cost(8),
    )(flat)


def per_device(
    source_ids,
    target_inputs,
    lengths,
    positions,
    target_ids,
    target_mask,
    table,
    backbone_attn,
    backbone_ffn_in,
    backbone_ffn_out,
    backbone_gains,
    inner_weights,
    first_moment,
    second_moment,
    anchor,
    outer_momentum,
):
    micro = source_ids.shape[0]
    src_tokens = source_ids.shape[2]
    tgt_tokens = target_inputs.shape[2]
    size = lax.axis_size("dp")
    me = lax.axis_index("dp")
    core = me & 1
    rows = table.shape[0]
    padded = -(-rows // 512) * 512
    sizes = [src_tokens] * micro + [tgt_tokens] * micro
    id_list = jnp.concatenate([source_ids.reshape(1, -1), target_inputs.reshape(1, -1)], axis=1)
    goals = jnp.concatenate([target_ids.reshape(-1), target_mask.reshape(-1)])
    embedded, told, slots, found = embed_rows(id_list, table, sizes, goals)
    down_t, in_t, out_t, ffn_in_t, ffn_out_t, attn_in, attn_out, ffn_in, ffn_out, up_b, small = (
        unpack_weights(after(inner_weights, slots))
    )
    ahead = [down_t, in_t, out_t, ffn_in_t, ffn_out_t, small]
    behind = [in_t, ffn_in_t, attn_in, attn_out, ffn_in, ffn_out, small]
    turned_table, weight = table_parts(after(table, found), up_b)
    told = told.reshape(size, 2, micro, -1).transpose(1, 2, 0, 3).reshape(2, micro, 1, -1)
    all_targets = told[0] - me * rows
    all_masks = told[1]
    count_total = jnp.sum(all_masks).astype(jnp.float32)
    aims = [target_rows(turned_table, all_targets[0], rows)]
    states, gathered = [], []
    previous = aims[0]
    for index in range(micro):
        embed_src, embed_tgt = embedded[index], embedded[micro + index]
        embed_src = after(embed_src, previous)
        lens = lengths[index, 0]
        encoded = encode(lens, embed_src, backbone_attn, backbone_ffn_in, backbone_ffn_out, backbone_gains)
        decoded = decode(lens, embed_tgt, encoded, backbone_attn, backbone_ffn_in, backbone_ffn_out, backbone_gains)
        picked_t, *kept = side(lens, embed_src, encoded, embed_tgt, decoded, positions[index], ahead)
        previous = picked_t
        gathered.append(gather_all(picked_t))
        states.append((lens, embed_src, encoded, embed_tgt, decoded, kept))
    heads = []
    for index in range(micro):
        mix, stats = softmax_part(after(weight, previous), turned_table, gathered[index], rows)
        previous = stats
        heads.append((mix, gather_all(stats[:2])))
    grads, grad_up, loss_part = None, 0.0, 0.0
    tops = []
    for index in range(micro):
        mix, peers = heads[index]
        if index > 0:
            aims.append(target_rows(turned_table, after(all_targets[index], previous), rows))
        top_parts, up_part, loss = head_finish(
            peers, after(mix, previous), aims[index], all_masks[index], up_b, gathered[index]
        )
        previous = top_parts
        grad_up = grad_up + up_part
        loss_part = loss_part + loss
        tops.append(answer(top_parts))
    losses = gather_all(loss_part)
    loss_total = tree_sum([losses[i, 0, 0] for i in range(size)])
    for index in range(micro):
        lens, embed_src, encoded, embed_tgt, decoded, kept = states[index]
        grads = side_back(
            lens, after(embed_src, previous), encoded, embed_tgt, decoded, positions[index], behind, kept, tops[index], grads
        )
    flat = flatten([*grads[:6], grad_up, grads[6]])
    half = FLAT_ROWS // 2
    halves = flat.reshape(2, half, 128)
    mine = lax.dynamic_index_in_dim(halves, core, 0, keepdims=False)
    other = lax.dynamic_index_in_dim(halves, 1 - core, 0, keepdims=False)
    sent = (mine + swap(other, "dp", 1)).astype(jnp.bfloat16)
    terms = [sent] + [swap(sent, "dp", s) for s in range(2, size, 2)]
    mine = tree_sum([term.astype(jnp.float32) for term in terms])
    other = swap(mine, "dp", 1)
    counts = jnp.full((8, 128), count_total)
    new_first, new_second, new_inner, gap, norm = adam(
        core[None], counts, mine, other, first_moment, second_moment, inner_weights, anchor
    )
    terms = gather_peers(gap, "grp")
    mine = tree_sum([term.astype(jnp.float32) for term in terms]) / lax.axis_size("grp")
    other = swap(mine, "dp", 1)
    delta, momentum, new_anchor = outer(core[None], mine, other, anchor, outer_momentum)
    return (
        loss_total[None],
        count_total[None],
        norm[0, :1],
        new_first,
        new_second,
        new_inner,
        delta,
        momentum,
        new_anchor,
    )


def solution(mesh):
    return jax.shard_map(
        per_device,
        mesh=mesh,
        in_specs=(
            P(None, ("grp", "dp"), None),
            P(None, ("grp", "dp"), None),
            P(None, ("grp", "dp"), None),
            P(None, ("grp", "dp"), None),
            P(None, ("grp", "dp"), None),
            P(None, ("grp", "dp"), None),
            P("dp", None),
            P(),
            P(),
            P(),
            P(),
            P("grp", None),
            P("grp", None),
            P("grp", None),
            P(),
            P(),
        ),
        out_specs=(
            P("grp"),
            P("grp"),
            P("grp"),
            P("grp", None),
            P("grp", None),
            P("grp", None),
            P(),
            P(),
            P(),
        ),
        check_vma=False,
    )
```

```python
import functools

import jax
import jax.numpy as jnp
from jax import lax
from jax.experimental import pallas as pl
from jax.experimental.pallas import tpu as pltpu
from jax.sharding import PartitionSpec as P

D = 512
HEADS = 8
SIDE = 64
SIDE_HEADS = 8
SIDE_FF = 256
STEP = 5


norm_eps = 1e-06
negative = -1000000000.0
beta_first = 0.9
beta_second = 0.99
adam_eps = 1e-08
learn_rate = 0.03
decay_rate = 0.01
clip_norm = 0.01
outer_rate = 0.7
outer_beta = 0.9


LOG2E = 1.4426950408889634
masked = -1e30

def dot(left, right):
    return jnp.dot(left, right, preferred_element_type=jnp.float32)

def dot_t(left, right):
    return lax.dot_general(left, right, (((1,), (1,)), ((), ())), preferred_element_type=jnp.float32)

def rms_rows(values, gain):
    return values * lax.rsqrt(jnp.mean(values * values, axis=1, keepdims=True) + norm_eps) * gain

def gelu(values):
    inner = values * (0.7978845608028654 + 0.035677408136300125 * (values * values))
    return (0.5 * values) * (1.0 + jnp.tanh(inner))

def lane_heads(query, keys, values, key_bias, causal_bias):
    lane = lax.broadcasted_iota(jnp.int32, (1, 128), 1)
    scale = 0.125 * LOG2E
    mixed = []
    for pair in range(4):
        span = slice(128 * pair, 128 * pair + 128)
        q_pair, k_pair, v_pair = query[:, span], keys[:, span], values[:, span]
        halves = []
        for side in range(2):
            own = (lane < 64) if side == 0 else (lane >= 64)
            spare = lane == (64 if side == 0 else 0)
            q_head = jnp.where(own, q_pair, spare.astype(jnp.bfloat16))
            k_head = jnp.where(own, k_pair, jnp.where(spare, key_bias, jnp.bfloat16(0)))
            scores = dot_t(q_head, k_head)
            if causal_bias is not None:
                scores = scores + causal_bias
            peak = jnp.max(scores, axis=1, keepdims=True)
            weight = jnp.exp2((scores - peak) * scale)
            total = jnp.sum(weight, axis=1, keepdims=True)
            halves.append(dot(weight.astype(jnp.bfloat16), v_pair) / total)
        mixed.append(jnp.where(lane < 64, halves[0], halves[1]).astype(jnp.bfloat16))
    return jnp.concatenate(mixed, axis=1)

def bias_column(count, valid):
    place = lax.broadcasted_iota(jnp.int32, (count, 1), 0)
    return jnp.where(place < valid, 0.0, masked).astype(jnp.bfloat16)

def frozen_ffn(state_ref, out_ref, gain, win_ref, wout_ref, finish):
    tokens = state_ref.shape[0]
    tile = 256
    def step(i, carry):
        at = pl.ds(i * tile, tile)
        state = state_ref[at]
        normed = rms_rows(state, gain).astype(jnp.bfloat16)
        total = state
        for start in range(0, win_ref.shape[1], 512):
            hidden = gelu(dot(normed, win_ref[:, start:start + 512])).astype(jnp.bfloat16)
            total = total + dot(hidden, wout_ref[start:start + 512])
        out_ref[at] = finish(total).astype(out_ref.dtype)
        return carry
    lax.fori_loop(0, tokens // tile, step, 0)

def fetch(pairs, sems):
    copies = [pltpu.make_async_copy(src, dst, sems.at[i]) for i, (src, dst) in enumerate(pairs)]
    for copy in copies:
        copy.start()
    return copies

def encoder_kernel(len_ref, x_ref, gains_ref, attn_hbm, win_hbm, wout_hbm, out_ref, attn_ref, win_ref, wout_ref, qkv_ref, state_ref, sems):
    first, second, third, fourth = fetch([(attn_hbm.at[0, :, :3 * D], attn_ref.at[:, :3 * D]), (attn_hbm.at[0, :, 3 * D:], attn_ref.at[:, 3 * D:]), (win_hbm.at[0], win_ref), (wout_hbm.at[0], wout_ref)], sems)
    tokens = x_ref.shape[0]
    x = x_ref[...].astype(jnp.float32)
    normed = rms_rows(x, gains_ref[0:1]).astype(jnp.bfloat16)
    first.wait()
    qkv_ref[...] = dot(normed, attn_ref[:, :3 * D]).astype(jnp.bfloat16)
    bias = bias_column(tokens, len_ref[0])
    second.wait()
    def step(i, carry):
        at = pl.ds(i * 256, 256)
        mixed = lane_heads(qkv_ref[at, :D], qkv_ref[:, D:2 * D], qkv_ref[:, 2 * D:], bias, None)
        state_ref[at] = x_ref[at].astype(jnp.float32) + dot(mixed, attn_ref[:, 3 * D:])
        return carry
    lax.fori_loop(0, tokens // 256, step, 0)
    third.wait()
    fourth.wait()
    frozen_ffn(state_ref, out_ref, gains_ref[1:2], win_ref, wout_ref, lambda v: rms_rows(v, gains_ref[2:3]))

def decoder_kernel(len_ref, x_ref, encoded_ref, gains_ref, attn_hbm, win_hbm, wout_hbm, out_ref, attn_ref, cross_ref, win_ref, wout_ref, kv_ref, state_ref, sems):
    first, second, third, fourth = fetch([(attn_hbm.at[1], attn_ref), (attn_hbm.at[2], cross_ref), (win_hbm.at[1], win_ref), (wout_hbm.at[1], wout_ref)], sems)
    tokens = x_ref.shape[0]
    sources = encoded_ref.shape[0]
    x = x_ref[...].astype(jnp.float32)
    normed = rms_rows(x, gains_ref[3:4]).astype(jnp.bfloat16)
    row = lax.broadcasted_iota(jnp.int32, (tokens, tokens), 0)
    column = lax.broadcasted_iota(jnp.int32, (tokens, tokens), 1)
    causal = jnp.where(column <= row, 0.0, masked)
    first.wait()
    qkv = dot(normed, attn_ref[:, :3 * D]).astype(jnp.bfloat16)
    mixed = lane_heads(qkv[:, :D], qkv[:, D:2 * D], qkv[:, 2 * D:], bias_column(tokens, len_ref[1]), causal)
    state = x + dot(mixed, attn_ref[:, 3 * D:])
    second.wait()
    kv_ref[...] = dot(encoded_ref[...], cross_ref[:, D:3 * D]).astype(jnp.bfloat16)
    normed = rms_rows(state, gains_ref[4:5]).astype(jnp.bfloat16)
    query = dot(normed, cross_ref[:, :D]).astype(jnp.bfloat16)
    mixed = lane_heads(query, kv_ref[:, :D], kv_ref[:, D:], bias_column(sources, len_ref[0]), None)
    state_ref[...] = state + dot(mixed, cross_ref[:, 3 * D:])
    third.wait()
    fourth.wait()
    frozen_ffn(state_ref, out_ref, gains_ref[5:6], win_ref, wout_ref, lambda v: v)

def cost(micros):
    return pl.CostEstimate(
        flops=int(micros * 8e8), bytes_accessed=int(micros * 3e6), transcendentals=0
    )


smem = pl.BlockSpec(memory_space=pltpu.SMEM)
vmem = pl.BlockSpec(memory_space=pltpu.VMEM)
hbm = pl.BlockSpec(memory_space=pl.ANY)
LIMIT = pltpu.CompilerParams(vmem_limit_bytes=56 * 2**20)

def encode(lens, x, attn, ffn_in, ffn_out, gains):
    tokens = x.shape[0]
    return pl.pallas_call(
        encoder_kernel,
        out_shape=jax.ShapeDtypeStruct((tokens, D), jnp.bfloat16),
        in_specs=[smem, vmem, vmem, hbm, hbm, hbm],
        out_specs=vmem,
        scratch_shapes=[pltpu.VMEM((D, 4 * D), jnp.bfloat16), pltpu.VMEM((D, 4 * D), jnp.bfloat16), pltpu.VMEM((4 * D, D), jnp.bfloat16),
            pltpu.VMEM((tokens, 3 * D), jnp.bfloat16), pltpu.VMEM((tokens, D), jnp.float32), pltpu.SemaphoreType.DMA((4,))],
        compiler_params=LIMIT,
        name="encoder",
        cost_estimate=cost(14),
    )(lens, x, gains, attn, ffn_in, ffn_out)

def decode(lens, x, encoded, attn, ffn_in, ffn_out, gains):
    tokens = x.shape[0]
    sources = encoded.shape[0]
    return pl.pallas_call(
        decoder_kernel,
        out_shape=jax.ShapeDtypeStruct((tokens, D), jnp.bfloat16),
        in_specs=[smem, vmem, vmem, vmem, hbm, hbm, hbm],
        out_specs=vmem,
        scratch_shapes=[pltpu.VMEM((D, 4 * D), jnp.bfloat16), pltpu.VMEM((D, 4 * D), jnp.bfloat16), pltpu.VMEM((D, 4 * D), jnp.bfloat16), pltpu.VMEM((4 * D, D), jnp.bfloat16),
            pltpu.VMEM((sources, 2 * D), jnp.bfloat16), pltpu.VMEM((tokens, D), jnp.float32), pltpu.SemaphoreType.DMA((4,))],
        compiler_params=LIMIT,
        name="decoder",
        cost_estimate=cost(10.5),
    )(lens, x, encoded, gains, attn, ffn_in, ffn_out)

def dot_l(left, right):
    return lax.dot_general(left, right, (((0,), (0,)), ((), ())), preferred_element_type=jnp.float32)

def rms_columns(values, gain):
    return values * lax.rsqrt(jnp.mean(values * values, axis=0, keepdims=True) + norm_eps) * gain

def rms_columns_back(values, gain, grad):
    inverse = lax.rsqrt(jnp.mean(values * values, axis=0, keepdims=True) + norm_eps)
    gained = grad * gain
    along = jnp.mean(values * gained, axis=0, keepdims=True)
    gain_grad = jnp.sum(grad * (values * inverse), axis=1, keepdims=True)
    return inverse * gained - values * (inverse * inverse * inverse * along), gain_grad

def gelu_back(values, grad):
    square = values * values
    tanh = jnp.tanh(values * (0.7978845608028654 + 0.035677408136300125 * square))
    slope = 0.5 * (1.0 + tanh) + (0.5 * values) * (1.0 - tanh * tanh) * (0.7978845608028654 + 0.107032224408900375 * square)
    return grad * slope

side_scale = (SIDE // SIDE_HEADS) ** -0.5

def keys_with_bias(keys_t, valid):
    count = keys_t.shape[1]
    place = lax.broadcasted_iota(jnp.int32, (64, count), 1)
    line = lax.broadcasted_iota(jnp.int32, (64, count), 0)
    bias = jnp.where((line == 0) & (place >= valid), masked, 0.0)
    return jnp.concatenate([keys_t.astype(jnp.float32), bias], axis=0).T.astype(jnp.bfloat16)

def head_query(query_t, head):
    line = lax.broadcasted_iota(jnp.int32, (64, 1), 0)
    own = jnp.where(line // 8 == head, query_t, 0.0)
    ones = jnp.broadcast_to(jnp.where(line == 0, 1.0, 0.0), own.shape)
    return jnp.concatenate([own, ones], axis=0).astype(jnp.bfloat16)

def rounded(values):
    return values.astype(jnp.bfloat16).astype(jnp.float32)

def causal_columns(count):
    key = lax.broadcasted_iota(jnp.int32, (count, count), 0)
    query = lax.broadcasted_iota(jnp.int32, (count, count), 1)
    return jnp.where(key <= query, 0.0, masked)

def side_heads(query_t, keys_t, values_t, valid, causal):
    keys = keys_with_bias(keys_t, valid)
    outs, sums = [], []
    for head in range(SIDE_HEADS):
        scores = dot(keys, head_query(query_t, head))
        if causal is not None:
            scores = scores + causal
        peak = jnp.max(scores, axis=0, keepdims=True)
        weight = jnp.exp2((scores - peak) * (side_scale * LOG2E))
        total = jnp.sum(weight, axis=0, keepdims=True)
        span = slice(8 * head, 8 * head + 8)
        outs.append(dot(values_t[span].astype(jnp.bfloat16), weight.astype(jnp.bfloat16)) / total)
        sums.append(peak * (side_scale * LOG2E) + jnp.log2(total))
    return jnp.concatenate(outs, axis=0), jnp.concatenate(sums, axis=0)

def side_heads_back(query_t, keys_t, values_t, sums, grad_t, valid, causal):
    keys = keys_with_bias(keys_t, valid)
    values = values_t.T.astype(jnp.bfloat16)
    line = lax.broadcasted_iota(jnp.int32, (64, 1), 0)
    grad_q, grad_k, grad_v = [], [], []
    for head in range(SIDE_HEADS):
        span = slice(8 * head, 8 * head + 8)
        scores = dot(keys, head_query(query_t, head))
        if causal is not None:
            scores = scores + causal
        weight = jnp.exp2(scores * (side_scale * LOG2E) - sums[head:head + 1])
        own_grad = jnp.where(line // 8 == head, grad_t, 0.0).astype(jnp.bfloat16)
        grad_w = rounded(dot(values, own_grad))
        along = jnp.sum(grad_w * weight, axis=0, keepdims=True)
        grad_s = (weight * (grad_w - along)).astype(jnp.bfloat16)
        grad_q.append(dot(keys_t[span].astype(jnp.bfloat16), grad_s))
        grad_k.append(dot_t(query_t[span].astype(jnp.bfloat16), grad_s))
        grad_v.append(dot_t(grad_t[span].astype(jnp.bfloat16), weight.astype(jnp.bfloat16)))
    return (jnp.concatenate(grad_q, axis=0) * side_scale, jnp.concatenate(grad_k, axis=0) * side_scale,
            jnp.concatenate(grad_v, axis=0))

def chosen_columns(tokens, positions_ref):
    token = lax.broadcasted_iota(jnp.int32, (tokens, positions_ref.shape[1]), 0)
    return jnp.where(token == positions_ref[...], 1.0, 0.0).astype(jnp.bfloat16)

def side_kernel(len_ref, src_ref, encoded_ref, tgt_ref, decoded_ref, positions_ref, down_ref, attn_in_ref, attn_out_ref, ffn_in_ref, ffn_out_ref, small_ref,
                picked_ref, enc_ref, dec_ref, enc_mixed_ref, self_mixed_ref, cross_mixed_ref, enc_sums_ref, self_sums_ref, cross_sums_ref):
    def gain(i):
        return small_ref[:, i:i + 1]

    def attend(which, query_n, key_n, valid, causal, mixed_ref, sums_ref):
        query = rounded(dot(attn_in_ref[which, :64], query_n))
        keyval = rounded(dot(attn_in_ref[which, 64:], key_n))
        mixed, sums = side_heads(query, keyval[:64], keyval[64:], valid, causal)
        mixed_b = mixed.astype(jnp.bfloat16)
        mixed_ref[...] = mixed_b
        sums_ref[...] = sums
        return dot(attn_out_ref[which], mixed_b)

    def ffn(which, normed):
        active = gelu(dot(ffn_in_ref[which], normed)).astype(jnp.bfloat16)
        return dot(ffn_out_ref[which], active)

    def norm(values, i):
        return rms_columns(values, gain(i)).astype(jnp.bfloat16)

    source_valid, target_valid = len_ref[0], len_ref[1]
    state = dot_t(down_ref[0], src_ref[...])
    enc_ref[0] = state
    normed = norm(state, 0)
    state = state + attend(0, normed, normed, source_valid, None, enc_mixed_ref, enc_sums_ref)
    enc_ref[1] = state
    state = state + ffn(0, norm(state, 1))
    enc_ref[2] = state
    joined = dot_t(down_ref[1], encoded_ref[...])
    enc_ref[3] = joined
    gate = jax.nn.sigmoid(gain(7))
    memory = norm(gate * joined + (1.0 - gate) * state, 2)
    flow = dot_t(down_ref[2], tgt_ref[...])
    dec_ref[0] = flow
    normed = norm(flow, 3)
    causal = causal_columns(flow.shape[1])
    flow = flow + attend(1, normed, normed, target_valid, causal, self_mixed_ref, self_sums_ref)
    dec_ref[1] = flow
    flow = flow + attend(2, norm(flow, 4), memory, source_valid, None, cross_mixed_ref, cross_sums_ref)
    dec_ref[2] = flow
    flow = flow + ffn(1, norm(flow, 5))
    dec_ref[3] = flow
    joined = dot_t(down_ref[3], decoded_ref[...])
    dec_ref[4] = joined
    gate = jax.nn.sigmoid(gain(8))
    top = norm(gate * joined + (1.0 - gate) * flow, 6)
    picked = dot(top, chosen_columns(flow.shape[1], positions_ref)).astype(jnp.bfloat16)
    picked_ref[...] = picked

def side(lens, src, encoded, tgt, decoded, positions, weights):
    s, t, p = src.shape[0], tgt.shape[0], positions.shape[1]
    f32, bf16 = jnp.float32, jnp.bfloat16
    shapes = [((64, p), bf16), ((4, 64, s), f32), ((5, 64, t), f32), ((64, s), bf16), ((64, t), bf16), ((64, t), bf16), ((8, s), f32), ((8, t), f32), ((8, t), f32)]
    return pl.pallas_call(
        side_kernel,
        out_shape=[jax.ShapeDtypeStruct(*item) for item in shapes],
        in_specs=[smem] + [vmem] * 11,
        out_specs=[vmem] * 9,
        compiler_params=LIMIT,
        name="side",
        cost_estimate=cost(14),
    )(lens, src, encoded, tgt, decoded, positions, *weights)

def back_kernel(*refs, started):
    (len_ref, src_ref, encoded_ref, tgt_ref, decoded_ref, positions_ref, attn_in_t_ref, ffn_in_t_ref, attn_in_ref, attn_out_ref, ffn_in_ref, ffn_out_ref, small_ref,
     enc_ref, dec_ref, enc_mixed_ref, self_mixed_ref, cross_mixed_ref, enc_sums_ref, self_sums_ref, cross_sums_ref, parts_ref) = refs[:22]
    before = refs[22:29] if started else (None,) * 7
    down_out, attn_in_out, in_rest_out, attn_out_out, ffn_in_out, ffn_out_out, small_out = refs[-7:]

    outs = {
        "down": (down_out, before[0]),
        "attn_in": (attn_in_out, before[1]),
        "in_rest": (in_rest_out, before[2]),
        "attn_out": (attn_out_out, before[3]),
        "ffn_in": (ffn_in_out, before[4]),
        "ffn_out": (ffn_out_out, before[5]),
    }

    def put(which, index, values):
        if values.shape[1] == 3 * SIDE:
            put("in_rest", index, values[:, 128:])
            values = values[:, :128]
        out, old = outs[which]
        out[index] = values if old is None else old[index] + values

    smalls = {}

    def gain(i):
        return small_ref[:, i:i + 1]

    def norm(values, i):
        return rms_columns(values, gain(i)).astype(jnp.bfloat16)

    def norm_back(values, i, grad):
        result, smalls[i] = rms_columns_back(values, gain(i), grad)
        return result

    def blend_back(i, joined, late, grad):
        gate = jax.nn.sigmoid(gain(i))
        smalls[i] = jnp.sum(grad * (joined - late), axis=1, keepdims=True) * (gate * (1.0 - gate))
        return gate * grad, (1.0 - gate) * grad

    def ffn_back(which, normed, grad):
        grad_b = grad.astype(jnp.bfloat16)
        hidden = dot(ffn_in_t_ref[which], normed)
        active = gelu(hidden).astype(jnp.bfloat16)
        put("ffn_out", which, dot_t(active, grad_b))
        grad_hidden = gelu_back(hidden, dot(ffn_out_ref[which], grad_b)).astype(jnp.bfloat16)
        put("ffn_in", which, dot_t(normed, grad_hidden))
        return dot(ffn_in_ref[which], grad_hidden)

    def attend_back(which, query_n, key_n, mixed_ref, sums_ref, grad, valid, causal):
        grad_b = grad.astype(jnp.bfloat16)
        put("attn_out", which, dot_t(mixed_ref[...], grad_b))
        grad_mixed = rounded(dot(attn_out_ref[which], grad_b))
        query = rounded(dot(attn_in_t_ref[which, :64], query_n))
        keyval = rounded(dot(attn_in_t_ref[which, 64:], key_n))
        grad_q, grad_k, grad_v = side_heads_back(query, keyval[:64], keyval[64:], sums_ref, grad_mixed, valid, causal)
        return grad_q.astype(jnp.bfloat16), jnp.concatenate([grad_k, grad_v], axis=0).astype(jnp.bfloat16)

    source_valid, target_valid = len_ref[0], len_ref[1]
    tokens = tgt_ref.shape[0]
    grad_picked = parts_ref[0].astype(jnp.float32)
    for i in range(1, parts_ref.shape[0]):
        grad_picked = grad_picked + parts_ref[i].astype(jnp.float32)
    chosen = chosen_columns(tokens, positions_ref)
    high = grad_picked.astype(jnp.bfloat16)
    low = (grad_picked - high.astype(jnp.float32)).astype(jnp.bfloat16)
    grad = dot_t(high, chosen) + dot_t(low, chosen)
    gate = jax.nn.sigmoid(gain(8))
    final = gate * dec_ref[4] + (1.0 - gate) * dec_ref[3]
    grad = norm_back(final, 6, grad)
    grad_joined, grad = blend_back(8, dec_ref[4], dec_ref[3], grad)
    put("down", 3, dot(grad_joined.astype(jnp.bfloat16), decoded_ref[...]))
    grad = grad + norm_back(dec_ref[2], 5, ffn_back(1, norm(dec_ref[2], 5), grad))
    gate = jax.nn.sigmoid(gain(7))
    final = gate * enc_ref[3] + (1.0 - gate) * enc_ref[2]
    memory = norm(final, 2)
    normed = norm(dec_ref[1], 4)
    grad_q, grad_kv = attend_back(2, normed, memory, cross_mixed_ref, cross_sums_ref, grad, source_valid, None)
    zero_q = jnp.zeros((128, tokens), jnp.bfloat16)
    zero_kv = jnp.zeros((64, src_ref.shape[0]), jnp.bfloat16)
    put("attn_in", 2, dot_t(normed, jnp.concatenate([grad_q, zero_q], axis=0)) + dot_t(memory, jnp.concatenate([zero_kv, grad_kv], axis=0)))
    weight = attn_in_ref[2]
    grad_memory = dot(weight, jnp.concatenate([zero_kv, grad_kv], axis=0))
    grad = grad + norm_back(dec_ref[1], 4, dot(weight, jnp.concatenate([grad_q, zero_q], axis=0)))
    normed = norm(dec_ref[0], 3)
    grad_q, grad_kv = attend_back(1, normed, normed, self_mixed_ref, self_sums_ref, grad, target_valid, causal_columns(tokens))
    grad_qkv = jnp.concatenate([grad_q, grad_kv], axis=0)
    put("attn_in", 1, dot_t(normed, grad_qkv))
    grad = grad + norm_back(dec_ref[0], 3, dot(attn_in_ref[1], grad_qkv))
    put("down", 2, dot(grad.astype(jnp.bfloat16), tgt_ref[...]))
    grad = norm_back(final, 2, grad_memory)
    grad_joined, grad = blend_back(7, enc_ref[3], enc_ref[2], grad)
    put("down", 1, dot(grad_joined.astype(jnp.bfloat16), encoded_ref[...]))
    grad = grad + norm_back(enc_ref[1], 1, ffn_back(0, norm(enc_ref[1], 1), grad))
    normed = norm(enc_ref[0], 0)
    grad_q, grad_kv = attend_back(0, normed, normed, enc_mixed_ref, enc_sums_ref, grad, source_valid, None)
    grad_qkv = jnp.concatenate([grad_q, grad_kv], axis=0)
    put("attn_in", 0, dot_t(normed, grad_qkv))
    grad = grad + norm_back(enc_ref[0], 0, dot(attn_in_ref[0], grad_qkv))
    put("down", 0, dot(grad.astype(jnp.bfloat16), src_ref[...]))
    lane = lax.broadcasted_iota(jnp.int32, (1, 128), 1)
    total = jnp.zeros((64, 128), jnp.float32) if before[6] is None else before[6][...]
    for i in range(9):
        total = total + jnp.where(lane == i, smalls[i], 0.0)
    small_out[...] = total

def side_back(lens, src, encoded, tgt, decoded, positions, weights, kept, parts, before):
    f32 = jnp.float32
    shapes = [(4, 64, 512), (3, 64, 128), (3, 64, 64), (3, 64, 64), (2, 64, 256), (2, 256, 64), (64, 128)]
    extra = list(before) if before is not None else []
    return pl.pallas_call(
        functools.partial(back_kernel, started=before is not None),
        out_shape=[jax.ShapeDtypeStruct(shape, f32) for shape in shapes],
        in_specs=[smem] + [vmem] * (21 + len(extra)),
        out_specs=[vmem] * 7,
        compiler_params=LIMIT,
        name="side_back",
        cost_estimate=cost(19),
    )(lens, src, encoded, tgt, decoded, positions, *weights, *kept, parts, *extra)


def swap(values, axis, distance):
    size = lax.axis_size(axis)
    return lax.ppermute(values, axis, [(i, i ^ distance) for i in range(size)])


def gather_peers(values, axis):
    return [values] + [swap(values, axis, s) for s in range(1, lax.axis_size(axis))]


def exchange(pieces, axis):
    return [pieces[0]] + [swap(pieces[s], axis, s) for s in range(1, lax.axis_size(axis))]


def tree_sum(terms):
    while len(terms) > 1:
        terms = [terms[i] + terms[i + 1] for i in range(0, len(terms), 2)]
    return terms[0]


def expand_kernel(slots_ref, column_ref, came_ref, *out_refs):
    slots = slots_ref[...].astype(jnp.float32)
    base = 0
    for out in out_refs:
        for start in range(0, out.shape[0], 256):
            at = base + start
            pick = jnp.where(column_ref[at : at + 256] == slots, 1.0, 0.0).astype(jnp.bfloat16)
            out[start : start + 256] = dot(pick, came_ref[...]).astype(jnp.bfloat16)
        base = base + out.shape[0]


def expand(slots, column, came, sizes):
    width = came.shape[1]
    return pl.pallas_call(
        expand_kernel,
        out_shape=[jax.ShapeDtypeStruct((size, width), jnp.bfloat16) for size in sizes],
        in_specs=[vmem] * 3,
        out_specs=[vmem] * len(sizes),
        compiler_params=LIMIT,
        name="expand",
        cost_estimate=cost(3.8),
    )(slots, column, came)


def ask(pieces):
    size = pieces.shape[0]
    near = swap(pieces[1::2], "dp", 1)
    pairs = jnp.stack([pieces[0::2], near], axis=1)
    far = [pairs[:1]] + [swap(pairs[i : i + 1], "dp", 2 * i) for i in range(1, size // 2)]
    return jnp.concatenate(far).reshape(pieces.shape)


def answer(pieces):
    size = pieces.shape[0]
    pairs = pieces.reshape((size // 2, 2) + pieces.shape[1:])
    far = [pairs[:1]] + [swap(pairs[i : i + 1], "dp", 2 * i) for i in range(1, size // 2)]
    far = jnp.concatenate(far)
    near = swap(far[:, 1], "dp", 1)
    return jnp.stack([far[:, 0], near], axis=1).reshape(pieces.shape)


def gather_all(values):
    pair = jnp.stack([values, swap(values, "dp", 1)])
    far = [pair] + [swap(pair, "dp", s) for s in range(2, lax.axis_size("dp"), 2)]
    return jnp.concatenate(far)


def owners_of(ids, rows, peers, me):
    owner = jnp.zeros(ids.shape, jnp.int32)
    for peer in range(1, peers):
        owner = owner + jnp.where(ids >= peer * rows, 1, 0)
    return owner ^ me


def ranks_within(own):
    peers, count = own.shape
    own_b = own.astype(jnp.bfloat16)
    before = jnp.where(
        lax.broadcasted_iota(jnp.int32, (128, 128), 0)
        < lax.broadcasted_iota(jnp.int32, (128, 128), 1),
        1.0,
        0.0,
    ).astype(jnp.bfloat16)
    seen = jnp.zeros((peers, 1), jnp.float32)
    ranks = []
    for start in range(0, count, 128):
        block = slice(start, start + 128)
        inside = dot(own_b[:, block], before) + seen
        ranks.append(jnp.sum(own[:, block] * (inside + 1.0), axis=0, keepdims=True) - 1.0)
        seen = seen + jnp.sum(own[:, block], axis=1, keepdims=True)
    return jnp.concatenate(ranks, axis=1), seen


def column_of(row):
    return jnp.broadcast_to(row, (8, row.shape[1])).T[:, :1]


def placed(own, values, hit):
    high = jnp.floor(values * (1.0 / 64.0))
    low = values - 64.0 * high
    return 64.0 * dot((own * high).astype(jnp.bfloat16), hit) + dot(
        (own * low).astype(jnp.bfloat16), hit
    )


def score_part(rows, peers, tokens, me, at_ref, goal_ref, mask_ref, token_ref, count_ref, entry_ref, info_ref):
    micro, spots = at_ref.shape
    token = lax.broadcasted_iota(jnp.int32, (tokens, 1), 0)
    token_f = token.astype(jnp.float32)
    spot_f = lax.broadcasted_iota(jnp.int32, (1, spots), 1).astype(jnp.float32)
    lower = jnp.where(
        lax.broadcasted_iota(jnp.int32, (tokens, tokens), 0)
        > lax.broadcasted_iota(jnp.int32, (tokens, tokens), 1),
        1.0,
        0.0,
    ).astype(jnp.bfloat16)
    goals, masks, slots, used = [], [], [], []
    for index in range(micro):
        mask = mask_ref[index : index + 1].astype(jnp.float32)
        met = jnp.where(token == at_ref[index : index + 1], mask, 0.0)
        times = jnp.sum(met, axis=1, keepdims=True)
        active = jnp.where(times > 0.0, 1.0, 0.0)
        wide = jnp.broadcast_to(active, (tokens, 128)).astype(jnp.bfloat16)
        slot = dot(lower, wide)[:, :1]
        here = jnp.where(slot == spot_f, active, 0.0)
        token_row = jnp.sum(here * (token_f + 1.0), axis=0, keepdims=True) - 1.0
        token_ref[index : index + 1] = token_row.astype(jnp.int32)
        count_ref[index : index + 1] = jnp.sum(here * times, axis=0, keepdims=True).astype(jnp.int32)
        slots.append(jnp.sum(met * slot, axis=0, keepdims=True) + float(index * spots))
        goals.append(goal_ref[index : index + 1])
        masks.append(mask)
        used.append(jnp.sum(active, axis=0, keepdims=True))
    goal, mask, slot = [jnp.concatenate(rows_, axis=1) for rows_ in (goals, masks, slots)]
    far = owners_of(goal, rows, peers, 0)
    local = (goal - far * rows).astype(jnp.float32)
    line = lax.broadcasted_iota(jnp.int32, (peers, goal.shape[1]), 0)
    own = jnp.where((line == (far ^ me)) & (mask > 0.0), 1.0, 0.0)
    rank, many = ranks_within(own)
    order = lax.broadcasted_iota(jnp.int32, (1, goal.shape[1]), 1).astype(jnp.float32)
    hit = jnp.where(column_of(rank) == order, 1.0, 0.0).astype(jnp.bfloat16)
    entry_ref[...] = placed(own, slot, hit).astype(jnp.int32) * 65536 + placed(own, local, hit).astype(
        jnp.int32
    )
    lane = lax.broadcasted_iota(jnp.int32, (peers, 128), 1)
    info = jnp.where(lane == 0, many, 0.0)
    for index in range(micro):
        info = jnp.where(lane == index + 1, used[index], info)
    info_ref[...] = info.astype(jnp.int32)


def plan_kernel(rows, peers, cap, tokens, at_ref, ids_ref, *refs):
    score_refs, (slots_ref, column_ref, busy_ref) = refs[:3], refs[3:6]
    count = ids_ref.shape[1]
    ids = ids_ref[...].astype(jnp.float32)
    column = column_of(ids)
    column_ref[...] = column
    first_at = jnp.full((1, count), float(count), jnp.float32)
    for start in range(0, count, 256):
        place = (lax.broadcasted_iota(jnp.int32, (256, 1), 0) + start).astype(jnp.float32)
        same = column[start : start + 256] == ids
        first_at = jnp.minimum(
            first_at, jnp.min(jnp.where(same, place, float(count)), axis=0, keepdims=True)
        )
    first = first_at == lax.broadcasted_iota(jnp.int32, (1, count), 1).astype(jnp.float32)
    owner = owners_of(ids_ref[...], rows, peers, at_ref[0])
    line = lax.broadcasted_iota(jnp.int32, (peers, count), 0)
    own = jnp.where((line == owner) & first, 1.0, 0.0)
    rank, seen = ranks_within(own)
    busy_ref[...] = jnp.broadcast_to(jnp.max(seen, axis=0, keepdims=True), (8, 128)).astype(
        jnp.int32
    )
    rank = rank - at_ref[1].astype(jnp.float32)
    width = -(-cap // 128) * 128
    spot = lax.broadcasted_iota(jnp.int32, (1, width), 1).astype(jnp.float32)
    hit = jnp.where(column_of(rank) == spot, 1.0, 0.0).astype(jnp.bfloat16)
    high = jnp.floor(ids * (1.0 / 256.0))
    low = ids - 256.0 * high
    filled = dot(own.astype(jnp.bfloat16), hit)
    found = 256.0 * dot((own * high).astype(jnp.bfloat16), hit) + dot(
        (own * low).astype(jnp.bfloat16), hit
    )
    slots_ref[...] = jnp.where(filled > 0.5, found, -1.0).astype(jnp.int32)[:, :cap]
    if len(refs) > 6:
        score_part(rows, peers, tokens, at_ref[0], *score_refs, *refs[6:])


def plan(at, ids, score, rows, peers, cap, tokens, scoring):
    count = ids.shape[1]
    micro, spots = score[0].shape
    shapes = [((peers, cap), jnp.int32), ((count, 1), jnp.float32), ((8, 128), jnp.int32)]
    if scoring:
        shapes += [
            ((micro, spots), jnp.int32),
            ((micro, spots), jnp.int32),
            ((peers, micro * spots), jnp.int32),
            ((peers, 128), jnp.int32),
        ]
    return pl.pallas_call(
        functools.partial(plan_kernel, rows, peers, cap, tokens),
        out_shape=[jax.ShapeDtypeStruct(*shape) for shape in shapes],
        in_specs=[smem] + [vmem] * 4,
        out_specs=[vmem] * len(shapes),
        compiler_params=LIMIT,
        name="plan",
        cost_estimate=cost(4),
    )(at, ids, *score)


def embed_rows(ids, table, sizes, score, tokens):
    size = lax.axis_size("dp")
    me = lax.axis_index("dp")
    rows = table.shape[0]
    count = ids.shape[1]
    micro, spots = score[0].shape
    cap = -(-(count * 5 // (size * 6)) // 16) * 16
    owners = jnp.arange(size, dtype=jnp.int32)[:, None] ^ me

    def one_round(start, scoring):
        at = jnp.stack([me, start])
        slots, column, busy, *extra = plan(at, ids, score, rows, size, cap, tokens, scoring)
        letter = jnp.maximum(slots - owners * rows, 0)
        if scoring:
            _, counts, entries, info = extra
            counts = jnp.broadcast_to(counts.reshape(1, -1), (size, micro * spots))
            busiest = jnp.broadcast_to(busy[:1, :1], (size, 1))
            letter = jnp.concatenate([letter, entries, counts, info[:, : micro + 1], busiest], axis=1)
        asked = ask(letter)
        found = jnp.take(table, asked[:, :cap].reshape(-1), axis=0, mode="clip")
        came = answer(found.reshape(size, cap, -1)).reshape(size * cap, -1)
        result = expand(slots.reshape(1, -1), column, came, sizes)
        return tuple(result), asked[:, cap:], slots, found, extra

    result, told, slots, found, extra = one_round(jnp.int32(0), True)
    most = jnp.full((8, 128), jnp.max(told[:, -1]), jnp.int32)
    distance = 1
    while distance < lax.axis_size("grp"):
        most = jnp.maximum(most, swap(most, "grp", distance))
        distance = 2 * distance

    def more(carry):
        again = one_round(carry[0], False)[0]
        return (carry[0] + cap, tuple(old + new for old, new in zip(carry[1], again)))

    result = lax.while_loop(lambda carry: carry[0] < most[0, 0], more, (jnp.int32(cap), result))[1]
    return result, told, slots, found, extra[0]


def table_kernel(rows, table_ref, up_ref, padded_ref, weight_ref):
    block = table_ref.shape[0]
    place = lax.broadcasted_iota(jnp.int32, (block, 1), 0) + pl.program_id(0) * block
    table = jnp.where(place < rows, table_ref[...], jnp.bfloat16(0))
    padded_ref[...] = table
    lifted = dot_t(table, up_ref[...]) * (D ** (-0.5) * LOG2E)
    high = lifted.astype(jnp.bfloat16)
    weight_ref[:, :SIDE] = high
    weight_ref[:, SIDE:] = (lifted - high.astype(jnp.float32)).astype(jnp.bfloat16)


VOCAB_BLOCK = 512
TILE = 512


def table_parts(table, up_b):
    rows, width = table.shape
    padded = -(-rows // VOCAB_BLOCK) * VOCAB_BLOCK
    return pl.pallas_call(
        functools.partial(table_kernel, rows),
        out_shape=[
            jax.ShapeDtypeStruct((padded, width), jnp.bfloat16),
            jax.ShapeDtypeStruct((padded, 2 * SIDE), jnp.bfloat16),
        ],
        grid=(padded // VOCAB_BLOCK,),
        in_specs=[
            pl.BlockSpec((VOCAB_BLOCK, width), lambda i: (i, 0)),
            pl.BlockSpec((SIDE, width), lambda i: (0, 0)),
        ],
        out_specs=[
            pl.BlockSpec((VOCAB_BLOCK, width), lambda i: (i, 0)),
            pl.BlockSpec((VOCAB_BLOCK, 2 * SIDE), lambda i: (i, 0)),
        ],
        compiler_params=LIMIT,
        name="table_parts",
        cost_estimate=cost(5),
    )(table, up_b)


def goals_kernel(spots, where_ref, many_ref, entry_ref, table_ref, out_ref, tall_ref, sum_ref, sem):
    peers = many_ref.shape[0]
    micro = entry_ref.shape[1] // spots
    tiles = where_ref[1]
    for start in range(0, table_ref.shape[0], VOCAB_BLOCK):
        tall_ref[start : start + VOCAB_BLOCK] = table_ref[start : start + VOCAB_BLOCK].astype(jnp.float32)

    def clear(i, carry):
        sum_ref[pl.ds(pl.multiple_of(i * TILE, TILE), TILE)] = jnp.zeros((TILE, sum_ref.shape[1]), jnp.float32)
        return carry

    lax.fori_loop(0, tiles, clear, 0)
    for peer in range(peers):
        base = 2 + (peer ^ where_ref[0]) * micro

        def add(j, carry):
            entry = entry_ref[peer, j]
            slot = entry // 65536
            local = entry - slot * 65536
            row = slot + where_ref[base]
            for index in range(1, micro):
                row = jnp.where(slot >= index * spots, slot - index * spots + where_ref[base + index], row)
            sum_ref[pl.ds(row, 1)] = sum_ref[pl.ds(row, 1)] + tall_ref[pl.ds(local, 1)]
            return carry

        lax.fori_loop(0, many_ref[peer], add, 0)

    def send(i, carry):
        at = pl.ds(pl.multiple_of(i * TILE, TILE), TILE)
        copy = pltpu.make_async_copy(sum_ref.at[at], out_ref.at[at], sem)
        copy.start()
        copy.wait()
        return carry

    lax.fori_loop(0, tiles, send, 0)


def goal_rows(where, many, entries, table_pad, spots):
    total = entries.shape[0] * entries.shape[1]
    padded, width = table_pad.shape
    return pl.pallas_call(
        functools.partial(goals_kernel, spots),
        out_shape=jax.ShapeDtypeStruct((total, width), jnp.float32),
        in_specs=[smem, smem, smem, vmem],
        out_specs=hbm,
        scratch_shapes=[
            pltpu.VMEM((padded, width), jnp.float32),
            pltpu.VMEM((total, width), jnp.float32),
            pltpu.SemaphoreType.DMA,
        ],
        compiler_params=LIMIT,
        name="goals",
        cost_estimate=cost(9),
    )(where, many, entries, table_pad)


def softmax_kernel(rows, where_ref, gathered_ref, count_ref, weight_ref, table_ref, mix_ref, stats_ref, packed_ref, all_ref):
    step = pl.program_id(0)
    peers, micro, _, spots = gathered_ref.shape
    tiles = where_ref[1]

    @pl.when(step == 0)
    def _():
        def clear(i, carry):
            all_ref[pl.ds(pl.multiple_of(i * TILE, TILE), TILE)] = jnp.zeros((TILE, 128), jnp.float32)
            return carry

        lax.fori_loop(0, tiles, clear, 0)
        for device in range(peers):
            for index in range(micro):
                peer = where_ref[0] ^ device
                block = jnp.concatenate(
                    [
                        gathered_ref[peer, index].astype(jnp.float32),
                        count_ref[peer, index : index + 1].astype(jnp.float32),
                        jnp.zeros((SIDE - 1, spots), jnp.float32),
                    ],
                    axis=0,
                )
                all_ref[pl.ds(where_ref[2 + device * micro + index], spots)] = block.T

    @pl.when(step < tiles)
    def _():
        mine = all_ref[pl.ds(pl.multiple_of(step * TILE, TILE), TILE)]
        packed_ref[...] = mine
        picked = jnp.concatenate([mine[:, :SIDE], mine[:, :SIDE]], axis=1).astype(jnp.bfloat16)
        padded = weight_ref.shape[0]
        chunk = min(1024, padded)
        peak = total = mix = None
        for start in range(0, padded, chunk):
            logits = dot_t(picked, weight_ref[start : start + chunk])
            if start + chunk > rows:
                place = lax.broadcasted_iota(jnp.int32, (1, chunk), 1)
                logits = jnp.where(place < rows - start, logits, -jnp.inf)
            above = jnp.max(logits, axis=1, keepdims=True)
            if peak is not None:
                above = jnp.maximum(peak, above)
            share = jnp.exp2(logits - above)
            part = dot(share.astype(jnp.bfloat16), table_ref[start : start + chunk])
            amount = jnp.sum(share, axis=1, keepdims=True)
            if peak is None:
                total, mix = amount, part
            else:
                fade = jnp.exp2(peak - above)
                total = total * fade + amount
                mix = mix * fade + part
            peak = above
        mix_ref[...] = mix
        lane = lax.broadcasted_iota(jnp.int32, (TILE, 128), 1)
        stats_ref[...] = jnp.where(lane == 0, peak, jnp.where(lane == 1, total, 0.0)).T[:8]


def in_use(i, where):
    return jnp.minimum(i, where[1] - 1)


def softmax_part(where, gathered, counts, weight, table_pad, rows):
    peers, micro, side_width, spots = gathered.shape
    padded, width = table_pad.shape
    total = peers * micro * spots
    return pl.pallas_call(
        functools.partial(softmax_kernel, rows),
        out_shape=[
            jax.ShapeDtypeStruct((total, width), jnp.float32),
            jax.ShapeDtypeStruct((8, total), jnp.float32),
            jax.ShapeDtypeStruct((total, 128), jnp.float32),
        ],
        grid_spec=pltpu.PrefetchScalarGridSpec(
            num_scalar_prefetch=1,
            grid=(total // TILE,),
            in_specs=[
                pl.BlockSpec((peers, micro, side_width, spots), lambda i, w: (0, 0, 0, 0)),
                pl.BlockSpec((peers, micro, spots), lambda i, w: (0, 0, 0)),
                pl.BlockSpec((padded, 2 * SIDE), lambda i, w: (0, 0)),
                pl.BlockSpec((padded, width), lambda i, w: (0, 0)),
            ],
            out_specs=[
                pl.BlockSpec((TILE, width), lambda i, w: (in_use(i, w), 0)),
                pl.BlockSpec((8, TILE), lambda i, w: (0, in_use(i, w))),
                pl.BlockSpec((TILE, 128), lambda i, w: (in_use(i, w), 0)),
            ],
            scratch_shapes=[pltpu.VMEM((total + spots, 128), jnp.float32)],
        ),
        compiler_params=LIMIT,
        name="softmax_part",
        cost_estimate=cost(22),
    )(where, gathered, counts, weight, table_pad)


def finish_kernel(where_ref, peers_ref, mix_ref, goal_ref, packed_ref, up_ref, top_ref, up_grad_ref, loss_ref, all_ref):
    step = pl.program_id(0)
    blocks, _, spots = top_ref.shape
    peers = peers_ref.shape[0]
    micro = blocks // peers
    tiles = where_ref[1]

    @pl.when(step == 0)
    def _():
        up_grad_ref[...] = jnp.zeros_like(up_grad_ref)
        loss_ref[...] = jnp.zeros_like(loss_ref)
        all_ref[...] = jnp.zeros_like(all_ref)

    @pl.when(step < tiles)
    def _():
        peaks = [peers_ref[i, 0:1] for i in range(peers)]
        peak = functools.reduce(jnp.maximum, peaks)
        total = tree_sum([peers_ref[i, 1:2] * jnp.exp2(peaks[i] - peak) for i in range(peers)])
        lse = peak + jnp.log2(total)
        rows = jnp.concatenate([jnp.exp2(peaks[0] - lse), lse, jnp.zeros((6, TILE), jnp.float32)], axis=0).T
        packed = packed_ref[...]
        times = packed[:, SIDE : SIDE + 1]
        picked = packed[:, :SIDE].astype(jnp.bfloat16)
        goal = goal_ref[...]
        lifted = (mix_ref[...] * (rows[:, :1] * times) - goal) * D ** (-0.5)
        lifted_b = lifted.astype(jnp.bfloat16)
        all_ref[pl.ds(pl.multiple_of(step * TILE, TILE), TILE), :SIDE] = dot_t(lifted_b, up_ref[...])
        up_grad_ref[...] += dot_l(picked, lifted_b)
        aim = jnp.sum(dot(picked, up_ref[...]) * goal, axis=1, keepdims=True) * D ** (-0.5)
        here = jnp.where(where_ref[0] == 0, times * rows[:, 1:2] * (1.0 / LOG2E), 0.0)
        loss = jnp.sum(here - aim, axis=0, keepdims=True)
        loss_ref[...] += jnp.broadcast_to(loss, loss_ref.shape)

    @pl.when(step == pl.num_programs(0) - 1)
    def _():
        for device in range(peers):
            for index in range(micro):
                block = all_ref[pl.ds(where_ref[2 + device * micro + index], spots)]
                top_ref[(where_ref[0] ^ device) * micro + index] = block.T[:SIDE].astype(jnp.bfloat16)


def head_finish(where, stats, mix, goals, packed, up_b, micro, spots):
    peers = stats.shape[0]
    total, width = mix.shape
    return pl.pallas_call(
        finish_kernel,
        out_shape=[
            jax.ShapeDtypeStruct((peers * micro, SIDE, spots), jnp.bfloat16),
            jax.ShapeDtypeStruct((SIDE, width), jnp.float32),
            jax.ShapeDtypeStruct((8, 128), jnp.float32),
        ],
        grid_spec=pltpu.PrefetchScalarGridSpec(
            num_scalar_prefetch=1,
            grid=(total // TILE,),
            in_specs=[
                pl.BlockSpec((peers, 2, TILE), lambda i, w: (0, 0, in_use(i, w))),
                pl.BlockSpec((TILE, width), lambda i, w: (in_use(i, w), 0)),
                pl.BlockSpec((TILE, width), lambda i, w: (in_use(i, w), 0)),
                pl.BlockSpec((TILE, 128), lambda i, w: (in_use(i, w), 0)),
                pl.BlockSpec((SIDE, width), lambda i, w: (0, 0)),
            ],
            out_specs=[
                pl.BlockSpec((peers * micro, SIDE, spots), lambda i, w: (0, 0, 0)),
                pl.BlockSpec((SIDE, width), lambda i, w: (0, 0)),
                pl.BlockSpec((8, 128), lambda i, w: (0, 0)),
            ],
            scratch_shapes=[pltpu.VMEM((total + spots, 128), jnp.float32)],
        ),
        compiler_params=LIMIT,
        name="head_finish",
        cost_estimate=cost(6),
    )(where, stats, mix, goals, packed, up_b)


def after(values, *others):
    return lax.optimization_barrier((values, others))[0]


def pair_lanes(even, odd):
    return jnp.concatenate([even, odd], axis=1)


def flatten_kernel(down_ref, in_ref, in_rest_ref, attn_out_ref, ffn_in_ref, ffn_out_ref, up_ref, small_ref, out_ref, turn_ref):
    at = 0
    for i in range(4):
        turn_ref[...] = down_ref[i].T
        out_ref[at : at + 256] = pair_lanes(
            turn_ref[pl.ds(0, 256, stride=2)], turn_ref[pl.ds(1, 256, stride=2)]
        )
        at += 256
    half = SIDE // 2
    for i in range(3):
        even = in_ref.at[i][pl.ds(0, half, stride=2)]
        odd = in_ref.at[i][pl.ds(1, half, stride=2)]
        even_rest = in_rest_ref.at[i][pl.ds(0, half, stride=2)]
        odd_rest = in_rest_ref.at[i][pl.ds(1, half, stride=2)]
        out_ref[pl.ds(at, half, stride=3)] = even
        out_ref[pl.ds(at + 1, half, stride=3)] = pair_lanes(even_rest, odd[:, :SIDE])
        out_ref[pl.ds(at + 2, half, stride=3)] = pair_lanes(odd[:, SIDE:], odd_rest)
        at += 3 * half
    for i in range(3):
        out_ref[at : at + half] = pair_lanes(
            attn_out_ref.at[i][pl.ds(0, half, stride=2)], attn_out_ref.at[i][pl.ds(1, half, stride=2)]
        )
        at += half
    for i in range(2):
        for j in range(2):
            out_ref[pl.ds(at + j, SIDE, stride=2)] = ffn_in_ref[i, :, 128 * j : 128 * j + 128]
        at += 2 * SIDE
    for i in range(2):
        out_ref[at : at + 128] = pair_lanes(
            ffn_out_ref.at[i][pl.ds(0, 128, stride=2)], ffn_out_ref.at[i][pl.ds(1, 128, stride=2)]
        )
        at += 128
    for j in range(4):
        out_ref[pl.ds(at + j, SIDE, stride=4)] = up_ref[:, 128 * j : 128 * j + 128]
    at += 4 * SIDE
    turn_ref[:128] = small_ref[...].T
    out_ref[at : at + 8] = pair_lanes(
        turn_ref[pl.ds(0, 8, stride=2)], turn_ref[pl.ds(1, 8, stride=2)]
    )
    at += 8
    out_ref[at:] = jnp.zeros((out_ref.shape[0] - at, 128), jnp.float32)


FLAT_ROWS = 2208


def flatten(pieces):
    return pl.pallas_call(
        flatten_kernel,
        out_shape=jax.ShapeDtypeStruct((FLAT_ROWS, 128), jnp.float32),
        in_specs=[vmem] * 8,
        out_specs=vmem,
        scratch_shapes=[pltpu.VMEM((512, 64), jnp.float32)],
        compiler_params=LIMIT,
        name="flatten",
        cost_estimate=cost(4),
    )(*pieces)


MAIN_ROWS = 2176


def rows_of(ref):
    main = 128 * MAIN_ROWS
    one = len(ref.shape) == 2
    load = (lambda a, b: ref[:, a:b]) if one else (lambda a, b: ref[a:b])
    rest = load(main, main + 512).reshape(4, 128)
    last = load(main + 512, main + 576).reshape(1, 64)
    return load(0, main).reshape(MAIN_ROWS, 128), jnp.concatenate(
        [rest, jnp.concatenate([last, jnp.zeros((1, 64), jnp.float32)], axis=1)], axis=0
    )


def put_rows(ref, main_values, rest_values):
    main = 128 * MAIN_ROWS
    if len(ref.shape) == 2:
        ref[:, :main] = main_values.reshape(1, main)
        ref[:, main : main + 512] = rest_values[:4].reshape(1, 512)
        ref[:, main + 512 : main + 576] = rest_values[4:5, :64]
    else:
        ref[:main] = main_values.reshape(main)
        ref[main : main + 512] = rest_values[:4].reshape(512)
        ref[main + 512 : main + 576] = rest_values[4:5, :64].reshape(64)


def adam_kernel(core_ref, count_ref, mine_ref, other_ref, first_ref, second_ref, inner_ref, anchor_ref, new_first_ref, new_second_ref, new_inner_ref, gap_ref, norm_ref, grad_ref):
    half = mine_ref.shape[0]
    core = core_ref[0]
    grad_ref[pl.ds(pl.multiple_of(core * half, 8), half)] = mine_ref[...]
    grad_ref[pl.ds(pl.multiple_of((1 - core) * half, 8), half)] = other_ref[...]
    mean = grad_ref[...] * (1.0 / count_ref[...][:1, :1])
    norm = jnp.sqrt(jnp.sum(jnp.sum(mean * mean, axis=0, keepdims=True), axis=1, keepdims=True))
    norm_ref[...] = jnp.broadcast_to(norm, norm_ref.shape)
    clipped = mean * jnp.minimum(1.0, clip_norm / norm)
    spans = ((0, MAIN_ROWS), (MAIN_ROWS, MAIN_ROWS + 5))
    news = []
    for span, first, second, inner, anchor in zip(
        spans, rows_of(first_ref), rows_of(second_ref), rows_of(inner_ref), rows_of(anchor_ref)
    ):
        part = clipped[span[0] : span[1]]
        new_first = beta_first * first + (1.0 - beta_first) * part
        new_second = beta_second * second + (1.0 - beta_second) * part * part
        fixed_one = new_first / (1.0 - beta_first**STEP)
        fixed_two = new_second / (1.0 - beta_second**STEP)
        new_inner = inner - learn_rate * (
            fixed_one / (jnp.sqrt(fixed_two) + adam_eps) + decay_rate * inner
        )
        news.append((new_first, new_second, new_inner))
        grad_ref[span[0] : span[1]] = anchor - new_inner
    for ref, main, rest in zip((new_first_ref, new_second_ref, new_inner_ref), news[0], news[1]):
        put_rows(ref, main, rest)
    gap_ref[...] = grad_ref[pl.ds(pl.multiple_of(core * half, 8), half)].astype(jnp.bfloat16)


def adam(core, count, mine, other, first, second, inner, anchor):
    flat = jax.ShapeDtypeStruct(first.shape, jnp.float32)
    return pl.pallas_call(
        adam_kernel,
        out_shape=[
            flat,
            flat,
            flat,
            jax.ShapeDtypeStruct(mine.shape, jnp.bfloat16),
            jax.ShapeDtypeStruct((8, 128), jnp.float32),
        ],
        in_specs=[smem] + [vmem] * 7,
        out_specs=[vmem] * 5,
        scratch_shapes=[pltpu.VMEM((FLAT_ROWS, 128), jnp.float32)],
        compiler_params=LIMIT,
        name="adam",
        cost_estimate=cost(7),
    )(core, count, mine, other, first, second, inner, anchor)


def outer_kernel(core_ref, mine_ref, other_ref, anchor_ref, momentum_ref, delta_ref, new_momentum_ref, new_anchor_ref, full_ref):
    half = mine_ref.shape[0]
    core = core_ref[0]
    full_ref[pl.ds(pl.multiple_of(core * half, 8), half)] = mine_ref[...]
    full_ref[pl.ds(pl.multiple_of((1 - core) * half, 8), half)] = other_ref[...]
    news = []
    for span, anchor, momentum in zip(
        ((0, MAIN_ROWS), (MAIN_ROWS, MAIN_ROWS + 5)), rows_of(anchor_ref), rows_of(momentum_ref)
    ):
        delta = full_ref[span[0] : span[1]]
        new_momentum = outer_beta * momentum + delta
        news.append((delta, new_momentum, anchor - outer_rate * (delta + outer_beta * new_momentum)))
    for ref, main, rest in zip((delta_ref, new_momentum_ref, new_anchor_ref), news[0], news[1]):
        put_rows(ref, main, rest)


def outer(core, mine, other, anchor, momentum):
    flat = jax.ShapeDtypeStruct(anchor.shape, jnp.float32)
    return pl.pallas_call(
        outer_kernel,
        out_shape=[flat] * 3,
        in_specs=[smem] + [vmem] * 4,
        out_specs=[vmem] * 3,
        scratch_shapes=[pltpu.VMEM((FLAT_ROWS, 128), jnp.float32)],
        compiler_params=LIMIT,
        name="outer",
        cost_estimate=cost(5),
    )(core, mine, other, anchor, momentum)


def unpack_kernel(flat_ref, down_ref, in_t_ref, out_t_ref, ffn_in_t_ref, ffn_out_t_ref, in_ref, out_ref, ffn_in_ref, ffn_out_ref, up_ref, small_ref, rows_ref, tall_ref):
    main, rest = rows_of(flat_ref)
    rows_ref[:MAIN_ROWS] = main
    rows_ref[MAIN_ROWS : MAIN_ROWS + 8] = jnp.concatenate([rest, jnp.zeros((3, 128), jnp.float32)], axis=0)

    def natural(at, count):
        packed = rows_ref[at : at + count // 2]
        tall_ref[pl.ds(0, count // 2, stride=2)] = packed[:, :SIDE]
        tall_ref[pl.ds(1, count // 2, stride=2)] = packed[:, SIDE:]
        return tall_ref[:count]

    at = 0
    for i in range(4):
        down_ref[i] = natural(at, 512).T.astype(jnp.bfloat16)
        at += 256
    half = SIDE // 2
    for i in range(3):
        one, two, three = [rows_ref[pl.ds(at + j, half, stride=3)] for j in range(3)]
        tall_ref[pl.ds(0, half, stride=2)] = one[:, :SIDE]
        tall_ref[pl.ds(1, half, stride=2)] = two[:, SIDE:]
        tall_ref[pl.ds(64, half, stride=2)] = one[:, SIDE:]
        tall_ref[pl.ds(65, half, stride=2)] = three[:, :SIDE]
        tall_ref[pl.ds(128, half, stride=2)] = two[:, :SIDE]
        tall_ref[pl.ds(129, half, stride=2)] = three[:, SIDE:]
        columns = [tall_ref[64 * j : 64 * j + 64] for j in range(3)]
        in_ref[i] = jnp.concatenate(columns, axis=1).astype(jnp.bfloat16)
        in_t_ref[i] = jnp.concatenate([column.T for column in columns], axis=0).astype(jnp.bfloat16)
        at += 3 * half
    for i in range(3):
        square = natural(at, SIDE)
        out_ref[i] = square.astype(jnp.bfloat16)
        out_t_ref[i] = square.T.astype(jnp.bfloat16)
        at += half
    for i in range(2):
        wide = jnp.concatenate([rows_ref[pl.ds(at + j, SIDE, stride=2)] for j in range(2)], axis=1)
        ffn_in_ref[i] = wide.astype(jnp.bfloat16)
        ffn_in_t_ref[i] = wide.T.astype(jnp.bfloat16)
        at += 2 * SIDE
    for i in range(2):
        tall = natural(at, 256)
        ffn_out_ref[i] = tall.astype(jnp.bfloat16)
        ffn_out_t_ref[i] = tall.T.astype(jnp.bfloat16)
        at += 128
    up_ref[...] = jnp.concatenate(
        [rows_ref[pl.ds(at + j, SIDE, stride=4)] for j in range(4)], axis=1
    ).astype(jnp.bfloat16)
    at += 4 * SIDE
    tall_ref[:128] = jnp.zeros((128, SIDE), jnp.float32)
    tall = natural(at, 16)
    tall_ref[16:128] = jnp.zeros((112, SIDE), jnp.float32)
    small_ref[...] = tall_ref[:128].T


def unpack_weights(flat):
    bf16 = jnp.bfloat16
    shapes = [
        (4, SIDE, D),
        (3, 3 * SIDE, SIDE),
        (3, SIDE, SIDE),
        (2, SIDE_FF, SIDE),
        (2, SIDE, SIDE_FF),
        (3, SIDE, 3 * SIDE),
        (3, SIDE, SIDE),
        (2, SIDE, SIDE_FF),
        (2, SIDE_FF, SIDE),
        (SIDE, D),
    ]
    return pl.pallas_call(
        unpack_kernel,
        out_shape=[jax.ShapeDtypeStruct(shape, bf16) for shape in shapes]
        + [jax.ShapeDtypeStruct((SIDE, 128), jnp.float32)],
        in_specs=[vmem],
        out_specs=[vmem] * 11,
        scratch_shapes=[
            pltpu.VMEM((MAIN_ROWS + 8, 128), jnp.float32),
            pltpu.VMEM((512, SIDE), jnp.float32),
        ],
        compiler_params=LIMIT,
        name="unpack",
        cost_estimate=cost(8),
    )(flat)


def per_device(
    source_ids,
    target_inputs,
    lengths,
    positions,
    target_ids,
    target_mask,
    table,
    backbone_attn,
    backbone_ffn_in,
    backbone_ffn_out,
    backbone_gains,
    inner_weights,
    first_moment,
    second_moment,
    anchor,
    outer_momentum,
):
    micro = source_ids.shape[0]
    src_tokens = source_ids.shape[2]
    tgt_tokens = target_inputs.shape[2]
    size = lax.axis_size("dp")
    me = lax.axis_index("dp")
    core = me & 1
    rows = table.shape[0]
    padded = -(-rows // 512) * 512
    sizes = [src_tokens] * micro + [tgt_tokens] * micro
    id_list = jnp.concatenate([source_ids.reshape(1, -1), target_inputs.reshape(1, -1)], axis=1)
    score = [positions[:, 0], target_ids[:, 0], target_mask[:, 0]]
    spots = positions.shape[2]
    embedded, told, slots, found, scored = embed_rows(id_list, table, sizes, score, tgt_tokens)
    down_t, in_t, out_t, ffn_in_t, ffn_out_t, attn_in, attn_out, ffn_in, ffn_out, up_b, small = (
        unpack_weights(after(inner_weights, slots))
    )
    ahead = [down_t, in_t, out_t, ffn_in_t, ffn_out_t, small]
    behind = [in_t, ffn_in_t, attn_in, attn_out, ffn_in, ffn_out, small]
    table_pad, weight = table_parts(after(table, found), up_b)
    entries = told[:, : micro * spots]
    counts = told[:, micro * spots : 2 * micro * spots].reshape(size, micro, spots)
    many = told[:, 2 * micro * spots]
    used = jnp.take(told[:, -1 - micro : -1], jnp.arange(size) ^ me, axis=0).reshape(-1)
    ends = jnp.cumsum(used)
    tiles = (ends[-1:] + TILE - 1) // TILE
    where = jnp.concatenate([me[None], tiles, ends - used]).astype(jnp.int32)
    count_total = jnp.sum(counts).astype(jnp.float32)
    goals = goal_rows(where, many, entries, table_pad, spots)
    states, picked = [], []
    previous = goals
    for index in range(micro):
        embed_src, embed_tgt = embedded[index], embedded[micro + index]
        embed_src = after(embed_src, previous)
        lens = lengths[index, 0]
        encoded = encode(lens, embed_src, backbone_attn, backbone_ffn_in, backbone_ffn_out, backbone_gains)
        decoded = decode(lens, embed_tgt, encoded, backbone_attn, backbone_ffn_in, backbone_ffn_out, backbone_gains)
        at = scored[index : index + 1]
        picked_t, *kept = side(lens, embed_src, encoded, embed_tgt, decoded, at, ahead)
        previous = picked_t
        picked.append(picked_t)
        states.append((lens, embed_src, encoded, embed_tgt, decoded, at, kept))
    gathered = gather_all(jnp.stack(picked)).reshape((size, micro) + picked[0].shape)
    mix, stats, packed = softmax_part(where, gathered, counts, weight, table_pad, rows)
    stats = gather_all(stats[:2]).reshape(size, 2, -1)
    top_parts, grad_up, loss_part = head_finish(where, stats, mix, goals, packed, up_b, micro, spots)
    tops = answer(top_parts.reshape((size, micro) + top_parts.shape[1:]))
    losses = gather_all(loss_part).reshape(size, 8, 128)
    loss_total = tree_sum([losses[i, 0, 0] for i in range(size)])
    grads = None
    for index in range(micro):
        lens, embed_src, encoded, embed_tgt, decoded, at, kept = states[index]
        grads = side_back(
            lens, after(embed_src, losses), encoded, embed_tgt, decoded, at, behind, kept, tops[:, index], grads
        )
    flat = flatten([*grads[:6], grad_up, grads[6]])
    half = FLAT_ROWS // 2
    halves = flat.reshape(2, half, 128)
    mine = lax.dynamic_index_in_dim(halves, core, 0, keepdims=False)
    other = lax.dynamic_index_in_dim(halves, 1 - core, 0, keepdims=False)
    sent = (mine + swap(other, "dp", 1)).astype(jnp.bfloat16)
    terms = [sent] + [swap(sent, "dp", s) for s in range(2, size, 2)]
    mine = tree_sum([term.astype(jnp.float32) for term in terms])
    other = swap(mine, "dp", 1)
    counts = jnp.full((8, 128), count_total)
    new_first, new_second, new_inner, gap, norm = adam(
        core[None], counts, mine, other, first_moment, second_moment, inner_weights, anchor
    )
    terms = gather_peers(gap, "grp")
    mine = tree_sum([term.astype(jnp.float32) for term in terms]) / lax.axis_size("grp")
    other = swap(mine, "dp", 1)
    delta, momentum, new_anchor = outer(core[None], mine, other, anchor, outer_momentum)
    return (
        loss_total[None],
        count_total[None],
        norm[0, :1],
        new_first,
        new_second,
        new_inner,
        delta,
        momentum,
        new_anchor,
    )


def solution(mesh):
    return jax.shard_map(
        per_device,
        mesh=mesh,
        in_specs=(
            P(None, ("grp", "dp"), None),
            P(None, ("grp", "dp"), None),
            P(None, ("grp", "dp"), None),
            P(None, ("grp", "dp"), None),
            P(None, ("grp", "dp"), None),
            P(None, ("grp", "dp"), None),
            P("dp", None),
            P(),
            P(),
            P(),
            P(),
            P("grp", None),
            P("grp", None),
            P("grp", None),
            P(),
            P(),
        ),
        out_specs=(
            P("grp"),
            P("grp"),
            P("grp"),
            P("grp", None),
            P("grp", None),
            P("grp", None),
            P(),
            P(),
            P(),
        ),
        check_vma=False,
    )
```

```python
import functools

import jax
import jax.numpy as jnp
from jax import lax
from jax.experimental import pallas as pl
from jax.experimental.pallas import tpu as pltpu
from jax.sharding import PartitionSpec as P

D = 512
HEADS = 8
SIDE = 64
SIDE_HEADS = 8
SIDE_FF = 256
STEP = 5


norm_eps = 1e-06
negative = -1000000000.0
beta_first = 0.9
beta_second = 0.99
adam_eps = 1e-08
learn_rate = 0.03
decay_rate = 0.01
clip_norm = 0.01
outer_rate = 0.7
outer_beta = 0.9


LOG2E = 1.4426950408889634
masked = -1e30

def dot(left, right):
    return jnp.dot(left, right, preferred_element_type=jnp.float32)

def dot_t(left, right):
    return lax.dot_general(left, right, (((1,), (1,)), ((), ())), preferred_element_type=jnp.float32)

def rms_rows(values, gain):
    return values * lax.rsqrt(jnp.mean(values * values, axis=1, keepdims=True) + norm_eps) * gain

def gelu(values):
    inner = values * (0.7978845608028654 + 0.035677408136300125 * (values * values))
    return (0.5 * values) * (1.0 + jnp.tanh(inner))

def lane_heads(query, keys, values, key_bias, causal_bias):
    lane = lax.broadcasted_iota(jnp.int32, (1, 128), 1)
    scale = 0.125 * LOG2E
    mixed = []
    for pair in range(4):
        span = slice(128 * pair, 128 * pair + 128)
        q_pair, k_pair, v_pair = query[:, span], keys[:, span], values[:, span]
        halves = []
        for side in range(2):
            own = (lane < 64) if side == 0 else (lane >= 64)
            spare = lane == (64 if side == 0 else 0)
            q_head = jnp.where(own, q_pair, spare.astype(jnp.bfloat16))
            k_head = jnp.where(own, k_pair, jnp.where(spare, key_bias, jnp.bfloat16(0)))
            scores = dot_t(q_head, k_head)
            if causal_bias is not None:
                scores = scores + causal_bias
            peak = jnp.max(scores, axis=1, keepdims=True)
            weight = jnp.exp2((scores - peak) * scale)
            total = jnp.sum(weight, axis=1, keepdims=True)
            halves.append(dot(weight.astype(jnp.bfloat16), v_pair) / total)
        mixed.append(jnp.where(lane < 64, halves[0], halves[1]).astype(jnp.bfloat16))
    return jnp.concatenate(mixed, axis=1)

def bias_column(count, valid):
    place = lax.broadcasted_iota(jnp.int32, (count, 1), 0)
    return jnp.where(place < valid, 0.0, masked).astype(jnp.bfloat16)

def fetch(pairs, sems):
    copies = [pltpu.make_async_copy(src, dst, sems.at[i]) for i, (src, dst) in enumerate(pairs)]
    for copy in copies:
        copy.start()
    return copies

def frozen_ffn(state_ref, out_ref, gain, win_ref, wout_ref, finish):
    tile = 512

    def step(i, carry):
        at = pl.ds(pl.multiple_of(i * tile, tile), tile)
        state = state_ref[at]
        normed = rms_rows(state, gain).astype(jnp.bfloat16)
        total = state
        for start in range(0, win_ref.shape[1], 512):
            hidden = gelu(dot(normed, win_ref[:, start : start + 512])).astype(jnp.bfloat16)
            total = total + dot(hidden, wout_ref[start : start + 512])
        out_ref[at] = finish(total).astype(out_ref.dtype)
        return carry

    lax.fori_loop(0, state_ref.shape[0] // tile, step, 0)


def encoder_kernel(
    len_ref, x_ref, gains_ref, attn_hbm, win_hbm, wout_hbm, out_ref, attn_ref, win_ref, wout_ref, qkv_ref, state_ref, sems
):
    first, second, third, fourth = fetch(
        [
            (attn_hbm.at[0, :, : 3 * D], attn_ref.at[:, : 3 * D]),
            (attn_hbm.at[0, :, 3 * D :], attn_ref.at[:, 3 * D :]),
            (win_hbm.at[0], win_ref),
            (wout_hbm.at[0], wout_ref),
        ],
        sems,
    )
    micro = len_ref.shape[0]
    tokens = x_ref.shape[0] // micro
    normed = rms_rows(x_ref[...].astype(jnp.float32), gains_ref[0:1]).astype(jnp.bfloat16)
    first.wait()
    qkv_ref[...] = dot(normed, attn_ref[:, : 3 * D]).astype(jnp.bfloat16)
    second.wait()

    def step(i, carry):
        at = pl.ds(pl.multiple_of(i * tokens, tokens), tokens)
        bias = bias_column(tokens, len_ref[i, 0])
        mixed = lane_heads(qkv_ref[at, :D], qkv_ref[at, D : 2 * D], qkv_ref[at, 2 * D :], bias, None)
        state_ref[at] = x_ref[at].astype(jnp.float32) + dot(mixed, attn_ref[:, 3 * D :])
        return carry

    lax.fori_loop(0, micro, step, 0)
    third.wait()
    fourth.wait()
    frozen_ffn(
        state_ref, out_ref, gains_ref[1:2], win_ref, wout_ref, lambda v: rms_rows(v, gains_ref[2:3])
    )


def decoder_kernel(
    len_ref, x_ref, encoded_ref, gains_ref, attn_hbm, win_hbm, wout_hbm, out_ref, attn_ref, cross_ref, win_ref, wout_ref, kv_ref, state_ref, sems
):
    first, second, third, fourth = fetch(
        [
            (attn_hbm.at[1], attn_ref),
            (attn_hbm.at[2], cross_ref),
            (win_hbm.at[1], win_ref),
            (wout_hbm.at[1], wout_ref),
        ],
        sems,
    )
    micro = len_ref.shape[0]
    tokens = x_ref.shape[0] // micro
    sources = encoded_ref.shape[0] // micro
    x = x_ref[...].astype(jnp.float32)
    normed = rms_rows(x, gains_ref[3:4]).astype(jnp.bfloat16)
    row = lax.broadcasted_iota(jnp.int32, (tokens, tokens), 0)
    column = lax.broadcasted_iota(jnp.int32, (tokens, tokens), 1)
    causal = jnp.where(column <= row, 0.0, masked)
    first.wait()
    qkv = dot(normed, attn_ref[:, : 3 * D]).astype(jnp.bfloat16)
    mixed = []
    for i in range(micro):
        own = qkv[i * tokens : (i + 1) * tokens]
        bias = bias_column(tokens, len_ref[i, 1])
        mixed.append(lane_heads(own[:, :D], own[:, D : 2 * D], own[:, 2 * D :], bias, causal))
    state = x + dot(jnp.concatenate(mixed, axis=0), attn_ref[:, 3 * D :])
    second.wait()
    kv_ref[...] = dot(encoded_ref[...], cross_ref[:, D : 3 * D]).astype(jnp.bfloat16)
    normed = rms_rows(state, gains_ref[4:5]).astype(jnp.bfloat16)
    query = dot(normed, cross_ref[:, :D]).astype(jnp.bfloat16)
    mixed = []
    for i in range(micro):
        own = query[i * tokens : (i + 1) * tokens]
        at = slice(i * sources, (i + 1) * sources)
        bias = bias_column(sources, len_ref[i, 0])
        mixed.append(lane_heads(own, kv_ref[at, :D], kv_ref[at, D:], bias, None))
    state_ref[...] = state + dot(jnp.concatenate(mixed, axis=0), cross_ref[:, 3 * D :])
    third.wait()
    fourth.wait()
    frozen_ffn(state_ref, out_ref, gains_ref[5:6], win_ref, wout_ref, lambda v: v)


def cost(micros):
    return pl.CostEstimate(
        flops=int(micros * 8e8), bytes_accessed=int(micros * 3e6), transcendentals=0
    )


smem = pl.BlockSpec(memory_space=pltpu.SMEM)
vmem = pl.BlockSpec(memory_space=pltpu.VMEM)
hbm = pl.BlockSpec(memory_space=pl.ANY)
LIMIT = pltpu.CompilerParams(vmem_limit_bytes=56 * 2**20)

def encode(lens, x, attn, ffn_in, ffn_out, gains):
    tokens = x.shape[0]
    return pl.pallas_call(
        encoder_kernel,
        out_shape=jax.ShapeDtypeStruct((tokens, D), jnp.bfloat16),
        in_specs=[smem, vmem, vmem, hbm, hbm, hbm],
        out_specs=vmem,
        scratch_shapes=[pltpu.VMEM((D, 4 * D), jnp.bfloat16), pltpu.VMEM((D, 4 * D), jnp.bfloat16), pltpu.VMEM((4 * D, D), jnp.bfloat16),
            pltpu.VMEM((tokens, 3 * D), jnp.bfloat16), pltpu.VMEM((tokens, D), jnp.float32), pltpu.SemaphoreType.DMA((4,))],
        compiler_params=LIMIT,
        name="encoder",
        cost_estimate=cost(14),
    )(lens, x, gains, attn, ffn_in, ffn_out)

def decode(lens, x, encoded, attn, ffn_in, ffn_out, gains):
    tokens = x.shape[0]
    sources = encoded.shape[0]
    return pl.pallas_call(
        decoder_kernel,
        out_shape=jax.ShapeDtypeStruct((tokens, D), jnp.bfloat16),
        in_specs=[smem, vmem, vmem, vmem, hbm, hbm, hbm],
        out_specs=vmem,
        scratch_shapes=[pltpu.VMEM((D, 4 * D), jnp.bfloat16), pltpu.VMEM((D, 4 * D), jnp.bfloat16), pltpu.VMEM((D, 4 * D), jnp.bfloat16), pltpu.VMEM((4 * D, D), jnp.bfloat16),
            pltpu.VMEM((sources, 2 * D), jnp.bfloat16), pltpu.VMEM((tokens, D), jnp.float32), pltpu.SemaphoreType.DMA((4,))],
        compiler_params=LIMIT,
        name="decoder",
        cost_estimate=cost(10.5),
    )(lens, x, encoded, gains, attn, ffn_in, ffn_out)

def dot_l(left, right):
    return lax.dot_general(left, right, (((0,), (0,)), ((), ())), preferred_element_type=jnp.float32)

def rms_columns(values, gain):
    return values * lax.rsqrt(jnp.mean(values * values, axis=0, keepdims=True) + norm_eps) * gain

def rms_columns_back(values, gain, grad):
    inverse = lax.rsqrt(jnp.mean(values * values, axis=0, keepdims=True) + norm_eps)
    gained = grad * gain
    along = jnp.mean(values * gained, axis=0, keepdims=True)
    gain_grad = jnp.sum(grad * (values * inverse), axis=1, keepdims=True)
    return inverse * gained - values * (inverse * inverse * inverse * along), gain_grad

def gelu_back(values, grad):
    square = values * values
    tanh = jnp.tanh(values * (0.7978845608028654 + 0.035677408136300125 * square))
    slope = 0.5 * (1.0 + tanh) + (0.5 * values) * (1.0 - tanh * tanh) * (0.7978845608028654 + 0.107032224408900375 * square)
    return grad * slope

side_scale = (SIDE // SIDE_HEADS) ** -0.5

def keys_with_bias(keys_t, valid):
    count = keys_t.shape[1]
    place = lax.broadcasted_iota(jnp.int32, (64, count), 1)
    line = lax.broadcasted_iota(jnp.int32, (64, count), 0)
    bias = jnp.where((line == 0) & (place >= valid), masked, 0.0)
    return jnp.concatenate([keys_t.astype(jnp.float32), bias], axis=0).T.astype(jnp.bfloat16)

def head_query(query_t, head):
    line = lax.broadcasted_iota(jnp.int32, (64, 1), 0)
    own = jnp.where(line // 8 == head, query_t, 0.0)
    ones = jnp.broadcast_to(jnp.where(line == 0, 1.0, 0.0), own.shape)
    return jnp.concatenate([own, ones], axis=0).astype(jnp.bfloat16)

def rounded(values):
    return values.astype(jnp.bfloat16).astype(jnp.float32)

def causal_columns(count):
    key = lax.broadcasted_iota(jnp.int32, (count, count), 0)
    query = lax.broadcasted_iota(jnp.int32, (count, count), 1)
    return jnp.where(key <= query, 0.0, masked)

def side_heads(query_t, keys_t, values_t, valid, causal):
    keys = keys_with_bias(keys_t, valid)
    outs, sums = [], []
    for head in range(SIDE_HEADS):
        scores = dot(keys, head_query(query_t, head))
        if causal is not None:
            scores = scores + causal
        peak = jnp.max(scores, axis=0, keepdims=True)
        weight = jnp.exp2((scores - peak) * (side_scale * LOG2E))
        total = jnp.sum(weight, axis=0, keepdims=True)
        span = slice(8 * head, 8 * head + 8)
        outs.append(dot(values_t[span].astype(jnp.bfloat16), weight.astype(jnp.bfloat16)) / total)
        sums.append(peak * (side_scale * LOG2E) + jnp.log2(total))
    return jnp.concatenate(outs, axis=0), jnp.concatenate(sums, axis=0)

def side_heads_back(query_t, keys_t, values_t, sums, grad_t, valid, causal):
    keys = keys_with_bias(keys_t, valid)
    values = values_t.T.astype(jnp.bfloat16)
    line = lax.broadcasted_iota(jnp.int32, (64, 1), 0)
    grad_q, grad_k, grad_v = [], [], []
    for head in range(SIDE_HEADS):
        span = slice(8 * head, 8 * head + 8)
        scores = dot(keys, head_query(query_t, head))
        if causal is not None:
            scores = scores + causal
        weight = jnp.exp2(scores * (side_scale * LOG2E) - sums[head:head + 1])
        own_grad = jnp.where(line // 8 == head, grad_t, 0.0).astype(jnp.bfloat16)
        grad_w = rounded(dot(values, own_grad))
        along = jnp.sum(grad_w * weight, axis=0, keepdims=True)
        grad_s = (weight * (grad_w - along)).astype(jnp.bfloat16)
        grad_q.append(dot(keys_t[span].astype(jnp.bfloat16), grad_s))
        grad_k.append(dot_t(query_t[span].astype(jnp.bfloat16), grad_s))
        grad_v.append(dot_t(grad_t[span].astype(jnp.bfloat16), weight.astype(jnp.bfloat16)))
    return (jnp.concatenate(grad_q, axis=0) * side_scale, jnp.concatenate(grad_k, axis=0) * side_scale,
            jnp.concatenate(grad_v, axis=0))

def chosen_columns(tokens, positions):
    token = lax.broadcasted_iota(jnp.int32, (tokens, positions.shape[1]), 0)
    return jnp.where(token == positions, 1.0, 0.0).astype(jnp.bfloat16)

def side_kernel(len_ref, src_ref, encoded_ref, tgt_ref, decoded_ref, positions_ref, down_ref, attn_in_ref, attn_out_ref, ffn_in_ref, ffn_out_ref, small_ref,
                picked_ref, enc_ref, dec_ref, enc_mixed_ref, self_mixed_ref, cross_mixed_ref, enc_sums_ref, self_sums_ref, cross_sums_ref):
    micro = len_ref.shape[0]

    def gain(i):
        return small_ref[:, i:i + 1]

    def attend(which, query_n, key_n, side_of, causal, mixed_ref, sums_ref):
        query = rounded(dot(attn_in_ref[which, :64], query_n))
        keyval = rounded(dot(attn_in_ref[which, 64:], key_n))
        width, far = query.shape[1] // micro, keyval.shape[1] // micro
        parts = []
        for i in range(micro):
            near, away = slice(i * width, (i + 1) * width), slice(i * far, (i + 1) * far)
            mixed, sums = side_heads(query[:, near], keyval[:64, away], keyval[64:, away], len_ref[i, side_of], causal)
            sums_ref[:, near] = sums
            parts.append(mixed.astype(jnp.bfloat16))
        mixed_b = jnp.concatenate(parts, axis=1)
        mixed_ref[...] = mixed_b
        return dot(attn_out_ref[which], mixed_b)

    def ffn(which, normed):
        active = gelu(dot(ffn_in_ref[which], normed)).astype(jnp.bfloat16)
        return dot(ffn_out_ref[which], active)

    def norm(values, i):
        return rms_columns(values, gain(i)).astype(jnp.bfloat16)

    state = dot_t(down_ref[0], src_ref[...])
    enc_ref[0] = state
    normed = norm(state, 0)
    flow = dot_t(down_ref[2], tgt_ref[...])
    dec_ref[0] = flow
    normed_flow = norm(flow, 3)
    tokens = flow.shape[1] // micro
    causal = causal_columns(tokens)
    state = state + attend(0, normed, normed, 0, None, enc_mixed_ref, enc_sums_ref)
    enc_ref[1] = state
    flow = flow + attend(1, normed_flow, normed_flow, 1, causal, self_mixed_ref, self_sums_ref)
    dec_ref[1] = flow
    state = state + ffn(0, norm(state, 1))
    enc_ref[2] = state
    joined = dot_t(down_ref[1], encoded_ref[...])
    enc_ref[3] = joined
    gate = jax.nn.sigmoid(gain(7))
    memory = norm(gate * joined + (1.0 - gate) * state, 2)
    flow = flow + attend(2, norm(flow, 4), memory, 0, None, cross_mixed_ref, cross_sums_ref)
    dec_ref[2] = flow
    flow = flow + ffn(1, norm(flow, 5))
    dec_ref[3] = flow
    joined = dot_t(down_ref[3], decoded_ref[...])
    dec_ref[4] = joined
    gate = jax.nn.sigmoid(gain(8))
    top = norm(gate * joined + (1.0 - gate) * flow, 6)
    for i in range(micro):
        chosen = chosen_columns(tokens, positions_ref[i : i + 1])
        picked_ref[i] = dot(top[:, i * tokens : (i + 1) * tokens], chosen).astype(jnp.bfloat16)


def side(lens, src, encoded, tgt, decoded, positions, weights):
    s, t = src.shape[0], tgt.shape[0]
    m, p = positions.shape
    f32, bf16 = jnp.float32, jnp.bfloat16
    shapes = [((m, 64, p), bf16), ((4, 64, s), f32), ((5, 64, t), f32), ((64, s), bf16), ((64, t), bf16), ((64, t), bf16), ((8, s), f32), ((8, t), f32), ((8, t), f32)]
    return pl.pallas_call(
        side_kernel,
        out_shape=[jax.ShapeDtypeStruct(*item) for item in shapes],
        in_specs=[smem] + [vmem] * 11,
        out_specs=[vmem] * 9,
        compiler_params=LIMIT,
        name="side",
        cost_estimate=cost(24),
    )(lens, src, encoded, tgt, decoded, positions, *weights)

def back_kernel(*refs):
    (len_ref, src_ref, encoded_ref, tgt_ref, decoded_ref, positions_ref, attn_in_t_ref, ffn_in_t_ref, attn_in_ref, attn_out_ref, ffn_in_ref, ffn_out_ref, small_ref,
     enc_ref, dec_ref, enc_mixed_ref, self_mixed_ref, cross_mixed_ref, enc_sums_ref, self_sums_ref, cross_sums_ref, parts_ref) = refs[:22]
    down_out, attn_in_out, in_rest_out, attn_out_out, ffn_in_out, ffn_out_out, small_out = refs[-7:]
    outs = {
        "down": down_out,
        "attn_in": attn_in_out,
        "in_rest": in_rest_out,
        "attn_out": attn_out_out,
        "ffn_in": ffn_in_out,
        "ffn_out": ffn_out_out,
    }
    micro = len_ref.shape[0]

    def put(which, index, values):
        if values.shape[1] == 3 * SIDE:
            put("in_rest", index, values[:, 128:])
            values = values[:, :128]
        outs[which][index] = values

    smalls = {}

    def gain(i):
        return small_ref[:, i:i + 1]

    def norm(values, i):
        return rms_columns(values, gain(i)).astype(jnp.bfloat16)

    def norm_back(values, i, grad):
        result, smalls[i] = rms_columns_back(values, gain(i), grad)
        return result

    def blend_back(i, joined, late, grad):
        gate = jax.nn.sigmoid(gain(i))
        smalls[i] = jnp.sum(grad * (joined - late), axis=1, keepdims=True) * (gate * (1.0 - gate))
        return gate * grad, (1.0 - gate) * grad

    def ffn_back(which, normed, grad):
        grad_b = grad.astype(jnp.bfloat16)
        hidden = dot(ffn_in_t_ref[which], normed)
        active = gelu(hidden).astype(jnp.bfloat16)
        put("ffn_out", which, dot_t(active, grad_b))
        grad_hidden = gelu_back(hidden, dot(ffn_out_ref[which], grad_b)).astype(jnp.bfloat16)
        put("ffn_in", which, dot_t(normed, grad_hidden))
        return dot(ffn_in_ref[which], grad_hidden)

    def attend_back(which, query_n, key_n, mixed_ref, sums_ref, grad, side_of, causal):
        grad_b = grad.astype(jnp.bfloat16)
        put("attn_out", which, dot_t(mixed_ref[...], grad_b))
        grad_mixed = rounded(dot(attn_out_ref[which], grad_b))
        query = rounded(dot(attn_in_t_ref[which, :64], query_n))
        keyval = rounded(dot(attn_in_t_ref[which, 64:], key_n))
        width, far = query.shape[1] // micro, keyval.shape[1] // micro
        grads_q, grads_kv = [], []
        for i in range(micro):
            near, away = slice(i * width, (i + 1) * width), slice(i * far, (i + 1) * far)
            grad_q, grad_k, grad_v = side_heads_back(
                query[:, near], keyval[:64, away], keyval[64:, away], sums_ref[:, near], grad_mixed[:, near], len_ref[i, side_of], causal
            )
            grads_q.append(grad_q.astype(jnp.bfloat16))
            grads_kv.append(jnp.concatenate([grad_k, grad_v], axis=0).astype(jnp.bfloat16))
        return jnp.concatenate(grads_q, axis=1), jnp.concatenate(grads_kv, axis=1)

    tokens = tgt_ref.shape[0] // micro
    grads = []
    for index in range(micro):
        grad_picked = tree_sum([parts_ref[i, index].astype(jnp.float32) for i in range(parts_ref.shape[0])])
        chosen = chosen_columns(tokens, positions_ref[index : index + 1])
        high = grad_picked.astype(jnp.bfloat16)
        low = (grad_picked - high.astype(jnp.float32)).astype(jnp.bfloat16)
        grads.append(dot_t(high, chosen) + dot_t(low, chosen))
    grad = jnp.concatenate(grads, axis=1)
    gate = jax.nn.sigmoid(gain(8))
    final = gate * dec_ref[4] + (1.0 - gate) * dec_ref[3]
    grad = norm_back(final, 6, grad)
    grad_joined, grad = blend_back(8, dec_ref[4], dec_ref[3], grad)
    put("down", 3, dot(grad_joined.astype(jnp.bfloat16), decoded_ref[...]))
    grad = grad + norm_back(dec_ref[2], 5, ffn_back(1, norm(dec_ref[2], 5), grad))
    gate = jax.nn.sigmoid(gain(7))
    final = gate * enc_ref[3] + (1.0 - gate) * enc_ref[2]
    memory = norm(final, 2)
    normed = norm(dec_ref[1], 4)
    grad_q, grad_kv = attend_back(2, normed, memory, cross_mixed_ref, cross_sums_ref, grad, 0, None)
    zero_q = jnp.zeros((128, tgt_ref.shape[0]), jnp.bfloat16)
    zero_kv = jnp.zeros((64, src_ref.shape[0]), jnp.bfloat16)
    put("attn_in", 2, dot_t(normed, jnp.concatenate([grad_q, zero_q], axis=0)) + dot_t(memory, jnp.concatenate([zero_kv, grad_kv], axis=0)))
    weight = attn_in_ref[2]
    grad_memory = dot(weight, jnp.concatenate([zero_kv, grad_kv], axis=0))
    grad = grad + norm_back(dec_ref[1], 4, dot(weight, jnp.concatenate([grad_q, zero_q], axis=0)))
    normed = norm(dec_ref[0], 3)
    grad_q, grad_kv = attend_back(1, normed, normed, self_mixed_ref, self_sums_ref, grad, 1, causal_columns(tokens))
    grad_qkv = jnp.concatenate([grad_q, grad_kv], axis=0)
    put("attn_in", 1, dot_t(normed, grad_qkv))
    grad = grad + norm_back(dec_ref[0], 3, dot(attn_in_ref[1], grad_qkv))
    put("down", 2, dot(grad.astype(jnp.bfloat16), tgt_ref[...]))
    grad = norm_back(final, 2, grad_memory)
    grad_joined, grad = blend_back(7, enc_ref[3], enc_ref[2], grad)
    put("down", 1, dot(grad_joined.astype(jnp.bfloat16), encoded_ref[...]))
    grad = grad + norm_back(enc_ref[1], 1, ffn_back(0, norm(enc_ref[1], 1), grad))
    normed = norm(enc_ref[0], 0)
    grad_q, grad_kv = attend_back(0, normed, normed, enc_mixed_ref, enc_sums_ref, grad, 0, None)
    grad_qkv = jnp.concatenate([grad_q, grad_kv], axis=0)
    put("attn_in", 0, dot_t(normed, grad_qkv))
    grad = grad + norm_back(enc_ref[0], 0, dot(attn_in_ref[0], grad_qkv))
    put("down", 0, dot(grad.astype(jnp.bfloat16), src_ref[...]))
    lane = lax.broadcasted_iota(jnp.int32, (1, 128), 1)
    total = jnp.zeros((64, 128), jnp.float32)
    for i in range(9):
        total = total + jnp.where(lane == i, smalls[i], 0.0)
    small_out[...] = total

def side_back(lens, src, encoded, tgt, decoded, positions, weights, kept, parts):
    f32 = jnp.float32
    shapes = [(4, 64, 512), (3, 64, 128), (3, 64, 64), (3, 64, 64), (2, 64, 256), (2, 256, 64), (64, 128)]
    return pl.pallas_call(
        back_kernel,
        out_shape=[jax.ShapeDtypeStruct(shape, f32) for shape in shapes],
        in_specs=[smem] + [vmem] * 21,
        out_specs=[vmem] * 7,
        compiler_params=LIMIT,
        name="side_back",
        cost_estimate=cost(34),
    )(lens, src, encoded, tgt, decoded, positions, *weights, *kept, parts)


def swap(values, axis, distance):
    size = lax.axis_size(axis)
    return lax.ppermute(values, axis, [(i, i ^ distance) for i in range(size)])


def gather_peers(values, axis):
    return [values] + [swap(values, axis, s) for s in range(1, lax.axis_size(axis))]


def exchange(pieces, axis):
    return [pieces[0]] + [swap(pieces[s], axis, s) for s in range(1, lax.axis_size(axis))]


def tree_sum(terms):
    while len(terms) > 1:
        terms = [terms[i] + terms[i + 1] for i in range(0, len(terms), 2)]
    return terms[0]


def owners_of(ids, rows, peers, me):
    owner = jnp.zeros(ids.shape, jnp.int32)
    for peer in range(1, peers):
        owner = owner + jnp.where(ids >= peer * rows, 1, 0)
    return owner ^ me


def ranks_within(own):
    peers, count = own.shape
    own_b = own.astype(jnp.bfloat16)
    before = jnp.where(
        lax.broadcasted_iota(jnp.int32, (128, 128), 0)
        < lax.broadcasted_iota(jnp.int32, (128, 128), 1),
        1.0,
        0.0,
    ).astype(jnp.bfloat16)
    seen = jnp.zeros((peers, 1), jnp.float32)
    ranks = []
    for start in range(0, count, 128):
        block = slice(start, start + 128)
        inside = dot(own_b[:, block], before) + seen
        ranks.append(jnp.sum(own[:, block] * (inside + 1.0), axis=0, keepdims=True) - 1.0)
        seen = seen + jnp.sum(own[:, block], axis=1, keepdims=True)
    return jnp.concatenate(ranks, axis=1), seen


def column_of(row):
    return jnp.broadcast_to(row, (8, row.shape[1])).T[:, :1]


def placed(own, values, hit):
    high = jnp.floor(values * (1.0 / 64.0))
    low = values - 64.0 * high
    return 64.0 * dot((own * high).astype(jnp.bfloat16), hit) + dot(
        (own * low).astype(jnp.bfloat16), hit
    )


def score_part(rows, peers, tokens, me, busy, at_ref, goal_ref, mask_ref, token_ref, letter_ref, at):
    micro, _, spots = at_ref.shape
    token = lax.broadcasted_iota(jnp.int32, (tokens, 1), 0)
    token_f = token.astype(jnp.float32)
    spot_f = lax.broadcasted_iota(jnp.int32, (1, spots), 1).astype(jnp.float32)
    lower = jnp.where(
        lax.broadcasted_iota(jnp.int32, (tokens, tokens), 0)
        > lax.broadcasted_iota(jnp.int32, (tokens, tokens), 1),
        1.0,
        0.0,
    ).astype(jnp.bfloat16)
    goals, masks, slots, used = [], [], [], []
    for index in range(micro):
        mask = mask_ref[index].astype(jnp.float32)
        met = jnp.where(token == at_ref[index], mask, 0.0)
        times = jnp.sum(met, axis=1, keepdims=True)
        active = jnp.where(times > 0.0, 1.0, 0.0)
        wide = jnp.broadcast_to(active, (tokens, 128)).astype(jnp.bfloat16)
        slot = dot(lower, wide)[:, :1]
        here = jnp.where(slot == spot_f, active, 0.0)
        token_row = jnp.sum(here * (token_f + 1.0), axis=0, keepdims=True) - 1.0
        token_ref[index : index + 1] = token_row.astype(jnp.int32)
        count = jnp.sum(here * times, axis=0, keepdims=True).astype(jnp.int32)
        first = at + (micro + index) * spots
        letter_ref[:, first : first + spots] = jnp.broadcast_to(count, (peers, spots))
        slots.append(jnp.sum(met * slot, axis=0, keepdims=True) + float(index * spots))
        goals.append(goal_ref[index])
        masks.append(mask)
        used.append(jnp.sum(active, axis=0, keepdims=True))
    goal, mask, slot = [jnp.concatenate(rows_, axis=1) for rows_ in (goals, masks, slots)]
    far = owners_of(goal, rows, peers, 0)
    local = (goal - far * rows).astype(jnp.float32)
    line = lax.broadcasted_iota(jnp.int32, (peers, goal.shape[1]), 0)
    own = jnp.where((line == (far ^ me)) & (mask > 0.0), 1.0, 0.0)
    rank, many = ranks_within(own)
    order = lax.broadcasted_iota(jnp.int32, (1, goal.shape[1]), 1).astype(jnp.float32)
    hit = jnp.where(column_of(rank) == order, 1.0, 0.0).astype(jnp.bfloat16)
    letter_ref[:, at : at + micro * spots] = placed(own, slot, hit).astype(
        jnp.int32
    ) * 65536 + placed(own, local, hit).astype(jnp.int32)
    lane = lax.broadcasted_iota(jnp.int32, (peers, 128), 1)
    info = jnp.where(lane == 0, many, jnp.where(lane == micro + 1, busy, 0.0))
    for index in range(micro):
        info = jnp.where(lane == index + 1, used[index], info)
    first = at + 2 * micro * spots
    letter_ref[:, first : first + 128] = info.astype(jnp.int32)


def plan_kernel(rows, peers, cap, tokens, me_ref, src_ref, tgt_ref, *refs):
    score_refs, (slots_ref, column_ref, near_ref, other_ref, token_ref, letter_ref) = refs[:3], refs[3:]
    ids_row = jnp.concatenate(
        [ref[index] for ref in (src_ref, tgt_ref) for index in range(ref.shape[0])], axis=1
    )
    count = ids_row.shape[1]
    ids = ids_row.astype(jnp.float32)
    column = column_of(ids)
    column_ref[...] = column
    first_at = jnp.full((1, count), float(count), jnp.float32)
    for start in range(0, count, 256):
        place = (lax.broadcasted_iota(jnp.int32, (256, 1), 0) + start).astype(jnp.float32)
        same = column[start : start + 256] == ids
        first_at = jnp.minimum(
            first_at, jnp.min(jnp.where(same, place, float(count)), axis=0, keepdims=True)
        )
    first = first_at == lax.broadcasted_iota(jnp.int32, (1, count), 1).astype(jnp.float32)
    far = owners_of(ids_row, rows, peers, 0)
    line = lax.broadcasted_iota(jnp.int32, (peers, count), 0)
    own = jnp.where((line == (far ^ me_ref[0])) & first, 1.0, 0.0)
    rank, seen = ranks_within(own)
    width = -(-cap // 128) * 128
    spot = lax.broadcasted_iota(jnp.int32, (1, width), 1).astype(jnp.float32)
    hit = jnp.where(column_of(rank) == spot, 1.0, 0.0).astype(jnp.bfloat16)
    filled = dot(own.astype(jnp.bfloat16), hit)
    local = placed(own, (ids_row - far * rows).astype(jnp.float32), hit).astype(jnp.int32)
    letter_ref[:, :width] = local
    owner = lax.broadcasted_iota(jnp.int32, (peers, 1), 0) ^ me_ref[0]
    slots = jnp.where(filled > 0.5, local + owner * rows, -1)[:, :cap]
    for peer in range(peers):
        slots_ref[peer % 2, peer // 2 : peer // 2 + 1] = slots[peer : peer + 1]
    busy = jnp.max(seen, axis=0, keepdims=True)
    score_part(rows, peers, tokens, me_ref[0], busy, *score_refs, token_ref, letter_ref, width)
    for peer in range(peers):
        letter = near_ref if peer % 2 == 0 else other_ref
        letter[peer // 2 : peer // 2 + 1] = letter_ref[peer : peer + 1]


def plan(me, source, target, score, rows, peers, cap, tokens):
    count = source.shape[0] * source.shape[2] + target.shape[0] * target.shape[2]
    micro, _, spots = score[0].shape
    letter = -(-cap // 128) * 128 + 2 * micro * spots + 128
    shapes = [
        ((2, peers // 2, cap), jnp.int32),
        ((count, 1), jnp.float32),
        ((peers // 2, letter), jnp.int32),
        ((peers // 2, letter), jnp.int32),
        ((micro, spots), jnp.int32),
    ]
    return pl.pallas_call(
        functools.partial(plan_kernel, rows, peers, cap, tokens),
        out_shape=[jax.ShapeDtypeStruct(*shape) for shape in shapes],
        in_specs=[smem] + [vmem] * 5,
        out_specs=[vmem] * len(shapes),
        scratch_shapes=[pltpu.VMEM((peers, letter), jnp.int32)],
        compiler_params=LIMIT,
        name="plan",
        cost_estimate=cost(4),
    )(me, source, target, *score)


def expand_kernel(sizes, slots_ref, column_ref, *refs):
    far_refs, near_ref, out_refs = refs[: -1 - len(sizes)], refs[-1 - len(sizes)], refs[-len(sizes) :]
    slots = slots_ref[...].astype(jnp.float32)
    rows = (jnp.concatenate([ref[0] for ref in far_refs], axis=0), near_ref[...])
    base = 0
    for out in out_refs:
        for start in range(0, out.shape[0], 256):
            at = base + start
            column = column_ref[at : at + 256]
            first, second = [
                dot(jnp.where(column == slots[i : i + 1], 1.0, 0.0).astype(jnp.bfloat16), rows[i])
                for i in range(2)
            ]
            out[start : start + 256] = (first + second).astype(jnp.bfloat16)
        base = base + out.shape[0]


def expand(slots, column, far, near, sizes):
    width = near.shape[1]
    return pl.pallas_call(
        functools.partial(expand_kernel, sizes),
        out_shape=[jax.ShapeDtypeStruct((size, width), jnp.bfloat16) for size in sizes],
        in_specs=[vmem] * (3 + len(far)),
        out_specs=[vmem] * len(sizes),
        compiler_params=LIMIT,
        name="expand",
        cost_estimate=cost(3.8),
    )(slots, column, *far, near)


def ask(near, other):
    count = near.shape[0]
    pairs = jnp.stack([near, swap(other, "dp", 1)], axis=1)
    far = [pairs[:1]] + [swap(pairs[i : i + 1], "dp", 2 * i) for i in range(1, count)]
    return jnp.concatenate(far).reshape(2 * count, -1)


def answer(pieces):
    size = pieces.shape[0]
    pairs = pieces.reshape((size // 2, 2) + pieces.shape[1:])
    far = [pairs[:1]] + [swap(pairs[i : i + 1], "dp", 2 * i) for i in range(1, size // 2)]
    far = jnp.concatenate(far)
    near = swap(far[:, 1], "dp", 1)
    return jnp.stack([far[:, 0], near], axis=1).reshape(pieces.shape)


def send_rows(slots, column, found, sizes, between):
    count = found.shape[0]
    far = [found[0]] + [swap(found[i], "dp", 2 * i) for i in range(1, count)]
    other = jnp.concatenate([part[1] for part in far])
    near = swap(after(other, *between), "dp", 1)
    return expand(slots.reshape(2, -1), column, far, near, sizes)


def every_row(ids, table, rows):
    size = lax.axis_size("dp")
    me = lax.axis_index("dp")

    def step(i, carry):
        shard, filled = carry
        local = ids - (me + i) % size * rows
        here = (local >= 0) & (local < rows)
        found = jnp.take(shard, jnp.clip(local, 0, rows - 1), axis=0)
        shard = lax.ppermute(shard, "dp", [((j + 1) % size, j) for j in range(size)])
        return shard, jnp.where(here[:, None], found, filled)

    empty = jnp.zeros((ids.shape[0], table.shape[1]), table.dtype)
    return lax.fori_loop(0, size, step, (table, empty))[1]


def embed_rows(slots, column, found, cap, most, source, target, table, between):
    sizes = [source.size, target.size]
    result = tuple(send_rows(slots, column, found, sizes, between))

    def long_way(carry):
        ids = jnp.concatenate([source.reshape(-1), target.reshape(-1)])
        filled = every_row(ids, table, table.shape[0])
        return (jnp.int32(0), (filled[: sizes[0]], filled[sizes[0] :]))

    return lax.while_loop(lambda carry: carry[0] > cap, long_way, (most, result))[1]


def gather_all(values):
    pair = jnp.stack([values, swap(values, "dp", 1)])
    far = [pair] + [swap(pair, "dp", s) for s in range(2, lax.axis_size("dp"), 2)]
    return jnp.concatenate(far)


def table_kernel(rows, table_ref, up_ref, padded_ref, weight_ref):
    block = table_ref.shape[0]
    place = lax.broadcasted_iota(jnp.int32, (block, 1), 0) + pl.program_id(0) * block
    table = jnp.where(place < rows, table_ref[...], jnp.bfloat16(0))
    padded_ref[...] = table
    lifted = dot_t(table, up_ref[...]) * (D ** (-0.5) * LOG2E)
    high = lifted.astype(jnp.bfloat16)
    weight_ref[:, :SIDE] = high
    weight_ref[:, SIDE:] = (lifted - high.astype(jnp.float32)).astype(jnp.bfloat16)


VOCAB_BLOCK = 512
TILE = 512


def table_parts(table, up_b):
    rows, width = table.shape
    padded = -(-rows // VOCAB_BLOCK) * VOCAB_BLOCK
    return pl.pallas_call(
        functools.partial(table_kernel, rows),
        out_shape=[
            jax.ShapeDtypeStruct((padded, width), jnp.bfloat16),
            jax.ShapeDtypeStruct((padded, 2 * SIDE), jnp.bfloat16),
        ],
        grid=(padded // VOCAB_BLOCK,),
        in_specs=[
            pl.BlockSpec((VOCAB_BLOCK, width), lambda i: (i, 0)),
            pl.BlockSpec((SIDE, width), lambda i: (0, 0)),
        ],
        out_specs=[
            pl.BlockSpec((VOCAB_BLOCK, width), lambda i: (i, 0)),
            pl.BlockSpec((VOCAB_BLOCK, 2 * SIDE), lambda i: (i, 0)),
        ],
        compiler_params=LIMIT,
        name="table_parts",
        cost_estimate=cost(5),
    )(table, up_b)


def goals_kernel(spots, where_ref, many_ref, entry_ref, table_ref, out_ref, tall_ref, sum_ref, sem):
    peers = many_ref.shape[0]
    micro = entry_ref.shape[1] // spots
    tiles = where_ref[1]
    for start in range(0, table_ref.shape[0], VOCAB_BLOCK):
        tall_ref[start : start + VOCAB_BLOCK] = table_ref[start : start + VOCAB_BLOCK].astype(jnp.float32)

    def clear(i, carry):
        sum_ref[pl.ds(pl.multiple_of(i * TILE, TILE), TILE)] = jnp.zeros((TILE, sum_ref.shape[1]), jnp.float32)
        return carry

    lax.fori_loop(0, tiles, clear, 0)
    for peer in range(peers):
        base = 2 + (peer ^ where_ref[0]) * micro

        def add(j, carry):
            entry = entry_ref[peer, j]
            slot = entry // 65536
            local = entry - slot * 65536
            row = slot + where_ref[base]
            for index in range(1, micro):
                row = jnp.where(slot >= index * spots, slot - index * spots + where_ref[base + index], row)
            sum_ref[pl.ds(row, 1)] = sum_ref[pl.ds(row, 1)] + tall_ref[pl.ds(local, 1)]
            return carry

        lax.fori_loop(0, many_ref[peer], add, 0)

    def send(i, carry):
        at = pl.ds(pl.multiple_of(i * TILE, TILE), TILE)
        copy = pltpu.make_async_copy(sum_ref.at[at], out_ref.at[at], sem)
        copy.start()
        copy.wait()
        return carry

    lax.fori_loop(0, tiles, send, 0)


def goal_rows(where, many, entries, table_pad, spots):
    total = entries.shape[0] * entries.shape[1]
    padded, width = table_pad.shape
    return pl.pallas_call(
        functools.partial(goals_kernel, spots),
        out_shape=jax.ShapeDtypeStruct((total, width), jnp.float32),
        in_specs=[smem, smem, smem, vmem],
        out_specs=hbm,
        scratch_shapes=[
            pltpu.VMEM((padded, width), jnp.float32),
            pltpu.VMEM((total, width), jnp.float32),
            pltpu.SemaphoreType.DMA,
        ],
        compiler_params=LIMIT,
        name="goals",
        cost_estimate=cost(9),
    )(where, many, entries, table_pad)


def softmax_kernel(rows, where_ref, gathered_ref, count_ref, weight_ref, table_ref, mix_ref, stats_ref, packed_ref, all_ref):
    step = pl.program_id(0)
    peers, micro, _, spots = gathered_ref.shape
    tiles = where_ref[1]

    @pl.when(step == 0)
    def _():
        def clear(i, carry):
            all_ref[pl.ds(pl.multiple_of(i * TILE, TILE), TILE)] = jnp.zeros((TILE, 128), jnp.float32)
            return carry

        lax.fori_loop(0, tiles, clear, 0)
        for device in range(peers):
            for index in range(micro):
                peer = where_ref[0] ^ device
                block = jnp.concatenate(
                    [
                        gathered_ref[peer, index].astype(jnp.float32),
                        count_ref[peer, index : index + 1].astype(jnp.float32),
                        jnp.zeros((SIDE - 1, spots), jnp.float32),
                    ],
                    axis=0,
                )
                all_ref[pl.ds(where_ref[2 + device * micro + index], spots)] = block.T

    @pl.when(step < tiles)
    def _():
        mine = all_ref[pl.ds(pl.multiple_of(step * TILE, TILE), TILE)]
        packed_ref[...] = mine
        picked = jnp.concatenate([mine[:, :SIDE], mine[:, :SIDE]], axis=1).astype(jnp.bfloat16)
        padded = weight_ref.shape[0]
        chunk = min(1024, padded)
        peak = total = mix = None
        for start in range(0, padded, chunk):
            logits = dot_t(picked, weight_ref[start : start + chunk])
            if start + chunk > rows:
                place = lax.broadcasted_iota(jnp.int32, (1, chunk), 1)
                logits = jnp.where(place < rows - start, logits, -jnp.inf)
            above = jnp.max(logits, axis=1, keepdims=True)
            if peak is not None:
                above = jnp.maximum(peak, above)
            share = jnp.exp2(logits - above)
            part = dot(share.astype(jnp.bfloat16), table_ref[start : start + chunk])
            amount = jnp.sum(share, axis=1, keepdims=True)
            if peak is None:
                total, mix = amount, part
            else:
                fade = jnp.exp2(peak - above)
                total = total * fade + amount
                mix = mix * fade + part
            peak = above
        mix_ref[...] = mix
        lane = lax.broadcasted_iota(jnp.int32, (TILE, 128), 1)
        stats_ref[...] = jnp.where(lane == 0, peak, jnp.where(lane == 1, total, 0.0)).T[:8]


def in_use(i, where):
    return jnp.minimum(i, where[1] - 1)


def softmax_part(where, gathered, counts, weight, table_pad, rows):
    peers, micro, side_width, spots = gathered.shape
    padded, width = table_pad.shape
    total = peers * micro * spots
    return pl.pallas_call(
        functools.partial(softmax_kernel, rows),
        out_shape=[
            jax.ShapeDtypeStruct((total, width), jnp.float32),
            jax.ShapeDtypeStruct((8, total), jnp.float32),
            jax.ShapeDtypeStruct((total, 128), jnp.float32),
        ],
        grid_spec=pltpu.PrefetchScalarGridSpec(
            num_scalar_prefetch=1,
            grid=(total // TILE,),
            in_specs=[
                pl.BlockSpec((peers, micro, side_width, spots), lambda i, w: (0, 0, 0, 0)),
                pl.BlockSpec((peers, micro, spots), lambda i, w: (0, 0, 0)),
                pl.BlockSpec((padded, 2 * SIDE), lambda i, w: (0, 0)),
                pl.BlockSpec((padded, width), lambda i, w: (0, 0)),
            ],
            out_specs=[
                pl.BlockSpec((TILE, width), lambda i, w: (in_use(i, w), 0)),
                pl.BlockSpec((8, TILE), lambda i, w: (0, in_use(i, w))),
                pl.BlockSpec((TILE, 128), lambda i, w: (in_use(i, w), 0)),
            ],
            scratch_shapes=[pltpu.VMEM((total + spots, 128), jnp.float32)],
        ),
        compiler_params=LIMIT,
        name="softmax_part",
        cost_estimate=cost(22),
    )(where, gathered, counts, weight, table_pad)


def finish_kernel(where_ref, peers_ref, mix_ref, goal_ref, packed_ref, up_ref, top_ref, up_grad_ref, loss_ref, all_ref):
    step = pl.program_id(0)
    blocks, _, spots = top_ref.shape
    peers = peers_ref.shape[0]
    micro = blocks // peers
    tiles = where_ref[1]

    @pl.when(step == 0)
    def _():
        up_grad_ref[...] = jnp.zeros_like(up_grad_ref)
        loss_ref[...] = jnp.zeros_like(loss_ref)
        all_ref[...] = jnp.zeros_like(all_ref)

    @pl.when(step < tiles)
    def _():
        peaks = [peers_ref[i, 0:1] for i in range(peers)]
        peak = functools.reduce(jnp.maximum, peaks)
        total = tree_sum([peers_ref[i, 1:2] * jnp.exp2(peaks[i] - peak) for i in range(peers)])
        lse = peak + jnp.log2(total)
        rows = jnp.concatenate([jnp.exp2(peaks[0] - lse), lse, jnp.zeros((6, TILE), jnp.float32)], axis=0).T
        packed = packed_ref[...]
        times = packed[:, SIDE : SIDE + 1]
        picked = packed[:, :SIDE].astype(jnp.bfloat16)
        goal = goal_ref[...]
        lifted = (mix_ref[...] * (rows[:, :1] * times) - goal) * D ** (-0.5)
        lifted_b = lifted.astype(jnp.bfloat16)
        all_ref[pl.ds(pl.multiple_of(step * TILE, TILE), TILE), :SIDE] = dot_t(lifted_b, up_ref[...])
        up_grad_ref[...] += dot_l(picked, lifted_b)
        aim = jnp.sum(dot(picked, up_ref[...]) * goal, axis=1, keepdims=True) * D ** (-0.5)
        here = jnp.where(where_ref[0] == 0, times * rows[:, 1:2] * (1.0 / LOG2E), 0.0)
        loss = jnp.sum(here - aim, axis=0, keepdims=True)
        loss_ref[...] += jnp.broadcast_to(loss, loss_ref.shape)

    @pl.when(step == pl.num_programs(0) - 1)
    def _():
        for device in range(peers):
            for index in range(micro):
                block = all_ref[pl.ds(where_ref[2 + device * micro + index], spots)]
                top_ref[(where_ref[0] ^ device) * micro + index] = block.T[:SIDE].astype(jnp.bfloat16)


def head_finish(where, stats, mix, goals, packed, up_b, micro, spots):
    peers = stats.shape[0]
    total, width = mix.shape
    return pl.pallas_call(
        finish_kernel,
        out_shape=[
            jax.ShapeDtypeStruct((peers * micro, SIDE, spots), jnp.bfloat16),
            jax.ShapeDtypeStruct((SIDE, width), jnp.float32),
            jax.ShapeDtypeStruct((8, 128), jnp.float32),
        ],
        grid_spec=pltpu.PrefetchScalarGridSpec(
            num_scalar_prefetch=1,
            grid=(total // TILE,),
            in_specs=[
                pl.BlockSpec((peers, 2, TILE), lambda i, w: (0, 0, in_use(i, w))),
                pl.BlockSpec((TILE, width), lambda i, w: (in_use(i, w), 0)),
                pl.BlockSpec((TILE, width), lambda i, w: (in_use(i, w), 0)),
                pl.BlockSpec((TILE, 128), lambda i, w: (in_use(i, w), 0)),
                pl.BlockSpec((SIDE, width), lambda i, w: (0, 0)),
            ],
            out_specs=[
                pl.BlockSpec((peers * micro, SIDE, spots), lambda i, w: (0, 0, 0)),
                pl.BlockSpec((SIDE, width), lambda i, w: (0, 0)),
                pl.BlockSpec((8, 128), lambda i, w: (0, 0)),
            ],
            scratch_shapes=[pltpu.VMEM((total + spots, 128), jnp.float32)],
        ),
        compiler_params=LIMIT,
        name="head_finish",
        cost_estimate=cost(6),
    )(where, stats, mix, goals, packed, up_b)


def after(values, *others):
    return lax.optimization_barrier((values, others))[0]


def pair_lanes(even, odd):
    return jnp.concatenate([even, odd], axis=1)


def flatten_kernel(me_ref, loss_ref, down_ref, in_ref, in_rest_ref, attn_out_ref, ffn_in_ref, ffn_out_ref, up_ref, small_ref, mine_ref, other_ref, turn_ref, out_ref):
    at = 0
    for i in range(4):
        turn_ref[...] = down_ref[i].T
        out_ref[at : at + 256] = pair_lanes(
            turn_ref[pl.ds(0, 256, stride=2)], turn_ref[pl.ds(1, 256, stride=2)]
        )
        at += 256
    half = SIDE // 2
    for i in range(3):
        even = in_ref.at[i][pl.ds(0, half, stride=2)]
        odd = in_ref.at[i][pl.ds(1, half, stride=2)]
        even_rest = in_rest_ref.at[i][pl.ds(0, half, stride=2)]
        odd_rest = in_rest_ref.at[i][pl.ds(1, half, stride=2)]
        out_ref[pl.ds(at, half, stride=3)] = even
        out_ref[pl.ds(at + 1, half, stride=3)] = pair_lanes(even_rest, odd[:, :SIDE])
        out_ref[pl.ds(at + 2, half, stride=3)] = pair_lanes(odd[:, SIDE:], odd_rest)
        at += 3 * half
    for i in range(3):
        out_ref[at : at + half] = pair_lanes(
            attn_out_ref.at[i][pl.ds(0, half, stride=2)], attn_out_ref.at[i][pl.ds(1, half, stride=2)]
        )
        at += half
    for i in range(2):
        for j in range(2):
            out_ref[pl.ds(at + j, SIDE, stride=2)] = ffn_in_ref[i, :, 128 * j : 128 * j + 128]
        at += 2 * SIDE
    for i in range(2):
        out_ref[at : at + 128] = pair_lanes(
            ffn_out_ref.at[i][pl.ds(0, 128, stride=2)], ffn_out_ref.at[i][pl.ds(1, 128, stride=2)]
        )
        at += 128
    for j in range(4):
        out_ref[pl.ds(at + j, SIDE, stride=4)] = up_ref[:, 128 * j : 128 * j + 128]
    at += 4 * SIDE
    turn_ref[:128] = small_ref[...].T
    out_ref[at : at + 8] = pair_lanes(
        turn_ref[pl.ds(0, 8, stride=2)], turn_ref[pl.ds(1, 8, stride=2)]
    )
    at += 8
    out_ref[at:] = jnp.zeros((out_ref.shape[0] - at, 128), jnp.float32)
    lane = lax.broadcasted_iota(jnp.int32, (8, 128), 1) - 3 * me_ref[0]
    loss = loss_ref[...]
    one = rounded(loss)
    two = rounded(loss - one)
    three = rounded(loss - one - two)
    loss = jnp.where(lane == 0, one, jnp.where(lane == 1, two, jnp.where(lane == 2, three, 0.0)))
    out_ref[LOSS_ROW : LOSS_ROW + 8] = loss
    half = mine_ref.shape[0]
    core = me_ref[0] % 2
    mine_ref[...] = out_ref[pl.ds(pl.multiple_of(core * half, 8), half)]
    other_ref[...] = out_ref[pl.ds(pl.multiple_of((1 - core) * half, 8), half)]


FLAT_ROWS = 2208
LOSS_ROW = 2192


def flatten(me, loss, pieces):
    return pl.pallas_call(
        flatten_kernel,
        out_shape=[jax.ShapeDtypeStruct((FLAT_ROWS // 2, 128), jnp.float32)] * 2,
        in_specs=[smem] + [vmem] * 9,
        out_specs=[vmem] * 2,
        scratch_shapes=[
            pltpu.VMEM((512, 64), jnp.float32),
            pltpu.VMEM((FLAT_ROWS, 128), jnp.float32),
        ],
        compiler_params=LIMIT,
        name="flatten",
        cost_estimate=cost(4),
    )(me, loss, *pieces)


MAIN_ROWS = 2176


def rows_of(ref):
    main = 128 * MAIN_ROWS
    one = len(ref.shape) == 2
    load = (lambda a, b: ref[:, a:b]) if one else (lambda a, b: ref[a:b])
    rest = load(main, main + 512).reshape(4, 128)
    last = load(main + 512, main + 576).reshape(1, 64)
    return load(0, main).reshape(MAIN_ROWS, 128), jnp.concatenate(
        [rest, jnp.concatenate([last, jnp.zeros((1, 64), jnp.float32)], axis=1)], axis=0
    )


def put_rows(ref, main_values, rest_values):
    main = 128 * MAIN_ROWS
    if len(ref.shape) == 2:
        ref[:, :main] = main_values.reshape(1, main)
        ref[:, main : main + 512] = rest_values[:4].reshape(1, 512)
        ref[:, main + 512 : main + 576] = rest_values[4:5, :64]
    else:
        ref[:main] = main_values.reshape(main)
        ref[main : main + 512] = rest_values[:4].reshape(512)
        ref[main + 512 : main + 576] = rest_values[4:5, :64].reshape(64)


def adam_kernel(core_ref, counts_ref, mine_ref, other_ref, first_ref, second_ref, inner_ref, anchor_ref, new_first_ref, new_second_ref, new_inner_ref, gap_ref, loss_ref, count_ref, norm_ref, grad_ref):
    half = mine_ref.shape[0]
    core = core_ref[0]
    grad_ref[pl.ds(pl.multiple_of(core * half, 8), half)] = mine_ref[...]
    grad_ref[pl.ds(pl.multiple_of((1 - core) * half, 8), half)] = other_ref[...]
    loss_ref[0] = jnp.sum(grad_ref[LOSS_ROW : LOSS_ROW + 1])
    grad_ref[LOSS_ROW : LOSS_ROW + 8] = jnp.zeros((8, 128), jnp.float32)
    count = jnp.sum(counts_ref[...].astype(jnp.float32))
    count_ref[0] = count
    mean = grad_ref[...] * (1.0 / jnp.full((1, 1), count))
    norm = jnp.sqrt(jnp.sum(jnp.sum(mean * mean, axis=0, keepdims=True), axis=1, keepdims=True))
    norm_ref[0] = jnp.sum(norm)
    clipped = mean * jnp.minimum(1.0, clip_norm / norm)
    spans = ((0, MAIN_ROWS), (MAIN_ROWS, MAIN_ROWS + 5))
    news = []
    for span, first, second, inner, anchor in zip(
        spans, rows_of(first_ref), rows_of(second_ref), rows_of(inner_ref), rows_of(anchor_ref)
    ):
        part = clipped[span[0] : span[1]]
        new_first = beta_first * first + (1.0 - beta_first) * part
        new_second = beta_second * second + (1.0 - beta_second) * part * part
        fixed_one = new_first / (1.0 - beta_first**STEP)
        fixed_two = new_second / (1.0 - beta_second**STEP)
        new_inner = inner - learn_rate * (
            fixed_one / (jnp.sqrt(fixed_two) + adam_eps) + decay_rate * inner
        )
        news.append((new_first, new_second, new_inner))
        grad_ref[span[0] : span[1]] = anchor - new_inner
    for ref, main, rest in zip((new_first_ref, new_second_ref, new_inner_ref), news[0], news[1]):
        put_rows(ref, main, rest)
    gap_ref[...] = grad_ref[pl.ds(pl.multiple_of(core * half, 8), half)].astype(jnp.bfloat16)


def adam(core, counts, mine, other, first, second, inner, anchor):
    flat = jax.ShapeDtypeStruct(first.shape, jnp.float32)
    return pl.pallas_call(
        adam_kernel,
        out_shape=[
            flat,
            flat,
            flat,
            jax.ShapeDtypeStruct(mine.shape, jnp.bfloat16),
            *[jax.ShapeDtypeStruct((1,), jnp.float32)] * 3,
        ],
        in_specs=[smem] + [vmem] * 7,
        out_specs=[vmem] * 4 + [smem] * 3,
        scratch_shapes=[pltpu.VMEM((FLAT_ROWS, 128), jnp.float32)],
        compiler_params=LIMIT,
        name="adam",
        cost_estimate=cost(7),
    )(core, counts, mine, other, first, second, inner, anchor)


def outer_kernel(core_ref, mine_ref, other_ref, anchor_ref, momentum_ref, delta_ref, new_momentum_ref, new_anchor_ref, full_ref):
    half = mine_ref.shape[0]
    core = core_ref[0]
    full_ref[pl.ds(pl.multiple_of(core * half, 8), half)] = mine_ref[...]
    full_ref[pl.ds(pl.multiple_of((1 - core) * half, 8), half)] = other_ref[...]
    news = []
    for span, anchor, momentum in zip(
        ((0, MAIN_ROWS), (MAIN_ROWS, MAIN_ROWS + 5)), rows_of(anchor_ref), rows_of(momentum_ref)
    ):
        delta = full_ref[span[0] : span[1]]
        new_momentum = outer_beta * momentum + delta
        news.append((delta, new_momentum, anchor - outer_rate * (delta + outer_beta * new_momentum)))
    for ref, main, rest in zip((delta_ref, new_momentum_ref, new_anchor_ref), news[0], news[1]):
        put_rows(ref, main, rest)


def outer(core, mine, other, anchor, momentum):
    flat = jax.ShapeDtypeStruct(anchor.shape, jnp.float32)
    return pl.pallas_call(
        outer_kernel,
        out_shape=[flat] * 3,
        in_specs=[smem] + [vmem] * 4,
        out_specs=[vmem] * 3,
        scratch_shapes=[pltpu.VMEM((FLAT_ROWS, 128), jnp.float32)],
        compiler_params=LIMIT,
        name="outer",
        cost_estimate=cost(5),
    )(core, mine, other, anchor, momentum)


def unpack_kernel(flat_ref, down_ref, in_t_ref, out_t_ref, ffn_in_t_ref, ffn_out_t_ref, in_ref, out_ref, ffn_in_ref, ffn_out_ref, up_ref, small_ref, rows_ref, tall_ref):
    main, rest = rows_of(flat_ref)
    rows_ref[:MAIN_ROWS] = main
    rows_ref[MAIN_ROWS : MAIN_ROWS + 8] = jnp.concatenate([rest, jnp.zeros((3, 128), jnp.float32)], axis=0)

    def natural(at, count):
        packed = rows_ref[at : at + count // 2]
        tall_ref[pl.ds(0, count // 2, stride=2)] = packed[:, :SIDE]
        tall_ref[pl.ds(1, count // 2, stride=2)] = packed[:, SIDE:]
        return tall_ref[:count]

    at = 0
    for i in range(4):
        down_ref[i] = natural(at, 512).T.astype(jnp.bfloat16)
        at += 256
    half = SIDE // 2
    for i in range(3):
        one, two, three = [rows_ref[pl.ds(at + j, half, stride=3)] for j in range(3)]
        tall_ref[pl.ds(0, half, stride=2)] = one[:, :SIDE]
        tall_ref[pl.ds(1, half, stride=2)] = two[:, SIDE:]
        tall_ref[pl.ds(64, half, stride=2)] = one[:, SIDE:]
        tall_ref[pl.ds(65, half, stride=2)] = three[:, :SIDE]
        tall_ref[pl.ds(128, half, stride=2)] = two[:, :SIDE]
        tall_ref[pl.ds(129, half, stride=2)] = three[:, SIDE:]
        columns = [tall_ref[64 * j : 64 * j + 64] for j in range(3)]
        in_ref[i] = jnp.concatenate(columns, axis=1).astype(jnp.bfloat16)
        in_t_ref[i] = jnp.concatenate([column.T for column in columns], axis=0).astype(jnp.bfloat16)
        at += 3 * half
    for i in range(3):
        square = natural(at, SIDE)
        out_ref[i] = square.astype(jnp.bfloat16)
        out_t_ref[i] = square.T.astype(jnp.bfloat16)
        at += half
    for i in range(2):
        wide = jnp.concatenate([rows_ref[pl.ds(at + j, SIDE, stride=2)] for j in range(2)], axis=1)
        ffn_in_ref[i] = wide.astype(jnp.bfloat16)
        ffn_in_t_ref[i] = wide.T.astype(jnp.bfloat16)
        at += 2 * SIDE
    for i in range(2):
        tall = natural(at, 256)
        ffn_out_ref[i] = tall.astype(jnp.bfloat16)
        ffn_out_t_ref[i] = tall.T.astype(jnp.bfloat16)
        at += 128
    up_ref[...] = jnp.concatenate(
        [rows_ref[pl.ds(at + j, SIDE, stride=4)] for j in range(4)], axis=1
    ).astype(jnp.bfloat16)
    at += 4 * SIDE
    tall_ref[:128] = jnp.zeros((128, SIDE), jnp.float32)
    tall = natural(at, 16)
    tall_ref[16:128] = jnp.zeros((112, SIDE), jnp.float32)
    small_ref[...] = tall_ref[:128].T


def unpack_weights(flat):
    bf16 = jnp.bfloat16
    shapes = [
        (4, SIDE, D),
        (3, 3 * SIDE, SIDE),
        (3, SIDE, SIDE),
        (2, SIDE_FF, SIDE),
        (2, SIDE, SIDE_FF),
        (3, SIDE, 3 * SIDE),
        (3, SIDE, SIDE),
        (2, SIDE, SIDE_FF),
        (2, SIDE_FF, SIDE),
        (SIDE, D),
    ]
    return pl.pallas_call(
        unpack_kernel,
        out_shape=[jax.ShapeDtypeStruct(shape, bf16) for shape in shapes]
        + [jax.ShapeDtypeStruct((SIDE, 128), jnp.float32)],
        in_specs=[vmem],
        out_specs=[vmem] * 11,
        scratch_shapes=[
            pltpu.VMEM((MAIN_ROWS + 8, 128), jnp.float32),
            pltpu.VMEM((512, SIDE), jnp.float32),
        ],
        compiler_params=LIMIT,
        name="unpack",
        cost_estimate=cost(8),
    )(flat)


def per_device(
    source_ids,
    target_inputs,
    lengths,
    positions,
    target_ids,
    target_mask,
    table,
    backbone_attn,
    backbone_ffn_in,
    backbone_ffn_out,
    backbone_gains,
    inner_weights,
    first_moment,
    second_moment,
    anchor,
    outer_momentum,
):
    micro = source_ids.shape[0]
    src_tokens = source_ids.shape[2]
    tgt_tokens = target_inputs.shape[2]
    size = lax.axis_size("dp")
    me = lax.axis_index("dp")
    core = me & 1
    rows = table.shape[0]
    padded = -(-rows // 512) * 512
    score = [positions, target_ids, target_mask]
    spots = positions.shape[2]
    ids_count = source_ids.size + target_inputs.size
    cap = -(-(ids_count * 5 // (size * 6)) // 16) * 16
    slots, column, near, other, scored = plan(
        me[None], source_ids, target_inputs, score, rows, size, cap, tgt_tokens
    )
    asked = ask(near, other)
    found = jnp.take(table, asked[:, :cap].reshape(-1), axis=0, mode="clip")
    told = after(asked, found)[:, -(2 * micro * spots + 128) :]
    entries = told[:, : micro * spots]
    counts = told[:, micro * spots : 2 * micro * spots].reshape(size, micro, spots)
    told = told[:, 2 * micro * spots :]
    many = told[:, 0]
    used = jnp.take(told[:, 1 : 1 + micro], jnp.arange(size) ^ me, axis=0).reshape(-1)
    ends = jnp.cumsum(used)
    tiles = (ends[-1:] + TILE - 1) // TILE
    where = jnp.concatenate([me[None], tiles, ends - used]).astype(jnp.int32)
    weights = []

    most = jnp.full((8, 128), jnp.max(told[:, 1 + micro]), jnp.int32)
    most = functools.reduce(jnp.maximum, gather_peers(most, "grp"))
    weights.extend(unpack_weights(after(inner_weights, found, most)))
    table_pad, weight = table_parts(after(table, found, most), weights[9])
    goals = goal_rows(after(where, most), many, entries, table_pad, spots)
    embed_src, embed_tgt = embed_rows(
        slots,
        column,
        found.reshape(size // 2, 2, cap, -1),
        cap,
        most[0, 0],
        source_ids,
        target_inputs,
        table,
        (goals, weight, weights[0]),
    )
    down_t, in_t, out_t, ffn_in_t, ffn_out_t, attn_in, attn_out, ffn_in, ffn_out, up_b, small = weights
    ahead = [down_t, in_t, out_t, ffn_in_t, ffn_out_t, small]
    behind = [in_t, ffn_in_t, attn_in, attn_out, ffn_in, ffn_out, small]
    lens = lengths[:, 0]
    encoded = encode(lens, embed_src, backbone_attn, backbone_ffn_in, backbone_ffn_out, backbone_gains)
    decoded = decode(lens, embed_tgt, encoded, backbone_attn, backbone_ffn_in, backbone_ffn_out, backbone_gains)
    picked, *kept = side(lens, embed_src, encoded, embed_tgt, decoded, scored, ahead)
    gathered = gather_all(picked).reshape((size,) + picked.shape)
    mix, stats, packed = softmax_part(where, gathered, counts, weight, table_pad, rows)
    stats = gather_all(stats[:2]).reshape(size, 2, -1)
    top_parts, grad_up, loss_part = head_finish(where, stats, mix, goals, packed, up_b, micro, spots)
    tops = answer(top_parts.reshape((size, micro) + top_parts.shape[1:]))
    grads = side_back(lens, embed_src, encoded, embed_tgt, decoded, scored, behind, kept, tops)
    mine, other = flatten(me[None], loss_part, [*grads[:6], grad_up, grads[6]])
    sent = (mine + swap(other, "dp", 1)).astype(jnp.bfloat16)
    terms = [sent] + [swap(sent, "dp", s) for s in range(2, size, 2)]
    mine = tree_sum([term.astype(jnp.float32) for term in terms])
    other = swap(mine, "dp", 1)
    new_first, new_second, new_inner, gap, loss_total, count_total, norm = adam(
        core[None], counts, mine, other, first_moment, second_moment, inner_weights, anchor
    )
    terms = gather_peers(gap, "grp")
    mine = tree_sum([term.astype(jnp.float32) for term in terms]) / lax.axis_size("grp")
    other = swap(mine, "dp", 1)
    delta, momentum, new_anchor = outer(core[None], mine, other, anchor, outer_momentum)
    return (
        loss_total,
        count_total,
        norm,
        new_first,
        new_second,
        new_inner,
        delta,
        momentum,
        new_anchor,
    )


def solution(mesh):
    return jax.shard_map(
        per_device,
        mesh=mesh,
        in_specs=(
            P(None, ("grp", "dp"), None),
            P(None, ("grp", "dp"), None),
            P(None, ("grp", "dp"), None),
            P(None, ("grp", "dp"), None),
            P(None, ("grp", "dp"), None),
            P(None, ("grp", "dp"), None),
            P("dp", None),
            P(),
            P(),
            P(),
            P(),
            P("grp", None),
            P("grp", None),
            P("grp", None),
            P(),
            P(),
        ),
        out_specs=(
            P("grp"),
            P("grp"),
            P("grp"),
            P("grp", None),
            P("grp", None),
            P("grp", None),
            P(),
            P(),
            P(),
        ),
        check_vma=False,
    )
```

```python
import functools

import jax
import jax.numpy as jnp
from jax import lax
from jax.experimental import pallas as pl
from jax.experimental.pallas import tpu as pltpu
from jax.sharding import PartitionSpec as P

D = 512
HEADS = 8
SIDE = 64
SIDE_HEADS = 8
SIDE_FF = 256
STEP = 5


norm_eps = 1e-06
negative = -1000000000.0
beta_first = 0.9
beta_second = 0.99
adam_eps = 1e-08
learn_rate = 0.03
decay_rate = 0.01
clip_norm = 0.01
outer_rate = 0.7
outer_beta = 0.9


LOG2E = 1.4426950408889634
masked = -1e30

def dot(left, right):
    return jnp.dot(left, right, preferred_element_type=jnp.float32)

def dot_t(left, right):
    return lax.dot_general(left, right, (((1,), (1,)), ((), ())), preferred_element_type=jnp.float32)

def rms_rows(values, gain):
    return values * lax.rsqrt(jnp.mean(values * values, axis=1, keepdims=True) + norm_eps) * gain

def gelu(values):
    inner = values * (0.7978845608028654 + 0.035677408136300125 * (values * values))
    return (0.5 * values) * (1.0 + jnp.tanh(inner))

def lane_heads(query, keys, values, key_bias, causal_bias):
    lane = lax.broadcasted_iota(jnp.int32, (1, 128), 1)
    scale = 0.125 * LOG2E
    mixed = []
    for pair in range(4):
        span = slice(128 * pair, 128 * pair + 128)
        q_pair, k_pair, v_pair = query[:, span], keys[:, span], values[:, span]
        halves = []
        for side in range(2):
            own = (lane < 64) if side == 0 else (lane >= 64)
            spare = lane == (64 if side == 0 else 0)
            q_head = jnp.where(own, q_pair, spare.astype(jnp.bfloat16))
            k_head = jnp.where(own, k_pair, jnp.where(spare, key_bias, jnp.bfloat16(0)))
            scores = dot_t(q_head, k_head)
            if causal_bias is not None:
                scores = scores + causal_bias
            peak = jnp.max(scores, axis=1, keepdims=True)
            weight = jnp.exp2((scores - peak) * scale)
            total = jnp.sum(weight, axis=1, keepdims=True)
            halves.append(dot(weight.astype(jnp.bfloat16), v_pair) / total)
        mixed.append(jnp.where(lane < 64, halves[0], halves[1]).astype(jnp.bfloat16))
    return jnp.concatenate(mixed, axis=1)

def bias_column(count, valid):
    place = lax.broadcasted_iota(jnp.int32, (count, 1), 0)
    return jnp.where(place < valid, 0.0, masked).astype(jnp.bfloat16)

def fetch(pairs, sems):
    copies = [pltpu.make_async_copy(src, dst, sems.at[i]) for i, (src, dst) in enumerate(pairs)]
    for copy in copies:
        copy.start()
    return copies

def frozen_ffn(state_ref, out_ref, gain, win_ref, wout_ref, finish):
    tile = 512

    def step(i, carry):
        at = pl.ds(pl.multiple_of(i * tile, tile), tile)
        state = state_ref[at]
        normed = rms_rows(state, gain).astype(jnp.bfloat16)
        total = state
        for start in range(0, win_ref.shape[1], 512):
            hidden = gelu(dot(normed, win_ref[:, start : start + 512])).astype(jnp.bfloat16)
            total = total + dot(hidden, wout_ref[start : start + 512])
        out_ref[at] = finish(total).astype(out_ref.dtype)
        return carry

    lax.fori_loop(0, state_ref.shape[0] // tile, step, 0)


def encoder_kernel(
    len_ref, x_ref, gains_ref, attn_hbm, win_hbm, wout_hbm, out_ref, attn_ref, win_ref, wout_ref, qkv_ref, state_ref, sems
):
    first, second, third, fourth = fetch(
        [
            (attn_hbm.at[0, :, : 3 * D], attn_ref.at[:, : 3 * D]),
            (attn_hbm.at[0, :, 3 * D :], attn_ref.at[:, 3 * D :]),
            (win_hbm.at[0], win_ref),
            (wout_hbm.at[0], wout_ref),
        ],
        sems,
    )
    micro = len_ref.shape[0]
    tokens = x_ref.shape[0] // micro
    normed = rms_rows(x_ref[...].astype(jnp.float32), gains_ref[0:1]).astype(jnp.bfloat16)
    first.wait()
    qkv_ref[...] = dot(normed, attn_ref[:, : 3 * D]).astype(jnp.bfloat16)
    second.wait()

    def step(i, carry):
        at = pl.ds(pl.multiple_of(i * tokens, tokens), tokens)
        bias = bias_column(tokens, len_ref[i, 0])
        mixed = lane_heads(qkv_ref[at, :D], qkv_ref[at, D : 2 * D], qkv_ref[at, 2 * D :], bias, None)
        state_ref[at] = x_ref[at].astype(jnp.float32) + dot(mixed, attn_ref[:, 3 * D :])
        return carry

    lax.fori_loop(0, micro, step, 0)
    third.wait()
    fourth.wait()
    frozen_ffn(
        state_ref, out_ref, gains_ref[1:2], win_ref, wout_ref, lambda v: rms_rows(v, gains_ref[2:3])
    )


def decoder_kernel(
    len_ref, x_ref, encoded_ref, gains_ref, attn_hbm, win_hbm, wout_hbm, out_ref, attn_ref, cross_ref, win_ref, wout_ref, kv_ref, state_ref, sems
):
    first, second, third, fourth = fetch(
        [
            (attn_hbm.at[1], attn_ref),
            (attn_hbm.at[2], cross_ref),
            (win_hbm.at[1], win_ref),
            (wout_hbm.at[1], wout_ref),
        ],
        sems,
    )
    micro = len_ref.shape[0]
    tokens = x_ref.shape[0] // micro
    sources = encoded_ref.shape[0] // micro
    x = x_ref[...].astype(jnp.float32)
    normed = rms_rows(x, gains_ref[3:4]).astype(jnp.bfloat16)
    row = lax.broadcasted_iota(jnp.int32, (tokens, tokens), 0)
    column = lax.broadcasted_iota(jnp.int32, (tokens, tokens), 1)
    causal = jnp.where(column <= row, 0.0, masked)
    first.wait()
    qkv = dot(normed, attn_ref[:, : 3 * D]).astype(jnp.bfloat16)
    mixed = []
    for i in range(micro):
        own = qkv[i * tokens : (i + 1) * tokens]
        bias = bias_column(tokens, len_ref[i, 1])
        mixed.append(lane_heads(own[:, :D], own[:, D : 2 * D], own[:, 2 * D :], bias, causal))
    state = x + dot(jnp.concatenate(mixed, axis=0), attn_ref[:, 3 * D :])
    second.wait()
    kv_ref[...] = dot(encoded_ref[...], cross_ref[:, D : 3 * D]).astype(jnp.bfloat16)
    normed = rms_rows(state, gains_ref[4:5]).astype(jnp.bfloat16)
    query = dot(normed, cross_ref[:, :D]).astype(jnp.bfloat16)
    mixed = []
    for i in range(micro):
        own = query[i * tokens : (i + 1) * tokens]
        at = slice(i * sources, (i + 1) * sources)
        bias = bias_column(sources, len_ref[i, 0])
        mixed.append(lane_heads(own, kv_ref[at, :D], kv_ref[at, D:], bias, None))
    state_ref[...] = state + dot(jnp.concatenate(mixed, axis=0), cross_ref[:, 3 * D :])
    third.wait()
    fourth.wait()
    frozen_ffn(state_ref, out_ref, gains_ref[5:6], win_ref, wout_ref, lambda v: v)


def cost(micros):
    return pl.CostEstimate(
        flops=int(micros * 8e8), bytes_accessed=int(micros * 3e6), transcendentals=0
    )


smem = pl.BlockSpec(memory_space=pltpu.SMEM)
vmem = pl.BlockSpec(memory_space=pltpu.VMEM)
hbm = pl.BlockSpec(memory_space=pl.ANY)
LIMIT = pltpu.CompilerParams(vmem_limit_bytes=56 * 2**20)

def encode(lens, x, attn, ffn_in, ffn_out, gains):
    tokens = x.shape[0]
    return pl.pallas_call(
        encoder_kernel,
        out_shape=jax.ShapeDtypeStruct((tokens, D), jnp.bfloat16),
        in_specs=[smem, vmem, vmem, hbm, hbm, hbm],
        out_specs=vmem,
        scratch_shapes=[pltpu.VMEM((D, 4 * D), jnp.bfloat16), pltpu.VMEM((D, 4 * D), jnp.bfloat16), pltpu.VMEM((4 * D, D), jnp.bfloat16),
            pltpu.VMEM((tokens, 3 * D), jnp.bfloat16), pltpu.VMEM((tokens, D), jnp.float32), pltpu.SemaphoreType.DMA((4,))],
        compiler_params=LIMIT,
        name="encoder",
        cost_estimate=cost(14),
    )(lens, x, gains, attn, ffn_in, ffn_out)

def decode(lens, x, encoded, attn, ffn_in, ffn_out, gains):
    tokens = x.shape[0]
    sources = encoded.shape[0]
    return pl.pallas_call(
        decoder_kernel,
        out_shape=jax.ShapeDtypeStruct((tokens, D), jnp.bfloat16),
        in_specs=[smem, vmem, vmem, vmem, hbm, hbm, hbm],
        out_specs=vmem,
        scratch_shapes=[pltpu.VMEM((D, 4 * D), jnp.bfloat16), pltpu.VMEM((D, 4 * D), jnp.bfloat16), pltpu.VMEM((D, 4 * D), jnp.bfloat16), pltpu.VMEM((4 * D, D), jnp.bfloat16),
            pltpu.VMEM((sources, 2 * D), jnp.bfloat16), pltpu.VMEM((tokens, D), jnp.float32), pltpu.SemaphoreType.DMA((4,))],
        compiler_params=LIMIT,
        name="decoder",
        cost_estimate=cost(10.5),
    )(lens, x, encoded, gains, attn, ffn_in, ffn_out)

def dot_l(left, right):
    return lax.dot_general(left, right, (((0,), (0,)), ((), ())), preferred_element_type=jnp.float32)

def rms_columns(values, gain):
    return values * lax.rsqrt(jnp.mean(values * values, axis=0, keepdims=True) + norm_eps) * gain

def rms_columns_back(values, gain, grad):
    inverse = lax.rsqrt(jnp.mean(values * values, axis=0, keepdims=True) + norm_eps)
    gained = grad * gain
    along = jnp.mean(values * gained, axis=0, keepdims=True)
    gain_grad = jnp.sum(grad * (values * inverse), axis=1, keepdims=True)
    return inverse * gained - values * (inverse * inverse * inverse * along), gain_grad

def gelu_back(values, grad):
    square = values * values
    tanh = jnp.tanh(values * (0.7978845608028654 + 0.035677408136300125 * square))
    slope = 0.5 * (1.0 + tanh) + (0.5 * values) * (1.0 - tanh * tanh) * (0.7978845608028654 + 0.107032224408900375 * square)
    return grad * slope

side_scale = (SIDE // SIDE_HEADS) ** -0.5

def keys_with_bias(keys_t, valid):
    count = keys_t.shape[1]
    place = lax.broadcasted_iota(jnp.int32, (64, count), 1)
    line = lax.broadcasted_iota(jnp.int32, (64, count), 0)
    bias = jnp.where((line == 0) & (place >= valid), masked, 0.0)
    return jnp.concatenate([keys_t.astype(jnp.float32), bias], axis=0).T.astype(jnp.bfloat16)

def head_query(query_t, head):
    line = lax.broadcasted_iota(jnp.int32, (64, 1), 0)
    own = jnp.where(line // 8 == head, query_t, 0.0)
    ones = jnp.broadcast_to(jnp.where(line == 0, 1.0, 0.0), own.shape)
    return jnp.concatenate([own, ones], axis=0).astype(jnp.bfloat16)

def rounded(values):
    return values.astype(jnp.bfloat16).astype(jnp.float32)

def causal_columns(count):
    key = lax.broadcasted_iota(jnp.int32, (count, count), 0)
    query = lax.broadcasted_iota(jnp.int32, (count, count), 1)
    return jnp.where(key <= query, 0.0, masked)

def staged(count, *stages):
    last = max(lag for lag, _ in stages)
    for step in range(count + last):
        for lag, stage in stages:
            if 0 <= step - lag < count:
                stage(step - lag)


def head_steps(keys):
    count = keys[0].shape[0]
    chunk = min(256, count)
    parts = count // chunk

    def place(step):
        head = step // parts
        return head, head // SIDE_HEADS, head % SIDE_HEADS, slice(step % parts * chunk, step % parts * chunk + chunk)

    return parts, place


def side_heads(items, causal):
    keys = [keys_with_bias(item[1], item[3]) for item in items]
    parts, place = head_steps(keys)
    scores, tops, weights, peaks, totals, mixed, queries = {}, {}, {}, {}, {}, {}, {}

    def score(step):
        unit, pair, head, span = place(step)
        if step % parts == 0:
            queries[unit] = head_query(items[pair][0], head)
        part = dot(keys[pair][span], queries[unit])
        scores[step] = part if causal is None else part + causal[span]

    def top(step):
        tops[step] = jnp.max(scores[step], axis=0, keepdims=True)

    def weigh(step):
        unit = place(step)[0]
        if step % parts == 0:
            peaks[unit] = functools.reduce(jnp.maximum, [tops.pop(step + i) for i in range(parts)])
        weight = jnp.exp2((scores.pop(step) - peaks[unit]) * (side_scale * LOG2E))
        amount = jnp.sum(weight, axis=0, keepdims=True)
        totals[unit] = totals[unit] + amount if unit in totals else amount
        weights[step] = weight.astype(jnp.bfloat16)

    def mix(step):
        unit, pair, head, span = place(step)
        values = items[pair][2][8 * head : 8 * head + 8, span].astype(jnp.bfloat16)
        piece = dot(values, weights.pop(step))
        mixed[unit] = mixed[unit] + piece if unit in mixed else piece

    staged(len(items) * SIDE_HEADS * parts, (0, score), (1, top), (parts, weigh), (parts + 2, mix))
    result = []
    for pair in range(len(items)):
        units = range(pair * SIDE_HEADS, (pair + 1) * SIDE_HEADS)
        outs = jnp.concatenate([mixed[unit] / totals[unit] for unit in units], axis=0)
        sums = [peaks[unit] * (side_scale * LOG2E) + jnp.log2(totals[unit]) for unit in units]
        result.append((outs, jnp.concatenate(sums, axis=0)))
    return result


def side_heads_back(items, causal):
    keys = [keys_with_bias(item[1], item[3]) for item in items]
    values = [item[2].T.astype(jnp.bfloat16) for item in items]
    parts, place = head_steps(keys)
    line = lax.broadcasted_iota(jnp.int32, (64, 1), 0)
    scores, grads, weights, along, queries, owns = {}, {}, {}, {}, {}, {}
    grad_q, grad_k, grad_v = {}, {}, {}

    def score(step):
        unit, pair, head, span = place(step)
        if step % parts == 0:
            queries[unit] = head_query(items[pair][0], head)
            owns[unit] = jnp.where(line // 8 == head, items[pair][5], 0.0).astype(jnp.bfloat16)
        part = dot(keys[pair][span], queries[unit])
        scores[step] = part if causal is None else part + causal[span]
        grads[step] = dot(values[pair][span], owns[unit])

    def weigh(step):
        unit, pair, head, _ = place(step)
        sums = items[pair][4][head : head + 1]
        weight = jnp.exp2(scores.pop(step) * (side_scale * LOG2E) - sums)
        grads[step] = rounded(grads[step])
        part = jnp.sum(grads[step] * weight, axis=0, keepdims=True)
        along[unit] = along[unit] + part if unit in along else part
        weights[step] = weight

    def finish(step):
        unit, pair, head, span = place(step)
        rows = slice(8 * head, 8 * head + 8)
        query, key, _, _, _, grad = items[pair]
        weight = weights.pop(step)
        grad_s = (weight * (grads.pop(step) - along[unit])).astype(jnp.bfloat16)
        part = dot(key[rows, span].astype(jnp.bfloat16), grad_s)
        grad_q[unit] = grad_q[unit] + part if unit in grad_q else part
        grad_k[step] = dot_t(query[rows].astype(jnp.bfloat16), grad_s)
        grad_v[step] = dot_t(grad[rows].astype(jnp.bfloat16), weight.astype(jnp.bfloat16))

    staged(len(items) * SIDE_HEADS * parts, (0, score), (2, weigh), (parts + 2, finish))

    def joined(pieces, units):
        rows = [
            jnp.concatenate([pieces[unit * parts + i] for i in range(parts)], axis=1) for unit in units
        ]
        return jnp.concatenate(rows, axis=0)

    result = []
    for pair in range(len(items)):
        units = range(pair * SIDE_HEADS, (pair + 1) * SIDE_HEADS)
        whole_q = jnp.concatenate([grad_q[unit] for unit in units], axis=0)
        result.append((whole_q * side_scale, joined(grad_k, units) * side_scale, joined(grad_v, units)))
    return result


def chosen_columns(tokens, positions):
    token = lax.broadcasted_iota(jnp.int32, (tokens, positions.shape[1]), 0)
    return jnp.where(token == positions, 1.0, 0.0).astype(jnp.bfloat16)

def side_kernel(len_ref, src_ref, encoded_ref, tgt_ref, decoded_ref, positions_ref, down_ref, attn_in_ref, attn_out_ref, ffn_in_ref, ffn_out_ref, small_ref,
                picked_ref, enc_ref, dec_ref, enc_mixed_ref, self_mixed_ref, cross_mixed_ref, enc_sums_ref, self_sums_ref, cross_sums_ref):
    micro = len_ref.shape[0]

    def gain(i):
        return small_ref[:, i:i + 1]

    def attend(which, query_n, key_n, side_of, causal, mixed_ref, sums_ref):
        query = rounded(dot(attn_in_ref[which, :64], query_n))
        keyval = rounded(dot(attn_in_ref[which, 64:], key_n))
        width, far = query.shape[1] // micro, keyval.shape[1] // micro
        spans = [
            (slice(i * width, (i + 1) * width), slice(i * far, (i + 1) * far)) for i in range(micro)
        ]
        items = [
            (query[:, near], keyval[:64, away], keyval[64:, away], len_ref[i, side_of])
            for i, (near, away) in enumerate(spans)
        ]
        parts = []
        for (near, _), (mixed, sums) in zip(spans, side_heads(items, causal)):
            sums_ref[:, near] = sums
            parts.append(mixed.astype(jnp.bfloat16))
        mixed_b = jnp.concatenate(parts, axis=1)
        mixed_ref[...] = mixed_b
        return dot(attn_out_ref[which], mixed_b)

    def ffn(which, normed):
        active = gelu(dot(ffn_in_ref[which], normed)).astype(jnp.bfloat16)
        return dot(ffn_out_ref[which], active)

    def norm(values, i):
        return rms_columns(values, gain(i)).astype(jnp.bfloat16)

    state = dot_t(down_ref[0], src_ref[...])
    enc_ref[0] = state
    normed = norm(state, 0)
    flow = dot_t(down_ref[2], tgt_ref[...])
    dec_ref[0] = flow
    normed_flow = norm(flow, 3)
    tokens = flow.shape[1] // micro
    causal = causal_columns(tokens)
    state = state + attend(0, normed, normed, 0, None, enc_mixed_ref, enc_sums_ref)
    enc_ref[1] = state
    flow = flow + attend(1, normed_flow, normed_flow, 1, causal, self_mixed_ref, self_sums_ref)
    dec_ref[1] = flow
    state = state + ffn(0, norm(state, 1))
    enc_ref[2] = state
    joined = dot_t(down_ref[1], encoded_ref[...])
    enc_ref[3] = joined
    gate = jax.nn.sigmoid(gain(7))
    memory = norm(gate * joined + (1.0 - gate) * state, 2)
    flow = flow + attend(2, norm(flow, 4), memory, 0, None, cross_mixed_ref, cross_sums_ref)
    dec_ref[2] = flow
    flow = flow + ffn(1, norm(flow, 5))
    dec_ref[3] = flow
    joined = dot_t(down_ref[3], decoded_ref[...])
    dec_ref[4] = joined
    gate = jax.nn.sigmoid(gain(8))
    top = norm(gate * joined + (1.0 - gate) * flow, 6)
    for i in range(micro):
        chosen = chosen_columns(tokens, positions_ref[i : i + 1])
        picked_ref[i] = dot(top[:, i * tokens : (i + 1) * tokens], chosen).astype(jnp.bfloat16)


def side(lens, src, encoded, tgt, decoded, positions, weights):
    s, t = src.shape[0], tgt.shape[0]
    m, p = positions.shape
    f32, bf16 = jnp.float32, jnp.bfloat16
    shapes = [((m, 64, p), bf16), ((4, 64, s), f32), ((5, 64, t), f32), ((64, s), bf16), ((64, t), bf16), ((64, t), bf16), ((8, s), f32), ((8, t), f32), ((8, t), f32)]
    return pl.pallas_call(
        side_kernel,
        out_shape=[jax.ShapeDtypeStruct(*item) for item in shapes],
        in_specs=[smem] + [vmem] * 11,
        out_specs=[vmem] * 9,
        compiler_params=LIMIT,
        name="side",
        cost_estimate=cost(24),
    )(lens, src, encoded, tgt, decoded, positions, *weights)

def back_kernel(*refs):
    (len_ref, src_ref, encoded_ref, tgt_ref, decoded_ref, positions_ref, attn_in_t_ref, ffn_in_t_ref, attn_in_ref, attn_out_ref, ffn_in_ref, ffn_out_ref, small_ref,
     enc_ref, dec_ref, enc_mixed_ref, self_mixed_ref, cross_mixed_ref, enc_sums_ref, self_sums_ref, cross_sums_ref) = refs[:21]
    parts_refs = refs[21:-7]
    down_out, attn_in_out, in_rest_out, attn_out_out, ffn_in_out, ffn_out_out, small_out = refs[-7:]
    outs = {
        "down": down_out,
        "attn_in": attn_in_out,
        "in_rest": in_rest_out,
        "attn_out": attn_out_out,
        "ffn_in": ffn_in_out,
        "ffn_out": ffn_out_out,
    }
    micro = len_ref.shape[0]

    def put(which, index, values):
        if values.shape[1] == 3 * SIDE:
            put("in_rest", index, values[:, 128:])
            values = values[:, :128]
        outs[which][index] = values

    smalls = {}

    def gain(i):
        return small_ref[:, i:i + 1]

    def norm(values, i):
        return rms_columns(values, gain(i)).astype(jnp.bfloat16)

    def norm_back(values, i, grad):
        result, smalls[i] = rms_columns_back(values, gain(i), grad)
        return result

    def blend_back(i, joined, late, grad):
        gate = jax.nn.sigmoid(gain(i))
        smalls[i] = jnp.sum(grad * (joined - late), axis=1, keepdims=True) * (gate * (1.0 - gate))
        return gate * grad, (1.0 - gate) * grad

    def ffn_back(which, normed, grad):
        grad_b = grad.astype(jnp.bfloat16)
        hidden = dot(ffn_in_t_ref[which], normed)
        active = gelu(hidden).astype(jnp.bfloat16)
        put("ffn_out", which, dot_t(active, grad_b))
        grad_hidden = gelu_back(hidden, dot(ffn_out_ref[which], grad_b)).astype(jnp.bfloat16)
        put("ffn_in", which, dot_t(normed, grad_hidden))
        return dot(ffn_in_ref[which], grad_hidden)

    def attend_back(which, query_n, key_n, mixed_ref, sums_ref, grad, side_of, causal):
        grad_b = grad.astype(jnp.bfloat16)
        put("attn_out", which, dot_t(mixed_ref[...], grad_b))
        grad_mixed = rounded(dot(attn_out_ref[which], grad_b))
        query = rounded(dot(attn_in_t_ref[which, :64], query_n))
        keyval = rounded(dot(attn_in_t_ref[which, 64:], key_n))
        width, far = query.shape[1] // micro, keyval.shape[1] // micro
        items = []
        for i in range(micro):
            near, away = slice(i * width, (i + 1) * width), slice(i * far, (i + 1) * far)
            items.append(
                (query[:, near], keyval[:64, away], keyval[64:, away], len_ref[i, side_of], sums_ref[:, near], grad_mixed[:, near])
            )
        grads_q, grads_kv = [], []
        for grad_q, grad_k, grad_v in side_heads_back(items, causal):
            grads_q.append(grad_q.astype(jnp.bfloat16))
            grads_kv.append(jnp.concatenate([grad_k, grad_v], axis=0).astype(jnp.bfloat16))
        return jnp.concatenate(grads_q, axis=1), jnp.concatenate(grads_kv, axis=1)

    tokens = tgt_ref.shape[0] // micro
    grads = []
    for index in range(micro):
        grad_picked = tree_sum([ref[index].astype(jnp.float32) for ref in parts_refs])
        chosen = chosen_columns(tokens, positions_ref[index : index + 1])
        high = grad_picked.astype(jnp.bfloat16)
        low = (grad_picked - high.astype(jnp.float32)).astype(jnp.bfloat16)
        grads.append(dot_t(high, chosen) + dot_t(low, chosen))
    grad = jnp.concatenate(grads, axis=1)
    gate = jax.nn.sigmoid(gain(8))
    final = gate * dec_ref[4] + (1.0 - gate) * dec_ref[3]
    grad = norm_back(final, 6, grad)
    grad_joined, grad = blend_back(8, dec_ref[4], dec_ref[3], grad)
    put("down", 3, dot(grad_joined.astype(jnp.bfloat16), decoded_ref[...]))
    grad = grad + norm_back(dec_ref[2], 5, ffn_back(1, norm(dec_ref[2], 5), grad))
    gate = jax.nn.sigmoid(gain(7))
    final = gate * enc_ref[3] + (1.0 - gate) * enc_ref[2]
    memory = norm(final, 2)
    normed = norm(dec_ref[1], 4)
    grad_q, grad_kv = attend_back(2, normed, memory, cross_mixed_ref, cross_sums_ref, grad, 0, None)
    zero_q = jnp.zeros((128, tgt_ref.shape[0]), jnp.bfloat16)
    zero_kv = jnp.zeros((64, src_ref.shape[0]), jnp.bfloat16)
    put("attn_in", 2, dot_t(normed, jnp.concatenate([grad_q, zero_q], axis=0)) + dot_t(memory, jnp.concatenate([zero_kv, grad_kv], axis=0)))
    weight = attn_in_ref[2]
    grad_memory = dot(weight, jnp.concatenate([zero_kv, grad_kv], axis=0))
    grad = grad + norm_back(dec_ref[1], 4, dot(weight, jnp.concatenate([grad_q, zero_q], axis=0)))
    normed = norm(dec_ref[0], 3)
    grad_q, grad_kv = attend_back(1, normed, normed, self_mixed_ref, self_sums_ref, grad, 1, causal_columns(tokens))
    grad_qkv = jnp.concatenate([grad_q, grad_kv], axis=0)
    put("attn_in", 1, dot_t(normed, grad_qkv))
    grad = grad + norm_back(dec_ref[0], 3, dot(attn_in_ref[1], grad_qkv))
    put("down", 2, dot(grad.astype(jnp.bfloat16), tgt_ref[...]))
    grad = norm_back(final, 2, grad_memory)
    grad_joined, grad = blend_back(7, enc_ref[3], enc_ref[2], grad)
    put("down", 1, dot(grad_joined.astype(jnp.bfloat16), encoded_ref[...]))
    grad = grad + norm_back(enc_ref[1], 1, ffn_back(0, norm(enc_ref[1], 1), grad))
    normed = norm(enc_ref[0], 0)
    grad_q, grad_kv = attend_back(0, normed, normed, enc_mixed_ref, enc_sums_ref, grad, 0, None)
    grad_qkv = jnp.concatenate([grad_q, grad_kv], axis=0)
    put("attn_in", 0, dot_t(normed, grad_qkv))
    grad = grad + norm_back(enc_ref[0], 0, dot(attn_in_ref[0], grad_qkv))
    put("down", 0, dot(grad.astype(jnp.bfloat16), src_ref[...]))
    lane = lax.broadcasted_iota(jnp.int32, (1, 128), 1)
    total = jnp.zeros((64, 128), jnp.float32)
    for i in range(9):
        total = total + jnp.where(lane == i, smalls[i], 0.0)
    small_out[...] = total

def side_back(lens, src, encoded, tgt, decoded, positions, weights, kept, parts):
    f32 = jnp.float32
    shapes = [(4, 64, 512), (3, 64, 128), (3, 64, 64), (3, 64, 64), (2, 64, 256), (2, 256, 64), (64, 128)]
    return pl.pallas_call(
        back_kernel,
        out_shape=[jax.ShapeDtypeStruct(shape, f32) for shape in shapes],
        in_specs=[smem] + [vmem] * (20 + len(parts)),
        out_specs=[vmem] * 7,
        compiler_params=LIMIT,
        name="side_back",
        cost_estimate=cost(34),
    )(lens, src, encoded, tgt, decoded, positions, *weights, *kept, *parts)


def swap(values, axis, distance):
    size = lax.axis_size(axis)
    return lax.ppermute(values, axis, [(i, i ^ distance) for i in range(size)])


def gather_peers(values, axis):
    return [values] + [swap(values, axis, s) for s in range(1, lax.axis_size(axis))]


def exchange(pieces, axis):
    return [pieces[0]] + [swap(pieces[s], axis, s) for s in range(1, lax.axis_size(axis))]


def tree_sum(terms):
    while len(terms) > 1:
        terms = [terms[i] + terms[i + 1] for i in range(0, len(terms), 2)]
    return terms[0]


def owners_of(ids, rows, peers, me):
    owner = jnp.zeros(ids.shape, jnp.int32)
    for peer in range(1, peers):
        owner = owner + jnp.where(ids >= peer * rows, 1, 0)
    return owner ^ me


def ranks_within(own):
    peers, count = own.shape
    own_b = own.astype(jnp.bfloat16)
    before = jnp.where(
        lax.broadcasted_iota(jnp.int32, (128, 128), 0)
        < lax.broadcasted_iota(jnp.int32, (128, 128), 1),
        1.0,
        0.0,
    ).astype(jnp.bfloat16)
    seen = jnp.zeros((peers, 1), jnp.float32)
    ranks = []
    for start in range(0, count, 128):
        block = slice(start, start + 128)
        inside = dot(own_b[:, block], before) + seen
        ranks.append(jnp.sum(own[:, block] * (inside + 1.0), axis=0, keepdims=True) - 1.0)
        seen = seen + jnp.sum(own[:, block], axis=1, keepdims=True)
    return jnp.concatenate(ranks, axis=1), seen


def column_of(row):
    return jnp.broadcast_to(row, (8, row.shape[1])).T[:, :1]


def placed(own, values, hit):
    high = jnp.floor(values * (1.0 / 64.0))
    low = values - 64.0 * high
    return 64.0 * dot((own * high).astype(jnp.bfloat16), hit) + dot(
        (own * low).astype(jnp.bfloat16), hit
    )


def score_part(rows, peers, tokens, me, busy, at_ref, goal_ref, mask_ref, token_ref, letter_ref, at):
    micro, _, spots = at_ref.shape
    token = lax.broadcasted_iota(jnp.int32, (tokens, 1), 0)
    token_f = token.astype(jnp.float32)
    spot_f = lax.broadcasted_iota(jnp.int32, (1, spots), 1).astype(jnp.float32)
    lower = jnp.where(
        lax.broadcasted_iota(jnp.int32, (tokens, tokens), 0)
        > lax.broadcasted_iota(jnp.int32, (tokens, tokens), 1),
        1.0,
        0.0,
    ).astype(jnp.bfloat16)
    goals, masks, slots, used = [], [], [], []
    for index in range(micro):
        mask = mask_ref[index].astype(jnp.float32)
        met = jnp.where(token == at_ref[index], mask, 0.0)
        times = jnp.sum(met, axis=1, keepdims=True)
        active = jnp.where(times > 0.0, 1.0, 0.0)
        wide = jnp.broadcast_to(active, (tokens, 128)).astype(jnp.bfloat16)
        slot = dot(lower, wide)[:, :1]
        here = jnp.where(slot == spot_f, active, 0.0)
        token_row = jnp.sum(here * (token_f + 1.0), axis=0, keepdims=True) - 1.0
        token_ref[index : index + 1] = token_row.astype(jnp.int32)
        count = jnp.sum(here * times, axis=0, keepdims=True).astype(jnp.int32)
        first = at + (micro + index) * spots
        letter_ref[:, first : first + spots] = jnp.broadcast_to(count, (peers, spots))
        slots.append(jnp.sum(met * slot, axis=0, keepdims=True) + float(index * spots))
        goals.append(goal_ref[index])
        masks.append(mask)
        used.append(jnp.sum(active, axis=0, keepdims=True))
    goal, mask, slot = [jnp.concatenate(rows_, axis=1) for rows_ in (goals, masks, slots)]
    far = owners_of(goal, rows, peers, 0)
    local = (goal - far * rows).astype(jnp.float32)
    line = lax.broadcasted_iota(jnp.int32, (peers, goal.shape[1]), 0)
    own = jnp.where((line == (far ^ me)) & (mask > 0.0), 1.0, 0.0)
    rank, many = ranks_within(own)
    order = lax.broadcasted_iota(jnp.int32, (1, goal.shape[1]), 1).astype(jnp.float32)
    hit = jnp.where(column_of(rank) == order, 1.0, 0.0).astype(jnp.bfloat16)
    letter_ref[:, at : at + micro * spots] = placed(own, slot, hit).astype(
        jnp.int32
    ) * 65536 + placed(own, local, hit).astype(jnp.int32)
    lane = lax.broadcasted_iota(jnp.int32, (peers, 128), 1)
    info = jnp.where(lane == 0, many, jnp.where(lane == micro + 1, busy, 0.0))
    for index in range(micro):
        info = jnp.where(lane == index + 1, used[index], info)
    first = at + 2 * micro * spots
    letter_ref[:, first : first + 128] = info.astype(jnp.int32)


def plan_kernel(rows, peers, cap, tokens, me_ref, src_ref, tgt_ref, *refs):
    score_refs, (slots_ref, column_ref, near_ref, other_ref, token_ref, letter_ref) = refs[:3], refs[3:]
    ids_row = jnp.concatenate(
        [ref[index] for ref in (src_ref, tgt_ref) for index in range(ref.shape[0])], axis=1
    )
    count = ids_row.shape[1]
    ids = ids_row.astype(jnp.float32)
    column = column_of(ids)
    column_ref[...] = column
    first_at = jnp.full((1, count), float(count), jnp.float32)
    for start in range(0, count, 256):
        place = (lax.broadcasted_iota(jnp.int32, (256, 1), 0) + start).astype(jnp.float32)
        same = column[start : start + 256] == ids
        first_at = jnp.minimum(
            first_at, jnp.min(jnp.where(same, place, float(count)), axis=0, keepdims=True)
        )
    first = first_at == lax.broadcasted_iota(jnp.int32, (1, count), 1).astype(jnp.float32)
    far = owners_of(ids_row, rows, peers, 0)
    line = lax.broadcasted_iota(jnp.int32, (peers, count), 0)
    own = jnp.where((line == (far ^ me_ref[0])) & first, 1.0, 0.0)
    rank, seen = ranks_within(own)
    width = -(-cap // 128) * 128
    spot = lax.broadcasted_iota(jnp.int32, (1, width), 1).astype(jnp.float32)
    hit = jnp.where(column_of(rank) == spot, 1.0, 0.0).astype(jnp.bfloat16)
    filled = dot(own.astype(jnp.bfloat16), hit)
    local = placed(own, (ids_row - far * rows).astype(jnp.float32), hit).astype(jnp.int32)
    letter_ref[:, :width] = local
    owner = lax.broadcasted_iota(jnp.int32, (peers, 1), 0) ^ me_ref[0]
    slots = jnp.where(filled > 0.5, local + owner * rows, -1)[:, :cap]
    for part in range(2):
        slots_ref[part : part + 1] = jnp.concatenate(
            [slots[peer : peer + 1] for peer in range(part, peers, 2)], axis=1
        )
    busy = jnp.max(seen, axis=0, keepdims=True)
    score_part(rows, peers, tokens, me_ref[0], busy, *score_refs, token_ref, letter_ref, width)
    for peer in range(peers):
        letter = near_ref if peer % 2 == 0 else other_ref
        letter[peer // 2 : peer // 2 + 1] = letter_ref[peer : peer + 1]


def plan(me, source, target, score, rows, peers, cap, tokens):
    count = source.shape[0] * source.shape[2] + target.shape[0] * target.shape[2]
    micro, _, spots = score[0].shape
    letter = -(-cap // 128) * 128 + 2 * micro * spots + 128
    shapes = [
        ((2, peers // 2 * cap), jnp.int32),
        ((count, 1), jnp.float32),
        ((peers // 2, letter), jnp.int32),
        ((peers // 2, letter), jnp.int32),
        ((micro, spots), jnp.int32),
    ]
    return pl.pallas_call(
        functools.partial(plan_kernel, rows, peers, cap, tokens),
        out_shape=[jax.ShapeDtypeStruct(*shape) for shape in shapes],
        in_specs=[smem] + [vmem] * 5,
        out_specs=[vmem] * len(shapes),
        scratch_shapes=[pltpu.VMEM((peers, letter), jnp.int32)],
        compiler_params=LIMIT,
        name="plan",
        cost_estimate=cost(4),
    )(me, source, target, *score)


def expand_kernel(sizes, slots_ref, column_ref, *refs):
    far_refs, near_ref, out_refs = refs[: -1 - len(sizes)], refs[-1 - len(sizes)], refs[-len(sizes) :]
    slots = slots_ref[...].astype(jnp.float32)
    rows = (jnp.concatenate([ref[0] for ref in far_refs], axis=0), near_ref[...])
    base = 0
    for out in out_refs:
        for start in range(0, out.shape[0], 256):
            at = base + start
            column = column_ref[at : at + 256]
            first, second = [
                dot(jnp.where(column == slots[i : i + 1], 1.0, 0.0).astype(jnp.bfloat16), rows[i])
                for i in range(2)
            ]
            out[start : start + 256] = (first + second).astype(jnp.bfloat16)
        base = base + out.shape[0]


def expand(slots, column, far, near, sizes):
    width = near.shape[1]
    return pl.pallas_call(
        functools.partial(expand_kernel, sizes),
        out_shape=[jax.ShapeDtypeStruct((size, width), jnp.bfloat16) for size in sizes],
        in_specs=[vmem] * (3 + len(far)),
        out_specs=[vmem] * len(sizes),
        compiler_params=LIMIT,
        name="expand",
        cost_estimate=cost(3.8),
    )(slots, column, *far, near)


def ask(near, other):
    count = near.shape[0]
    pairs = jnp.stack([near, swap(other, "dp", 1)], axis=1)
    far = [pairs[:1]] + [swap(pairs[i : i + 1], "dp", 2 * i) for i in range(1, count)]
    return jnp.concatenate(far).reshape(2 * count, -1)


def send_rows(slots, column, found, sizes, between):
    count = found.shape[0]
    far = [found[0]] + [swap(found[i], "dp", 2 * i) for i in range(1, count)]
    other = jnp.concatenate([part[1] for part in far])
    near = swap(after(other, *between), "dp", 1)
    return expand(slots, column, far, near, sizes)


def every_row(ids, table, rows):
    size = lax.axis_size("dp")
    me = lax.axis_index("dp")

    def step(i, carry):
        shard, filled = carry
        local = ids - (me + i) % size * rows
        here = (local >= 0) & (local < rows)
        found = jnp.take(shard, jnp.clip(local, 0, rows - 1), axis=0)
        shard = lax.ppermute(shard, "dp", [((j + 1) % size, j) for j in range(size)])
        return shard, jnp.where(here[:, None], found, filled)

    empty = jnp.zeros((ids.shape[0], table.shape[1]), table.dtype)
    return lax.fori_loop(0, size, step, (table, empty))[1]


def embed_rows(slots, column, found, cap, most, source, target, table, between):
    sizes = [source.size, target.size]
    result = tuple(send_rows(slots, column, found, sizes, between))

    def long_way(carry):
        ids = jnp.concatenate([source.reshape(-1), target.reshape(-1)])
        filled = every_row(ids, table, table.shape[0])
        return (jnp.zeros_like(carry[0]), (filled[: sizes[0]], filled[sizes[0] :]))

    return lax.while_loop(lambda carry: jnp.max(carry[0]) > cap, long_way, (most, result))[1]


def gather_all(values):
    far = [values] + [swap(values, "dp", s) for s in range(2, lax.axis_size("dp"), 2)]
    return far, swap(jnp.stack(far), "dp", 1)


def add_home(own, other):
    pair = (own.astype(jnp.float32) + swap(other, "dp", 1).astype(jnp.float32)).astype(own.dtype)
    return [pair[0]] + [swap(pair[i], "dp", 2 * i) for i in range(1, pair.shape[0])]


def table_kernel(rows, table_ref, up_ref, padded_ref, weight_ref):
    block = table_ref.shape[0]
    place = lax.broadcasted_iota(jnp.int32, (block, 1), 0) + pl.program_id(0) * block
    table = jnp.where(place < rows, table_ref[...], jnp.bfloat16(0))
    padded_ref[...] = table
    lifted = dot_t(table, up_ref[...]) * (D ** (-0.5) * LOG2E)
    high = lifted.astype(jnp.bfloat16)
    weight_ref[:, :SIDE] = high
    weight_ref[:, SIDE:] = (lifted - high.astype(jnp.float32)).astype(jnp.bfloat16)


VOCAB_BLOCK = 512
TILE = 512


def table_parts(table, up_b):
    rows, width = table.shape
    padded = -(-rows // VOCAB_BLOCK) * VOCAB_BLOCK
    return pl.pallas_call(
        functools.partial(table_kernel, rows),
        out_shape=[
            jax.ShapeDtypeStruct((padded, width), jnp.bfloat16),
            jax.ShapeDtypeStruct((padded, 2 * SIDE), jnp.bfloat16),
        ],
        grid=(padded // VOCAB_BLOCK,),
        in_specs=[
            pl.BlockSpec((VOCAB_BLOCK, width), lambda i: (i, 0)),
            pl.BlockSpec((SIDE, width), lambda i: (0, 0)),
        ],
        out_specs=[
            pl.BlockSpec((VOCAB_BLOCK, width), lambda i: (i, 0)),
            pl.BlockSpec((VOCAB_BLOCK, 2 * SIDE), lambda i: (i, 0)),
        ],
        compiler_params=LIMIT,
        name="table_parts",
        cost_estimate=cost(5),
    )(table, up_b)


def goals_kernel(spots, micro, me_ref, letter_ref, table_ref, out_ref, where_ref, tall_ref, sum_ref, sem):
    peers, length = letter_ref.shape
    entry_at = length - 128 - 2 * micro * spots
    where_ref[0] = me_ref[0]
    first = jnp.int32(0)
    for device in range(peers):
        for index in range(micro):
            where_ref[2 + device * micro + index] = first
            first = first + letter_ref[me_ref[0] ^ device, length - 128 + 1 + index]
    where_ref[1] = (first + TILE - 1) // TILE
    tiles = where_ref[1]
    for start in range(0, table_ref.shape[0], VOCAB_BLOCK):
        tall_ref[start : start + VOCAB_BLOCK] = table_ref[start : start + VOCAB_BLOCK].astype(jnp.float32)

    def clear(i, carry):
        sum_ref[pl.ds(pl.multiple_of(i * TILE, TILE), TILE)] = jnp.zeros((TILE, sum_ref.shape[1]), jnp.float32)
        return carry

    lax.fori_loop(0, tiles, clear, 0)
    for peer in range(peers):
        base = 2 + (peer ^ where_ref[0]) * micro

        def add(j, carry):
            entry = letter_ref[peer, entry_at + j]
            slot = entry // 65536
            local = entry - slot * 65536
            row = slot + where_ref[base]
            for index in range(1, micro):
                row = jnp.where(slot >= index * spots, slot - index * spots + where_ref[base + index], row)
            sum_ref[pl.ds(row, 1)] = sum_ref[pl.ds(row, 1)] + tall_ref[pl.ds(local, 1)]
            return carry

        lax.fori_loop(0, letter_ref[peer, length - 128], add, 0)

    def send(i, carry):
        at = pl.ds(pl.multiple_of(i * TILE, TILE), TILE)
        copy = pltpu.make_async_copy(sum_ref.at[at], out_ref.at[at], sem)
        copy.start()
        copy.wait()
        return carry

    lax.fori_loop(0, tiles, send, 0)


def goal_rows(me, letters, table_pad, micro, spots):
    total = letters.shape[0] * micro * spots
    padded, width = table_pad.shape
    return pl.pallas_call(
        functools.partial(goals_kernel, spots, micro),
        out_shape=[
            jax.ShapeDtypeStruct((total, width), jnp.float32),
            jax.ShapeDtypeStruct((2 + letters.shape[0] * micro,), jnp.int32),
        ],
        in_specs=[smem, smem, vmem],
        out_specs=[hbm, smem],
        scratch_shapes=[
            pltpu.VMEM((padded, width), jnp.float32),
            pltpu.VMEM((total, width), jnp.float32),
            pltpu.SemaphoreType.DMA,
        ],
        compiler_params=LIMIT,
        name="goals",
        cost_estimate=cost(9),
    )(me, letters, table_pad)


def softmax_kernel(rows, where_ref, *refs):
    far_refs = refs[:-9]
    near_ref, letter_ref, weight_ref, table_ref, mix_ref, stats_ref, packed_ref, all_ref, gathered_ref = refs[-9:]
    step = pl.program_id(0)
    peers, micro, _, spots = gathered_ref.shape
    tiles = where_ref[1]
    count_at = letter_ref.shape[1] - 128 - micro * spots

    @pl.when(step == 0)
    def _():
        def clear(i, carry):
            all_ref[pl.ds(pl.multiple_of(i * TILE, TILE), TILE)] = jnp.zeros((TILE, 128), jnp.float32)
            return carry

        lax.fori_loop(0, tiles, clear, 0)
        for i, far_ref in enumerate(far_refs):
            gathered_ref[2 * i] = far_ref[...]
            gathered_ref[2 * i + 1] = near_ref[i]
        for device in range(peers):
            for index in range(micro):
                peer = where_ref[0] ^ device
                block = jnp.concatenate(
                    [
                        gathered_ref[peer, index].astype(jnp.float32),
                        letter_ref[
                            pl.ds(peer, 1), count_at + index * spots : count_at + (index + 1) * spots
                        ].astype(jnp.float32),
                        jnp.zeros((SIDE - 1, spots), jnp.float32),
                    ],
                    axis=0,
                )
                all_ref[pl.ds(where_ref[2 + device * micro + index], spots)] = block.T

    @pl.when(step < tiles)
    def _():
        mine = all_ref[pl.ds(pl.multiple_of(step * TILE, TILE), TILE)]
        packed_ref[...] = mine
        picked = jnp.concatenate([mine[:, :SIDE], mine[:, :SIDE]], axis=1).astype(jnp.bfloat16)
        padded = weight_ref.shape[0]
        chunk = min(1024, padded)
        logits, shares = {}, {}
        kept = {"peak": None}

        def score(part):
            start = part * chunk
            values = dot_t(picked, weight_ref[start : start + chunk])
            if start + chunk > rows:
                place = lax.broadcasted_iota(jnp.int32, (1, chunk), 1)
                values = jnp.where(place < rows - start, values, -jnp.inf)
            logits[part] = values

        def weigh(part):
            values = logits.pop(part)
            above = jnp.max(values, axis=1, keepdims=True)
            fade = None
            if part > 0:
                above = jnp.maximum(kept["peak"], above)
                fade = jnp.exp2(kept["peak"] - above)
            share = jnp.exp2(values - above)
            amount = jnp.sum(share, axis=1, keepdims=True)
            kept["total"] = amount if fade is None else kept["total"] * fade + amount
            kept["peak"] = above
            shares[part] = (share.astype(jnp.bfloat16), fade)

        def add(part):
            share, fade = shares.pop(part)
            piece = dot(share, table_ref[part * chunk : (part + 1) * chunk])
            kept["mix"] = piece if fade is None else kept["mix"] * fade + piece

        staged(padded // chunk, (0, score), (1, weigh), (2, add))
        peak, total, mix = kept["peak"], kept["total"], kept["mix"]
        mix_ref[...] = mix
        lane = lax.broadcasted_iota(jnp.int32, (TILE, 128), 1)
        stats_ref[...] = jnp.where(lane == 0, peak, jnp.where(lane == 1, total, 0.0)).T[:8]


def in_use(i, where):
    return jnp.minimum(i, where[1] - 1)


def softmax_part(where, far, near, letters, weight, table_pad, rows):
    micro, side_width, spots = far[0].shape
    peers = 2 * len(far)
    padded, width = table_pad.shape
    total = peers * micro * spots
    return pl.pallas_call(
        functools.partial(softmax_kernel, rows),
        out_shape=[
            jax.ShapeDtypeStruct((total, width), jnp.float32),
            jax.ShapeDtypeStruct((8, total), jnp.float32),
            jax.ShapeDtypeStruct((total, 128), jnp.float32),
        ],
        grid_spec=pltpu.PrefetchScalarGridSpec(
            num_scalar_prefetch=1,
            grid=(total // TILE,),
            in_specs=[
                *[pl.BlockSpec((micro, side_width, spots), lambda i, w: (0, 0, 0))] * len(far),
                pl.BlockSpec((len(far), micro, side_width, spots), lambda i, w: (0, 0, 0, 0)),
                pl.BlockSpec(letters.shape, lambda i, w: (0, 0)),
                pl.BlockSpec((padded, 2 * SIDE), lambda i, w: (0, 0)),
                pl.BlockSpec((padded, width), lambda i, w: (0, 0)),
            ],
            out_specs=[
                pl.BlockSpec((TILE, width), lambda i, w: (in_use(i, w), 0)),
                pl.BlockSpec((8, TILE), lambda i, w: (0, in_use(i, w))),
                pl.BlockSpec((TILE, 128), lambda i, w: (in_use(i, w), 0)),
            ],
            scratch_shapes=[
                pltpu.VMEM((total + spots, 128), jnp.float32),
                pltpu.VMEM((peers, micro, side_width, spots), jnp.bfloat16),
            ],
        ),
        compiler_params=LIMIT,
        name="softmax_part",
        cost_estimate=cost(22),
    )(where, *far, near, letters, weight, table_pad)


def finish_kernel(micro, where_ref, *refs):
    far_refs = refs[:-11]
    near_ref, mix_ref, goal_ref, packed_ref, up_ref, own_ref, other_ref, up_grad_ref, loss_ref, all_ref, top_ref = refs[-11:]
    step = pl.program_id(0)
    blocks, _, spots = top_ref.shape
    peers = blocks // micro
    tiles = where_ref[1]

    @pl.when(step == 0)
    def _():
        up_grad_ref[...] = jnp.zeros_like(up_grad_ref)
        loss_ref[...] = jnp.zeros_like(loss_ref)
        all_ref[...] = jnp.zeros_like(all_ref)

    @pl.when(step < tiles)
    def _():
        stats = [(ref[...], near_ref[i]) for i, ref in enumerate(far_refs)]
        stats = [part for pair in stats for part in pair]
        peaks = [part[0:1] for part in stats]
        peak = functools.reduce(jnp.maximum, peaks)
        total = tree_sum([part[1:2] * jnp.exp2(part[0:1] - peak) for part in stats])
        lse = peak + jnp.log2(total)
        rows = jnp.concatenate([jnp.exp2(peaks[0] - lse), lse, jnp.zeros((6, TILE), jnp.float32)], axis=0).T
        packed = packed_ref[...]
        times = packed[:, SIDE : SIDE + 1]
        picked = packed[:, :SIDE].astype(jnp.bfloat16)
        goal = goal_ref[...]
        lifted = (mix_ref[...] * (rows[:, :1] * times) - goal) * D ** (-0.5)
        lifted_b = lifted.astype(jnp.bfloat16)
        all_ref[pl.ds(pl.multiple_of(step * TILE, TILE), TILE), :SIDE] = dot_t(lifted_b, up_ref[...])
        up_grad_ref[...] += dot_l(picked, lifted_b)
        aim = jnp.sum(dot(picked, up_ref[...]) * goal, axis=1, keepdims=True) * D ** (-0.5)
        here = jnp.where(where_ref[0] == 0, times * rows[:, 1:2] * (1.0 / LOG2E), 0.0)
        loss = jnp.sum(here - aim, axis=0, keepdims=True)
        loss_ref[...] += jnp.broadcast_to(loss, loss_ref.shape)

    @pl.when(step == pl.num_programs(0) - 1)
    def _():
        for device in range(peers):
            for index in range(micro):
                block = all_ref[pl.ds(where_ref[2 + device * micro + index], spots)]
                top_ref[(where_ref[0] ^ device) * micro + index] = block.T[:SIDE].astype(jnp.bfloat16)
        for i in range(peers // 2):
            own_ref[i] = top_ref[2 * i * micro : (2 * i + 1) * micro]
            other_ref[i] = top_ref[(2 * i + 1) * micro : (2 * i + 2) * micro]


def head_finish(where, far, near, mix, goals, packed, up_b, micro, spots):
    peers = 2 * len(far)
    total, width = mix.shape
    return pl.pallas_call(
        functools.partial(finish_kernel, micro),
        out_shape=[
            *[jax.ShapeDtypeStruct((len(far), micro, SIDE, spots), jnp.bfloat16)] * 2,
            jax.ShapeDtypeStruct((SIDE, width), jnp.float32),
            jax.ShapeDtypeStruct((8, 128), jnp.float32),
        ],
        grid_spec=pltpu.PrefetchScalarGridSpec(
            num_scalar_prefetch=1,
            grid=(total // TILE,),
            in_specs=[
                *[pl.BlockSpec((2, TILE), lambda i, w: (0, in_use(i, w)))] * len(far),
                pl.BlockSpec((len(far), 2, TILE), lambda i, w: (0, 0, in_use(i, w))),
                pl.BlockSpec((TILE, width), lambda i, w: (in_use(i, w), 0)),
                pl.BlockSpec((TILE, width), lambda i, w: (in_use(i, w), 0)),
                pl.BlockSpec((TILE, 128), lambda i, w: (in_use(i, w), 0)),
                pl.BlockSpec((SIDE, width), lambda i, w: (0, 0)),
            ],
            out_specs=[
                *[pl.BlockSpec((len(far), micro, SIDE, spots), lambda i, w: (0, 0, 0, 0))] * 2,
                pl.BlockSpec((SIDE, width), lambda i, w: (0, 0)),
                pl.BlockSpec((8, 128), lambda i, w: (0, 0)),
            ],
            scratch_shapes=[
                pltpu.VMEM((total + spots, 128), jnp.float32),
                pltpu.VMEM((peers * micro, SIDE, spots), jnp.bfloat16),
            ],
        ),
        compiler_params=LIMIT,
        name="head_finish",
        cost_estimate=cost(6),
    )(where, *far, near, mix, goals, packed, up_b)


def after(values, *others):
    return lax.optimization_barrier((values, others))[0]


def pair_lanes(even, odd):
    return jnp.concatenate([even, odd], axis=1)


def flatten_kernel(me_ref, loss_ref, down_ref, in_ref, in_rest_ref, attn_out_ref, ffn_in_ref, ffn_out_ref, up_ref, small_ref, mine_ref, other_ref, turn_ref, out_ref):
    at = 0
    for i in range(4):
        turn_ref[...] = down_ref[i].T
        out_ref[at : at + 256] = pair_lanes(
            turn_ref[pl.ds(0, 256, stride=2)], turn_ref[pl.ds(1, 256, stride=2)]
        )
        at += 256
    half = SIDE // 2
    for i in range(3):
        even = in_ref.at[i][pl.ds(0, half, stride=2)]
        odd = in_ref.at[i][pl.ds(1, half, stride=2)]
        even_rest = in_rest_ref.at[i][pl.ds(0, half, stride=2)]
        odd_rest = in_rest_ref.at[i][pl.ds(1, half, stride=2)]
        out_ref[pl.ds(at, half, stride=3)] = even
        out_ref[pl.ds(at + 1, half, stride=3)] = pair_lanes(even_rest, odd[:, :SIDE])
        out_ref[pl.ds(at + 2, half, stride=3)] = pair_lanes(odd[:, SIDE:], odd_rest)
        at += 3 * half
    for i in range(3):
        out_ref[at : at + half] = pair_lanes(
            attn_out_ref.at[i][pl.ds(0, half, stride=2)], attn_out_ref.at[i][pl.ds(1, half, stride=2)]
        )
        at += half
    for i in range(2):
        for j in range(2):
            out_ref[pl.ds(at + j, SIDE, stride=2)] = ffn_in_ref[i, :, 128 * j : 128 * j + 128]
        at += 2 * SIDE
    for i in range(2):
        out_ref[at : at + 128] = pair_lanes(
            ffn_out_ref.at[i][pl.ds(0, 128, stride=2)], ffn_out_ref.at[i][pl.ds(1, 128, stride=2)]
        )
        at += 128
    for j in range(4):
        out_ref[pl.ds(at + j, SIDE, stride=4)] = up_ref[:, 128 * j : 128 * j + 128]
    at += 4 * SIDE
    turn_ref[:128] = small_ref[...].T
    out_ref[at : at + 8] = pair_lanes(
        turn_ref[pl.ds(0, 8, stride=2)], turn_ref[pl.ds(1, 8, stride=2)]
    )
    at += 8
    out_ref[at:] = jnp.zeros((out_ref.shape[0] - at, 128), jnp.float32)
    lane = lax.broadcasted_iota(jnp.int32, (8, 128), 1) - 3 * me_ref[0]
    loss = loss_ref[...]
    one = rounded(loss)
    two = rounded(loss - one)
    three = rounded(loss - one - two)
    loss = jnp.where(lane == 0, one, jnp.where(lane == 1, two, jnp.where(lane == 2, three, 0.0)))
    out_ref[LOSS_ROW : LOSS_ROW + 8] = loss
    half = mine_ref.shape[0]
    core = me_ref[0] % 2
    mine_ref[...] = out_ref[pl.ds(pl.multiple_of(core * half, 8), half)]
    other_ref[...] = out_ref[pl.ds(pl.multiple_of((1 - core) * half, 8), half)]


FLAT_ROWS = 2208
LOSS_ROW = 2192


def flatten(me, loss, pieces):
    return pl.pallas_call(
        flatten_kernel,
        out_shape=[jax.ShapeDtypeStruct((FLAT_ROWS // 2, 128), jnp.float32)] * 2,
        in_specs=[smem] + [vmem] * 9,
        out_specs=[vmem] * 2,
        scratch_shapes=[
            pltpu.VMEM((512, 64), jnp.float32),
            pltpu.VMEM((FLAT_ROWS, 128), jnp.float32),
        ],
        compiler_params=LIMIT,
        name="flatten",
        cost_estimate=cost(4),
    )(me, loss, *pieces)


MAIN_ROWS = 2176


def rows_of(ref):
    main = 128 * MAIN_ROWS
    one = len(ref.shape) == 2
    load = (lambda a, b: ref[:, a:b]) if one else (lambda a, b: ref[a:b])
    rest = load(main, main + 512).reshape(4, 128)
    last = load(main + 512, main + 576).reshape(1, 64)
    return load(0, main).reshape(MAIN_ROWS, 128), jnp.concatenate(
        [rest, jnp.concatenate([last, jnp.zeros((1, 64), jnp.float32)], axis=1)], axis=0
    )


def put_rows(ref, main_values, rest_values):
    main = 128 * MAIN_ROWS
    if len(ref.shape) == 2:
        ref[:, :main] = main_values.reshape(1, main)
        ref[:, main : main + 512] = rest_values[:4].reshape(1, 512)
        ref[:, main + 512 : main + 576] = rest_values[4:5, :64]
    else:
        ref[:main] = main_values.reshape(main)
        ref[main : main + 512] = rest_values[:4].reshape(512)
        ref[main + 512 : main + 576] = rest_values[4:5, :64].reshape(64)


def adam_kernel(count_at, core_ref, letter_ref, mine_ref, other_ref, first_ref, second_ref, inner_ref, anchor_ref, new_first_ref, new_second_ref, new_inner_ref, gap_ref, loss_ref, count_ref, norm_ref, grad_ref):
    half = mine_ref.shape[0]
    core = core_ref[0]
    grad_ref[pl.ds(pl.multiple_of(core * half, 8), half)] = mine_ref[...]
    grad_ref[pl.ds(pl.multiple_of((1 - core) * half, 8), half)] = other_ref[...]
    loss_ref[0] = jnp.sum(grad_ref[LOSS_ROW : LOSS_ROW + 1])
    grad_ref[LOSS_ROW : LOSS_ROW + 8] = jnp.zeros((8, 128), jnp.float32)
    count = jnp.sum(letter_ref[:, count_at : letter_ref.shape[1] - 128].astype(jnp.float32))
    count_ref[0] = count
    mean = grad_ref[...] * (1.0 / jnp.full((1, 1), count))
    norm = jnp.sqrt(jnp.sum(jnp.sum(mean * mean, axis=0, keepdims=True), axis=1, keepdims=True))
    norm_ref[0] = jnp.sum(norm)
    clipped = mean * jnp.minimum(1.0, clip_norm / norm)
    spans = ((0, MAIN_ROWS), (MAIN_ROWS, MAIN_ROWS + 5))
    news = []
    for span, first, second, inner, anchor in zip(
        spans, rows_of(first_ref), rows_of(second_ref), rows_of(inner_ref), rows_of(anchor_ref)
    ):
        part = clipped[span[0] : span[1]]
        new_first = beta_first * first + (1.0 - beta_first) * part
        new_second = beta_second * second + (1.0 - beta_second) * part * part
        fixed_one = new_first / (1.0 - beta_first**STEP)
        fixed_two = new_second / (1.0 - beta_second**STEP)
        new_inner = inner - learn_rate * (
            fixed_one / (jnp.sqrt(fixed_two) + adam_eps) + decay_rate * inner
        )
        news.append((new_first, new_second, new_inner))
        grad_ref[span[0] : span[1]] = anchor - new_inner
    for ref, main, rest in zip((new_first_ref, new_second_ref, new_inner_ref), news[0], news[1]):
        put_rows(ref, main, rest)
    gap_ref[...] = grad_ref[pl.ds(pl.multiple_of(core * half, 8), half)].astype(jnp.bfloat16)


def adam(core, letters, count_at, mine, other, first, second, inner, anchor):
    flat = jax.ShapeDtypeStruct(first.shape, jnp.float32)
    return pl.pallas_call(
        functools.partial(adam_kernel, count_at),
        out_shape=[
            flat,
            flat,
            flat,
            jax.ShapeDtypeStruct(mine.shape, jnp.bfloat16),
            *[jax.ShapeDtypeStruct((1,), jnp.float32)] * 3,
        ],
        in_specs=[smem] + [vmem] * 7,
        out_specs=[vmem] * 4 + [smem] * 3,
        scratch_shapes=[pltpu.VMEM((FLAT_ROWS, 128), jnp.float32)],
        compiler_params=LIMIT,
        name="adam",
        cost_estimate=cost(7),
    )(core, letters, mine, other, first, second, inner, anchor)


def outer_kernel(core_ref, mine_ref, other_ref, anchor_ref, momentum_ref, delta_ref, new_momentum_ref, new_anchor_ref, full_ref):
    half = mine_ref.shape[0]
    core = core_ref[0]
    full_ref[pl.ds(pl.multiple_of(core * half, 8), half)] = mine_ref[...]
    full_ref[pl.ds(pl.multiple_of((1 - core) * half, 8), half)] = other_ref[...]
    news = []
    for span, anchor, momentum in zip(
        ((0, MAIN_ROWS), (MAIN_ROWS, MAIN_ROWS + 5)), rows_of(anchor_ref), rows_of(momentum_ref)
    ):
        delta = full_ref[span[0] : span[1]]
        new_momentum = outer_beta * momentum + delta
        news.append((delta, new_momentum, anchor - outer_rate * (delta + outer_beta * new_momentum)))
    for ref, main, rest in zip((delta_ref, new_momentum_ref, new_anchor_ref), news[0], news[1]):
        put_rows(ref, main, rest)


def outer(core, mine, other, anchor, momentum):
    flat = jax.ShapeDtypeStruct(anchor.shape, jnp.float32)
    return pl.pallas_call(
        outer_kernel,
        out_shape=[flat] * 3,
        in_specs=[smem] + [vmem] * 4,
        out_specs=[vmem] * 3,
        scratch_shapes=[pltpu.VMEM((FLAT_ROWS, 128), jnp.float32)],
        compiler_params=LIMIT,
        name="outer",
        cost_estimate=cost(5),
    )(core, mine, other, anchor, momentum)


def unpack_kernel(flat_ref, down_ref, in_t_ref, out_t_ref, ffn_in_t_ref, ffn_out_t_ref, in_ref, out_ref, ffn_in_ref, ffn_out_ref, up_ref, small_ref, rows_ref, tall_ref):
    main, rest = rows_of(flat_ref)
    rows_ref[:MAIN_ROWS] = main
    rows_ref[MAIN_ROWS : MAIN_ROWS + 8] = jnp.concatenate([rest, jnp.zeros((3, 128), jnp.float32)], axis=0)

    def natural(at, count):
        packed = rows_ref[at : at + count // 2]
        tall_ref[pl.ds(0, count // 2, stride=2)] = packed[:, :SIDE]
        tall_ref[pl.ds(1, count // 2, stride=2)] = packed[:, SIDE:]
        return tall_ref[:count]

    at = 0
    for i in range(4):
        down_ref[i] = natural(at, 512).T.astype(jnp.bfloat16)
        at += 256
    half = SIDE // 2
    for i in range(3):
        one, two, three = [rows_ref[pl.ds(at + j, half, stride=3)] for j in range(3)]
        tall_ref[pl.ds(0, half, stride=2)] = one[:, :SIDE]
        tall_ref[pl.ds(1, half, stride=2)] = two[:, SIDE:]
        tall_ref[pl.ds(64, half, stride=2)] = one[:, SIDE:]
        tall_ref[pl.ds(65, half, stride=2)] = three[:, :SIDE]
        tall_ref[pl.ds(128, half, stride=2)] = two[:, :SIDE]
        tall_ref[pl.ds(129, half, stride=2)] = three[:, SIDE:]
        columns = [tall_ref[64 * j : 64 * j + 64] for j in range(3)]
        in_ref[i] = jnp.concatenate(columns, axis=1).astype(jnp.bfloat16)
        in_t_ref[i] = jnp.concatenate([column.T for column in columns], axis=0).astype(jnp.bfloat16)
        at += 3 * half
    for i in range(3):
        square = natural(at, SIDE)
        out_ref[i] = square.astype(jnp.bfloat16)
        out_t_ref[i] = square.T.astype(jnp.bfloat16)
        at += half
    for i in range(2):
        wide = jnp.concatenate([rows_ref[pl.ds(at + j, SIDE, stride=2)] for j in range(2)], axis=1)
        ffn_in_ref[i] = wide.astype(jnp.bfloat16)
        ffn_in_t_ref[i] = wide.T.astype(jnp.bfloat16)
        at += 2 * SIDE
    for i in range(2):
        tall = natural(at, 256)
        ffn_out_ref[i] = tall.astype(jnp.bfloat16)
        ffn_out_t_ref[i] = tall.T.astype(jnp.bfloat16)
        at += 128
    up_ref[...] = jnp.concatenate(
        [rows_ref[pl.ds(at + j, SIDE, stride=4)] for j in range(4)], axis=1
    ).astype(jnp.bfloat16)
    at += 4 * SIDE
    tall_ref[:128] = jnp.zeros((128, SIDE), jnp.float32)
    tall = natural(at, 16)
    tall_ref[16:128] = jnp.zeros((112, SIDE), jnp.float32)
    small_ref[...] = tall_ref[:128].T


def unpack_weights(flat):
    bf16 = jnp.bfloat16
    shapes = [
        (4, SIDE, D),
        (3, 3 * SIDE, SIDE),
        (3, SIDE, SIDE),
        (2, SIDE_FF, SIDE),
        (2, SIDE, SIDE_FF),
        (3, SIDE, 3 * SIDE),
        (3, SIDE, SIDE),
        (2, SIDE, SIDE_FF),
        (2, SIDE_FF, SIDE),
        (SIDE, D),
    ]
    return pl.pallas_call(
        unpack_kernel,
        out_shape=[jax.ShapeDtypeStruct(shape, bf16) for shape in shapes]
        + [jax.ShapeDtypeStruct((SIDE, 128), jnp.float32)],
        in_specs=[vmem],
        out_specs=[vmem] * 11,
        scratch_shapes=[
            pltpu.VMEM((MAIN_ROWS + 8, 128), jnp.float32),
            pltpu.VMEM((512, SIDE), jnp.float32),
        ],
        compiler_params=LIMIT,
        name="unpack",
        cost_estimate=cost(8),
    )(flat)


def per_device(
    source_ids,
    target_inputs,
    lengths,
    positions,
    target_ids,
    target_mask,
    table,
    backbone_attn,
    backbone_ffn_in,
    backbone_ffn_out,
    backbone_gains,
    inner_weights,
    first_moment,
    second_moment,
    anchor,
    outer_momentum,
):
    micro = source_ids.shape[0]
    src_tokens = source_ids.shape[2]
    tgt_tokens = target_inputs.shape[2]
    size = lax.axis_size("dp")
    me = lax.axis_index("dp")
    core = me & 1
    rows = table.shape[0]
    padded = -(-rows // 512) * 512
    score = [positions, target_ids, target_mask]
    spots = positions.shape[2]
    ids_count = source_ids.size + target_inputs.size
    cap = -(-(ids_count * 5 // (size * 6)) // 16) * 16
    slots, column, near, other, scored = plan(
        me[None], source_ids, target_inputs, score, rows, size, cap, tgt_tokens
    )
    asked = ask(near, other)
    found = jnp.take(table, asked[:, :cap].reshape(-1), axis=0, mode="clip")
    most = functools.reduce(jnp.maximum, gather_peers(after(asked, found)[:, -128:], "grp"))
    weights = unpack_weights(after(inner_weights, found, most))
    table_pad, weight = table_parts(after(table, found, most), weights[9])
    goals, where = goal_rows(me[None], after(asked, most), table_pad, micro, spots)
    embed_src, embed_tgt = embed_rows(
        slots,
        column,
        found.reshape(size // 2, 2, cap, -1),
        cap,
        most[:, 1 + micro],
        source_ids,
        target_inputs,
        table,
        (goals, weight, weights[0]),
    )
    down_t, in_t, out_t, ffn_in_t, ffn_out_t, attn_in, attn_out, ffn_in, ffn_out, up_b, small = weights
    ahead = [down_t, in_t, out_t, ffn_in_t, ffn_out_t, small]
    behind = [in_t, ffn_in_t, attn_in, attn_out, ffn_in, ffn_out, small]
    lens = lengths[:, 0]
    encoded = encode(lens, embed_src, backbone_attn, backbone_ffn_in, backbone_ffn_out, backbone_gains)
    decoded = decode(lens, embed_tgt, encoded, backbone_attn, backbone_ffn_in, backbone_ffn_out, backbone_gains)
    picked, *kept = side(lens, embed_src, encoded, embed_tgt, decoded, scored, ahead)
    far, near = gather_all(picked)
    mix, stats, packed = softmax_part(where, far, near, asked, weight, table_pad, rows)
    far, near = gather_all(stats[:2])
    own, other, grad_up, loss_part = head_finish(
        where, far, near, mix, goals, packed, up_b, micro, spots
    )
    tops = add_home(own, other)
    grads = side_back(lens, embed_src, encoded, embed_tgt, decoded, scored, behind, kept, tops)
    mine, other = flatten(me[None], loss_part, [*grads[:6], grad_up, grads[6]])
    sent = (mine + swap(other, "dp", 1)).astype(jnp.bfloat16)
    terms = [sent] + [swap(sent, "dp", s) for s in range(2, size, 2)]
    mine = tree_sum([term.astype(jnp.float32) for term in terms])
    other = swap(mine, "dp", 1)
    new_first, new_second, new_inner, gap, loss_total, count_total, norm = adam(
        core[None], asked, asked.shape[1] - 128 - micro * spots, mine, other, first_moment, second_moment, inner_weights, anchor
    )
    terms = gather_peers(gap, "grp")
    mine = tree_sum([term.astype(jnp.float32) for term in terms]) / lax.axis_size("grp")
    other = swap(mine, "dp", 1)
    delta, momentum, new_anchor = outer(core[None], mine, other, anchor, outer_momentum)
    return (
        loss_total,
        count_total,
        norm,
        new_first,
        new_second,
        new_inner,
        delta,
        momentum,
        new_anchor,
    )


def solution(mesh):
    return jax.shard_map(
        per_device,
        mesh=mesh,
        in_specs=(
            P(None, ("grp", "dp"), None),
            P(None, ("grp", "dp"), None),
            P(None, ("grp", "dp"), None),
            P(None, ("grp", "dp"), None),
            P(None, ("grp", "dp"), None),
            P(None, ("grp", "dp"), None),
            P("dp", None),
            P(),
            P(),
            P(),
            P(),
            P("grp", None),
            P("grp", None),
            P("grp", None),
            P(),
            P(),
        ),
        out_specs=(
            P("grp"),
            P("grp"),
            P("grp"),
            P("grp", None),
            P("grp", None),
            P("grp", None),
            P(),
            P(),
            P(),
        ),
        check_vma=False,
    )
```

```python
import functools

import jax
import jax.numpy as jnp
from jax import lax
from jax.experimental import pallas as pl
from jax.experimental.pallas import tpu as pltpu
from jax.sharding import PartitionSpec as P

D = 512
HEADS = 8
SIDE = 64
SIDE_HEADS = 8
SIDE_FF = 256
STEP = 5


norm_eps = 1e-06
negative = -1000000000.0
beta_first = 0.9
beta_second = 0.99
adam_eps = 1e-08
learn_rate = 0.03
decay_rate = 0.01
clip_norm = 0.01
outer_rate = 0.7
outer_beta = 0.9


LOG2E = 1.4426950408889634
masked = -1e30

def dot(left, right):
    return jnp.dot(left, right, preferred_element_type=jnp.float32)

def dot_t(left, right):
    return lax.dot_general(left, right, (((1,), (1,)), ((), ())), preferred_element_type=jnp.float32)

def rms_rows(values, gain):
    return values * lax.rsqrt(jnp.mean(values * values, axis=1, keepdims=True) + norm_eps) * gain

def gelu(values):
    inner = values * (0.7978845608028654 + 0.035677408136300125 * (values * values))
    return (0.5 * values) * (1.0 + jnp.tanh(inner))

def staged(count, *stages):
    last = max(lag for lag, _ in stages)
    for step in range(count + last):
        for lag, stage in stages:
            if 0 <= step - lag < count:
                stage(step - lag)


def lane_heads(items, causal_bias):
    lane = lax.broadcasted_iota(jnp.int32, (1, 128), 1)
    scale = 0.125 * LOG2E
    scores, peaks, weights, totals, mixed = {}, {}, {}, {}, {}

    def place(step):
        head = step % HEADS
        return items[step // HEADS], head, slice(head // 2 * 128, head // 2 * 128 + 128)

    def score(step):
        (query, keys, _, key_bias), head, span = place(step)
        own = (lane < 64) if head % 2 == 0 else (lane >= 64)
        spare = lane == (64 if head % 2 == 0 else 0)
        q_head = jnp.where(own, query[:, span], spare.astype(jnp.bfloat16))
        k_head = jnp.where(own, keys[:, span], jnp.where(spare, key_bias, jnp.bfloat16(0)))
        part = dot_t(q_head, k_head)
        scores[step] = part if causal_bias is None else part + causal_bias

    def top(step):
        peaks[step] = jnp.max(scores[step], axis=1, keepdims=True)

    def weigh(step):
        weight = jnp.exp2((scores.pop(step) - peaks.pop(step)) * scale)
        totals[step] = jnp.sum(weight, axis=1, keepdims=True)
        weights[step] = weight.astype(jnp.bfloat16)

    def mix(step):
        values, span = place(step)[0][2], place(step)[2]
        mixed[step] = dot(weights.pop(step), values[:, span]) / totals.pop(step)

    staged(len(items) * HEADS, (0, score), (0, top), (1, weigh), (2, mix))
    return [
        jnp.concatenate(
            [
                jnp.where(lane < 64, mixed[at + 2 * pair], mixed[at + 2 * pair + 1]).astype(jnp.bfloat16)
                for pair in range(HEADS // 2)
            ],
            axis=1,
        )
        for at in range(0, len(items) * HEADS, HEADS)
    ]


def bias_column(count, valid):
    place = lax.broadcasted_iota(jnp.int32, (count, 1), 0)
    return jnp.where(place < valid, 0.0, masked).astype(jnp.bfloat16)

def fetch(pairs, sems):
    copies = [pltpu.make_async_copy(src, dst, sems.at[i]) for i, (src, dst) in enumerate(pairs)]
    for copy in copies:
        copy.start()
    return copies

def frozen_ffn(state_ref, out_ref, gain, win_ref, wout_ref, finish):
    tile = 512

    def step(i, carry):
        at = pl.ds(pl.multiple_of(i * tile, tile), tile)
        state = state_ref[at]
        normed = rms_rows(state, gain).astype(jnp.bfloat16)
        hidden, active, kept = {}, {}, {"total": state}

        def widen(part):
            hidden[part] = dot(normed, win_ref[:, part * 512 : (part + 1) * 512])

        def bend(part):
            active[part] = gelu(hidden.pop(part)).astype(jnp.bfloat16)

        def narrow(part):
            kept["total"] = kept["total"] + dot(active.pop(part), wout_ref[part * 512 : (part + 1) * 512])

        staged(win_ref.shape[1] // 512, (0, widen), (1, bend), (2, narrow))
        total = kept["total"]
        out_ref[at] = finish(total).astype(out_ref.dtype)
        return carry

    lax.fori_loop(0, state_ref.shape[0] // tile, step, 0)


def encoder_kernel(
    len_ref, x_ref, gains_ref, attn_hbm, win_hbm, wout_hbm, out_ref, attn_ref, win_ref, wout_ref, qkv_ref, state_ref, sems
):
    first, second, third, fourth = fetch(
        [
            (attn_hbm.at[0, :, : 3 * D], attn_ref.at[:, : 3 * D]),
            (attn_hbm.at[0, :, 3 * D :], attn_ref.at[:, 3 * D :]),
            (win_hbm.at[0], win_ref),
            (wout_hbm.at[0], wout_ref),
        ],
        sems,
    )
    micro = len_ref.shape[0]
    tokens = x_ref.shape[0] // micro
    normed = rms_rows(x_ref[...].astype(jnp.float32), gains_ref[0:1]).astype(jnp.bfloat16)
    first.wait()
    qkv_ref[...] = dot(normed, attn_ref[:, : 3 * D]).astype(jnp.bfloat16)
    second.wait()

    def step(i, carry):
        at = pl.ds(pl.multiple_of(i * tokens, tokens), tokens)
        bias = bias_column(tokens, len_ref[i, 0])
        (mixed,) = lane_heads(
            [(qkv_ref[at, :D], qkv_ref[at, D : 2 * D], qkv_ref[at, 2 * D :], bias)], None
        )
        state_ref[at] = x_ref[at].astype(jnp.float32) + dot(mixed, attn_ref[:, 3 * D :])
        return carry

    lax.fori_loop(0, micro, step, 0)
    third.wait()
    fourth.wait()
    frozen_ffn(
        state_ref, out_ref, gains_ref[1:2], win_ref, wout_ref, lambda v: rms_rows(v, gains_ref[2:3])
    )


def decoder_kernel(
    len_ref, x_ref, encoded_ref, gains_ref, attn_hbm, win_hbm, wout_hbm, out_ref, attn_ref, cross_ref, win_ref, wout_ref, kv_ref, state_ref, sems
):
    first, second, third, fourth = fetch(
        [
            (attn_hbm.at[1], attn_ref),
            (attn_hbm.at[2], cross_ref),
            (win_hbm.at[1], win_ref),
            (wout_hbm.at[1], wout_ref),
        ],
        sems,
    )
    micro = len_ref.shape[0]
    tokens = x_ref.shape[0] // micro
    sources = encoded_ref.shape[0] // micro
    x = x_ref[...].astype(jnp.float32)
    normed = rms_rows(x, gains_ref[3:4]).astype(jnp.bfloat16)
    row = lax.broadcasted_iota(jnp.int32, (tokens, tokens), 0)
    column = lax.broadcasted_iota(jnp.int32, (tokens, tokens), 1)
    causal = jnp.where(column <= row, 0.0, masked)
    first.wait()
    qkv = dot(normed, attn_ref[:, : 3 * D]).astype(jnp.bfloat16)
    items = []
    for i in range(micro):
        own = qkv[i * tokens : (i + 1) * tokens]
        bias = bias_column(tokens, len_ref[i, 1])
        items.append((own[:, :D], own[:, D : 2 * D], own[:, 2 * D :], bias))
    mixed = lane_heads(items, causal)
    state = x + dot(jnp.concatenate(mixed, axis=0), attn_ref[:, 3 * D :])
    second.wait()
    kv_ref[...] = dot(encoded_ref[...], cross_ref[:, D : 3 * D]).astype(jnp.bfloat16)
    normed = rms_rows(state, gains_ref[4:5]).astype(jnp.bfloat16)
    query = dot(normed, cross_ref[:, :D]).astype(jnp.bfloat16)
    items = []
    for i in range(micro):
        at = slice(i * sources, (i + 1) * sources)
        bias = bias_column(sources, len_ref[i, 0])
        items.append((query[i * tokens : (i + 1) * tokens], kv_ref[at, :D], kv_ref[at, D:], bias))
    mixed = lane_heads(items, None)
    state_ref[...] = state + dot(jnp.concatenate(mixed, axis=0), cross_ref[:, 3 * D :])
    third.wait()
    fourth.wait()
    frozen_ffn(state_ref, out_ref, gains_ref[5:6], win_ref, wout_ref, lambda v: v)


def cost(micros):
    return pl.CostEstimate(
        flops=int(micros * 8e8), bytes_accessed=int(micros * 3e6), transcendentals=0
    )


smem = pl.BlockSpec(memory_space=pltpu.SMEM)
vmem = pl.BlockSpec(memory_space=pltpu.VMEM)
hbm = pl.BlockSpec(memory_space=pl.ANY)
LIMIT = pltpu.CompilerParams(vmem_limit_bytes=56 * 2**20)

def encode(lens, x, attn, ffn_in, ffn_out, gains):
    tokens = x.shape[0]
    return pl.pallas_call(
        encoder_kernel,
        out_shape=jax.ShapeDtypeStruct((tokens, D), jnp.bfloat16),
        in_specs=[smem, vmem, vmem, hbm, hbm, hbm],
        out_specs=vmem,
        scratch_shapes=[pltpu.VMEM((D, 4 * D), jnp.bfloat16), pltpu.VMEM((D, 4 * D), jnp.bfloat16), pltpu.VMEM((4 * D, D), jnp.bfloat16),
            pltpu.VMEM((tokens, 3 * D), jnp.bfloat16), pltpu.VMEM((tokens, D), jnp.float32), pltpu.SemaphoreType.DMA((4,))],
        compiler_params=LIMIT,
        name="encoder",
        cost_estimate=cost(14),
    )(lens, x, gains, attn, ffn_in, ffn_out)

def decode(lens, x, encoded, attn, ffn_in, ffn_out, gains):
    tokens = x.shape[0]
    sources = encoded.shape[0]
    return pl.pallas_call(
        decoder_kernel,
        out_shape=jax.ShapeDtypeStruct((tokens, D), jnp.bfloat16),
        in_specs=[smem, vmem, vmem, vmem, hbm, hbm, hbm],
        out_specs=vmem,
        scratch_shapes=[pltpu.VMEM((D, 4 * D), jnp.bfloat16), pltpu.VMEM((D, 4 * D), jnp.bfloat16), pltpu.VMEM((D, 4 * D), jnp.bfloat16), pltpu.VMEM((4 * D, D), jnp.bfloat16),
            pltpu.VMEM((sources, 2 * D), jnp.bfloat16), pltpu.VMEM((tokens, D), jnp.float32), pltpu.SemaphoreType.DMA((4,))],
        compiler_params=LIMIT,
        name="decoder",
        cost_estimate=cost(10.5),
    )(lens, x, encoded, gains, attn, ffn_in, ffn_out)

def dot_l(left, right):
    return lax.dot_general(left, right, (((0,), (0,)), ((), ())), preferred_element_type=jnp.float32)

def rms_columns(values, gain):
    return values * lax.rsqrt(jnp.mean(values * values, axis=0, keepdims=True) + norm_eps) * gain

def rms_columns_back(values, gain, grad):
    inverse = lax.rsqrt(jnp.mean(values * values, axis=0, keepdims=True) + norm_eps)
    gained = grad * gain
    along = jnp.mean(values * gained, axis=0, keepdims=True)
    gain_grad = jnp.sum(grad * (values * inverse), axis=1, keepdims=True)
    return inverse * gained - values * (inverse * inverse * inverse * along), gain_grad

def gelu_back(values, grad):
    square = values * values
    tanh = jnp.tanh(values * (0.7978845608028654 + 0.035677408136300125 * square))
    slope = 0.5 * (1.0 + tanh) + (0.5 * values) * (1.0 - tanh * tanh) * (0.7978845608028654 + 0.107032224408900375 * square)
    return grad * slope

side_scale = (SIDE // SIDE_HEADS) ** -0.5

def keys_with_bias(keys_t, valid):
    count = keys_t.shape[1]
    place = lax.broadcasted_iota(jnp.int32, (64, count), 1)
    line = lax.broadcasted_iota(jnp.int32, (64, count), 0)
    bias = jnp.where((line == 0) & (place >= valid), masked, 0.0)
    return jnp.concatenate([keys_t.astype(jnp.float32), bias], axis=0).T.astype(jnp.bfloat16)

def head_query(query_t, head):
    line = lax.broadcasted_iota(jnp.int32, (64, 1), 0)
    own = jnp.where(line // 8 == head, query_t, 0.0)
    ones = jnp.broadcast_to(jnp.where(line == 0, 1.0, 0.0), own.shape)
    return jnp.concatenate([own, ones], axis=0).astype(jnp.bfloat16)

def rounded(values):
    return values.astype(jnp.bfloat16).astype(jnp.float32)

def causal_columns(count):
    key = lax.broadcasted_iota(jnp.int32, (count, count), 0)
    query = lax.broadcasted_iota(jnp.int32, (count, count), 1)
    return jnp.where(key <= query, 0.0, masked)

def head_steps(keys):
    count = keys[0].shape[0]
    chunk = min(256, count)
    parts = count // chunk

    def place(step):
        head = step // parts
        return head, head // SIDE_HEADS, head % SIDE_HEADS, slice(step % parts * chunk, step % parts * chunk + chunk)

    return parts, place


def side_heads(items, causal):
    keys = [keys_with_bias(item[1], item[3]) for item in items]
    parts, place = head_steps(keys)
    scores, tops, weights, peaks, totals, mixed, queries = {}, {}, {}, {}, {}, {}, {}

    def score(step):
        unit, pair, head, span = place(step)
        if step % parts == 0:
            queries[unit] = head_query(items[pair][0], head)
        part = dot(keys[pair][span], queries[unit])
        scores[step] = part if causal is None else part + causal[span]

    def top(step):
        tops[step] = jnp.max(scores[step], axis=0, keepdims=True)

    def weigh(step):
        unit = place(step)[0]
        if step % parts == 0:
            peaks[unit] = functools.reduce(jnp.maximum, [tops.pop(step + i) for i in range(parts)])
        weight = jnp.exp2((scores.pop(step) - peaks[unit]) * (side_scale * LOG2E))
        amount = jnp.sum(weight, axis=0, keepdims=True)
        totals[unit] = totals[unit] + amount if unit in totals else amount
        weights[step] = weight.astype(jnp.bfloat16)

    def mix(step):
        unit, pair, head, span = place(step)
        values = items[pair][2][8 * head : 8 * head + 8, span].astype(jnp.bfloat16)
        piece = dot(values, weights.pop(step))
        mixed[unit] = mixed[unit] + piece if unit in mixed else piece

    staged(len(items) * SIDE_HEADS * parts, (0, score), (1, top), (parts, weigh), (parts + 2, mix))
    result = []
    for pair in range(len(items)):
        units = range(pair * SIDE_HEADS, (pair + 1) * SIDE_HEADS)
        outs = jnp.concatenate([mixed[unit] / totals[unit] for unit in units], axis=0)
        sums = [peaks[unit] * (side_scale * LOG2E) + jnp.log2(totals[unit]) for unit in units]
        result.append((outs, jnp.concatenate(sums, axis=0)))
    return result


def side_heads_back(items, causal):
    keys = [keys_with_bias(item[1], item[3]) for item in items]
    values = [item[2].T.astype(jnp.bfloat16) for item in items]
    parts, place = head_steps(keys)
    line = lax.broadcasted_iota(jnp.int32, (64, 1), 0)
    scores, grads, weights, along, queries, owns = {}, {}, {}, {}, {}, {}
    grad_q, grad_k, grad_v = {}, {}, {}

    def score(step):
        unit, pair, head, span = place(step)
        if step % parts == 0:
            queries[unit] = head_query(items[pair][0], head)
            owns[unit] = jnp.where(line // 8 == head, items[pair][5], 0.0).astype(jnp.bfloat16)
        part = dot(keys[pair][span], queries[unit])
        scores[step] = part if causal is None else part + causal[span]
        grads[step] = dot(values[pair][span], owns[unit])

    def weigh(step):
        unit, pair, head, _ = place(step)
        sums = items[pair][4][head : head + 1]
        weight = jnp.exp2(scores.pop(step) * (side_scale * LOG2E) - sums)
        grads[step] = rounded(grads[step])
        part = jnp.sum(grads[step] * weight, axis=0, keepdims=True)
        along[unit] = along[unit] + part if unit in along else part
        weights[step] = weight

    def finish(step):
        unit, pair, head, span = place(step)
        rows = slice(8 * head, 8 * head + 8)
        query, key, _, _, _, grad = items[pair]
        weight = weights.pop(step)
        grad_s = (weight * (grads.pop(step) - along[unit])).astype(jnp.bfloat16)
        part = dot(key[rows, span].astype(jnp.bfloat16), grad_s)
        grad_q[unit] = grad_q[unit] + part if unit in grad_q else part
        grad_k[step] = dot_t(query[rows].astype(jnp.bfloat16), grad_s)
        grad_v[step] = dot_t(grad[rows].astype(jnp.bfloat16), weight.astype(jnp.bfloat16))

    staged(len(items) * SIDE_HEADS * parts, (0, score), (2, weigh), (parts + 2, finish))

    def joined(pieces, units):
        rows = [
            jnp.concatenate([pieces[unit * parts + i] for i in range(parts)], axis=1) for unit in units
        ]
        return jnp.concatenate(rows, axis=0)

    result = []
    for pair in range(len(items)):
        units = range(pair * SIDE_HEADS, (pair + 1) * SIDE_HEADS)
        whole_q = jnp.concatenate([grad_q[unit] for unit in units], axis=0)
        result.append((whole_q * side_scale, joined(grad_k, units) * side_scale, joined(grad_v, units)))
    return result


def chosen_columns(tokens, positions):
    token = lax.broadcasted_iota(jnp.int32, (tokens, positions.shape[1]), 0)
    return jnp.where(token == positions, 1.0, 0.0).astype(jnp.bfloat16)

def side_kernel(len_ref, src_ref, encoded_ref, tgt_ref, decoded_ref, positions_ref, down_ref, attn_in_ref, attn_out_ref, ffn_in_ref, ffn_out_ref, small_ref,
                picked_ref, enc_ref, dec_ref, enc_mixed_ref, self_mixed_ref, cross_mixed_ref, enc_sums_ref, self_sums_ref, cross_sums_ref):
    micro = len_ref.shape[0]

    def gain(i):
        return small_ref[:, i:i + 1]

    def attend(which, query_n, key_n, side_of, causal, mixed_ref, sums_ref):
        query = rounded(dot(attn_in_ref[which, :64], query_n))
        keyval = rounded(dot(attn_in_ref[which, 64:], key_n))
        width, far = query.shape[1] // micro, keyval.shape[1] // micro
        spans = [
            (slice(i * width, (i + 1) * width), slice(i * far, (i + 1) * far)) for i in range(micro)
        ]
        items = [
            (query[:, near], keyval[:64, away], keyval[64:, away], len_ref[i, side_of])
            for i, (near, away) in enumerate(spans)
        ]
        parts = []
        for (near, _), (mixed, sums) in zip(spans, side_heads(items, causal)):
            sums_ref[:, near] = sums
            parts.append(mixed.astype(jnp.bfloat16))
        mixed_b = jnp.concatenate(parts, axis=1)
        mixed_ref[...] = mixed_b
        return dot(attn_out_ref[which], mixed_b)

    def ffn(which, normed):
        active = gelu(dot(ffn_in_ref[which], normed)).astype(jnp.bfloat16)
        return dot(ffn_out_ref[which], active)

    def norm(values, i):
        return rms_columns(values, gain(i)).astype(jnp.bfloat16)

    state = dot_t(down_ref[0], src_ref[...])
    enc_ref[0] = state
    normed = norm(state, 0)
    flow = dot_t(down_ref[2], tgt_ref[...])
    dec_ref[0] = flow
    normed_flow = norm(flow, 3)
    tokens = flow.shape[1] // micro
    causal = causal_columns(tokens)
    state = state + attend(0, normed, normed, 0, None, enc_mixed_ref, enc_sums_ref)
    enc_ref[1] = state
    flow = flow + attend(1, normed_flow, normed_flow, 1, causal, self_mixed_ref, self_sums_ref)
    dec_ref[1] = flow
    state = state + ffn(0, norm(state, 1))
    enc_ref[2] = state
    joined = dot_t(down_ref[1], encoded_ref[...])
    enc_ref[3] = joined
    gate = jax.nn.sigmoid(gain(7))
    memory = norm(gate * joined + (1.0 - gate) * state, 2)
    flow = flow + attend(2, norm(flow, 4), memory, 0, None, cross_mixed_ref, cross_sums_ref)
    dec_ref[2] = flow
    flow = flow + ffn(1, norm(flow, 5))
    dec_ref[3] = flow
    joined = dot_t(down_ref[3], decoded_ref[...])
    dec_ref[4] = joined
    gate = jax.nn.sigmoid(gain(8))
    top = norm(gate * joined + (1.0 - gate) * flow, 6)
    for i in range(micro):
        chosen = chosen_columns(tokens, positions_ref[i : i + 1])
        picked_ref[i] = dot(top[:, i * tokens : (i + 1) * tokens], chosen).astype(jnp.bfloat16)


def side(lens, src, encoded, tgt, decoded, positions, weights):
    s, t = src.shape[0], tgt.shape[0]
    m, p = positions.shape
    f32, bf16 = jnp.float32, jnp.bfloat16
    shapes = [((m, 64, p), bf16), ((4, 64, s), f32), ((5, 64, t), f32), ((64, s), bf16), ((64, t), bf16), ((64, t), bf16), ((8, s), f32), ((8, t), f32), ((8, t), f32)]
    return pl.pallas_call(
        side_kernel,
        out_shape=[jax.ShapeDtypeStruct(*item) for item in shapes],
        in_specs=[smem] + [vmem] * 11,
        out_specs=[vmem] * 9,
        compiler_params=LIMIT,
        name="side",
        cost_estimate=cost(24),
    )(lens, src, encoded, tgt, decoded, positions, *weights)

def back_kernel(*refs):
    (len_ref, src_ref, encoded_ref, tgt_ref, decoded_ref, positions_ref, attn_in_t_ref, ffn_in_t_ref, attn_in_ref, attn_out_ref, ffn_in_ref, ffn_out_ref, small_ref,
     enc_ref, dec_ref, enc_mixed_ref, self_mixed_ref, cross_mixed_ref, enc_sums_ref, self_sums_ref, cross_sums_ref) = refs[:21]
    parts_refs = refs[21:-7]
    down_out, attn_in_out, in_rest_out, attn_out_out, ffn_in_out, ffn_out_out, small_out = refs[-7:]
    outs = {
        "down": down_out,
        "attn_in": attn_in_out,
        "in_rest": in_rest_out,
        "attn_out": attn_out_out,
        "ffn_in": ffn_in_out,
        "ffn_out": ffn_out_out,
    }
    micro = len_ref.shape[0]

    def put(which, index, values):
        if values.shape[1] == 3 * SIDE:
            put("in_rest", index, values[:, 128:])
            values = values[:, :128]
        outs[which][index] = values

    smalls = {}

    def gain(i):
        return small_ref[:, i:i + 1]

    def norm(values, i):
        return rms_columns(values, gain(i)).astype(jnp.bfloat16)

    def norm_back(values, i, grad):
        result, smalls[i] = rms_columns_back(values, gain(i), grad)
        return result

    def blend_back(i, joined, late, grad):
        gate = jax.nn.sigmoid(gain(i))
        smalls[i] = jnp.sum(grad * (joined - late), axis=1, keepdims=True) * (gate * (1.0 - gate))
        return gate * grad, (1.0 - gate) * grad

    def ffn_back(which, normed, grad):
        grad_b = grad.astype(jnp.bfloat16)
        hidden = dot(ffn_in_t_ref[which], normed)
        active = gelu(hidden).astype(jnp.bfloat16)
        put("ffn_out", which, dot_t(active, grad_b))
        grad_hidden = gelu_back(hidden, dot(ffn_out_ref[which], grad_b)).astype(jnp.bfloat16)
        put("ffn_in", which, dot_t(normed, grad_hidden))
        return dot(ffn_in_ref[which], grad_hidden)

    def attend_back(which, query_n, key_n, mixed_ref, sums_ref, grad, side_of, causal):
        grad_b = grad.astype(jnp.bfloat16)
        put("attn_out", which, dot_t(mixed_ref[...], grad_b))
        grad_mixed = rounded(dot(attn_out_ref[which], grad_b))
        query = rounded(dot(attn_in_t_ref[which, :64], query_n))
        keyval = rounded(dot(attn_in_t_ref[which, 64:], key_n))
        width, far = query.shape[1] // micro, keyval.shape[1] // micro
        items = []
        for i in range(micro):
            near, away = slice(i * width, (i + 1) * width), slice(i * far, (i + 1) * far)
            items.append(
                (query[:, near], keyval[:64, away], keyval[64:, away], len_ref[i, side_of], sums_ref[:, near], grad_mixed[:, near])
            )
        grads_q, grads_kv = [], []
        for grad_q, grad_k, grad_v in side_heads_back(items, causal):
            grads_q.append(grad_q.astype(jnp.bfloat16))
            grads_kv.append(jnp.concatenate([grad_k, grad_v], axis=0).astype(jnp.bfloat16))
        return jnp.concatenate(grads_q, axis=1), jnp.concatenate(grads_kv, axis=1)

    tokens = tgt_ref.shape[0] // micro
    grads = []
    for index in range(micro):
        grad_picked = tree_sum([ref[index].astype(jnp.float32) for ref in parts_refs])
        chosen = chosen_columns(tokens, positions_ref[index : index + 1])
        high = grad_picked.astype(jnp.bfloat16)
        low = (grad_picked - high.astype(jnp.float32)).astype(jnp.bfloat16)
        grads.append(dot_t(high, chosen) + dot_t(low, chosen))
    grad = jnp.concatenate(grads, axis=1)
    gate = jax.nn.sigmoid(gain(8))
    final = gate * dec_ref[4] + (1.0 - gate) * dec_ref[3]
    grad = norm_back(final, 6, grad)
    grad_joined, grad = blend_back(8, dec_ref[4], dec_ref[3], grad)
    put("down", 3, dot(grad_joined.astype(jnp.bfloat16), decoded_ref[...]))
    grad = grad + norm_back(dec_ref[2], 5, ffn_back(1, norm(dec_ref[2], 5), grad))
    gate = jax.nn.sigmoid(gain(7))
    final = gate * enc_ref[3] + (1.0 - gate) * enc_ref[2]
    memory = norm(final, 2)
    normed = norm(dec_ref[1], 4)
    grad_q, grad_kv = attend_back(2, normed, memory, cross_mixed_ref, cross_sums_ref, grad, 0, None)
    zero_q = jnp.zeros((128, tgt_ref.shape[0]), jnp.bfloat16)
    zero_kv = jnp.zeros((64, src_ref.shape[0]), jnp.bfloat16)
    put("attn_in", 2, dot_t(normed, jnp.concatenate([grad_q, zero_q], axis=0)) + dot_t(memory, jnp.concatenate([zero_kv, grad_kv], axis=0)))
    weight = attn_in_ref[2]
    grad_memory = dot(weight, jnp.concatenate([zero_kv, grad_kv], axis=0))
    grad = grad + norm_back(dec_ref[1], 4, dot(weight, jnp.concatenate([grad_q, zero_q], axis=0)))
    normed = norm(dec_ref[0], 3)
    grad_q, grad_kv = attend_back(1, normed, normed, self_mixed_ref, self_sums_ref, grad, 1, causal_columns(tokens))
    grad_qkv = jnp.concatenate([grad_q, grad_kv], axis=0)
    put("attn_in", 1, dot_t(normed, grad_qkv))
    grad = grad + norm_back(dec_ref[0], 3, dot(attn_in_ref[1], grad_qkv))
    put("down", 2, dot(grad.astype(jnp.bfloat16), tgt_ref[...]))
    grad = norm_back(final, 2, grad_memory)
    grad_joined, grad = blend_back(7, enc_ref[3], enc_ref[2], grad)
    put("down", 1, dot(grad_joined.astype(jnp.bfloat16), encoded_ref[...]))
    grad = grad + norm_back(enc_ref[1], 1, ffn_back(0, norm(enc_ref[1], 1), grad))
    normed = norm(enc_ref[0], 0)
    grad_q, grad_kv = attend_back(0, normed, normed, enc_mixed_ref, enc_sums_ref, grad, 0, None)
    grad_qkv = jnp.concatenate([grad_q, grad_kv], axis=0)
    put("attn_in", 0, dot_t(normed, grad_qkv))
    grad = grad + norm_back(enc_ref[0], 0, dot(attn_in_ref[0], grad_qkv))
    put("down", 0, dot(grad.astype(jnp.bfloat16), src_ref[...]))
    lane = lax.broadcasted_iota(jnp.int32, (1, 128), 1)
    total = jnp.zeros((64, 128), jnp.float32)
    for i in range(9):
        total = total + jnp.where(lane == i, smalls[i], 0.0)
    small_out[...] = total

def side_back(lens, src, encoded, tgt, decoded, positions, weights, kept, parts):
    f32 = jnp.float32
    shapes = [(4, 64, 512), (3, 64, 128), (3, 64, 64), (3, 64, 64), (2, 64, 256), (2, 256, 64), (64, 128)]
    return pl.pallas_call(
        back_kernel,
        out_shape=[jax.ShapeDtypeStruct(shape, f32) for shape in shapes],
        in_specs=[smem] + [vmem] * (20 + len(parts)),
        out_specs=[vmem] * 7,
        compiler_params=LIMIT,
        name="side_back",
        cost_estimate=cost(34),
    )(lens, src, encoded, tgt, decoded, positions, *weights, *kept, *parts)


def swap(values, axis, distance):
    size = lax.axis_size(axis)
    return lax.ppermute(values, axis, [(i, i ^ distance) for i in range(size)])


def gather_peers(values, axis):
    return [values] + [swap(values, axis, s) for s in range(1, lax.axis_size(axis))]


def exchange(pieces, axis):
    return [pieces[0]] + [swap(pieces[s], axis, s) for s in range(1, lax.axis_size(axis))]


def tree_sum(terms):
    while len(terms) > 1:
        terms = [terms[i] + terms[i + 1] for i in range(0, len(terms), 2)]
    return terms[0]


def owners_of(ids, rows, peers, me):
    owner = jnp.zeros(ids.shape, jnp.int32)
    for peer in range(1, peers):
        owner = owner + jnp.where(ids >= peer * rows, 1, 0)
    return owner ^ me


def ranks_within(own):
    peers, count = own.shape
    own_b = own.astype(jnp.bfloat16)
    before = jnp.where(
        lax.broadcasted_iota(jnp.int32, (128, 128), 0)
        < lax.broadcasted_iota(jnp.int32, (128, 128), 1),
        1.0,
        0.0,
    ).astype(jnp.bfloat16)
    seen = jnp.zeros((peers, 1), jnp.float32)
    ranks = []
    for start in range(0, count, 128):
        block = slice(start, start + 128)
        inside = dot(own_b[:, block], before) + seen
        ranks.append(jnp.sum(own[:, block] * (inside + 1.0), axis=0, keepdims=True) - 1.0)
        seen = seen + jnp.sum(own[:, block], axis=1, keepdims=True)
    return jnp.concatenate(ranks, axis=1), seen


def column_of(row):
    return jnp.broadcast_to(row, (8, row.shape[1])).T[:, :1]


def placed(own, values, hit):
    high = jnp.floor(values * (1.0 / 64.0))
    low = values - 64.0 * high
    return 64.0 * dot((own * high).astype(jnp.bfloat16), hit) + dot(
        (own * low).astype(jnp.bfloat16), hit
    )


def score_part(rows, peers, tokens, me, busy, at_ref, goal_ref, mask_ref, token_ref, letter_ref, at):
    micro, _, spots = at_ref.shape
    token = lax.broadcasted_iota(jnp.int32, (tokens, 1), 0)
    token_f = token.astype(jnp.float32)
    spot_f = lax.broadcasted_iota(jnp.int32, (1, spots), 1).astype(jnp.float32)
    lower = jnp.where(
        lax.broadcasted_iota(jnp.int32, (tokens, tokens), 0)
        > lax.broadcasted_iota(jnp.int32, (tokens, tokens), 1),
        1.0,
        0.0,
    ).astype(jnp.bfloat16)
    goals, masks, slots, used = [], [], [], []
    for index in range(micro):
        mask = mask_ref[index].astype(jnp.float32)
        met = jnp.where(token == at_ref[index], mask, 0.0)
        times = jnp.sum(met, axis=1, keepdims=True)
        active = jnp.where(times > 0.0, 1.0, 0.0)
        wide = jnp.broadcast_to(active, (tokens, 128)).astype(jnp.bfloat16)
        slot = dot(lower, wide)[:, :1]
        here = jnp.where(slot == spot_f, active, 0.0)
        token_row = jnp.sum(here * (token_f + 1.0), axis=0, keepdims=True) - 1.0
        token_ref[index : index + 1] = token_row.astype(jnp.int32)
        count = jnp.sum(here * times, axis=0, keepdims=True).astype(jnp.int32)
        first = at + (micro + index) * spots
        letter_ref[:, first : first + spots] = jnp.broadcast_to(count, (peers, spots))
        slots.append(jnp.sum(met * slot, axis=0, keepdims=True) + float(index * spots))
        goals.append(goal_ref[index])
        masks.append(mask)
        used.append(jnp.sum(active, axis=0, keepdims=True))
    goal, mask, slot = [jnp.concatenate(rows_, axis=1) for rows_ in (goals, masks, slots)]
    far = owners_of(goal, rows, peers, 0)
    local = (goal - far * rows).astype(jnp.float32)
    line = lax.broadcasted_iota(jnp.int32, (peers, goal.shape[1]), 0)
    own = jnp.where((line == (far ^ me)) & (mask > 0.0), 1.0, 0.0)
    rank, many = ranks_within(own)
    order = lax.broadcasted_iota(jnp.int32, (1, goal.shape[1]), 1).astype(jnp.float32)
    hit = jnp.where(column_of(rank) == order, 1.0, 0.0).astype(jnp.bfloat16)
    letter_ref[:, at : at + micro * spots] = placed(own, slot, hit).astype(
        jnp.int32
    ) * 65536 + placed(own, local, hit).astype(jnp.int32)
    lane = lax.broadcasted_iota(jnp.int32, (peers, 128), 1)
    info = jnp.where(lane == 0, many, jnp.where(lane == micro + 1, busy, 0.0))
    for index in range(micro):
        info = jnp.where(lane == index + 1, used[index], info)
    first = at + 2 * micro * spots
    letter_ref[:, first : first + 128] = info.astype(jnp.int32)


def plan_kernel(rows, peers, cap, tokens, me_ref, src_ref, tgt_ref, *refs):
    score_refs, (slots_ref, column_ref, near_ref, other_ref, token_ref, letter_ref) = refs[:3], refs[3:]
    ids_row = jnp.concatenate(
        [ref[index] for ref in (src_ref, tgt_ref) for index in range(ref.shape[0])], axis=1
    )
    count = ids_row.shape[1]
    ids = ids_row.astype(jnp.float32)
    column = column_of(ids)
    column_ref[...] = column
    first_at = jnp.full((1, count), float(count), jnp.float32)
    for start in range(0, count, 256):
        place = (lax.broadcasted_iota(jnp.int32, (256, 1), 0) + start).astype(jnp.float32)
        same = column[start : start + 256] == ids
        first_at = jnp.minimum(
            first_at, jnp.min(jnp.where(same, place, float(count)), axis=0, keepdims=True)
        )
    first = first_at == lax.broadcasted_iota(jnp.int32, (1, count), 1).astype(jnp.float32)
    far = owners_of(ids_row, rows, peers, 0)
    line = lax.broadcasted_iota(jnp.int32, (peers, count), 0)
    own = jnp.where((line == (far ^ me_ref[0])) & first, 1.0, 0.0)
    rank, seen = ranks_within(own)
    width = -(-cap // 128) * 128
    spot = lax.broadcasted_iota(jnp.int32, (1, width), 1).astype(jnp.float32)
    hit = jnp.where(column_of(rank) == spot, 1.0, 0.0).astype(jnp.bfloat16)
    filled = dot(own.astype(jnp.bfloat16), hit)
    local = placed(own, (ids_row - far * rows).astype(jnp.float32), hit).astype(jnp.int32)
    letter_ref[:, :width] = local
    owner = lax.broadcasted_iota(jnp.int32, (peers, 1), 0) ^ me_ref[0]
    slots = jnp.where(filled > 0.5, local + owner * rows, -1)[:, :cap]
    for part in range(2):
        slots_ref[part : part + 1] = jnp.concatenate(
            [slots[peer : peer + 1] for peer in range(part, peers, 2)], axis=1
        )
    busy = jnp.max(seen, axis=0, keepdims=True)
    score_part(rows, peers, tokens, me_ref[0], busy, *score_refs, token_ref, letter_ref, width)
    for peer in range(peers):
        letter = near_ref if peer % 2 == 0 else other_ref
        letter[peer // 2 : peer // 2 + 1] = letter_ref[peer : peer + 1]


def plan(me, source, target, score, rows, peers, cap, tokens):
    count = source.shape[0] * source.shape[2] + target.shape[0] * target.shape[2]
    micro, _, spots = score[0].shape
    letter = -(-cap // 128) * 128 + 2 * micro * spots + 128
    shapes = [
        ((2, peers // 2 * cap), jnp.int32),
        ((count, 1), jnp.float32),
        ((peers // 2, letter), jnp.int32),
        ((peers // 2, letter), jnp.int32),
        ((micro, spots), jnp.int32),
    ]
    return pl.pallas_call(
        functools.partial(plan_kernel, rows, peers, cap, tokens),
        out_shape=[jax.ShapeDtypeStruct(*shape) for shape in shapes],
        in_specs=[smem] + [vmem] * 5,
        out_specs=[vmem] * len(shapes),
        scratch_shapes=[pltpu.VMEM((peers, letter), jnp.int32)],
        compiler_params=LIMIT,
        name="plan",
        cost_estimate=cost(4),
    )(me, source, target, *score)


def expand_kernel(sizes, slots_ref, column_ref, *refs):
    far_refs, near_ref, out_refs = refs[: -1 - len(sizes)], refs[-1 - len(sizes)], refs[-len(sizes) :]
    slots = slots_ref[...].astype(jnp.float32)
    rows = (jnp.concatenate([ref[0] for ref in far_refs], axis=0), near_ref[...])
    blocks, base = [], 0
    for out in out_refs:
        blocks += [(out, start, base + start) for start in range(0, out.shape[0], 256)]
        base = base + out.shape[0]
    picks = {}

    def match(step):
        column = column_ref[blocks[step][2] : blocks[step][2] + 256]
        picks[step] = [
            jnp.where(column == slots[i : i + 1], 1.0, 0.0).astype(jnp.bfloat16) for i in range(2)
        ]

    def fill(step):
        first, second = [dot(pick, rows[i]) for i, pick in enumerate(picks.pop(step))]
        out, start, _ = blocks[step]
        out[start : start + 256] = (first + second).astype(jnp.bfloat16)

    staged(len(blocks), (0, match), (1, fill))


def expand(slots, column, far, near, sizes):
    width = near.shape[1]
    return pl.pallas_call(
        functools.partial(expand_kernel, sizes),
        out_shape=[jax.ShapeDtypeStruct((size, width), jnp.bfloat16) for size in sizes],
        in_specs=[vmem] * (3 + len(far)),
        out_specs=[vmem] * len(sizes),
        compiler_params=LIMIT,
        name="expand",
        cost_estimate=cost(3.8),
    )(slots, column, *far, near)


def ask(near, other):
    count = near.shape[0]
    pairs = jnp.stack([near, swap(other, "dp", 1)], axis=1)
    far = [pairs[:1]] + [swap(pairs[i : i + 1], "dp", 2 * i) for i in range(1, count)]
    return jnp.concatenate(far).reshape(2 * count, -1)


def send_rows(slots, column, found, sizes, between):
    count = found.shape[0]
    far = [found[0]] + [swap(found[i], "dp", 2 * i) for i in range(1, count)]
    other = jnp.concatenate([part[1] for part in far])
    near = swap(after(other, *between), "dp", 1)
    return expand(slots, column, far, near, sizes)


def every_row(ids, table, rows):
    size = lax.axis_size("dp")
    me = lax.axis_index("dp")

    def step(i, carry):
        shard, filled = carry
        local = ids - (me + i) % size * rows
        here = (local >= 0) & (local < rows)
        found = jnp.take(shard, jnp.clip(local, 0, rows - 1), axis=0)
        shard = lax.ppermute(shard, "dp", [((j + 1) % size, j) for j in range(size)])
        return shard, jnp.where(here[:, None], found, filled)

    empty = jnp.zeros((ids.shape[0], table.shape[1]), table.dtype)
    return lax.fori_loop(0, size, step, (table, empty))[1]


def embed_rows(slots, column, found, cap, most, source, target, table, between):
    sizes = [source.size, target.size]
    result = tuple(send_rows(slots, column, found, sizes, between))

    def long_way(carry):
        ids = jnp.concatenate([source.reshape(-1), target.reshape(-1)])
        filled = every_row(ids, table, table.shape[0])
        return (jnp.zeros_like(carry[0]), (filled[: sizes[0]], filled[sizes[0] :]))

    return lax.while_loop(lambda carry: carry[0] > cap, long_way, (most, result))[1]


def gather_all(values):
    far = [values] + [swap(values, "dp", s) for s in range(2, lax.axis_size("dp"), 2)]
    return far, swap(jnp.stack(far), "dp", 1)


def add_home(own, other):
    pair = (own.astype(jnp.float32) + swap(other, "dp", 1).astype(jnp.float32)).astype(own.dtype)
    return [pair[0]] + [swap(pair[i], "dp", 2 * i) for i in range(1, pair.shape[0])]


def table_kernel(rows, table_ref, up_ref, padded_ref, weight_ref):
    block = table_ref.shape[0]
    place = lax.broadcasted_iota(jnp.int32, (block, 1), 0) + pl.program_id(0) * block
    table = jnp.where(place < rows, table_ref[...], jnp.bfloat16(0))
    padded_ref[...] = table
    lifted = dot_t(table, up_ref[...]) * (D ** (-0.5) * LOG2E)
    high = lifted.astype(jnp.bfloat16)
    weight_ref[:, :SIDE] = high
    weight_ref[:, SIDE:] = (lifted - high.astype(jnp.float32)).astype(jnp.bfloat16)


VOCAB_BLOCK = 512
TILE = 512
SCORE_TILE = 256


def table_parts(table, up_b):
    rows, width = table.shape
    padded = -(-rows // VOCAB_BLOCK) * VOCAB_BLOCK
    return pl.pallas_call(
        functools.partial(table_kernel, rows),
        out_shape=[
            jax.ShapeDtypeStruct((padded, width), jnp.bfloat16),
            jax.ShapeDtypeStruct((padded, 2 * SIDE), jnp.bfloat16),
        ],
        grid=(padded // VOCAB_BLOCK,),
        in_specs=[
            pl.BlockSpec((VOCAB_BLOCK, width), lambda i: (i, 0)),
            pl.BlockSpec((SIDE, width), lambda i: (0, 0)),
        ],
        out_specs=[
            pl.BlockSpec((VOCAB_BLOCK, width), lambda i: (i, 0)),
            pl.BlockSpec((VOCAB_BLOCK, 2 * SIDE), lambda i: (i, 0)),
        ],
        compiler_params=LIMIT,
        name="table_parts",
        cost_estimate=cost(5),
    )(table, up_b)


def goals_kernel(spots, micro, me_ref, letter_ref, table_ref, out_ref, where_ref, tall_ref, sum_ref, sem):
    peers, length = letter_ref.shape
    entry_at = length - 128 - 2 * micro * spots
    where_ref[0] = me_ref[0]
    first = jnp.int32(0)
    for device in range(peers):
        for index in range(micro):
            where_ref[2 + device * micro + index] = first
            first = first + letter_ref[me_ref[0] ^ device, length - 128 + 1 + index]
    where_ref[1] = first
    tiles = (first + TILE - 1) // TILE
    for start in range(0, table_ref.shape[0], VOCAB_BLOCK):
        tall_ref[start : start + VOCAB_BLOCK] = table_ref[start : start + VOCAB_BLOCK].astype(jnp.float32)

    def clear(i, carry):
        sum_ref[pl.ds(pl.multiple_of(i * TILE, TILE), TILE)] = jnp.zeros((TILE, sum_ref.shape[1]), jnp.float32)
        return carry

    lax.fori_loop(0, tiles, clear, 0)
    for peer in range(peers):
        base = 2 + (peer ^ where_ref[0]) * micro

        def add(j, carry):
            entry = letter_ref[peer, entry_at + j]
            slot = entry // 65536
            local = entry - slot * 65536
            row = slot + where_ref[base]
            for index in range(1, micro):
                row = jnp.where(slot >= index * spots, slot - index * spots + where_ref[base + index], row)
            sum_ref[pl.ds(row, 1)] = sum_ref[pl.ds(row, 1)] + tall_ref[pl.ds(local, 1)]
            return carry

        lax.fori_loop(0, letter_ref[peer, length - 128], add, 0)

    def send(i, carry):
        at = pl.ds(pl.multiple_of(i * TILE, TILE), TILE)
        copy = pltpu.make_async_copy(sum_ref.at[at], out_ref.at[at], sem)
        copy.start()
        copy.wait()
        return carry

    lax.fori_loop(0, tiles, send, 0)


def goal_rows(me, letters, table_pad, micro, spots):
    total = letters.shape[0] * micro * spots
    padded, width = table_pad.shape
    return pl.pallas_call(
        functools.partial(goals_kernel, spots, micro),
        out_shape=[
            jax.ShapeDtypeStruct((total, width), jnp.float32),
            jax.ShapeDtypeStruct((2 + letters.shape[0] * micro,), jnp.int32),
        ],
        in_specs=[smem, smem, vmem],
        out_specs=[hbm, smem],
        scratch_shapes=[
            pltpu.VMEM((padded, width), jnp.float32),
            pltpu.VMEM((total, width), jnp.float32),
            pltpu.SemaphoreType.DMA,
        ],
        compiler_params=LIMIT,
        name="goals",
        cost_estimate=cost(9),
    )(me, letters, table_pad)


def softmax_kernel(rows, where_ref, *refs):
    far_refs = refs[:-9]
    near_ref, letter_ref, weight_ref, table_ref, mix_ref, stats_ref, packed_ref, all_ref, gathered_ref = refs[-9:]
    step = pl.program_id(0)
    peers, micro, _, spots = gathered_ref.shape
    tiles = (where_ref[1] + SCORE_TILE - 1) // SCORE_TILE
    count_at = letter_ref.shape[1] - 128 - micro * spots

    @pl.when(step == 0)
    def _():
        def clear(i, carry):
            all_ref[pl.ds(pl.multiple_of(i * SCORE_TILE, SCORE_TILE), SCORE_TILE)] = jnp.zeros((SCORE_TILE, 128), jnp.float32)
            return carry

        lax.fori_loop(0, tiles, clear, 0)
        for i, far_ref in enumerate(far_refs):
            gathered_ref[2 * i] = far_ref[...]
            gathered_ref[2 * i + 1] = near_ref[i]
        for device in range(peers):
            for index in range(micro):
                peer = where_ref[0] ^ device
                block = jnp.concatenate(
                    [
                        gathered_ref[peer, index].astype(jnp.float32),
                        letter_ref[
                            pl.ds(peer, 1), count_at + index * spots : count_at + (index + 1) * spots
                        ].astype(jnp.float32),
                        jnp.zeros((SIDE - 1, spots), jnp.float32),
                    ],
                    axis=0,
                )
                all_ref[pl.ds(where_ref[2 + device * micro + index], spots)] = block.T

    @pl.when(step < tiles)
    def _():
        mine = all_ref[pl.ds(pl.multiple_of(step * SCORE_TILE, SCORE_TILE), SCORE_TILE)]
        packed_ref[...] = mine
        picked = jnp.concatenate([mine[:, :SIDE], mine[:, :SIDE]], axis=1).astype(jnp.bfloat16)
        padded = weight_ref.shape[0]
        chunk = min(1024, padded)
        logits, shares = {}, {}
        kept = {"peak": None}

        def score(part):
            start = part * chunk
            values = dot_t(picked, weight_ref[start : start + chunk])
            if start + chunk > rows:
                place = lax.broadcasted_iota(jnp.int32, (1, chunk), 1)
                values = jnp.where(place < rows - start, values, -jnp.inf)
            logits[part] = values

        def weigh(part):
            values = logits.pop(part)
            above = jnp.max(values, axis=1, keepdims=True)
            fade = None
            if part > 0:
                above = jnp.maximum(kept["peak"], above)
                fade = jnp.exp2(kept["peak"] - above)
            share = jnp.exp2(values - above)
            amount = jnp.sum(share, axis=1, keepdims=True)
            kept["total"] = amount if fade is None else kept["total"] * fade + amount
            kept["peak"] = above
            shares[part] = (share.astype(jnp.bfloat16), fade)

        def add(part):
            share, fade = shares.pop(part)
            piece = dot(share, table_ref[part * chunk : (part + 1) * chunk])
            kept["mix"] = piece if fade is None else kept["mix"] * fade + piece

        staged(padded // chunk, (0, score), (1, weigh), (2, add))
        peak, total, mix = kept["peak"], kept["total"], kept["mix"]
        mix_ref[...] = mix
        lane = lax.broadcasted_iota(jnp.int32, (SCORE_TILE, 128), 1)
        stats_ref[...] = jnp.where(lane == 0, peak, jnp.where(lane == 1, total, 0.0)).T[:8]


def in_use(tile, i, where):
    return jnp.minimum(i, (where[1] + tile - 1) // tile - 1)


def softmax_part(where, far, near, letters, weight, table_pad, rows):
    micro, side_width, spots = far[0].shape
    peers = 2 * len(far)
    padded, width = table_pad.shape
    total = peers * micro * spots
    return pl.pallas_call(
        functools.partial(softmax_kernel, rows),
        out_shape=[
            jax.ShapeDtypeStruct((total, width), jnp.float32),
            jax.ShapeDtypeStruct((8, total), jnp.float32),
            jax.ShapeDtypeStruct((total, 128), jnp.float32),
        ],
        grid_spec=pltpu.PrefetchScalarGridSpec(
            num_scalar_prefetch=1,
            grid=(total // SCORE_TILE,),
            in_specs=[
                *[pl.BlockSpec((micro, side_width, spots), lambda i, w: (0, 0, 0))] * len(far),
                pl.BlockSpec((len(far), micro, side_width, spots), lambda i, w: (0, 0, 0, 0)),
                pl.BlockSpec(letters.shape, lambda i, w: (0, 0)),
                pl.BlockSpec((padded, 2 * SIDE), lambda i, w: (0, 0)),
                pl.BlockSpec((padded, width), lambda i, w: (0, 0)),
            ],
            out_specs=[
                pl.BlockSpec((SCORE_TILE, width), lambda i, w: (in_use(SCORE_TILE, i, w), 0)),
                pl.BlockSpec((8, SCORE_TILE), lambda i, w: (0, in_use(SCORE_TILE, i, w))),
                pl.BlockSpec((SCORE_TILE, 128), lambda i, w: (in_use(SCORE_TILE, i, w), 0)),
            ],
            scratch_shapes=[
                pltpu.VMEM((total + spots, 128), jnp.float32),
                pltpu.VMEM((peers, micro, side_width, spots), jnp.bfloat16),
            ],
        ),
        compiler_params=LIMIT,
        name="softmax_part",
        cost_estimate=cost(22),
    )(where, *far, near, letters, weight, table_pad)


def finish_kernel(micro, where_ref, *refs):
    far_refs = refs[:-11]
    near_ref, mix_ref, goal_ref, packed_ref, up_ref, own_ref, other_ref, up_grad_ref, loss_ref, all_ref, top_ref = refs[-11:]
    step = pl.program_id(0)
    blocks, _, spots = top_ref.shape
    peers = blocks // micro
    tiles = (where_ref[1] + TILE - 1) // TILE

    @pl.when(step == 0)
    def _():
        up_grad_ref[...] = jnp.zeros_like(up_grad_ref)
        loss_ref[...] = jnp.zeros_like(loss_ref)
        all_ref[...] = jnp.zeros_like(all_ref)

    @pl.when(step < tiles)
    def _():
        stats = [(ref[...], near_ref[i]) for i, ref in enumerate(far_refs)]
        stats = [part for pair in stats for part in pair]
        peaks = [part[0:1] for part in stats]
        peak = functools.reduce(jnp.maximum, peaks)
        total = tree_sum([part[1:2] * jnp.exp2(part[0:1] - peak) for part in stats])
        lse = peak + jnp.log2(total)
        rows = jnp.concatenate([jnp.exp2(peaks[0] - lse), lse, jnp.zeros((6, TILE), jnp.float32)], axis=0).T
        heads, lifts, losses = {}, {}, []
        half = TILE // 2

        def valid(part):
            place = lax.broadcasted_iota(jnp.int32, (half, 1), 0) + (step * TILE + part * half)
            return place < where_ref[1]

        def span(part):
            return slice(part * half, (part + 1) * half)

        def picked(part):
            return jnp.where(valid(part), packed_ref[span(part), :SIDE], 0.0).astype(jnp.bfloat16)

        def lift(part):
            heads[part] = dot(picked(part), up_ref[...])

        def scale(part):
            at, here = span(part), valid(part)
            goal = goal_ref[at]
            times = packed_ref[at, SIDE : SIDE + 1]
            lifted = (mix_ref[at] * (rows[at, :1] * times) - goal) * D ** (-0.5)
            lifts[part] = jnp.where(here, lifted, 0.0).astype(jnp.bfloat16)
            aim = jnp.sum(heads.pop(part) * goal, axis=1, keepdims=True) * D ** (-0.5)
            every = jnp.where(where_ref[0] == 0, times * rows[at, 1:2] * (1.0 / LOG2E), 0.0)
            losses.append(jnp.sum(jnp.where(here, every - aim, 0.0), axis=0, keepdims=True))

        def lower(part):
            lifted = lifts.pop(part)
            at = pl.ds(pl.multiple_of(step * TILE + part * half, half), half)
            all_ref[at, :SIDE] = dot_t(lifted, up_ref[...])
            up_grad_ref[...] += dot_l(picked(part), lifted)

        staged(2, (0, lift), (1, scale), (2, lower))
        loss_ref[...] += jnp.broadcast_to(losses[0] + losses[1], loss_ref.shape)

    @pl.when(step == pl.num_programs(0) - 1)
    def _():
        for device in range(peers):
            for index in range(micro):
                block = all_ref[pl.ds(where_ref[2 + device * micro + index], spots)]
                top_ref[(where_ref[0] ^ device) * micro + index] = block.T[:SIDE].astype(jnp.bfloat16)
        for i in range(peers // 2):
            own_ref[i] = top_ref[2 * i * micro : (2 * i + 1) * micro]
            other_ref[i] = top_ref[(2 * i + 1) * micro : (2 * i + 2) * micro]


def head_finish(where, far, near, mix, goals, packed, up_b, micro, spots):
    peers = 2 * len(far)
    total, width = mix.shape
    return pl.pallas_call(
        functools.partial(finish_kernel, micro),
        out_shape=[
            *[jax.ShapeDtypeStruct((len(far), micro, SIDE, spots), jnp.bfloat16)] * 2,
            jax.ShapeDtypeStruct((SIDE, width), jnp.float32),
            jax.ShapeDtypeStruct((8, 128), jnp.float32),
        ],
        grid_spec=pltpu.PrefetchScalarGridSpec(
            num_scalar_prefetch=1,
            grid=(total // TILE,),
            in_specs=[
                *[pl.BlockSpec((2, TILE), lambda i, w: (0, in_use(TILE, i, w)))] * len(far),
                pl.BlockSpec((len(far), 2, TILE), lambda i, w: (0, 0, in_use(TILE, i, w))),
                pl.BlockSpec((TILE, width), lambda i, w: (in_use(TILE, i, w), 0)),
                pl.BlockSpec((TILE, width), lambda i, w: (in_use(TILE, i, w), 0)),
                pl.BlockSpec((TILE, 128), lambda i, w: (in_use(TILE, i, w), 0)),
                pl.BlockSpec((SIDE, width), lambda i, w: (0, 0)),
            ],
            out_specs=[
                *[pl.BlockSpec((len(far), micro, SIDE, spots), lambda i, w: (0, 0, 0, 0))] * 2,
                pl.BlockSpec((SIDE, width), lambda i, w: (0, 0)),
                pl.BlockSpec((8, 128), lambda i, w: (0, 0)),
            ],
            scratch_shapes=[
                pltpu.VMEM((total + spots, 128), jnp.float32),
                pltpu.VMEM((peers * micro, SIDE, spots), jnp.bfloat16),
            ],
        ),
        compiler_params=LIMIT,
        name="head_finish",
        cost_estimate=cost(6),
    )(where, *far, near, mix, goals, packed, up_b)


def after(values, *others):
    return lax.optimization_barrier((values, others))[0]


def pair_lanes(even, odd):
    return jnp.concatenate([even, odd], axis=1)


def flatten_kernel(me_ref, loss_ref, down_ref, in_ref, in_rest_ref, attn_out_ref, ffn_in_ref, ffn_out_ref, up_ref, small_ref, mine_ref, other_ref, turn_ref, out_ref):
    at = 0
    for i in range(4):
        turn_ref[...] = down_ref[i].T
        out_ref[at : at + 256] = pair_lanes(
            turn_ref[pl.ds(0, 256, stride=2)], turn_ref[pl.ds(1, 256, stride=2)]
        )
        at += 256
    half = SIDE // 2
    for i in range(3):
        even = in_ref.at[i][pl.ds(0, half, stride=2)]
        odd = in_ref.at[i][pl.ds(1, half, stride=2)]
        even_rest = in_rest_ref.at[i][pl.ds(0, half, stride=2)]
        odd_rest = in_rest_ref.at[i][pl.ds(1, half, stride=2)]
        out_ref[pl.ds(at, half, stride=3)] = even
        out_ref[pl.ds(at + 1, half, stride=3)] = pair_lanes(even_rest, odd[:, :SIDE])
        out_ref[pl.ds(at + 2, half, stride=3)] = pair_lanes(odd[:, SIDE:], odd_rest)
        at += 3 * half
    for i in range(3):
        out_ref[at : at + half] = pair_lanes(
            attn_out_ref.at[i][pl.ds(0, half, stride=2)], attn_out_ref.at[i][pl.ds(1, half, stride=2)]
        )
        at += half
    for i in range(2):
        for j in range(2):
            out_ref[pl.ds(at + j, SIDE, stride=2)] = ffn_in_ref[i, :, 128 * j : 128 * j + 128]
        at += 2 * SIDE
    for i in range(2):
        out_ref[at : at + 128] = pair_lanes(
            ffn_out_ref.at[i][pl.ds(0, 128, stride=2)], ffn_out_ref.at[i][pl.ds(1, 128, stride=2)]
        )
        at += 128
    for j in range(4):
        out_ref[pl.ds(at + j, SIDE, stride=4)] = up_ref[:, 128 * j : 128 * j + 128]
    at += 4 * SIDE
    turn_ref[:128] = small_ref[...].T
    out_ref[at : at + 8] = pair_lanes(
        turn_ref[pl.ds(0, 8, stride=2)], turn_ref[pl.ds(1, 8, stride=2)]
    )
    at += 8
    out_ref[at:] = jnp.zeros((out_ref.shape[0] - at, 128), jnp.float32)
    lane = lax.broadcasted_iota(jnp.int32, (8, 128), 1) - 3 * me_ref[0]
    loss = loss_ref[...]
    one = rounded(loss)
    two = rounded(loss - one)
    three = rounded(loss - one - two)
    loss = jnp.where(lane == 0, one, jnp.where(lane == 1, two, jnp.where(lane == 2, three, 0.0)))
    out_ref[LOSS_ROW : LOSS_ROW + 8] = loss
    half = mine_ref.shape[0]
    core = me_ref[0] % 2
    mine_ref[...] = out_ref[pl.ds(pl.multiple_of(core * half, 8), half)]
    other_ref[...] = out_ref[pl.ds(pl.multiple_of((1 - core) * half, 8), half)]


FLAT_ROWS = 2208
LOSS_ROW = 2192


def flatten(me, loss, pieces):
    return pl.pallas_call(
        flatten_kernel,
        out_shape=[jax.ShapeDtypeStruct((FLAT_ROWS // 2, 128), jnp.float32)] * 2,
        in_specs=[smem] + [vmem] * 9,
        out_specs=[vmem] * 2,
        scratch_shapes=[
            pltpu.VMEM((512, 64), jnp.float32),
            pltpu.VMEM((FLAT_ROWS, 128), jnp.float32),
        ],
        compiler_params=LIMIT,
        name="flatten",
        cost_estimate=cost(4),
    )(me, loss, *pieces)


MAIN_ROWS = 2176


def rows_of(ref):
    main = 128 * MAIN_ROWS
    one = len(ref.shape) == 2
    load = (lambda a, b: ref[:, a:b]) if one else (lambda a, b: ref[a:b])
    rest = load(main, main + 512).reshape(4, 128)
    last = load(main + 512, main + 576).reshape(1, 64)
    return load(0, main).reshape(MAIN_ROWS, 128), jnp.concatenate(
        [rest, jnp.concatenate([last, jnp.zeros((1, 64), jnp.float32)], axis=1)], axis=0
    )


def put_rows(ref, main_values, rest_values):
    main = 128 * MAIN_ROWS
    if len(ref.shape) == 2:
        ref[:, :main] = main_values.reshape(1, main)
        ref[:, main : main + 512] = rest_values[:4].reshape(1, 512)
        ref[:, main + 512 : main + 576] = rest_values[4:5, :64]
    else:
        ref[:main] = main_values.reshape(main)
        ref[main : main + 512] = rest_values[:4].reshape(512)
        ref[main + 512 : main + 576] = rest_values[4:5, :64].reshape(64)


def adam_kernel(count_at, core_ref, letter_ref, mine_ref, other_ref, first_ref, second_ref, inner_ref, anchor_ref, new_first_ref, new_second_ref, new_inner_ref, gap_ref, loss_ref, count_ref, norm_ref, grad_ref):
    half = mine_ref.shape[0]
    core = core_ref[0]
    grad_ref[pl.ds(pl.multiple_of(core * half, 8), half)] = mine_ref[...]
    grad_ref[pl.ds(pl.multiple_of((1 - core) * half, 8), half)] = other_ref[...]
    loss_ref[0] = jnp.sum(grad_ref[LOSS_ROW : LOSS_ROW + 1])
    grad_ref[LOSS_ROW : LOSS_ROW + 8] = jnp.zeros((8, 128), jnp.float32)
    count = jnp.sum(letter_ref[:, count_at : letter_ref.shape[1] - 128].astype(jnp.float32))
    count_ref[0] = count
    mean = grad_ref[...] * (1.0 / jnp.full((1, 1), count))
    norm = jnp.sqrt(jnp.sum(jnp.sum(mean * mean, axis=0, keepdims=True), axis=1, keepdims=True))
    norm_ref[0] = jnp.sum(norm)
    clipped = mean * jnp.minimum(1.0, clip_norm / norm)
    spans = ((0, MAIN_ROWS), (MAIN_ROWS, MAIN_ROWS + 5))
    news = []
    for span, first, second, inner, anchor in zip(
        spans, rows_of(first_ref), rows_of(second_ref), rows_of(inner_ref), rows_of(anchor_ref)
    ):
        part = clipped[span[0] : span[1]]
        new_first = beta_first * first + (1.0 - beta_first) * part
        new_second = beta_second * second + (1.0 - beta_second) * part * part
        fixed_one = new_first / (1.0 - beta_first**STEP)
        fixed_two = new_second / (1.0 - beta_second**STEP)
        new_inner = inner - learn_rate * (
            fixed_one / (jnp.sqrt(fixed_two) + adam_eps) + decay_rate * inner
        )
        news.append((new_first, new_second, new_inner))
        grad_ref[span[0] : span[1]] = anchor - new_inner
    for ref, main, rest in zip((new_first_ref, new_second_ref, new_inner_ref), news[0], news[1]):
        put_rows(ref, main, rest)
    gap_ref[...] = grad_ref[pl.ds(pl.multiple_of(core * half, 8), half)].astype(jnp.bfloat16)


def adam(core, letters, count_at, mine, other, first, second, inner, anchor):
    flat = jax.ShapeDtypeStruct(first.shape, jnp.float32)
    return pl.pallas_call(
        functools.partial(adam_kernel, count_at),
        out_shape=[
            flat,
            flat,
            flat,
            jax.ShapeDtypeStruct(mine.shape, jnp.bfloat16),
            *[jax.ShapeDtypeStruct((1,), jnp.float32)] * 3,
        ],
        in_specs=[smem] + [vmem] * 7,
        out_specs=[vmem] * 4 + [smem] * 3,
        scratch_shapes=[pltpu.VMEM((FLAT_ROWS, 128), jnp.float32)],
        compiler_params=LIMIT,
        name="adam",
        cost_estimate=cost(7),
    )(core, letters, mine, other, first, second, inner, anchor)


def outer_kernel(core_ref, mine_ref, other_ref, anchor_ref, momentum_ref, delta_ref, new_momentum_ref, new_anchor_ref, full_ref):
    half = mine_ref.shape[0]
    core = core_ref[0]
    full_ref[pl.ds(pl.multiple_of(core * half, 8), half)] = mine_ref[...]
    full_ref[pl.ds(pl.multiple_of((1 - core) * half, 8), half)] = other_ref[...]
    news = []
    for span, anchor, momentum in zip(
        ((0, MAIN_ROWS), (MAIN_ROWS, MAIN_ROWS + 5)), rows_of(anchor_ref), rows_of(momentum_ref)
    ):
        delta = full_ref[span[0] : span[1]]
        new_momentum = outer_beta * momentum + delta
        news.append((delta, new_momentum, anchor - outer_rate * (delta + outer_beta * new_momentum)))
    for ref, main, rest in zip((delta_ref, new_momentum_ref, new_anchor_ref), news[0], news[1]):
        put_rows(ref, main, rest)


def outer(core, mine, other, anchor, momentum):
    flat = jax.ShapeDtypeStruct(anchor.shape, jnp.float32)
    return pl.pallas_call(
        outer_kernel,
        out_shape=[flat] * 3,
        in_specs=[smem] + [vmem] * 4,
        out_specs=[vmem] * 3,
        scratch_shapes=[pltpu.VMEM((FLAT_ROWS, 128), jnp.float32)],
        compiler_params=LIMIT,
        name="outer",
        cost_estimate=cost(5),
    )(core, mine, other, anchor, momentum)


def unpack_kernel(flat_ref, down_ref, in_t_ref, out_t_ref, ffn_in_t_ref, ffn_out_t_ref, in_ref, out_ref, ffn_in_ref, ffn_out_ref, up_ref, small_ref, rows_ref, tall_ref):
    main, rest = rows_of(flat_ref)
    rows_ref[:MAIN_ROWS] = main
    rows_ref[MAIN_ROWS : MAIN_ROWS + 8] = jnp.concatenate([rest, jnp.zeros((3, 128), jnp.float32)], axis=0)

    def natural(at, count):
        packed = rows_ref[at : at + count // 2]
        tall_ref[pl.ds(0, count // 2, stride=2)] = packed[:, :SIDE]
        tall_ref[pl.ds(1, count // 2, stride=2)] = packed[:, SIDE:]
        return tall_ref[:count]

    at = 0
    for i in range(4):
        down_ref[i] = natural(at, 512).T.astype(jnp.bfloat16)
        at += 256
    half = SIDE // 2
    for i in range(3):
        one, two, three = [rows_ref[pl.ds(at + j, half, stride=3)] for j in range(3)]
        tall_ref[pl.ds(0, half, stride=2)] = one[:, :SIDE]
        tall_ref[pl.ds(1, half, stride=2)] = two[:, SIDE:]
        tall_ref[pl.ds(64, half, stride=2)] = one[:, SIDE:]
        tall_ref[pl.ds(65, half, stride=2)] = three[:, :SIDE]
        tall_ref[pl.ds(128, half, stride=2)] = two[:, :SIDE]
        tall_ref[pl.ds(129, half, stride=2)] = three[:, SIDE:]
        columns = [tall_ref[64 * j : 64 * j + 64] for j in range(3)]
        in_ref[i] = jnp.concatenate(columns, axis=1).astype(jnp.bfloat16)
        in_t_ref[i] = jnp.concatenate([column.T for column in columns], axis=0).astype(jnp.bfloat16)
        at += 3 * half
    for i in range(3):
        square = natural(at, SIDE)
        out_ref[i] = square.astype(jnp.bfloat16)
        out_t_ref[i] = square.T.astype(jnp.bfloat16)
        at += half
    for i in range(2):
        wide = jnp.concatenate([rows_ref[pl.ds(at + j, SIDE, stride=2)] for j in range(2)], axis=1)
        ffn_in_ref[i] = wide.astype(jnp.bfloat16)
        ffn_in_t_ref[i] = wide.T.astype(jnp.bfloat16)
        at += 2 * SIDE
    for i in range(2):
        tall = natural(at, 256)
        ffn_out_ref[i] = tall.astype(jnp.bfloat16)
        ffn_out_t_ref[i] = tall.T.astype(jnp.bfloat16)
        at += 128
    up_ref[...] = jnp.concatenate(
        [rows_ref[pl.ds(at + j, SIDE, stride=4)] for j in range(4)], axis=1
    ).astype(jnp.bfloat16)
    at += 4 * SIDE
    tall_ref[:128] = jnp.zeros((128, SIDE), jnp.float32)
    tall = natural(at, 16)
    tall_ref[16:128] = jnp.zeros((112, SIDE), jnp.float32)
    small_ref[...] = tall_ref[:128].T


def unpack_weights(flat):
    bf16 = jnp.bfloat16
    shapes = [
        (4, SIDE, D),
        (3, 3 * SIDE, SIDE),
        (3, SIDE, SIDE),
        (2, SIDE_FF, SIDE),
        (2, SIDE, SIDE_FF),
        (3, SIDE, 3 * SIDE),
        (3, SIDE, SIDE),
        (2, SIDE, SIDE_FF),
        (2, SIDE_FF, SIDE),
        (SIDE, D),
    ]
    return pl.pallas_call(
        unpack_kernel,
        out_shape=[jax.ShapeDtypeStruct(shape, bf16) for shape in shapes]
        + [jax.ShapeDtypeStruct((SIDE, 128), jnp.float32)],
        in_specs=[vmem],
        out_specs=[vmem] * 11,
        scratch_shapes=[
            pltpu.VMEM((MAIN_ROWS + 8, 128), jnp.float32),
            pltpu.VMEM((512, SIDE), jnp.float32),
        ],
        compiler_params=LIMIT,
        name="unpack",
        cost_estimate=cost(8),
    )(flat)


def per_device(
    source_ids,
    target_inputs,
    lengths,
    positions,
    target_ids,
    target_mask,
    table,
    backbone_attn,
    backbone_ffn_in,
    backbone_ffn_out,
    backbone_gains,
    inner_weights,
    first_moment,
    second_moment,
    anchor,
    outer_momentum,
):
    micro = source_ids.shape[0]
    src_tokens = source_ids.shape[2]
    tgt_tokens = target_inputs.shape[2]
    size = lax.axis_size("dp")
    me = lax.axis_index("dp")
    core = me & 1
    rows = table.shape[0]
    padded = -(-rows // 512) * 512
    score = [positions, target_ids, target_mask]
    spots = positions.shape[2]
    ids_count = source_ids.size + target_inputs.size
    cap = -(-(ids_count * 5 // (size * 6)) // 16) * 16
    slots, column, near, other, scored = plan(
        me[None], source_ids, target_inputs, score, rows, size, cap, tgt_tokens
    )
    asked = ask(near, other)
    found = jnp.take(table, asked[:, :cap].reshape(-1), axis=0, mode="clip")
    most = functools.reduce(jnp.maximum, gather_peers(after(asked, found)[:, -128:], "grp"))
    weights = unpack_weights(after(inner_weights, found, most))
    table_pad, weight = table_parts(after(table, found, most), weights[9])
    most = jnp.max(most[:, 1 + micro])
    goals, where = goal_rows(after(me[None], most), asked, table_pad, micro, spots)
    embed_src, embed_tgt = embed_rows(
        slots,
        column,
        found.reshape(size // 2, 2, cap, -1),
        cap,
        most,
        source_ids,
        target_inputs,
        table,
        (goals, weight, weights[0]),
    )
    down_t, in_t, out_t, ffn_in_t, ffn_out_t, attn_in, attn_out, ffn_in, ffn_out, up_b, small = weights
    ahead = [down_t, in_t, out_t, ffn_in_t, ffn_out_t, small]
    behind = [in_t, ffn_in_t, attn_in, attn_out, ffn_in, ffn_out, small]
    lens = lengths[:, 0]
    encoded = encode(lens, embed_src, backbone_attn, backbone_ffn_in, backbone_ffn_out, backbone_gains)
    decoded = decode(lens, embed_tgt, encoded, backbone_attn, backbone_ffn_in, backbone_ffn_out, backbone_gains)
    picked, *kept = side(lens, embed_src, encoded, embed_tgt, decoded, scored, ahead)
    far, near = gather_all(picked)
    mix, stats, packed = softmax_part(where, far, near, asked, weight, table_pad, rows)
    far, near = gather_all(stats[:2])
    own, other, grad_up, loss_part = head_finish(
        where, far, near, mix, goals, packed, up_b, micro, spots
    )
    tops = add_home(own, other)
    grads = side_back(lens, embed_src, encoded, embed_tgt, decoded, scored, behind, kept, tops)
    mine, other = flatten(me[None], loss_part, [*grads[:6], grad_up, grads[6]])
    sent = (mine + swap(other, "dp", 1)).astype(jnp.bfloat16)
    terms = [sent] + [swap(sent, "dp", s) for s in range(2, size, 2)]
    mine = tree_sum([term.astype(jnp.float32) for term in terms])
    other = swap(mine, "dp", 1)
    new_first, new_second, new_inner, gap, loss_total, count_total, norm = adam(
        core[None], asked, asked.shape[1] - 128 - micro * spots, mine, other, first_moment, second_moment, inner_weights, anchor
    )
    terms = gather_peers(gap, "grp")
    mine = tree_sum([term.astype(jnp.float32) for term in terms]) / lax.axis_size("grp")
    other = swap(mine, "dp", 1)
    delta, momentum, new_anchor = outer(core[None], mine, other, anchor, outer_momentum)
    return (
        loss_total,
        count_total,
        norm,
        new_first,
        new_second,
        new_inner,
        delta,
        momentum,
        new_anchor,
    )


def solution(mesh):
    return jax.shard_map(
        per_device,
        mesh=mesh,
        in_specs=(
            P(None, ("grp", "dp"), None),
            P(None, ("grp", "dp"), None),
            P(None, ("grp", "dp"), None),
            P(None, ("grp", "dp"), None),
            P(None, ("grp", "dp"), None),
            P(None, ("grp", "dp"), None),
            P("dp", None),
            P(),
            P(),
            P(),
            P(),
            P("grp", None),
            P("grp", None),
            P("grp", None),
            P(),
            P(),
        ),
        out_specs=(
            P("grp"),
            P("grp"),
            P("grp"),
            P("grp", None),
            P("grp", None),
            P("grp", None),
            P(),
            P(),
            P(),
        ),
        check_vma=False,
    )
```

```python
import functools

import jax
import jax.numpy as jnp
from jax import lax
from jax.experimental import pallas as pl
from jax.experimental.pallas import tpu as pltpu
from jax.sharding import PartitionSpec as P

D = 512
HEADS = 8
SIDE = 64
SIDE_HEADS = 8
SIDE_FF = 256
STEP = 5


norm_eps = 1e-06
negative = -1000000000.0
beta_first = 0.9
beta_second = 0.99
adam_eps = 1e-08
learn_rate = 0.03
decay_rate = 0.01
clip_norm = 0.01
outer_rate = 0.7
outer_beta = 0.9


LOG2E = 1.4426950408889634
masked = -1e30

def dot(left, right):
    return jnp.dot(left, right, preferred_element_type=jnp.float32)

def dot_t(left, right):
    return lax.dot_general(left, right, (((1,), (1,)), ((), ())), preferred_element_type=jnp.float32)

def rms_rows(values, gain):
    return values * lax.rsqrt(jnp.mean(values * values, axis=1, keepdims=True) + norm_eps) * gain

def gelu(values):
    inner = values * (0.7978845608028654 + 0.035677408136300125 * (values * values))
    return (0.5 * values) * (1.0 + jnp.tanh(inner))

def staged(count, *stages):
    last = max(lag for lag, _ in stages)
    for step in range(count + last):
        for lag, stage in stages:
            if 0 <= step - lag < count:
                stage(step - lag)


def lane_heads(items, causal_bias):
    lane = lax.broadcasted_iota(jnp.int32, (1, 128), 1)
    scale = 0.125 * LOG2E
    scores, peaks, weights, totals, mixed = {}, {}, {}, {}, {}

    def place(step):
        head = step % HEADS
        return items[step // HEADS], head, slice(head // 2 * 128, head // 2 * 128 + 128)

    def score(step):
        (query, keys, _, key_bias), head, span = place(step)
        own = (lane < 64) if head % 2 == 0 else (lane >= 64)
        spare = lane == (64 if head % 2 == 0 else 0)
        q_head = jnp.where(own, query[:, span], spare.astype(jnp.bfloat16))
        k_head = jnp.where(own, keys[:, span], jnp.where(spare, key_bias, jnp.bfloat16(0)))
        part = dot_t(q_head, k_head)
        scores[step] = part if causal_bias is None else part + causal_bias

    def top(step):
        peaks[step] = jnp.max(scores[step], axis=1, keepdims=True)

    def weigh(step):
        weight = jnp.exp2((scores.pop(step) - peaks.pop(step)) * scale)
        totals[step] = jnp.sum(weight, axis=1, keepdims=True)
        weights[step] = weight.astype(jnp.bfloat16)

    def mix(step):
        values, span = place(step)[0][2], place(step)[2]
        mixed[step] = dot(weights.pop(step), values[:, span]) / totals.pop(step)

    staged(len(items) * HEADS, (0, score), (0, top), (1, weigh), (2, mix))
    return [
        jnp.concatenate(
            [
                jnp.where(lane < 64, mixed[at + 2 * pair], mixed[at + 2 * pair + 1]).astype(jnp.bfloat16)
                for pair in range(HEADS // 2)
            ],
            axis=1,
        )
        for at in range(0, len(items) * HEADS, HEADS)
    ]


def bias_column(count, valid):
    place = lax.broadcasted_iota(jnp.int32, (count, 1), 0)
    return jnp.where(place < valid, 0.0, masked).astype(jnp.bfloat16)

def fetch(pairs, sems):
    copies = [pltpu.make_async_copy(src, dst, sems.at[i]) for i, (src, dst) in enumerate(pairs)]
    for copy in copies:
        copy.start()
    return copies

def frozen_ffn(state_ref, out_ref, gain, win_ref, wout_ref, finish):
    tile = 512

    def step(i, carry):
        at = pl.ds(pl.multiple_of(i * tile, tile), tile)
        state = state_ref[at]
        normed = rms_rows(state, gain).astype(jnp.bfloat16)
        hidden, active, kept = {}, {}, {"total": state}

        def widen(part):
            hidden[part] = dot(normed, win_ref[:, part * 512 : (part + 1) * 512])

        def bend(part):
            active[part] = gelu(hidden.pop(part)).astype(jnp.bfloat16)

        def narrow(part):
            kept["total"] = kept["total"] + dot(active.pop(part), wout_ref[part * 512 : (part + 1) * 512])

        staged(win_ref.shape[1] // 512, (0, widen), (1, bend), (2, narrow))
        total = kept["total"]
        out_ref[at] = finish(total).astype(out_ref.dtype)
        return carry

    lax.fori_loop(0, state_ref.shape[0] // tile, step, 0)


def encoder_kernel(
    len_ref, x_ref, gains_ref, attn_hbm, win_hbm, wout_hbm, out_ref, attn_ref, win_ref, wout_ref, qkv_ref, state_ref, sems
):
    first, second, third, fourth = fetch(
        [
            (attn_hbm.at[0, :, : 3 * D], attn_ref.at[:, : 3 * D]),
            (attn_hbm.at[0, :, 3 * D :], attn_ref.at[:, 3 * D :]),
            (win_hbm.at[0], win_ref),
            (wout_hbm.at[0], wout_ref),
        ],
        sems,
    )
    micro = len_ref.shape[0]
    tokens = x_ref.shape[0] // micro
    normed = rms_rows(x_ref[...].astype(jnp.float32), gains_ref[0:1]).astype(jnp.bfloat16)
    first.wait()
    qkv_ref[...] = dot(normed, attn_ref[:, : 3 * D]).astype(jnp.bfloat16)
    second.wait()

    def step(i, carry):
        at = pl.ds(pl.multiple_of(i * tokens, tokens), tokens)
        bias = bias_column(tokens, len_ref[i, 0])
        (mixed,) = lane_heads(
            [(qkv_ref[at, :D], qkv_ref[at, D : 2 * D], qkv_ref[at, 2 * D :], bias)], None
        )
        state_ref[at] = x_ref[at].astype(jnp.float32) + dot(mixed, attn_ref[:, 3 * D :])
        return carry

    lax.fori_loop(0, micro, step, 0)
    third.wait()
    fourth.wait()
    frozen_ffn(
        state_ref, out_ref, gains_ref[1:2], win_ref, wout_ref, lambda v: rms_rows(v, gains_ref[2:3])
    )


def decoder_kernel(
    len_ref, x_ref, encoded_ref, gains_ref, attn_hbm, win_hbm, wout_hbm, out_ref, attn_ref, cross_ref, win_ref, wout_ref, kv_ref, state_ref, sems
):
    first, second, third, fourth = fetch(
        [
            (attn_hbm.at[1], attn_ref),
            (attn_hbm.at[2], cross_ref),
            (win_hbm.at[1], win_ref),
            (wout_hbm.at[1], wout_ref),
        ],
        sems,
    )
    micro = len_ref.shape[0]
    tokens = x_ref.shape[0] // micro
    sources = encoded_ref.shape[0] // micro
    x = x_ref[...].astype(jnp.float32)
    normed = rms_rows(x, gains_ref[3:4]).astype(jnp.bfloat16)
    row = lax.broadcasted_iota(jnp.int32, (tokens, tokens), 0)
    column = lax.broadcasted_iota(jnp.int32, (tokens, tokens), 1)
    causal = jnp.where(column <= row, 0.0, masked)
    first.wait()
    qkv = dot(normed, attn_ref[:, : 3 * D]).astype(jnp.bfloat16)
    items = []
    for i in range(micro):
        own = qkv[i * tokens : (i + 1) * tokens]
        bias = bias_column(tokens, len_ref[i, 1])
        items.append((own[:, :D], own[:, D : 2 * D], own[:, 2 * D :], bias))
    mixed = lane_heads(items, causal)
    state = x + dot(jnp.concatenate(mixed, axis=0), attn_ref[:, 3 * D :])
    second.wait()
    kv_ref[...] = dot(encoded_ref[...], cross_ref[:, D : 3 * D]).astype(jnp.bfloat16)
    normed = rms_rows(state, gains_ref[4:5]).astype(jnp.bfloat16)
    query = dot(normed, cross_ref[:, :D]).astype(jnp.bfloat16)
    items = []
    for i in range(micro):
        at = slice(i * sources, (i + 1) * sources)
        bias = bias_column(sources, len_ref[i, 0])
        items.append((query[i * tokens : (i + 1) * tokens], kv_ref[at, :D], kv_ref[at, D:], bias))
    mixed = lane_heads(items, None)
    state_ref[...] = state + dot(jnp.concatenate(mixed, axis=0), cross_ref[:, 3 * D :])
    third.wait()
    fourth.wait()
    frozen_ffn(state_ref, out_ref, gains_ref[5:6], win_ref, wout_ref, lambda v: v)


def cost(micros):
    return pl.CostEstimate(
        flops=int(micros * 8e8), bytes_accessed=int(micros * 3e6), transcendentals=0
    )


smem = pl.BlockSpec(memory_space=pltpu.SMEM)
vmem = pl.BlockSpec(memory_space=pltpu.VMEM)
hbm = pl.BlockSpec(memory_space=pl.ANY)
LIMIT = pltpu.CompilerParams(vmem_limit_bytes=56 * 2**20)

def encode(lens, x, attn, ffn_in, ffn_out, gains):
    tokens = x.shape[0]
    return pl.pallas_call(
        encoder_kernel,
        out_shape=jax.ShapeDtypeStruct((tokens, D), jnp.bfloat16),
        in_specs=[smem, vmem, vmem, hbm, hbm, hbm],
        out_specs=vmem,
        scratch_shapes=[pltpu.VMEM((D, 4 * D), jnp.bfloat16), pltpu.VMEM((D, 4 * D), jnp.bfloat16), pltpu.VMEM((4 * D, D), jnp.bfloat16),
            pltpu.VMEM((tokens, 3 * D), jnp.bfloat16), pltpu.VMEM((tokens, D), jnp.float32), pltpu.SemaphoreType.DMA((4,))],
        compiler_params=LIMIT,
        name="encoder",
        cost_estimate=cost(14),
    )(lens, x, gains, attn, ffn_in, ffn_out)

def decode(lens, x, encoded, attn, ffn_in, ffn_out, gains):
    tokens = x.shape[0]
    sources = encoded.shape[0]
    return pl.pallas_call(
        decoder_kernel,
        out_shape=jax.ShapeDtypeStruct((tokens, D), jnp.bfloat16),
        in_specs=[smem, vmem, vmem, vmem, hbm, hbm, hbm],
        out_specs=vmem,
        scratch_shapes=[pltpu.VMEM((D, 4 * D), jnp.bfloat16), pltpu.VMEM((D, 4 * D), jnp.bfloat16), pltpu.VMEM((D, 4 * D), jnp.bfloat16), pltpu.VMEM((4 * D, D), jnp.bfloat16),
            pltpu.VMEM((sources, 2 * D), jnp.bfloat16), pltpu.VMEM((tokens, D), jnp.float32), pltpu.SemaphoreType.DMA((4,))],
        compiler_params=LIMIT,
        name="decoder",
        cost_estimate=cost(10.5),
    )(lens, x, encoded, gains, attn, ffn_in, ffn_out)

def dot_l(left, right):
    return lax.dot_general(left, right, (((0,), (0,)), ((), ())), preferred_element_type=jnp.float32)

def rms_columns(values, gain):
    return values * lax.rsqrt(jnp.mean(values * values, axis=0, keepdims=True) + norm_eps) * gain

def rms_columns_back(values, gain, grad):
    inverse = lax.rsqrt(jnp.mean(values * values, axis=0, keepdims=True) + norm_eps)
    gained = grad * gain
    along = jnp.mean(values * gained, axis=0, keepdims=True)
    gain_grad = jnp.sum(grad * (values * inverse), axis=1, keepdims=True)
    return inverse * gained - values * (inverse * inverse * inverse * along), gain_grad

def gelu_back(values, grad):
    square = values * values
    tanh = jnp.tanh(values * (0.7978845608028654 + 0.035677408136300125 * square))
    slope = 0.5 * (1.0 + tanh) + (0.5 * values) * (1.0 - tanh * tanh) * (0.7978845608028654 + 0.107032224408900375 * square)
    return grad * slope

side_scale = (SIDE // SIDE_HEADS) ** -0.5

def keys_with_bias(keys_t, valid):
    count = keys_t.shape[1]
    place = lax.broadcasted_iota(jnp.int32, (64, count), 1)
    line = lax.broadcasted_iota(jnp.int32, (64, count), 0)
    bias = jnp.where((line == 0) & (place >= valid), masked, 0.0)
    return jnp.concatenate([keys_t.astype(jnp.float32), bias], axis=0).T.astype(jnp.bfloat16)

def head_query(query_t, head):
    line = lax.broadcasted_iota(jnp.int32, (64, 1), 0)
    own = jnp.where(line // 8 == head, query_t, 0.0)
    ones = jnp.broadcast_to(jnp.where(line == 0, 1.0, 0.0), own.shape)
    return jnp.concatenate([own, ones], axis=0).astype(jnp.bfloat16)

def rounded(values):
    return values.astype(jnp.bfloat16).astype(jnp.float32)

def causal_columns(count):
    key = lax.broadcasted_iota(jnp.int32, (count, count), 0)
    query = lax.broadcasted_iota(jnp.int32, (count, count), 1)
    return jnp.where(key <= query, 0.0, masked)

def head_steps(keys):
    count = keys[0].shape[0]
    chunk = min(256, count)
    parts = count // chunk

    def place(step):
        head = step // parts
        return head, head // SIDE_HEADS, head % SIDE_HEADS, slice(step % parts * chunk, step % parts * chunk + chunk)

    return parts, place


def side_heads(items, causal):
    keys = [keys_with_bias(item[1], item[3]) for item in items]
    parts, place = head_steps(keys)
    scores, tops, weights, peaks, totals, mixed, queries = {}, {}, {}, {}, {}, {}, {}

    def score(step):
        unit, pair, head, span = place(step)
        if step % parts == 0:
            queries[unit] = head_query(items[pair][0], head)
        part = dot(keys[pair][span], queries[unit])
        scores[step] = part if causal is None else part + causal[span]

    def top(step):
        tops[step] = jnp.max(scores[step], axis=0, keepdims=True)

    def weigh(step):
        unit = place(step)[0]
        if step % parts == 0:
            peaks[unit] = functools.reduce(jnp.maximum, [tops.pop(step + i) for i in range(parts)])
        weight = jnp.exp2((scores.pop(step) - peaks[unit]) * (side_scale * LOG2E))
        amount = jnp.sum(weight, axis=0, keepdims=True)
        totals[unit] = totals[unit] + amount if unit in totals else amount
        weights[step] = weight.astype(jnp.bfloat16)

    def mix(step):
        unit, pair, head, span = place(step)
        values = items[pair][2][8 * head : 8 * head + 8, span].astype(jnp.bfloat16)
        piece = dot(values, weights.pop(step))
        mixed[unit] = mixed[unit] + piece if unit in mixed else piece

    staged(len(items) * SIDE_HEADS * parts, (0, score), (1, top), (parts, weigh), (parts + 2, mix))
    result = []
    for pair in range(len(items)):
        units = range(pair * SIDE_HEADS, (pair + 1) * SIDE_HEADS)
        outs = jnp.concatenate([mixed[unit] / totals[unit] for unit in units], axis=0)
        sums = [peaks[unit] * (side_scale * LOG2E) + jnp.log2(totals[unit]) for unit in units]
        result.append((outs, jnp.concatenate(sums, axis=0)))
    return result


def side_heads_back(items, causal):
    keys = [keys_with_bias(item[1], item[3]) for item in items]
    values = [item[2].T.astype(jnp.bfloat16) for item in items]
    parts, place = head_steps(keys)
    line = lax.broadcasted_iota(jnp.int32, (64, 1), 0)
    scores, grads, weights, along, queries, owns = {}, {}, {}, {}, {}, {}
    grad_q, grad_k, grad_v = {}, {}, {}

    def score(step):
        unit, pair, head, span = place(step)
        if step % parts == 0:
            queries[unit] = head_query(items[pair][0], head)
            owns[unit] = jnp.where(line // 8 == head, items[pair][5], 0.0).astype(jnp.bfloat16)
        part = dot(keys[pair][span], queries[unit])
        scores[step] = part if causal is None else part + causal[span]
        grads[step] = dot(values[pair][span], owns[unit])

    def weigh(step):
        unit, pair, head, _ = place(step)
        sums = items[pair][4][head : head + 1]
        weight = jnp.exp2(scores.pop(step) * (side_scale * LOG2E) - sums)
        grads[step] = rounded(grads[step])
        part = jnp.sum(grads[step] * weight, axis=0, keepdims=True)
        along[unit] = along[unit] + part if unit in along else part
        weights[step] = weight

    def finish(step):
        unit, pair, head, span = place(step)
        rows = slice(8 * head, 8 * head + 8)
        query, key, _, _, _, grad = items[pair]
        weight = weights.pop(step)
        grad_s = (weight * (grads.pop(step) - along[unit])).astype(jnp.bfloat16)
        part = dot(key[rows, span].astype(jnp.bfloat16), grad_s)
        grad_q[unit] = grad_q[unit] + part if unit in grad_q else part
        grad_k[step] = dot_t(query[rows].astype(jnp.bfloat16), grad_s)
        grad_v[step] = dot_t(grad[rows].astype(jnp.bfloat16), weight.astype(jnp.bfloat16))

    staged(len(items) * SIDE_HEADS * parts, (0, score), (2, weigh), (parts + 2, finish))

    def joined(pieces, units):
        rows = [
            jnp.concatenate([pieces[unit * parts + i] for i in range(parts)], axis=1) for unit in units
        ]
        return jnp.concatenate(rows, axis=0)

    result = []
    for pair in range(len(items)):
        units = range(pair * SIDE_HEADS, (pair + 1) * SIDE_HEADS)
        whole_q = jnp.concatenate([grad_q[unit] for unit in units], axis=0)
        result.append((whole_q * side_scale, joined(grad_k, units) * side_scale, joined(grad_v, units)))
    return result


def chosen_columns(tokens, positions):
    token = lax.broadcasted_iota(jnp.int32, (tokens, positions.shape[1]), 0)
    return jnp.where(token == positions, 1.0, 0.0).astype(jnp.bfloat16)

def side_kernel(len_ref, src_ref, encoded_ref, tgt_ref, decoded_ref, positions_ref, down_ref, attn_in_ref, attn_out_ref, ffn_in_ref, ffn_out_ref, small_ref,
                picked_ref, enc_ref, dec_ref, enc_mixed_ref, self_mixed_ref, cross_mixed_ref, enc_sums_ref, self_sums_ref, cross_sums_ref):
    micro = len_ref.shape[0]

    def gain(i):
        return small_ref[:, i:i + 1]

    def attend(which, query_n, key_n, side_of, causal, mixed_ref, sums_ref):
        query = rounded(dot(attn_in_ref[which, :64], query_n))
        keyval = rounded(dot(attn_in_ref[which, 64:], key_n))
        width, far = query.shape[1] // micro, keyval.shape[1] // micro
        spans = [
            (slice(i * width, (i + 1) * width), slice(i * far, (i + 1) * far)) for i in range(micro)
        ]
        items = [
            (query[:, near], keyval[:64, away], keyval[64:, away], len_ref[i, side_of])
            for i, (near, away) in enumerate(spans)
        ]
        parts = []
        for (near, _), (mixed, sums) in zip(spans, side_heads(items, causal)):
            sums_ref[:, near] = sums
            parts.append(mixed.astype(jnp.bfloat16))
        mixed_b = jnp.concatenate(parts, axis=1)
        mixed_ref[...] = mixed_b
        return dot(attn_out_ref[which], mixed_b)

    def ffn(which, normed):
        active = gelu(dot(ffn_in_ref[which], normed)).astype(jnp.bfloat16)
        return dot(ffn_out_ref[which], active)

    def norm(values, i):
        return rms_columns(values, gain(i)).astype(jnp.bfloat16)

    state = dot_t(down_ref[0], src_ref[...])
    enc_ref[0] = state
    normed = norm(state, 0)
    flow = dot_t(down_ref[2], tgt_ref[...])
    dec_ref[0] = flow
    normed_flow = norm(flow, 3)
    tokens = flow.shape[1] // micro
    causal = causal_columns(tokens)
    state = state + attend(0, normed, normed, 0, None, enc_mixed_ref, enc_sums_ref)
    enc_ref[1] = state
    flow = flow + attend(1, normed_flow, normed_flow, 1, causal, self_mixed_ref, self_sums_ref)
    dec_ref[1] = flow
    state = state + ffn(0, norm(state, 1))
    enc_ref[2] = state
    joined = dot_t(down_ref[1], encoded_ref[...])
    enc_ref[3] = joined
    gate = jax.nn.sigmoid(gain(7))
    memory = norm(gate * joined + (1.0 - gate) * state, 2)
    flow = flow + attend(2, norm(flow, 4), memory, 0, None, cross_mixed_ref, cross_sums_ref)
    dec_ref[2] = flow
    flow = flow + ffn(1, norm(flow, 5))
    dec_ref[3] = flow
    joined = dot_t(down_ref[3], decoded_ref[...])
    dec_ref[4] = joined
    gate = jax.nn.sigmoid(gain(8))
    top = norm(gate * joined + (1.0 - gate) * flow, 6)
    for i in range(micro):
        chosen = chosen_columns(tokens, positions_ref[i : i + 1])
        picked_ref[i] = dot(top[:, i * tokens : (i + 1) * tokens], chosen).astype(jnp.bfloat16)


def side(lens, src, encoded, tgt, decoded, positions, weights):
    s, t = src.shape[0], tgt.shape[0]
    m, p = positions.shape
    f32, bf16 = jnp.float32, jnp.bfloat16
    shapes = [((m, 64, p), bf16), ((4, 64, s), f32), ((5, 64, t), f32), ((64, s), bf16), ((64, t), bf16), ((64, t), bf16), ((8, s), f32), ((8, t), f32), ((8, t), f32)]
    return pl.pallas_call(
        side_kernel,
        out_shape=[jax.ShapeDtypeStruct(*item) for item in shapes],
        in_specs=[smem] + [vmem] * 11,
        out_specs=[vmem] * 9,
        compiler_params=LIMIT,
        name="side",
        cost_estimate=cost(24),
    )(lens, src, encoded, tgt, decoded, positions, *weights)

def back_kernel(*refs):
    (len_ref, src_ref, encoded_ref, tgt_ref, decoded_ref, positions_ref, attn_in_t_ref, ffn_in_t_ref, attn_in_ref, attn_out_ref, ffn_in_ref, ffn_out_ref, small_ref,
     enc_ref, dec_ref, enc_mixed_ref, self_mixed_ref, cross_mixed_ref, enc_sums_ref, self_sums_ref, cross_sums_ref) = refs[:21]
    parts_refs = refs[21:-7]
    down_out, attn_in_out, in_rest_out, attn_out_out, ffn_in_out, ffn_out_out, small_out = refs[-7:]
    outs = {
        "down": down_out,
        "attn_in": attn_in_out,
        "in_rest": in_rest_out,
        "attn_out": attn_out_out,
        "ffn_in": ffn_in_out,
        "ffn_out": ffn_out_out,
    }
    micro = len_ref.shape[0]

    def put(which, index, values):
        if values.shape[1] == 3 * SIDE:
            put("in_rest", index, values[:, 128:])
            values = values[:, :128]
        outs[which][index] = values

    smalls = {}

    def gain(i):
        return small_ref[:, i:i + 1]

    def norm(values, i):
        return rms_columns(values, gain(i)).astype(jnp.bfloat16)

    def norm_back(values, i, grad):
        result, smalls[i] = rms_columns_back(values, gain(i), grad)
        return result

    def blend_back(i, joined, late, grad):
        gate = jax.nn.sigmoid(gain(i))
        smalls[i] = jnp.sum(grad * (joined - late), axis=1, keepdims=True) * (gate * (1.0 - gate))
        return gate * grad, (1.0 - gate) * grad

    def ffn_back(which, normed, grad):
        grad_b = grad.astype(jnp.bfloat16)
        hidden = dot(ffn_in_t_ref[which], normed)
        active = gelu(hidden).astype(jnp.bfloat16)
        put("ffn_out", which, dot_t(active, grad_b))
        grad_hidden = gelu_back(hidden, dot(ffn_out_ref[which], grad_b)).astype(jnp.bfloat16)
        put("ffn_in", which, dot_t(normed, grad_hidden))
        return dot(ffn_in_ref[which], grad_hidden)

    def attend_back(which, query_n, key_n, mixed_ref, sums_ref, grad, side_of, causal):
        grad_b = grad.astype(jnp.bfloat16)
        put("attn_out", which, dot_t(mixed_ref[...], grad_b))
        grad_mixed = rounded(dot(attn_out_ref[which], grad_b))
        query = rounded(dot(attn_in_t_ref[which, :64], query_n))
        keyval = rounded(dot(attn_in_t_ref[which, 64:], key_n))
        width, far = query.shape[1] // micro, keyval.shape[1] // micro
        items = []
        for i in range(micro):
            near, away = slice(i * width, (i + 1) * width), slice(i * far, (i + 1) * far)
            items.append(
                (query[:, near], keyval[:64, away], keyval[64:, away], len_ref[i, side_of], sums_ref[:, near], grad_mixed[:, near])
            )
        grads_q, grads_kv = [], []
        for grad_q, grad_k, grad_v in side_heads_back(items, causal):
            grads_q.append(grad_q.astype(jnp.bfloat16))
            grads_kv.append(jnp.concatenate([grad_k, grad_v], axis=0).astype(jnp.bfloat16))
        return jnp.concatenate(grads_q, axis=1), jnp.concatenate(grads_kv, axis=1)

    tokens = tgt_ref.shape[0] // micro
    grads = []
    for index in range(micro):
        grad_picked = tree_sum([ref[index].astype(jnp.float32) for ref in parts_refs])
        chosen = chosen_columns(tokens, positions_ref[index : index + 1])
        high = grad_picked.astype(jnp.bfloat16)
        low = (grad_picked - high.astype(jnp.float32)).astype(jnp.bfloat16)
        grads.append(dot_t(high, chosen) + dot_t(low, chosen))
    grad = jnp.concatenate(grads, axis=1)
    gate = jax.nn.sigmoid(gain(8))
    final = gate * dec_ref[4] + (1.0 - gate) * dec_ref[3]
    grad = norm_back(final, 6, grad)
    grad_joined, grad = blend_back(8, dec_ref[4], dec_ref[3], grad)
    put("down", 3, dot(grad_joined.astype(jnp.bfloat16), decoded_ref[...]))
    grad = grad + norm_back(dec_ref[2], 5, ffn_back(1, norm(dec_ref[2], 5), grad))
    gate = jax.nn.sigmoid(gain(7))
    final = gate * enc_ref[3] + (1.0 - gate) * enc_ref[2]
    memory = norm(final, 2)
    normed = norm(dec_ref[1], 4)
    grad_q, grad_kv = attend_back(2, normed, memory, cross_mixed_ref, cross_sums_ref, grad, 0, None)
    zero_q = jnp.zeros((128, tgt_ref.shape[0]), jnp.bfloat16)
    zero_kv = jnp.zeros((64, src_ref.shape[0]), jnp.bfloat16)
    put("attn_in", 2, dot_t(normed, jnp.concatenate([grad_q, zero_q], axis=0)) + dot_t(memory, jnp.concatenate([zero_kv, grad_kv], axis=0)))
    weight = attn_in_ref[2]
    grad_memory = dot(weight, jnp.concatenate([zero_kv, grad_kv], axis=0))
    grad = grad + norm_back(dec_ref[1], 4, dot(weight, jnp.concatenate([grad_q, zero_q], axis=0)))
    normed = norm(dec_ref[0], 3)
    grad_q, grad_kv = attend_back(1, normed, normed, self_mixed_ref, self_sums_ref, grad, 1, causal_columns(tokens))
    grad_qkv = jnp.concatenate([grad_q, grad_kv], axis=0)
    put("attn_in", 1, dot_t(normed, grad_qkv))
    grad = grad + norm_back(dec_ref[0], 3, dot(attn_in_ref[1], grad_qkv))
    put("down", 2, dot(grad.astype(jnp.bfloat16), tgt_ref[...]))
    grad = norm_back(final, 2, grad_memory)
    grad_joined, grad = blend_back(7, enc_ref[3], enc_ref[2], grad)
    put("down", 1, dot(grad_joined.astype(jnp.bfloat16), encoded_ref[...]))
    grad = grad + norm_back(enc_ref[1], 1, ffn_back(0, norm(enc_ref[1], 1), grad))
    normed = norm(enc_ref[0], 0)
    grad_q, grad_kv = attend_back(0, normed, normed, enc_mixed_ref, enc_sums_ref, grad, 0, None)
    grad_qkv = jnp.concatenate([grad_q, grad_kv], axis=0)
    put("attn_in", 0, dot_t(normed, grad_qkv))
    grad = grad + norm_back(enc_ref[0], 0, dot(attn_in_ref[0], grad_qkv))
    put("down", 0, dot(grad.astype(jnp.bfloat16), src_ref[...]))
    lane = lax.broadcasted_iota(jnp.int32, (1, 128), 1)
    total = jnp.zeros((64, 128), jnp.float32)
    for i in range(9):
        total = total + jnp.where(lane == i, smalls[i], 0.0)
    small_out[...] = total

def side_back(lens, src, encoded, tgt, decoded, positions, weights, kept, parts):
    f32 = jnp.float32
    shapes = [(4, 64, 512), (3, 64, 128), (3, 64, 64), (3, 64, 64), (2, 64, 256), (2, 256, 64), (64, 128)]
    return pl.pallas_call(
        back_kernel,
        out_shape=[jax.ShapeDtypeStruct(shape, f32) for shape in shapes],
        in_specs=[smem] + [vmem] * (20 + len(parts)),
        out_specs=[vmem] * 7,
        compiler_params=LIMIT,
        name="side_back",
        cost_estimate=cost(34),
    )(lens, src, encoded, tgt, decoded, positions, *weights, *kept, *parts)


def swap(values, axis, distance):
    size = lax.axis_size(axis)
    return lax.ppermute(values, axis, [(i, i ^ distance) for i in range(size)])


def gather_peers(values, axis):
    return [values] + [swap(values, axis, s) for s in range(1, lax.axis_size(axis))]


def tree_sum(terms):
    while len(terms) > 1:
        terms = [terms[i] + terms[i + 1] for i in range(0, len(terms), 2)]
    return terms[0]


def owners_of(ids, rows, peers, me):
    owner = jnp.zeros(ids.shape, jnp.int32)
    for peer in range(1, peers):
        owner = owner + jnp.where(ids >= peer * rows, 1, 0)
    return owner ^ me


def ranks_within(own):
    peers, count = own.shape
    own_b = own.astype(jnp.bfloat16)
    before = jnp.where(
        lax.broadcasted_iota(jnp.int32, (128, 128), 0)
        < lax.broadcasted_iota(jnp.int32, (128, 128), 1),
        1.0,
        0.0,
    ).astype(jnp.bfloat16)
    seen = jnp.zeros((peers, 1), jnp.float32)
    ranks = []
    for start in range(0, count, 128):
        block = slice(start, start + 128)
        inside = dot(own_b[:, block], before) + seen
        ranks.append(jnp.sum(own[:, block] * (inside + 1.0), axis=0, keepdims=True) - 1.0)
        seen = seen + jnp.sum(own[:, block], axis=1, keepdims=True)
    return jnp.concatenate(ranks, axis=1), seen


def column_of(row):
    return jnp.broadcast_to(row, (8, row.shape[1])).T[:, :1]


def placed(own, values, hit):
    high = jnp.floor(values * (1.0 / 64.0))
    low = values - 64.0 * high
    return 64.0 * dot((own * high).astype(jnp.bfloat16), hit) + dot(
        (own * low).astype(jnp.bfloat16), hit
    )


def score_part(rows, peers, tokens, me, busy, at_ref, goal_ref, mask_ref, token_ref, letter_ref, at):
    micro, _, spots = at_ref.shape
    token = lax.broadcasted_iota(jnp.int32, (tokens, 1), 0)
    token_f = token.astype(jnp.float32)
    spot_f = lax.broadcasted_iota(jnp.int32, (1, spots), 1).astype(jnp.float32)
    lower = jnp.where(
        lax.broadcasted_iota(jnp.int32, (tokens, tokens), 0)
        > lax.broadcasted_iota(jnp.int32, (tokens, tokens), 1),
        1.0,
        0.0,
    ).astype(jnp.bfloat16)
    goals, masks, slots, used = [], [], [], []
    for index in range(micro):
        mask = mask_ref[index].astype(jnp.float32)
        met = jnp.where(token == at_ref[index], mask, 0.0)
        times = jnp.sum(met, axis=1, keepdims=True)
        active = jnp.where(times > 0.0, 1.0, 0.0)
        wide = jnp.broadcast_to(active, (tokens, 128)).astype(jnp.bfloat16)
        slot = dot(lower, wide)[:, :1]
        here = jnp.where(slot == spot_f, active, 0.0)
        token_row = jnp.sum(here * (token_f + 1.0), axis=0, keepdims=True) - 1.0
        token_ref[index : index + 1] = token_row.astype(jnp.int32)
        count = jnp.sum(here * times, axis=0, keepdims=True).astype(jnp.int32)
        first = at + (micro + index) * spots
        letter_ref[:, first : first + spots] = jnp.broadcast_to(count, (peers, spots))
        slots.append(jnp.sum(met * slot, axis=0, keepdims=True) + float(index * spots))
        goals.append(goal_ref[index])
        masks.append(mask)
        used.append(jnp.sum(active, axis=0, keepdims=True))
    goal, mask, slot = [jnp.concatenate(rows_, axis=1) for rows_ in (goals, masks, slots)]
    far = owners_of(goal, rows, peers, 0)
    local = (goal - far * rows).astype(jnp.float32)
    line = lax.broadcasted_iota(jnp.int32, (peers, goal.shape[1]), 0)
    own = jnp.where((line == (far ^ me)) & (mask > 0.0), 1.0, 0.0)
    rank, many = ranks_within(own)
    order = lax.broadcasted_iota(jnp.int32, (1, goal.shape[1]), 1).astype(jnp.float32)
    hit = jnp.where(column_of(rank) == order, 1.0, 0.0).astype(jnp.bfloat16)
    letter_ref[:, at : at + micro * spots] = placed(own, slot, hit).astype(
        jnp.int32
    ) * 65536 + placed(own, local, hit).astype(jnp.int32)
    lane = lax.broadcasted_iota(jnp.int32, (peers, 128), 1)
    info = jnp.where(lane == 0, many, jnp.where(lane == micro + 1, busy, 0.0))
    for index in range(micro):
        info = jnp.where(lane == index + 1, used[index], info)
    first = at + 2 * micro * spots
    letter_ref[:, first : first + 128] = info.astype(jnp.int32)


def plan_kernel(rows, peers, cap, tokens, me_ref, src_ref, tgt_ref, *refs):
    score_refs, (slots_ref, column_ref, near_ref, other_ref, token_ref, letter_ref) = refs[:3], refs[3:]
    ids_row = jnp.concatenate(
        [ref[index] for ref in (src_ref, tgt_ref) for index in range(ref.shape[0])], axis=1
    )
    count = ids_row.shape[1]
    ids = ids_row.astype(jnp.float32)
    column = column_of(ids)
    column_ref[...] = column
    first_at = jnp.full((1, count), float(count), jnp.float32)
    for start in range(0, count, 256):
        place = (lax.broadcasted_iota(jnp.int32, (256, 1), 0) + start).astype(jnp.float32)
        same = column[start : start + 256] == ids
        first_at = jnp.minimum(
            first_at, jnp.min(jnp.where(same, place, float(count)), axis=0, keepdims=True)
        )
    first = first_at == lax.broadcasted_iota(jnp.int32, (1, count), 1).astype(jnp.float32)
    far = owners_of(ids_row, rows, peers, 0)
    line = lax.broadcasted_iota(jnp.int32, (peers, count), 0)
    own = jnp.where((line == (far ^ me_ref[0])) & first, 1.0, 0.0)
    rank, seen = ranks_within(own)
    width = -(-cap // 128) * 128
    spot = lax.broadcasted_iota(jnp.int32, (1, width), 1).astype(jnp.float32)
    hit = jnp.where(column_of(rank) == spot, 1.0, 0.0).astype(jnp.bfloat16)
    filled = dot(own.astype(jnp.bfloat16), hit)
    local = placed(own, (ids_row - far * rows).astype(jnp.float32), hit).astype(jnp.int32)
    letter_ref[:, :width] = local
    owner = lax.broadcasted_iota(jnp.int32, (peers, 1), 0) ^ me_ref[0]
    slots = jnp.where(filled > 0.5, local + owner * rows, -1)[:, :cap]
    for part in range(2):
        slots_ref[part : part + 1] = jnp.concatenate(
            [slots[peer : peer + 1] for peer in range(part, peers, 2)], axis=1
        )
    busy = jnp.max(seen, axis=0, keepdims=True)
    score_part(rows, peers, tokens, me_ref[0], busy, *score_refs, token_ref, letter_ref, width)
    for peer in range(peers):
        letter = near_ref if peer % 2 == 0 else other_ref
        letter[peer // 2 : peer // 2 + 1] = letter_ref[peer : peer + 1]


def plan(me, source, target, score, rows, peers, cap, tokens):
    count = source.shape[0] * source.shape[2] + target.shape[0] * target.shape[2]
    micro, _, spots = score[0].shape
    letter = -(-cap // 128) * 128 + 2 * micro * spots + 128
    shapes = [
        ((2, peers // 2 * cap), jnp.int32),
        ((count, 1), jnp.float32),
        ((peers // 2, letter), jnp.int32),
        ((peers // 2, letter), jnp.int32),
        ((micro, spots), jnp.int32),
    ]
    return pl.pallas_call(
        functools.partial(plan_kernel, rows, peers, cap, tokens),
        out_shape=[jax.ShapeDtypeStruct(*shape) for shape in shapes],
        in_specs=[smem] + [vmem] * 5,
        out_specs=[vmem] * len(shapes),
        scratch_shapes=[pltpu.VMEM((peers, letter), jnp.int32)],
        compiler_params=LIMIT,
        name="plan",
        cost_estimate=cost(4),
    )(me, source, target, *score)


def expand_kernel(sizes, slots_ref, column_ref, *refs):
    far_refs, near_ref, out_refs = refs[: -1 - len(sizes)], refs[-1 - len(sizes)], refs[-len(sizes) :]
    slots = slots_ref[...].astype(jnp.float32)
    rows = (jnp.concatenate([ref[0] for ref in far_refs], axis=0), near_ref[...])
    blocks, base = [], 0
    for out in out_refs:
        blocks += [(out, start, base + start) for start in range(0, out.shape[0], 256)]
        base = base + out.shape[0]
    picks = {}

    def match(step):
        column = column_ref[blocks[step][2] : blocks[step][2] + 256]
        picks[step] = [
            jnp.where(column == slots[i : i + 1], 1.0, 0.0).astype(jnp.bfloat16) for i in range(2)
        ]

    def fill(step):
        first, second = [dot(pick, rows[i]) for i, pick in enumerate(picks.pop(step))]
        out, start, _ = blocks[step]
        out[start : start + 256] = (first + second).astype(jnp.bfloat16)

    staged(len(blocks), (0, match), (1, fill))


def expand(slots, column, far, near, sizes):
    width = near.shape[1]
    return pl.pallas_call(
        functools.partial(expand_kernel, sizes),
        out_shape=[jax.ShapeDtypeStruct((size, width), jnp.bfloat16) for size in sizes],
        in_specs=[vmem] * (3 + len(far)),
        out_specs=[vmem] * len(sizes),
        compiler_params=LIMIT,
        name="expand",
        cost_estimate=cost(3.8),
    )(slots, column, *far, near)


def ask(near, other):
    count = near.shape[0]
    pairs = jnp.stack([near, swap(other, "dp", 1)], axis=1)
    far = [pairs[:1]] + [swap(pairs[i : i + 1], "dp", 2 * i) for i in range(1, count)]
    return jnp.concatenate(far).reshape(2 * count, -1)


def send_rows(slots, column, found, sizes, between):
    count = found.shape[0]
    far = [found[0]] + [swap(found[i], "dp", 2 * i) for i in range(1, count)]
    other = jnp.concatenate([part[1] for part in far])
    near = swap(after(other, *between), "dp", 1)
    return expand(slots, column, far, near, sizes)


def every_row(ids, table, rows):
    size = lax.axis_size("dp")
    me = lax.axis_index("dp")

    def step(i, carry):
        shard, filled = carry
        local = ids - (me + i) % size * rows
        here = (local >= 0) & (local < rows)
        found = jnp.take(shard, jnp.clip(local, 0, rows - 1), axis=0)
        shard = lax.ppermute(shard, "dp", [((j + 1) % size, j) for j in range(size)])
        return shard, jnp.where(here[:, None], found, filled)

    empty = jnp.zeros((ids.shape[0], table.shape[1]), table.dtype)
    return lax.fori_loop(0, size, step, (table, empty))[1]


def embed_rows(slots, column, found, cap, most, source, target, table, between):
    sizes = [source.size, target.size]
    result = tuple(send_rows(slots, column, found, sizes, between))

    def long_way(carry):
        ids = jnp.concatenate([source.reshape(-1), target.reshape(-1)])
        filled = every_row(ids, table, table.shape[0])
        return (jnp.zeros_like(carry[0]), (filled[: sizes[0]], filled[sizes[0] :]))

    return lax.while_loop(lambda carry: carry[0] > cap, long_way, (most, result))[1]


def gather_all(values):
    far = [values] + [swap(values, "dp", s) for s in range(2, lax.axis_size("dp"), 2)]
    return far, swap(jnp.stack(far), "dp", 1)


def add_home(own, other):
    pair = (own.astype(jnp.float32) + swap(other, "dp", 1).astype(jnp.float32)).astype(own.dtype)
    return [pair[0]] + [swap(pair[i], "dp", 2 * i) for i in range(1, pair.shape[0])]


def table_kernel(rows, table_ref, up_ref, padded_ref, weight_ref):
    block = table_ref.shape[0]
    place = lax.broadcasted_iota(jnp.int32, (block, 1), 0) + pl.program_id(0) * block
    table = jnp.where(place < rows, table_ref[...], jnp.bfloat16(0))
    padded_ref[...] = table
    lifted = dot_t(table, up_ref[...]) * (D ** (-0.5) * LOG2E)
    high = lifted.astype(jnp.bfloat16)
    weight_ref[:, :SIDE] = high
    weight_ref[:, SIDE:] = (lifted - high.astype(jnp.float32)).astype(jnp.bfloat16)


VOCAB_BLOCK = 512
TILE = 512
SCORE_TILE = 256


def table_parts(table, up_b):
    rows, width = table.shape
    padded = -(-rows // VOCAB_BLOCK) * VOCAB_BLOCK
    return pl.pallas_call(
        functools.partial(table_kernel, rows),
        out_shape=[
            jax.ShapeDtypeStruct((padded, width), jnp.bfloat16),
            jax.ShapeDtypeStruct((padded, 2 * SIDE), jnp.bfloat16),
        ],
        grid=(padded // VOCAB_BLOCK,),
        in_specs=[
            pl.BlockSpec((VOCAB_BLOCK, width), lambda i: (i, 0)),
            pl.BlockSpec((SIDE, width), lambda i: (0, 0)),
        ],
        out_specs=[
            pl.BlockSpec((VOCAB_BLOCK, width), lambda i: (i, 0)),
            pl.BlockSpec((VOCAB_BLOCK, 2 * SIDE), lambda i: (i, 0)),
        ],
        compiler_params=LIMIT,
        name="table_parts",
        cost_estimate=cost(5),
    )(table, up_b)


def goals_kernel(spots, micro, me_ref, letter_ref, table_ref, out_ref, where_ref, tall_ref, sum_ref, sem):
    peers, length = letter_ref.shape
    entry_at = length - 128 - 2 * micro * spots
    where_ref[0] = me_ref[0]
    first = jnp.int32(0)
    for device in range(peers):
        for index in range(micro):
            where_ref[2 + device * micro + index] = first
            first = first + letter_ref[me_ref[0] ^ device, length - 128 + 1 + index]
    where_ref[1] = first
    tiles = (first + TILE - 1) // TILE
    for start in range(0, table_ref.shape[0], VOCAB_BLOCK):
        tall_ref[start : start + VOCAB_BLOCK] = table_ref[start : start + VOCAB_BLOCK].astype(jnp.float32)

    def clear(i, carry):
        sum_ref[pl.ds(pl.multiple_of(i * TILE, TILE), TILE)] = jnp.zeros((TILE, sum_ref.shape[1]), jnp.float32)
        return carry

    lax.fori_loop(0, tiles, clear, 0)
    for peer in range(peers):
        base = 2 + (peer ^ where_ref[0]) * micro

        def add(j, carry):
            entry = letter_ref[peer, entry_at + j]
            slot = entry // 65536
            local = entry - slot * 65536
            row = slot + where_ref[base]
            for index in range(1, micro):
                row = jnp.where(slot >= index * spots, slot - index * spots + where_ref[base + index], row)
            sum_ref[pl.ds(row, 1)] = sum_ref[pl.ds(row, 1)] + tall_ref[pl.ds(local, 1)]
            return carry

        lax.fori_loop(0, letter_ref[peer, length - 128], add, 0)

    def send(i, carry):
        at = pl.ds(pl.multiple_of(i * TILE, TILE), TILE)
        copy = pltpu.make_async_copy(sum_ref.at[at], out_ref.at[at], sem)
        copy.start()
        copy.wait()
        return carry

    lax.fori_loop(0, tiles, send, 0)


def goal_rows(me, letters, table_pad, micro, spots):
    total = letters.shape[0] * micro * spots
    padded, width = table_pad.shape
    return pl.pallas_call(
        functools.partial(goals_kernel, spots, micro),
        out_shape=[
            jax.ShapeDtypeStruct((total, width), jnp.float32),
            jax.ShapeDtypeStruct((2 + letters.shape[0] * micro,), jnp.int32),
        ],
        in_specs=[smem, smem, vmem],
        out_specs=[hbm, smem],
        scratch_shapes=[
            pltpu.VMEM((padded, width), jnp.float32),
            pltpu.VMEM((total, width), jnp.float32),
            pltpu.SemaphoreType.DMA,
        ],
        compiler_params=LIMIT,
        name="goals",
        cost_estimate=cost(9),
    )(me, letters, table_pad)


def softmax_kernel(rows, where_ref, *refs):
    far_refs = refs[:-9]
    near_ref, letter_ref, weight_ref, table_ref, mix_ref, stats_ref, packed_ref, all_ref, gathered_ref = refs[-9:]
    step = pl.program_id(0)
    peers, micro, _, spots = gathered_ref.shape
    tiles = (where_ref[1] + SCORE_TILE - 1) // SCORE_TILE
    count_at = letter_ref.shape[1] - 128 - micro * spots

    @pl.when(step == 0)
    def _():
        def clear(i, carry):
            all_ref[pl.ds(pl.multiple_of(i * SCORE_TILE, SCORE_TILE), SCORE_TILE)] = jnp.zeros((SCORE_TILE, 128), jnp.float32)
            return carry

        lax.fori_loop(0, tiles, clear, 0)
        for i, far_ref in enumerate(far_refs):
            gathered_ref[2 * i] = far_ref[...]
            gathered_ref[2 * i + 1] = near_ref[i]
        for device in range(peers):
            for index in range(micro):
                peer = where_ref[0] ^ device
                block = jnp.concatenate(
                    [
                        gathered_ref[peer, index].astype(jnp.float32),
                        letter_ref[
                            pl.ds(peer, 1), count_at + index * spots : count_at + (index + 1) * spots
                        ].astype(jnp.float32),
                        jnp.zeros((SIDE - 1, spots), jnp.float32),
                    ],
                    axis=0,
                )
                all_ref[pl.ds(where_ref[2 + device * micro + index], spots)] = block.T

    @pl.when(step < tiles)
    def _():
        mine = all_ref[pl.ds(pl.multiple_of(step * SCORE_TILE, SCORE_TILE), SCORE_TILE)]
        packed_ref[...] = mine
        picked = jnp.concatenate([mine[:, :SIDE], mine[:, :SIDE]], axis=1).astype(jnp.bfloat16)
        padded = weight_ref.shape[0]
        chunk = min(1024, padded)
        logits, shares = {}, {}
        kept = {"peak": None}

        def score(part):
            start = part * chunk
            values = dot_t(picked, weight_ref[start : start + chunk])
            if start + chunk > rows:
                place = lax.broadcasted_iota(jnp.int32, (1, chunk), 1)
                values = jnp.where(place < rows - start, values, -jnp.inf)
            logits[part] = values

        def weigh(part):
            values = logits.pop(part)
            above = jnp.max(values, axis=1, keepdims=True)
            fade = None
            if part > 0:
                above = jnp.maximum(kept["peak"], above)
                fade = jnp.exp2(kept["peak"] - above)
            share = jnp.exp2(values - above)
            amount = jnp.sum(share, axis=1, keepdims=True)
            kept["total"] = amount if fade is None else kept["total"] * fade + amount
            kept["peak"] = above
            shares[part] = (share.astype(jnp.bfloat16), fade)

        def add(part):
            share, fade = shares.pop(part)
            piece = dot(share, table_ref[part * chunk : (part + 1) * chunk])
            kept["mix"] = piece if fade is None else kept["mix"] * fade + piece

        staged(padded // chunk, (0, score), (1, weigh), (2, add))
        peak, total, mix = kept["peak"], kept["total"], kept["mix"]
        mix_ref[...] = mix
        lane = lax.broadcasted_iota(jnp.int32, (SCORE_TILE, 128), 1)
        stats_ref[...] = jnp.where(lane == 0, peak, jnp.where(lane == 1, total, 0.0)).T[:8]


def in_use(tile, i, where):
    return jnp.minimum(i, (where[1] + tile - 1) // tile - 1)


def softmax_part(where, far, near, letters, weight, table_pad, rows):
    micro, side_width, spots = far[0].shape
    peers = 2 * len(far)
    padded, width = table_pad.shape
    total = peers * micro * spots
    return pl.pallas_call(
        functools.partial(softmax_kernel, rows),
        out_shape=[
            jax.ShapeDtypeStruct((total, width), jnp.float32),
            jax.ShapeDtypeStruct((8, total), jnp.float32),
            jax.ShapeDtypeStruct((total, 128), jnp.float32),
        ],
        grid_spec=pltpu.PrefetchScalarGridSpec(
            num_scalar_prefetch=1,
            grid=(total // SCORE_TILE,),
            in_specs=[
                *[pl.BlockSpec((micro, side_width, spots), lambda i, w: (0, 0, 0))] * len(far),
                pl.BlockSpec((len(far), micro, side_width, spots), lambda i, w: (0, 0, 0, 0)),
                pl.BlockSpec(letters.shape, lambda i, w: (0, 0)),
                pl.BlockSpec((padded, 2 * SIDE), lambda i, w: (0, 0)),
                pl.BlockSpec((padded, width), lambda i, w: (0, 0)),
            ],
            out_specs=[
                pl.BlockSpec((SCORE_TILE, width), lambda i, w: (in_use(SCORE_TILE, i, w), 0)),
                pl.BlockSpec((8, SCORE_TILE), lambda i, w: (0, in_use(SCORE_TILE, i, w))),
                pl.BlockSpec((SCORE_TILE, 128), lambda i, w: (in_use(SCORE_TILE, i, w), 0)),
            ],
            scratch_shapes=[
                pltpu.VMEM((total + spots, 128), jnp.float32),
                pltpu.VMEM((peers, micro, side_width, spots), jnp.bfloat16),
            ],
        ),
        compiler_params=LIMIT,
        name="softmax_part",
        cost_estimate=cost(22),
    )(where, *far, near, letters, weight, table_pad)


def finish_kernel(micro, where_ref, *refs):
    far_refs = refs[:-11]
    near_ref, mix_ref, goal_ref, packed_ref, up_ref, own_ref, other_ref, up_grad_ref, loss_ref, all_ref, top_ref = refs[-11:]
    step = pl.program_id(0)
    blocks, _, spots = top_ref.shape
    peers = blocks // micro
    tiles = (where_ref[1] + TILE - 1) // TILE

    @pl.when(step == 0)
    def _():
        up_grad_ref[...] = jnp.zeros_like(up_grad_ref)
        loss_ref[...] = jnp.zeros_like(loss_ref)
        all_ref[...] = jnp.zeros_like(all_ref)

    @pl.when(step < tiles)
    def _():
        stats = [(ref[...], near_ref[i]) for i, ref in enumerate(far_refs)]
        stats = [part for pair in stats for part in pair]
        peaks = [part[0:1] for part in stats]
        peak = functools.reduce(jnp.maximum, peaks)
        total = tree_sum([part[1:2] * jnp.exp2(part[0:1] - peak) for part in stats])
        lse = peak + jnp.log2(total)
        rows = jnp.concatenate([jnp.exp2(peaks[0] - lse), lse, jnp.zeros((6, TILE), jnp.float32)], axis=0).T
        heads, lifts, losses = {}, {}, []
        half = TILE // 2

        def valid(part):
            place = lax.broadcasted_iota(jnp.int32, (half, 1), 0) + (step * TILE + part * half)
            return place < where_ref[1]

        def span(part):
            return slice(part * half, (part + 1) * half)

        def picked(part):
            return jnp.where(valid(part), packed_ref[span(part), :SIDE], 0.0).astype(jnp.bfloat16)

        def lift(part):
            heads[part] = dot(picked(part), up_ref[...])

        def scale(part):
            at, here = span(part), valid(part)
            goal = goal_ref[at]
            times = packed_ref[at, SIDE : SIDE + 1]
            lifted = (mix_ref[at] * (rows[at, :1] * times) - goal) * D ** (-0.5)
            lifts[part] = jnp.where(here, lifted, 0.0).astype(jnp.bfloat16)
            aim = jnp.sum(heads.pop(part) * goal, axis=1, keepdims=True) * D ** (-0.5)
            every = jnp.where(where_ref[0] == 0, times * rows[at, 1:2] * (1.0 / LOG2E), 0.0)
            losses.append(jnp.sum(jnp.where(here, every - aim, 0.0), axis=0, keepdims=True))

        def lower(part):
            lifted = lifts.pop(part)
            at = pl.ds(pl.multiple_of(step * TILE + part * half, half), half)
            all_ref[at, :SIDE] = dot_t(lifted, up_ref[...])
            up_grad_ref[...] += dot_l(picked(part), lifted)

        staged(2, (0, lift), (1, scale), (2, lower))
        loss_ref[...] += jnp.broadcast_to(losses[0] + losses[1], loss_ref.shape)

    @pl.when(step == pl.num_programs(0) - 1)
    def _():
        for device in range(peers):
            for index in range(micro):
                block = all_ref[pl.ds(where_ref[2 + device * micro + index], spots)]
                top_ref[(where_ref[0] ^ device) * micro + index] = block.T[:SIDE].astype(jnp.bfloat16)
        for i in range(peers // 2):
            own_ref[i] = top_ref[2 * i * micro : (2 * i + 1) * micro]
            other_ref[i] = top_ref[(2 * i + 1) * micro : (2 * i + 2) * micro]


def head_finish(where, far, near, mix, goals, packed, up_b, micro, spots):
    peers = 2 * len(far)
    total, width = mix.shape
    return pl.pallas_call(
        functools.partial(finish_kernel, micro),
        out_shape=[
            *[jax.ShapeDtypeStruct((len(far), micro, SIDE, spots), jnp.bfloat16)] * 2,
            jax.ShapeDtypeStruct((SIDE, width), jnp.float32),
            jax.ShapeDtypeStruct((8, 128), jnp.float32),
        ],
        grid_spec=pltpu.PrefetchScalarGridSpec(
            num_scalar_prefetch=1,
            grid=(total // TILE,),
            in_specs=[
                *[pl.BlockSpec((2, TILE), lambda i, w: (0, in_use(TILE, i, w)))] * len(far),
                pl.BlockSpec((len(far), 2, TILE), lambda i, w: (0, 0, in_use(TILE, i, w))),
                pl.BlockSpec((TILE, width), lambda i, w: (in_use(TILE, i, w), 0)),
                pl.BlockSpec((TILE, width), lambda i, w: (in_use(TILE, i, w), 0)),
                pl.BlockSpec((TILE, 128), lambda i, w: (in_use(TILE, i, w), 0)),
                pl.BlockSpec((SIDE, width), lambda i, w: (0, 0)),
            ],
            out_specs=[
                *[pl.BlockSpec((len(far), micro, SIDE, spots), lambda i, w: (0, 0, 0, 0))] * 2,
                pl.BlockSpec((SIDE, width), lambda i, w: (0, 0)),
                pl.BlockSpec((8, 128), lambda i, w: (0, 0)),
            ],
            scratch_shapes=[
                pltpu.VMEM((total + spots, 128), jnp.float32),
                pltpu.VMEM((peers * micro, SIDE, spots), jnp.bfloat16),
            ],
        ),
        compiler_params=LIMIT,
        name="head_finish",
        cost_estimate=cost(6),
    )(where, *far, near, mix, goals, packed, up_b)


def after(values, *others):
    return lax.optimization_barrier((values, others))[0]


def pair_lanes(even, odd):
    return jnp.concatenate([even, odd], axis=1)


def flatten_kernel(me_ref, loss_ref, down_ref, in_ref, in_rest_ref, attn_out_ref, ffn_in_ref, ffn_out_ref, up_ref, small_ref, mine_ref, other_ref, turn_ref, out_ref):
    at = 0
    for i in range(4):
        turn_ref[...] = down_ref[i].T
        out_ref[at : at + 256] = pair_lanes(
            turn_ref[pl.ds(0, 256, stride=2)], turn_ref[pl.ds(1, 256, stride=2)]
        )
        at += 256
    half = SIDE // 2
    for i in range(3):
        even = in_ref.at[i][pl.ds(0, half, stride=2)]
        odd = in_ref.at[i][pl.ds(1, half, stride=2)]
        even_rest = in_rest_ref.at[i][pl.ds(0, half, stride=2)]
        odd_rest = in_rest_ref.at[i][pl.ds(1, half, stride=2)]
        out_ref[pl.ds(at, half, stride=3)] = even
        out_ref[pl.ds(at + 1, half, stride=3)] = pair_lanes(even_rest, odd[:, :SIDE])
        out_ref[pl.ds(at + 2, half, stride=3)] = pair_lanes(odd[:, SIDE:], odd_rest)
        at += 3 * half
    for i in range(3):
        out_ref[at : at + half] = pair_lanes(
            attn_out_ref.at[i][pl.ds(0, half, stride=2)], attn_out_ref.at[i][pl.ds(1, half, stride=2)]
        )
        at += half
    for i in range(2):
        for j in range(2):
            out_ref[pl.ds(at + j, SIDE, stride=2)] = ffn_in_ref[i, :, 128 * j : 128 * j + 128]
        at += 2 * SIDE
    for i in range(2):
        out_ref[at : at + 128] = pair_lanes(
            ffn_out_ref.at[i][pl.ds(0, 128, stride=2)], ffn_out_ref.at[i][pl.ds(1, 128, stride=2)]
        )
        at += 128
    for j in range(4):
        out_ref[pl.ds(at + j, SIDE, stride=4)] = up_ref[:, 128 * j : 128 * j + 128]
    at += 4 * SIDE
    turn_ref[:128] = small_ref[...].T
    out_ref[at : at + 8] = pair_lanes(
        turn_ref[pl.ds(0, 8, stride=2)], turn_ref[pl.ds(1, 8, stride=2)]
    )
    at += 8
    out_ref[at:] = jnp.zeros((out_ref.shape[0] - at, 128), jnp.float32)
    lane = lax.broadcasted_iota(jnp.int32, (8, 128), 1) - 3 * me_ref[0]
    loss = loss_ref[...]
    one = rounded(loss)
    two = rounded(loss - one)
    three = rounded(loss - one - two)
    loss = jnp.where(lane == 0, one, jnp.where(lane == 1, two, jnp.where(lane == 2, three, 0.0)))
    out_ref[LOSS_ROW : LOSS_ROW + 8] = loss
    half = mine_ref.shape[0]
    core = me_ref[0] % 2
    mine_ref[...] = out_ref[pl.ds(pl.multiple_of(core * half, 8), half)]
    other_ref[...] = out_ref[pl.ds(pl.multiple_of((1 - core) * half, 8), half)]


FLAT_ROWS = 2208
LOSS_ROW = 2192


def flatten(me, loss, pieces):
    return pl.pallas_call(
        flatten_kernel,
        out_shape=[jax.ShapeDtypeStruct((FLAT_ROWS // 2, 128), jnp.float32)] * 2,
        in_specs=[smem] + [vmem] * 9,
        out_specs=[vmem] * 2,
        scratch_shapes=[
            pltpu.VMEM((512, 64), jnp.float32),
            pltpu.VMEM((FLAT_ROWS, 128), jnp.float32),
        ],
        compiler_params=LIMIT,
        name="flatten",
        cost_estimate=cost(4),
    )(me, loss, *pieces)


MAIN_ROWS = 2176


def rows_of(ref):
    main = 128 * MAIN_ROWS
    one = len(ref.shape) == 2
    load = (lambda a, b: ref[:, a:b]) if one else (lambda a, b: ref[a:b])
    rest = load(main, main + 512).reshape(4, 128)
    last = load(main + 512, main + 576).reshape(1, 64)
    return load(0, main).reshape(MAIN_ROWS, 128), jnp.concatenate(
        [rest, jnp.concatenate([last, jnp.zeros((1, 64), jnp.float32)], axis=1)], axis=0
    )


def put_rows(ref, main_values, rest_values):
    main = 128 * MAIN_ROWS
    if len(ref.shape) == 2:
        ref[:, :main] = main_values.reshape(1, main)
        ref[:, main : main + 512] = rest_values[:4].reshape(1, 512)
        ref[:, main + 512 : main + 576] = rest_values[4:5, :64]
    else:
        ref[:main] = main_values.reshape(main)
        ref[main : main + 512] = rest_values[:4].reshape(512)
        ref[main + 512 : main + 576] = rest_values[4:5, :64].reshape(64)


def stepped(first, second, inner, part):
    new_first = beta_first * first + (1.0 - beta_first) * part
    new_second = beta_second * second + (1.0 - beta_second) * part * part
    fixed_one = new_first / (1.0 - beta_first**STEP)
    fixed_two = new_second / (1.0 - beta_second**STEP)
    new_inner = inner - learn_rate * (
        fixed_one / (jnp.sqrt(fixed_two) + adam_eps) + decay_rate * inner
    )
    return new_first, new_second, new_inner


def gap_kernel(count_at, core_ref, letter_ref, mine_ref, other_ref, first_ref, second_ref, inner_ref, anchor_ref, gap_ref, loss_ref, count_ref, norm_ref, factor_ref):
    half = mine_ref.shape[0]
    core = core_ref[0]
    count = jnp.sum(letter_ref[:, count_at : letter_ref.shape[1] - 128].astype(jnp.float32))
    count_ref[0] = count
    loss_at = LOSS_ROW - half
    mine, other = mine_ref[...], other_ref[...]
    line = lax.broadcasted_iota(jnp.int32, (half, 1), 0)
    lossy = (line >= loss_at) & (line < loss_at + 8)
    late = jnp.where(core == 0, other_ref[loss_at : loss_at + 1], mine_ref[loss_at : loss_at + 1])
    loss_ref[0] = jnp.sum(late)
    mine = jnp.where(lossy & (core == 1), 0.0, mine)
    other = jnp.where(lossy & (core == 0), 0.0, other)
    low, high = jnp.where(core == 0, mine, other), jnp.where(core == 0, other, mine)
    scale = 1.0 / jnp.full((1, 1), count)
    low, high = low * scale, high * scale
    squares = jnp.sum(low * low, axis=0, keepdims=True) + jnp.sum(high * high, axis=0, keepdims=True)
    norm = jnp.sqrt(jnp.sum(squares, axis=1, keepdims=True))
    norm_ref[0] = jnp.sum(norm)
    clip = jnp.minimum(1.0, clip_norm / norm)
    factor_ref[...] = jnp.broadcast_to(jnp.where(lax.broadcasted_iota(jnp.int32, (8, 128), 1) == 0, scale, clip), (8, 128))
    main = 128 * half
    refs = (first_ref, second_ref, inner_ref)

    @pl.when(core == 0)
    def _():
        values = [ref[:, :main].reshape(half, 128) for ref in refs]
        new_inner = stepped(*values, low * clip)[2]
        gap_ref[...] = (anchor_ref[:main].reshape(half, 128) - new_inner).astype(jnp.bfloat16)

    @pl.when(core == 1)
    def _():
        own = MAIN_ROWS - half
        end = 128 * MAIN_ROWS
        part = high * clip
        values = [ref[:, main:end].reshape(own, 128) for ref in refs]
        new_inner = stepped(*values, part[:own])[2]
        gap_ref[:own] = (anchor_ref[main:end].reshape(own, 128) - new_inner).astype(jnp.bfloat16)
        rests = [rest_of(ref) for ref in refs]
        new_inner = stepped(*rests, part[own : own + 8])[2]
        gap_ref[own : own + 8] = (rest_of(anchor_ref) - new_inner).astype(jnp.bfloat16)
        gap_ref[own + 8 :] = jnp.zeros((half - own - 8, 128), jnp.bfloat16)


def rest_of(ref):
    main = 128 * MAIN_ROWS
    load = (lambda a, b: ref[:, a:b]) if len(ref.shape) == 2 else (lambda a, b: ref[a:b])
    last = load(main + 512, main + 576).reshape(1, 64)
    return jnp.concatenate(
        [
            load(main, main + 512).reshape(4, 128),
            jnp.concatenate([last, jnp.zeros((1, 64), jnp.float32)], axis=1),
            jnp.zeros((3, 128), jnp.float32),
        ],
        axis=0,
    )


def gap_part(core, letters, count_at, mine, other, first, second, inner, anchor):
    return pl.pallas_call(
        functools.partial(gap_kernel, count_at),
        out_shape=[
            jax.ShapeDtypeStruct(mine.shape, jnp.bfloat16),
            *[jax.ShapeDtypeStruct((1,), jnp.float32)] * 3,
            jax.ShapeDtypeStruct((8, 128), jnp.float32),
        ],
        in_specs=[smem] + [vmem] * 7,
        out_specs=[vmem] + [smem] * 3 + [vmem],
        compiler_params=LIMIT,
        name="gap",
        cost_estimate=cost(4),
    )(core, letters, mine, other, first, second, inner, anchor)


def adam_kernel(core_ref, factor_ref, mine_ref, other_ref, first_ref, second_ref, inner_ref, new_first_ref, new_second_ref, new_inner_ref, grad_ref):
    half = mine_ref.shape[0]
    core = core_ref[0]
    grad_ref[pl.ds(pl.multiple_of(core * half, 8), half)] = mine_ref[...]
    grad_ref[pl.ds(pl.multiple_of((1 - core) * half, 8), half)] = other_ref[...]
    scale, clip = factor_ref[0:1, 0:1], factor_ref[0:1, 1:2]
    spans = ((0, MAIN_ROWS), (MAIN_ROWS, MAIN_ROWS + 5))
    news = []
    for span, first, second, inner in zip(
        spans, rows_of(first_ref), rows_of(second_ref), rows_of(inner_ref)
    ):
        news.append(stepped(first, second, inner, grad_ref[span[0] : span[1]] * scale * clip))
    for ref, main, rest in zip((new_first_ref, new_second_ref, new_inner_ref), news[0], news[1]):
        put_rows(ref, main, rest)


def adam(core, factor, mine, other, first, second, inner):
    return pl.pallas_call(
        adam_kernel,
        out_shape=[jax.ShapeDtypeStruct(first.shape, jnp.float32)] * 3,
        in_specs=[smem] + [vmem] * 6,
        out_specs=[vmem] * 3,
        scratch_shapes=[pltpu.VMEM((FLAT_ROWS, 128), jnp.float32)],
        compiler_params=LIMIT,
        name="adam",
        cost_estimate=cost(6),
    )(core, factor, mine, other, first, second, inner)


def outer_kernel(core_ref, mine_ref, other_ref, anchor_ref, momentum_ref, delta_ref, new_momentum_ref, new_anchor_ref, full_ref):
    half = mine_ref.shape[0]
    core = core_ref[0]
    full_ref[pl.ds(pl.multiple_of(core * half, 8), half)] = mine_ref[...]
    full_ref[pl.ds(pl.multiple_of((1 - core) * half, 8), half)] = other_ref[...]
    news = []
    for span, anchor, momentum in zip(
        ((0, MAIN_ROWS), (MAIN_ROWS, MAIN_ROWS + 5)), rows_of(anchor_ref), rows_of(momentum_ref)
    ):
        delta = full_ref[span[0] : span[1]]
        new_momentum = outer_beta * momentum + delta
        news.append((delta, new_momentum, anchor - outer_rate * (delta + outer_beta * new_momentum)))
    for ref, main, rest in zip((delta_ref, new_momentum_ref, new_anchor_ref), news[0], news[1]):
        put_rows(ref, main, rest)


def outer(core, mine, other, anchor, momentum):
    flat = jax.ShapeDtypeStruct(anchor.shape, jnp.float32)
    return pl.pallas_call(
        outer_kernel,
        out_shape=[flat] * 3,
        in_specs=[smem] + [vmem] * 4,
        out_specs=[vmem] * 3,
        scratch_shapes=[pltpu.VMEM((FLAT_ROWS, 128), jnp.float32)],
        compiler_params=LIMIT,
        name="outer",
        cost_estimate=cost(5),
    )(core, mine, other, anchor, momentum)


def unpack_kernel(flat_ref, down_ref, in_t_ref, out_t_ref, ffn_in_t_ref, ffn_out_t_ref, in_ref, out_ref, ffn_in_ref, ffn_out_ref, up_ref, small_ref, rows_ref, tall_ref):
    main, rest = rows_of(flat_ref)
    rows_ref[:MAIN_ROWS] = main
    rows_ref[MAIN_ROWS : MAIN_ROWS + 8] = jnp.concatenate([rest, jnp.zeros((3, 128), jnp.float32)], axis=0)

    def natural(at, count):
        packed = rows_ref[at : at + count // 2]
        tall_ref[pl.ds(0, count // 2, stride=2)] = packed[:, :SIDE]
        tall_ref[pl.ds(1, count // 2, stride=2)] = packed[:, SIDE:]
        return tall_ref[:count]

    at = 0
    for i in range(4):
        down_ref[i] = natural(at, 512).T.astype(jnp.bfloat16)
        at += 256
    half = SIDE // 2
    for i in range(3):
        one, two, three = [rows_ref[pl.ds(at + j, half, stride=3)] for j in range(3)]
        tall_ref[pl.ds(0, half, stride=2)] = one[:, :SIDE]
        tall_ref[pl.ds(1, half, stride=2)] = two[:, SIDE:]
        tall_ref[pl.ds(64, half, stride=2)] = one[:, SIDE:]
        tall_ref[pl.ds(65, half, stride=2)] = three[:, :SIDE]
        tall_ref[pl.ds(128, half, stride=2)] = two[:, :SIDE]
        tall_ref[pl.ds(129, half, stride=2)] = three[:, SIDE:]
        columns = [tall_ref[64 * j : 64 * j + 64] for j in range(3)]
        in_ref[i] = jnp.concatenate(columns, axis=1).astype(jnp.bfloat16)
        in_t_ref[i] = jnp.concatenate([column.T for column in columns], axis=0).astype(jnp.bfloat16)
        at += 3 * half
    for i in range(3):
        square = natural(at, SIDE)
        out_ref[i] = square.astype(jnp.bfloat16)
        out_t_ref[i] = square.T.astype(jnp.bfloat16)
        at += half
    for i in range(2):
        wide = jnp.concatenate([rows_ref[pl.ds(at + j, SIDE, stride=2)] for j in range(2)], axis=1)
        ffn_in_ref[i] = wide.astype(jnp.bfloat16)
        ffn_in_t_ref[i] = wide.T.astype(jnp.bfloat16)
        at += 2 * SIDE
    for i in range(2):
        tall = natural(at, 256)
        ffn_out_ref[i] = tall.astype(jnp.bfloat16)
        ffn_out_t_ref[i] = tall.T.astype(jnp.bfloat16)
        at += 128
    up_ref[...] = jnp.concatenate(
        [rows_ref[pl.ds(at + j, SIDE, stride=4)] for j in range(4)], axis=1
    ).astype(jnp.bfloat16)
    at += 4 * SIDE
    tall_ref[:128] = jnp.zeros((128, SIDE), jnp.float32)
    tall = natural(at, 16)
    tall_ref[16:128] = jnp.zeros((112, SIDE), jnp.float32)
    small_ref[...] = tall_ref[:128].T


def unpack_weights(flat):
    bf16 = jnp.bfloat16
    shapes = [
        (4, SIDE, D),
        (3, 3 * SIDE, SIDE),
        (3, SIDE, SIDE),
        (2, SIDE_FF, SIDE),
        (2, SIDE, SIDE_FF),
        (3, SIDE, 3 * SIDE),
        (3, SIDE, SIDE),
        (2, SIDE, SIDE_FF),
        (2, SIDE_FF, SIDE),
        (SIDE, D),
    ]
    return pl.pallas_call(
        unpack_kernel,
        out_shape=[jax.ShapeDtypeStruct(shape, bf16) for shape in shapes]
        + [jax.ShapeDtypeStruct((SIDE, 128), jnp.float32)],
        in_specs=[vmem],
        out_specs=[vmem] * 11,
        scratch_shapes=[
            pltpu.VMEM((MAIN_ROWS + 8, 128), jnp.float32),
            pltpu.VMEM((512, SIDE), jnp.float32),
        ],
        compiler_params=LIMIT,
        name="unpack",
        cost_estimate=cost(8),
    )(flat)


def per_device(
    source_ids,
    target_inputs,
    lengths,
    positions,
    target_ids,
    target_mask,
    table,
    backbone_attn,
    backbone_ffn_in,
    backbone_ffn_out,
    backbone_gains,
    inner_weights,
    first_moment,
    second_moment,
    anchor,
    outer_momentum,
):
    micro = source_ids.shape[0]
    src_tokens = source_ids.shape[2]
    tgt_tokens = target_inputs.shape[2]
    size = lax.axis_size("dp")
    me = lax.axis_index("dp")
    core = me & 1
    rows = table.shape[0]
    score = [positions, target_ids, target_mask]
    spots = positions.shape[2]
    ids_count = source_ids.size + target_inputs.size
    cap = -(-(ids_count * 5 // (size * 6)) // 16) * 16
    slots, column, near, other, scored = plan(
        me[None], source_ids, target_inputs, score, rows, size, cap, tgt_tokens
    )
    asked = ask(near, other)
    found = jnp.take(table, asked[:, :cap].reshape(-1), axis=0, mode="clip")
    most = functools.reduce(jnp.maximum, gather_peers(after(asked, found)[:, -128:], "grp"))
    weights = unpack_weights(after(inner_weights, found, most))
    table_pad, weight = table_parts(after(table, found, most), weights[9])
    most = jnp.max(most[:, 1 + micro])
    goals, where = goal_rows(after(me[None], most), asked, table_pad, micro, spots)
    embed_src, embed_tgt = embed_rows(
        slots,
        column,
        found.reshape(size // 2, 2, cap, -1),
        cap,
        most,
        source_ids,
        target_inputs,
        table,
        (goals, weight, weights[0]),
    )
    down_t, in_t, out_t, ffn_in_t, ffn_out_t, attn_in, attn_out, ffn_in, ffn_out, up_b, small = weights
    ahead = [down_t, in_t, out_t, ffn_in_t, ffn_out_t, small]
    behind = [in_t, ffn_in_t, attn_in, attn_out, ffn_in, ffn_out, small]
    lens = lengths[:, 0]
    encoded = encode(lens, embed_src, backbone_attn, backbone_ffn_in, backbone_ffn_out, backbone_gains)
    decoded = decode(lens, embed_tgt, encoded, backbone_attn, backbone_ffn_in, backbone_ffn_out, backbone_gains)
    picked, *kept = side(lens, embed_src, encoded, embed_tgt, decoded, scored, ahead)
    far, near = gather_all(picked)
    mix, stats, packed = softmax_part(where, far, near, asked, weight, table_pad, rows)
    far, near = gather_all(stats[:2])
    own, other, grad_up, loss_part = head_finish(
        where, far, near, mix, goals, packed, up_b, micro, spots
    )
    tops = add_home(own, other)
    grads = side_back(lens, embed_src, encoded, embed_tgt, decoded, scored, behind, kept, tops)
    mine, other = flatten(me[None], loss_part, [*grads[:6], grad_up, grads[6]])
    sent = (mine + swap(other, "dp", 1)).astype(jnp.bfloat16)
    terms = [sent] + [swap(sent, "dp", s) for s in range(2, size, 2)]
    mine = tree_sum([term.astype(jnp.float32) for term in terms])
    other = swap(mine, "dp", 1)
    gap, loss_total, count_total, norm, factor = gap_part(
        core[None], asked, asked.shape[1] - 128 - micro * spots, mine, other, first_moment, second_moment, inner_weights, anchor
    )
    new_first, new_second, new_inner = adam(
        core[None], factor, mine, other, first_moment, second_moment, inner_weights
    )
    terms = gather_peers(gap, "grp")
    mine = tree_sum([term.astype(jnp.float32) for term in terms]) / lax.axis_size("grp")
    other = swap(after(mine, new_first), "dp", 1)
    delta, momentum, new_anchor = outer(core[None], mine, other, anchor, outer_momentum)
    return (
        loss_total,
        count_total,
        norm,
        new_first,
        new_second,
        new_inner,
        delta,
        momentum,
        new_anchor,
    )


def solution(mesh):
    return jax.shard_map(
        per_device,
        mesh=mesh,
        in_specs=(
            P(None, ("grp", "dp"), None),
            P(None, ("grp", "dp"), None),
            P(None, ("grp", "dp"), None),
            P(None, ("grp", "dp"), None),
            P(None, ("grp", "dp"), None),
            P(None, ("grp", "dp"), None),
            P("dp", None),
            P(),
            P(),
            P(),
            P(),
            P("grp", None),
            P("grp", None),
            P("grp", None),
            P(),
            P(),
        ),
        out_specs=(
            P("grp"),
            P("grp"),
            P("grp"),
            P("grp", None),
            P("grp", None),
            P("grp", None),
            P(),
            P(),
            P(),
        ),
        check_vma=False,
    )
```

```python
import functools

import jax
import jax.numpy as jnp
from jax import lax
from jax.experimental import pallas as pl
from jax.experimental.pallas import tpu as pltpu
from jax.sharding import PartitionSpec as P

D = 512
HEADS = 8
SIDE = 64
SIDE_HEADS = 8
SIDE_FF = 256
STEP = 5


norm_eps = 1e-06
negative = -1000000000.0
beta_first = 0.9
beta_second = 0.99
adam_eps = 1e-08
learn_rate = 0.03
decay_rate = 0.01
clip_norm = 0.01
outer_rate = 0.7
outer_beta = 0.9


LOG2E = 1.4426950408889634
masked = -1e30

def dot(left, right):
    return jnp.dot(left, right, preferred_element_type=jnp.float32)

def dot_t(left, right):
    return lax.dot_general(left, right, (((1,), (1,)), ((), ())), preferred_element_type=jnp.float32)

def rms_rows(values, gain):
    return values * lax.rsqrt(jnp.mean(values * values, axis=1, keepdims=True) + norm_eps) * gain

def gelu(values):
    inner = values * (0.7978845608028654 + 0.035677408136300125 * (values * values))
    return (0.5 * values) * (1.0 + jnp.tanh(inner))

def staged(count, *stages):
    last = max(lag for lag, _ in stages)
    for step in range(count + last):
        for lag, stage in stages:
            if 0 <= step - lag < count:
                stage(step - lag)


def lane_heads(items, causal_bias):
    lane = lax.broadcasted_iota(jnp.int32, (1, 128), 1)
    scale = 0.125 * LOG2E
    scores, peaks, weights, totals, mixed = {}, {}, {}, {}, {}

    def place(step):
        head = step % HEADS
        return items[step // HEADS], head, slice(head // 2 * 128, head // 2 * 128 + 128)

    def score(step):
        (query, keys, _, key_bias), head, span = place(step)
        own = (lane < 64) if head % 2 == 0 else (lane >= 64)
        spare = lane == (64 if head % 2 == 0 else 0)
        q_head = jnp.where(own, query[:, span], spare.astype(jnp.bfloat16))
        k_head = jnp.where(own, keys[:, span], jnp.where(spare, key_bias, jnp.bfloat16(0)))
        part = dot_t(q_head, k_head)
        scores[step] = part if causal_bias is None else part + causal_bias

    def top(step):
        peaks[step] = jnp.max(scores[step], axis=1, keepdims=True)

    def weigh(step):
        weight = jnp.exp2((scores.pop(step) - peaks.pop(step)) * scale)
        totals[step] = jnp.sum(weight, axis=1, keepdims=True)
        weights[step] = weight.astype(jnp.bfloat16)

    def mix(step):
        values, span = place(step)[0][2], place(step)[2]
        mixed[step] = dot(weights.pop(step), values[:, span]) / totals.pop(step)

    staged(len(items) * HEADS, (0, score), (0, top), (1, weigh), (2, mix))
    return [
        jnp.concatenate(
            [
                jnp.where(lane < 64, mixed[at + 2 * pair], mixed[at + 2 * pair + 1]).astype(jnp.bfloat16)
                for pair in range(HEADS // 2)
            ],
            axis=1,
        )
        for at in range(0, len(items) * HEADS, HEADS)
    ]


def bias_column(count, valid):
    place = lax.broadcasted_iota(jnp.int32, (count, 1), 0)
    return jnp.where(place < valid, 0.0, masked).astype(jnp.bfloat16)

def fetch(pairs, sems):
    copies = [pltpu.make_async_copy(src, dst, sems.at[i]) for i, (src, dst) in enumerate(pairs)]
    for copy in copies:
        copy.start()
    return copies

def frozen_ffn(state_ref, out_ref, gain, win_ref, wout_ref, finish):
    tile = 512

    def step(i, carry):
        at = pl.ds(pl.multiple_of(i * tile, tile), tile)
        state = state_ref[at]
        normed = rms_rows(state, gain).astype(jnp.bfloat16)
        hidden, active, kept = {}, {}, {"total": state}

        def widen(part):
            hidden[part] = dot(normed, win_ref[:, part * 512 : (part + 1) * 512])

        def bend(part):
            active[part] = gelu(hidden.pop(part)).astype(jnp.bfloat16)

        def narrow(part):
            kept["total"] = kept["total"] + dot(active.pop(part), wout_ref[part * 512 : (part + 1) * 512])

        staged(win_ref.shape[1] // 512, (0, widen), (1, bend), (2, narrow))
        total = kept["total"]
        out_ref[at] = finish(total).astype(out_ref.dtype)
        return carry

    lax.fori_loop(0, state_ref.shape[0] // tile, step, 0)


def encoder_kernel(
    len_ref, x_ref, gains_ref, attn_hbm, win_hbm, wout_hbm, out_ref, attn_ref, win_ref, wout_ref, qkv_ref, state_ref, sems
):
    first, second, third, fourth = fetch(
        [
            (attn_hbm.at[0, :, : 3 * D], attn_ref.at[:, : 3 * D]),
            (attn_hbm.at[0, :, 3 * D :], attn_ref.at[:, 3 * D :]),
            (win_hbm.at[0], win_ref),
            (wout_hbm.at[0], wout_ref),
        ],
        sems,
    )
    micro = len_ref.shape[0]
    tokens = x_ref.shape[0] // micro
    normed = rms_rows(x_ref[...].astype(jnp.float32), gains_ref[0:1]).astype(jnp.bfloat16)
    first.wait()
    qkv_ref[...] = dot(normed, attn_ref[:, : 3 * D]).astype(jnp.bfloat16)
    second.wait()

    def step(i, carry):
        at = pl.ds(pl.multiple_of(i * tokens, tokens), tokens)
        bias = bias_column(tokens, len_ref[i, 0])
        (mixed,) = lane_heads(
            [(qkv_ref[at, :D], qkv_ref[at, D : 2 * D], qkv_ref[at, 2 * D :], bias)], None
        )
        state_ref[at] = x_ref[at].astype(jnp.float32) + dot(mixed, attn_ref[:, 3 * D :])
        return carry

    lax.fori_loop(0, micro, step, 0)
    third.wait()
    fourth.wait()
    frozen_ffn(
        state_ref, out_ref, gains_ref[1:2], win_ref, wout_ref, lambda v: rms_rows(v, gains_ref[2:3])
    )


def decoder_kernel(
    len_ref, x_ref, encoded_ref, gains_ref, attn_hbm, win_hbm, wout_hbm, out_ref, attn_ref, cross_ref, win_ref, wout_ref, kv_ref, state_ref, sems
):
    first, second, third, fourth = fetch(
        [
            (attn_hbm.at[1], attn_ref),
            (attn_hbm.at[2], cross_ref),
            (win_hbm.at[1], win_ref),
            (wout_hbm.at[1], wout_ref),
        ],
        sems,
    )
    micro = len_ref.shape[0]
    tokens = x_ref.shape[0] // micro
    sources = encoded_ref.shape[0] // micro
    x = x_ref[...].astype(jnp.float32)
    normed = rms_rows(x, gains_ref[3:4]).astype(jnp.bfloat16)
    row = lax.broadcasted_iota(jnp.int32, (tokens, tokens), 0)
    column = lax.broadcasted_iota(jnp.int32, (tokens, tokens), 1)
    causal = jnp.where(column <= row, 0.0, masked)
    first.wait()
    qkv = dot(normed, attn_ref[:, : 3 * D]).astype(jnp.bfloat16)
    items = []
    for i in range(micro):
        own = qkv[i * tokens : (i + 1) * tokens]
        bias = bias_column(tokens, len_ref[i, 1])
        items.append((own[:, :D], own[:, D : 2 * D], own[:, 2 * D :], bias))
    mixed = lane_heads(items, causal)
    state = x + dot(jnp.concatenate(mixed, axis=0), attn_ref[:, 3 * D :])
    second.wait()
    kv_ref[...] = dot(encoded_ref[...], cross_ref[:, D : 3 * D]).astype(jnp.bfloat16)
    normed = rms_rows(state, gains_ref[4:5]).astype(jnp.bfloat16)
    query = dot(normed, cross_ref[:, :D]).astype(jnp.bfloat16)
    items = []
    for i in range(micro):
        at = slice(i * sources, (i + 1) * sources)
        bias = bias_column(sources, len_ref[i, 0])
        items.append((query[i * tokens : (i + 1) * tokens], kv_ref[at, :D], kv_ref[at, D:], bias))
    mixed = lane_heads(items, None)
    state_ref[...] = state + dot(jnp.concatenate(mixed, axis=0), cross_ref[:, 3 * D :])
    third.wait()
    fourth.wait()
    frozen_ffn(state_ref, out_ref, gains_ref[5:6], win_ref, wout_ref, lambda v: v)


def cost(micros):
    return pl.CostEstimate(
        flops=int(micros * 8e8), bytes_accessed=int(micros * 3e6), transcendentals=0
    )


smem = pl.BlockSpec(memory_space=pltpu.SMEM)
vmem = pl.BlockSpec(memory_space=pltpu.VMEM)
hbm = pl.BlockSpec(memory_space=pl.ANY)
LIMIT = pltpu.CompilerParams(vmem_limit_bytes=56 * 2**20)

def encode(lens, x, attn, ffn_in, ffn_out, gains):
    tokens = x.shape[0]
    return pl.pallas_call(
        encoder_kernel,
        out_shape=jax.ShapeDtypeStruct((tokens, D), jnp.bfloat16),
        in_specs=[smem, vmem, vmem, hbm, hbm, hbm],
        out_specs=vmem,
        scratch_shapes=[pltpu.VMEM((D, 4 * D), jnp.bfloat16), pltpu.VMEM((D, 4 * D), jnp.bfloat16), pltpu.VMEM((4 * D, D), jnp.bfloat16),
            pltpu.VMEM((tokens, 3 * D), jnp.bfloat16), pltpu.VMEM((tokens, D), jnp.float32), pltpu.SemaphoreType.DMA((4,))],
        compiler_params=LIMIT,
        name="encoder",
        cost_estimate=cost(14),
    )(lens, x, gains, attn, ffn_in, ffn_out)

def decode(lens, x, encoded, attn, ffn_in, ffn_out, gains):
    tokens = x.shape[0]
    sources = encoded.shape[0]
    return pl.pallas_call(
        decoder_kernel,
        out_shape=jax.ShapeDtypeStruct((tokens, D), jnp.bfloat16),
        in_specs=[smem, vmem, vmem, vmem, hbm, hbm, hbm],
        out_specs=vmem,
        scratch_shapes=[pltpu.VMEM((D, 4 * D), jnp.bfloat16), pltpu.VMEM((D, 4 * D), jnp.bfloat16), pltpu.VMEM((D, 4 * D), jnp.bfloat16), pltpu.VMEM((4 * D, D), jnp.bfloat16),
            pltpu.VMEM((sources, 2 * D), jnp.bfloat16), pltpu.VMEM((tokens, D), jnp.float32), pltpu.SemaphoreType.DMA((4,))],
        compiler_params=LIMIT,
        name="decoder",
        cost_estimate=cost(10.5),
    )(lens, x, encoded, gains, attn, ffn_in, ffn_out)

def dot_l(left, right):
    return lax.dot_general(left, right, (((0,), (0,)), ((), ())), preferred_element_type=jnp.float32)

def rms_columns(values, gain):
    return values * lax.rsqrt(jnp.mean(values * values, axis=0, keepdims=True) + norm_eps) * gain

def rms_columns_back(values, gain, grad):
    inverse = lax.rsqrt(jnp.mean(values * values, axis=0, keepdims=True) + norm_eps)
    gained = grad * gain
    along = jnp.mean(values * gained, axis=0, keepdims=True)
    gain_grad = jnp.sum(grad * (values * inverse), axis=1, keepdims=True)
    return inverse * gained - values * (inverse * inverse * inverse * along), gain_grad

def gelu_back(values, grad):
    square = values * values
    tanh = jnp.tanh(values * (0.7978845608028654 + 0.035677408136300125 * square))
    slope = 0.5 * (1.0 + tanh) + (0.5 * values) * (1.0 - tanh * tanh) * (0.7978845608028654 + 0.107032224408900375 * square)
    return grad * slope

side_scale = (SIDE // SIDE_HEADS) ** -0.5

def keys_with_bias(keys_t, valid):
    count = keys_t.shape[1]
    place = lax.broadcasted_iota(jnp.int32, (64, count), 1)
    line = lax.broadcasted_iota(jnp.int32, (64, count), 0)
    bias = jnp.where((line == 0) & (place >= valid), masked, 0.0)
    return jnp.concatenate([keys_t.astype(jnp.float32), bias], axis=0).T.astype(jnp.bfloat16)

def head_query(query_t, head):
    line = lax.broadcasted_iota(jnp.int32, (64, 1), 0)
    own = jnp.where(line // 8 == head, query_t, 0.0)
    ones = jnp.broadcast_to(jnp.where(line == 0, 1.0, 0.0), own.shape)
    return jnp.concatenate([own, ones], axis=0).astype(jnp.bfloat16)

def rounded(values):
    return values.astype(jnp.bfloat16).astype(jnp.float32)

def causal_columns(count):
    key = lax.broadcasted_iota(jnp.int32, (count, count), 0)
    query = lax.broadcasted_iota(jnp.int32, (count, count), 1)
    return jnp.where(key <= query, 0.0, masked)

def head_steps(keys, block):
    count = keys[0].shape[0]
    chunk = min(block, count)
    parts = count // chunk

    def place(step):
        head = step // parts
        return head, head // SIDE_HEADS, head % SIDE_HEADS, slice(step % parts * chunk, step % parts * chunk + chunk)

    return parts, place


def side_heads(items, causal):
    keys = [keys_with_bias(item[1], item[3]) for item in items]
    parts, place = head_steps(keys, 512)
    scores, tops, weights, peaks, totals, mixed, queries = {}, {}, {}, {}, {}, {}, {}

    def score(step):
        unit, pair, head, span = place(step)
        if step % parts == 0:
            queries[unit] = head_query(items[pair][0], head)
        part = dot(keys[pair][span], queries[unit])
        scores[step] = part if causal is None else part + causal[span]

    def top(step):
        tops[step] = jnp.max(scores[step], axis=0, keepdims=True)

    def weigh(step):
        unit = place(step)[0]
        if step % parts == 0:
            peaks[unit] = functools.reduce(jnp.maximum, [tops.pop(step + i) for i in range(parts)])
        weight = jnp.exp2((scores.pop(step) - peaks[unit]) * (side_scale * LOG2E))
        amount = jnp.sum(weight, axis=0, keepdims=True)
        totals[unit] = totals[unit] + amount if unit in totals else amount
        weights[step] = weight.astype(jnp.bfloat16)

    def mix(step):
        unit, pair, head, span = place(step)
        values = items[pair][2][8 * head : 8 * head + 8, span].astype(jnp.bfloat16)
        piece = dot(values, weights.pop(step))
        mixed[unit] = mixed[unit] + piece if unit in mixed else piece

    staged(len(items) * SIDE_HEADS * parts, (0, score), (1, top), (parts, weigh), (parts + 2, mix))
    result = []
    for pair in range(len(items)):
        units = range(pair * SIDE_HEADS, (pair + 1) * SIDE_HEADS)
        outs = jnp.concatenate([mixed[unit] / totals[unit] for unit in units], axis=0)
        sums = [peaks[unit] * (side_scale * LOG2E) + jnp.log2(totals[unit]) for unit in units]
        result.append((outs, jnp.concatenate(sums, axis=0)))
    return result


def side_heads_back(items, causal):
    keys = [keys_with_bias(item[1], item[3]) for item in items]
    values = [item[2].T.astype(jnp.bfloat16) for item in items]
    parts, place = head_steps(keys, 256)
    line = lax.broadcasted_iota(jnp.int32, (64, 1), 0)
    scores, grads, weights, along, queries, owns = {}, {}, {}, {}, {}, {}
    grad_q, grad_k, grad_v = {}, {}, {}

    def score(step):
        unit, pair, head, span = place(step)
        if step % parts == 0:
            queries[unit] = head_query(items[pair][0], head)
            owns[unit] = jnp.where(line // 8 == head, items[pair][5], 0.0).astype(jnp.bfloat16)
        part = dot(keys[pair][span], queries[unit])
        scores[step] = part if causal is None else part + causal[span]
        grads[step] = dot(values[pair][span], owns[unit])

    def weigh(step):
        unit, pair, head, _ = place(step)
        sums = items[pair][4][head : head + 1]
        weight = jnp.exp2(scores.pop(step) * (side_scale * LOG2E) - sums)
        grads[step] = rounded(grads[step])
        part = jnp.sum(grads[step] * weight, axis=0, keepdims=True)
        along[unit] = along[unit] + part if unit in along else part
        weights[step] = weight

    def finish(step):
        unit, pair, head, span = place(step)
        rows = slice(8 * head, 8 * head + 8)
        query, key, _, _, _, grad = items[pair]
        weight = weights.pop(step)
        grad_s = (weight * (grads.pop(step) - along[unit])).astype(jnp.bfloat16)
        part = dot(key[rows, span].astype(jnp.bfloat16), grad_s)
        grad_q[unit] = grad_q[unit] + part if unit in grad_q else part
        grad_k[step] = dot_t(query[rows].astype(jnp.bfloat16), grad_s)
        grad_v[step] = dot_t(grad[rows].astype(jnp.bfloat16), weight.astype(jnp.bfloat16))

    staged(len(items) * SIDE_HEADS * parts, (0, score), (2, weigh), (parts + 2, finish))

    def joined(pieces, units):
        rows = [
            jnp.concatenate([pieces[unit * parts + i] for i in range(parts)], axis=1) for unit in units
        ]
        return jnp.concatenate(rows, axis=0)

    result = []
    for pair in range(len(items)):
        units = range(pair * SIDE_HEADS, (pair + 1) * SIDE_HEADS)
        whole_q = jnp.concatenate([grad_q[unit] for unit in units], axis=0)
        result.append((whole_q * side_scale, joined(grad_k, units) * side_scale, joined(grad_v, units)))
    return result


def chosen_columns(tokens, positions):
    token = lax.broadcasted_iota(jnp.int32, (tokens, positions.shape[1]), 0)
    return jnp.where(token == positions, 1.0, 0.0).astype(jnp.bfloat16)

def side_kernel(len_ref, src_ref, encoded_ref, tgt_ref, decoded_ref, positions_ref, down_ref, attn_in_ref, attn_out_ref, ffn_in_ref, ffn_out_ref, small_ref,
                picked_ref, enc_ref, dec_ref, enc_mixed_ref, self_mixed_ref, cross_mixed_ref, enc_sums_ref, self_sums_ref, cross_sums_ref):
    micro = len_ref.shape[0]

    def gain(i):
        return small_ref[:, i:i + 1]

    def attend(which, query_n, key_n, side_of, causal, mixed_ref, sums_ref):
        query = rounded(dot(attn_in_ref[which, :64], query_n))
        keyval = rounded(dot(attn_in_ref[which, 64:], key_n))
        width, far = query.shape[1] // micro, keyval.shape[1] // micro
        spans = [
            (slice(i * width, (i + 1) * width), slice(i * far, (i + 1) * far)) for i in range(micro)
        ]
        items = [
            (query[:, near], keyval[:64, away], keyval[64:, away], len_ref[i, side_of])
            for i, (near, away) in enumerate(spans)
        ]
        parts = []
        for (near, _), (mixed, sums) in zip(spans, side_heads(items, causal)):
            sums_ref[:, near] = sums
            parts.append(mixed.astype(jnp.bfloat16))
        mixed_b = jnp.concatenate(parts, axis=1)
        mixed_ref[...] = mixed_b
        return dot(attn_out_ref[which], mixed_b)

    def ffn(which, normed):
        active = gelu(dot(ffn_in_ref[which], normed)).astype(jnp.bfloat16)
        return dot(ffn_out_ref[which], active)

    def norm(values, i):
        return rms_columns(values, gain(i)).astype(jnp.bfloat16)

    state = dot_t(down_ref[0], src_ref[...])
    enc_ref[0] = state
    normed = norm(state, 0)
    flow = dot_t(down_ref[2], tgt_ref[...])
    dec_ref[0] = flow
    normed_flow = norm(flow, 3)
    tokens = flow.shape[1] // micro
    causal = causal_columns(tokens)
    state = state + attend(0, normed, normed, 0, None, enc_mixed_ref, enc_sums_ref)
    enc_ref[1] = state
    flow = flow + attend(1, normed_flow, normed_flow, 1, causal, self_mixed_ref, self_sums_ref)
    dec_ref[1] = flow
    state = state + ffn(0, norm(state, 1))
    enc_ref[2] = state
    joined = dot_t(down_ref[1], encoded_ref[...])
    enc_ref[3] = joined
    gate = jax.nn.sigmoid(gain(7))
    memory = norm(gate * joined + (1.0 - gate) * state, 2)
    flow = flow + attend(2, norm(flow, 4), memory, 0, None, cross_mixed_ref, cross_sums_ref)
    dec_ref[2] = flow
    flow = flow + ffn(1, norm(flow, 5))
    dec_ref[3] = flow
    joined = dot_t(down_ref[3], decoded_ref[...])
    dec_ref[4] = joined
    gate = jax.nn.sigmoid(gain(8))
    top = norm(gate * joined + (1.0 - gate) * flow, 6)
    for i in range(micro):
        chosen = chosen_columns(tokens, positions_ref[i : i + 1])
        picked_ref[i] = dot(top[:, i * tokens : (i + 1) * tokens], chosen).astype(jnp.bfloat16)


def side(lens, src, encoded, tgt, decoded, positions, weights):
    s, t = src.shape[0], tgt.shape[0]
    m, p = positions.shape
    f32, bf16 = jnp.float32, jnp.bfloat16
    shapes = [((m, 64, p), bf16), ((4, 64, s), f32), ((5, 64, t), f32), ((64, s), bf16), ((64, t), bf16), ((64, t), bf16), ((8, s), f32), ((8, t), f32), ((8, t), f32)]
    return pl.pallas_call(
        side_kernel,
        out_shape=[jax.ShapeDtypeStruct(*item) for item in shapes],
        in_specs=[smem] + [vmem] * 11,
        out_specs=[vmem] * 9,
        compiler_params=LIMIT,
        name="side",
        cost_estimate=cost(24),
    )(lens, src, encoded, tgt, decoded, positions, *weights)

def back_kernel(*refs):
    (len_ref, src_ref, encoded_ref, tgt_ref, decoded_ref, positions_ref, attn_in_t_ref, ffn_in_t_ref, attn_in_ref, attn_out_ref, ffn_in_ref, ffn_out_ref, small_ref,
     enc_ref, dec_ref, enc_mixed_ref, self_mixed_ref, cross_mixed_ref, enc_sums_ref, self_sums_ref, cross_sums_ref) = refs[:21]
    parts_refs = refs[21:-7]
    down_out, attn_in_out, in_rest_out, attn_out_out, ffn_in_out, ffn_out_out, small_out = refs[-7:]
    outs = {
        "down": down_out,
        "attn_in": attn_in_out,
        "in_rest": in_rest_out,
        "attn_out": attn_out_out,
        "ffn_in": ffn_in_out,
        "ffn_out": ffn_out_out,
    }
    micro = len_ref.shape[0]

    def put(which, index, values):
        if values.shape[1] == 3 * SIDE:
            put("in_rest", index, values[:, 128:])
            values = values[:, :128]
        outs[which][index] = values

    smalls = {}

    def gain(i):
        return small_ref[:, i:i + 1]

    def norm(values, i):
        return rms_columns(values, gain(i)).astype(jnp.bfloat16)

    def norm_back(values, i, grad):
        result, smalls[i] = rms_columns_back(values, gain(i), grad)
        return result

    def blend_back(i, joined, late, grad):
        gate = jax.nn.sigmoid(gain(i))
        smalls[i] = jnp.sum(grad * (joined - late), axis=1, keepdims=True) * (gate * (1.0 - gate))
        return gate * grad, (1.0 - gate) * grad

    def ffn_back(which, normed, grad):
        grad_b = grad.astype(jnp.bfloat16)
        hidden = dot(ffn_in_t_ref[which], normed)
        active = gelu(hidden).astype(jnp.bfloat16)
        put("ffn_out", which, dot_t(active, grad_b))
        grad_hidden = gelu_back(hidden, dot(ffn_out_ref[which], grad_b)).astype(jnp.bfloat16)
        put("ffn_in", which, dot_t(normed, grad_hidden))
        return dot(ffn_in_ref[which], grad_hidden)

    def attend_back(which, query_n, key_n, mixed_ref, sums_ref, grad, side_of, causal):
        grad_b = grad.astype(jnp.bfloat16)
        put("attn_out", which, dot_t(mixed_ref[...], grad_b))
        grad_mixed = rounded(dot(attn_out_ref[which], grad_b))
        query = rounded(dot(attn_in_t_ref[which, :64], query_n))
        keyval = rounded(dot(attn_in_t_ref[which, 64:], key_n))
        width, far = query.shape[1] // micro, keyval.shape[1] // micro
        items = []
        for i in range(micro):
            near, away = slice(i * width, (i + 1) * width), slice(i * far, (i + 1) * far)
            items.append(
                (query[:, near], keyval[:64, away], keyval[64:, away], len_ref[i, side_of], sums_ref[:, near], grad_mixed[:, near])
            )
        grads_q, grads_kv = [], []
        for grad_q, grad_k, grad_v in side_heads_back(items, causal):
            grads_q.append(grad_q.astype(jnp.bfloat16))
            grads_kv.append(jnp.concatenate([grad_k, grad_v], axis=0).astype(jnp.bfloat16))
        return jnp.concatenate(grads_q, axis=1), jnp.concatenate(grads_kv, axis=1)

    tokens = tgt_ref.shape[0] // micro
    grads = []
    for index in range(micro):
        grad_picked = tree_sum([ref[index].astype(jnp.float32) for ref in parts_refs])
        chosen = chosen_columns(tokens, positions_ref[index : index + 1])
        high = grad_picked.astype(jnp.bfloat16)
        low = (grad_picked - high.astype(jnp.float32)).astype(jnp.bfloat16)
        grads.append(dot_t(high, chosen) + dot_t(low, chosen))
    grad = jnp.concatenate(grads, axis=1)
    gate = jax.nn.sigmoid(gain(8))
    final = gate * dec_ref[4] + (1.0 - gate) * dec_ref[3]
    grad = norm_back(final, 6, grad)
    grad_joined, grad = blend_back(8, dec_ref[4], dec_ref[3], grad)
    put("down", 3, dot(grad_joined.astype(jnp.bfloat16), decoded_ref[...]))
    grad = grad + norm_back(dec_ref[2], 5, ffn_back(1, norm(dec_ref[2], 5), grad))
    gate = jax.nn.sigmoid(gain(7))
    final = gate * enc_ref[3] + (1.0 - gate) * enc_ref[2]
    memory = norm(final, 2)
    normed = norm(dec_ref[1], 4)
    grad_q, grad_kv = attend_back(2, normed, memory, cross_mixed_ref, cross_sums_ref, grad, 0, None)
    zero_q = jnp.zeros((128, tgt_ref.shape[0]), jnp.bfloat16)
    zero_kv = jnp.zeros((64, src_ref.shape[0]), jnp.bfloat16)
    put("attn_in", 2, dot_t(normed, jnp.concatenate([grad_q, zero_q], axis=0)) + dot_t(memory, jnp.concatenate([zero_kv, grad_kv], axis=0)))
    weight = attn_in_ref[2]
    grad_memory = dot(weight, jnp.concatenate([zero_kv, grad_kv], axis=0))
    grad = grad + norm_back(dec_ref[1], 4, dot(weight, jnp.concatenate([grad_q, zero_q], axis=0)))
    normed = norm(dec_ref[0], 3)
    grad_q, grad_kv = attend_back(1, normed, normed, self_mixed_ref, self_sums_ref, grad, 1, causal_columns(tokens))
    grad_qkv = jnp.concatenate([grad_q, grad_kv], axis=0)
    put("attn_in", 1, dot_t(normed, grad_qkv))
    grad = grad + norm_back(dec_ref[0], 3, dot(attn_in_ref[1], grad_qkv))
    put("down", 2, dot(grad.astype(jnp.bfloat16), tgt_ref[...]))
    grad = norm_back(final, 2, grad_memory)
    grad_joined, grad = blend_back(7, enc_ref[3], enc_ref[2], grad)
    put("down", 1, dot(grad_joined.astype(jnp.bfloat16), encoded_ref[...]))
    grad = grad + norm_back(enc_ref[1], 1, ffn_back(0, norm(enc_ref[1], 1), grad))
    normed = norm(enc_ref[0], 0)
    grad_q, grad_kv = attend_back(0, normed, normed, enc_mixed_ref, enc_sums_ref, grad, 0, None)
    grad_qkv = jnp.concatenate([grad_q, grad_kv], axis=0)
    put("attn_in", 0, dot_t(normed, grad_qkv))
    grad = grad + norm_back(enc_ref[0], 0, dot(attn_in_ref[0], grad_qkv))
    put("down", 0, dot(grad.astype(jnp.bfloat16), src_ref[...]))
    lane = lax.broadcasted_iota(jnp.int32, (1, 128), 1)
    total = jnp.zeros((64, 128), jnp.float32)
    for i in range(9):
        total = total + jnp.where(lane == i, smalls[i], 0.0)
    small_out[...] = total

def side_back(lens, src, encoded, tgt, decoded, positions, weights, kept, parts):
    f32 = jnp.float32
    shapes = [(4, 64, 512), (3, 64, 128), (3, 64, 64), (3, 64, 64), (2, 64, 256), (2, 256, 64), (64, 128)]
    return pl.pallas_call(
        back_kernel,
        out_shape=[jax.ShapeDtypeStruct(shape, f32) for shape in shapes],
        in_specs=[smem] + [vmem] * (20 + len(parts)),
        out_specs=[vmem] * 7,
        compiler_params=LIMIT,
        name="side_back",
        cost_estimate=cost(34),
    )(lens, src, encoded, tgt, decoded, positions, *weights, *kept, *parts)


def swap(values, axis, distance):
    size = lax.axis_size(axis)
    return lax.ppermute(values, axis, [(i, i ^ distance) for i in range(size)])


def gather_peers(values, axis):
    return [values] + [swap(values, axis, s) for s in range(1, lax.axis_size(axis))]


def tree_sum(terms):
    while len(terms) > 1:
        terms = [terms[i] + terms[i + 1] for i in range(0, len(terms), 2)]
    return terms[0]


def owners_of(ids, rows, peers, me):
    owner = jnp.zeros(ids.shape, jnp.int32)
    for peer in range(1, peers):
        owner = owner + jnp.where(ids >= peer * rows, 1, 0)
    return owner ^ me


def ranks_within(own):
    peers, count = own.shape
    own_b = own.astype(jnp.bfloat16)
    before = jnp.where(
        lax.broadcasted_iota(jnp.int32, (128, 128), 0)
        < lax.broadcasted_iota(jnp.int32, (128, 128), 1),
        1.0,
        0.0,
    ).astype(jnp.bfloat16)
    seen = jnp.zeros((peers, 1), jnp.float32)
    ranks = []
    for start in range(0, count, 128):
        block = slice(start, start + 128)
        inside = dot(own_b[:, block], before) + seen
        ranks.append(jnp.sum(own[:, block] * (inside + 1.0), axis=0, keepdims=True) - 1.0)
        seen = seen + jnp.sum(own[:, block], axis=1, keepdims=True)
    return jnp.concatenate(ranks, axis=1), seen


def column_of(row):
    return jnp.broadcast_to(row, (8, row.shape[1])).T[:, :1]


def placed(own, values, hit):
    high = jnp.floor(values * (1.0 / 64.0))
    low = values - 64.0 * high
    return 64.0 * dot((own * high).astype(jnp.bfloat16), hit) + dot(
        (own * low).astype(jnp.bfloat16), hit
    )


def score_part(rows, peers, tokens, me, busy, at_ref, goal_ref, mask_ref, token_ref, letter_ref, at):
    micro, _, spots = at_ref.shape
    token = lax.broadcasted_iota(jnp.int32, (tokens, 1), 0)
    token_f = token.astype(jnp.float32)
    spot_f = lax.broadcasted_iota(jnp.int32, (1, spots), 1).astype(jnp.float32)
    lower = jnp.where(
        lax.broadcasted_iota(jnp.int32, (tokens, tokens), 0)
        > lax.broadcasted_iota(jnp.int32, (tokens, tokens), 1),
        1.0,
        0.0,
    ).astype(jnp.bfloat16)
    goals, masks, slots, used = [], [], [], []
    for index in range(micro):
        mask = mask_ref[index].astype(jnp.float32)
        met = jnp.where(token == at_ref[index], mask, 0.0)
        times = jnp.sum(met, axis=1, keepdims=True)
        active = jnp.where(times > 0.0, 1.0, 0.0)
        wide = jnp.broadcast_to(active, (tokens, 128)).astype(jnp.bfloat16)
        slot = dot(lower, wide)[:, :1]
        here = jnp.where(slot == spot_f, active, 0.0)
        token_row = jnp.sum(here * (token_f + 1.0), axis=0, keepdims=True) - 1.0
        token_ref[index : index + 1] = token_row.astype(jnp.int32)
        count = jnp.sum(here * times, axis=0, keepdims=True).astype(jnp.int32)
        first = at + (micro + index) * spots
        letter_ref[:, first : first + spots] = jnp.broadcast_to(count, (peers, spots))
        slots.append(jnp.sum(met * slot, axis=0, keepdims=True) + float(index * spots))
        goals.append(goal_ref[index])
        masks.append(mask)
        used.append(jnp.sum(active, axis=0, keepdims=True))
    goal, mask, slot = [jnp.concatenate(rows_, axis=1) for rows_ in (goals, masks, slots)]
    far = owners_of(goal, rows, peers, 0)
    local = (goal - far * rows).astype(jnp.float32)
    line = lax.broadcasted_iota(jnp.int32, (peers, goal.shape[1]), 0)
    own = jnp.where((line == (far ^ me)) & (mask > 0.0), 1.0, 0.0)
    rank, many = ranks_within(own)
    order = lax.broadcasted_iota(jnp.int32, (1, goal.shape[1]), 1).astype(jnp.float32)
    hit = jnp.where(column_of(rank) == order, 1.0, 0.0).astype(jnp.bfloat16)
    letter_ref[:, at : at + micro * spots] = placed(own, slot, hit).astype(
        jnp.int32
    ) * 65536 + placed(own, local, hit).astype(jnp.int32)
    lane = lax.broadcasted_iota(jnp.int32, (peers, 128), 1)
    info = jnp.where(lane == 0, many, jnp.where(lane == micro + 1, busy, 0.0))
    for index in range(micro):
        info = jnp.where(lane == index + 1, used[index], info)
    first = at + 2 * micro * spots
    letter_ref[:, first : first + 128] = info.astype(jnp.int32)


def plan_kernel(rows, peers, cap, tokens, me_ref, src_ref, tgt_ref, *refs):
    score_refs, (slots_ref, column_ref, near_ref, other_ref, token_ref, letter_ref) = refs[:3], refs[3:]
    ids_row = jnp.concatenate(
        [ref[index] for ref in (src_ref, tgt_ref) for index in range(ref.shape[0])], axis=1
    )
    count = ids_row.shape[1]
    ids = ids_row.astype(jnp.float32)
    column = column_of(ids)
    column_ref[...] = column
    first_at = jnp.full((1, count), float(count), jnp.float32)
    for start in range(0, count, 256):
        place = (lax.broadcasted_iota(jnp.int32, (256, 1), 0) + start).astype(jnp.float32)
        same = column[start : start + 256] == ids
        first_at = jnp.minimum(
            first_at, jnp.min(jnp.where(same, place, float(count)), axis=0, keepdims=True)
        )
    first = first_at == lax.broadcasted_iota(jnp.int32, (1, count), 1).astype(jnp.float32)
    far = owners_of(ids_row, rows, peers, 0)
    line = lax.broadcasted_iota(jnp.int32, (peers, count), 0)
    own = jnp.where((line == (far ^ me_ref[0])) & first, 1.0, 0.0)
    rank, seen = ranks_within(own)
    width = -(-cap // 128) * 128
    spot = lax.broadcasted_iota(jnp.int32, (1, width), 1).astype(jnp.float32)
    hit = jnp.where(column_of(rank) == spot, 1.0, 0.0).astype(jnp.bfloat16)
    filled = dot(own.astype(jnp.bfloat16), hit)
    local = placed(own, (ids_row - far * rows).astype(jnp.float32), hit).astype(jnp.int32)
    letter_ref[:, :width] = local
    owner = lax.broadcasted_iota(jnp.int32, (peers, 1), 0) ^ me_ref[0]
    slots = jnp.where(filled > 0.5, local + owner * rows, -1)[:, :cap]
    for part in range(2):
        slots_ref[part : part + 1] = jnp.concatenate(
            [slots[peer : peer + 1] for peer in range(part, peers, 2)], axis=1
        )
    busy = jnp.max(seen, axis=0, keepdims=True)
    score_part(rows, peers, tokens, me_ref[0], busy, *score_refs, token_ref, letter_ref, width)
    for peer in range(peers):
        letter = near_ref if peer % 2 == 0 else other_ref
        letter[peer // 2 : peer // 2 + 1] = letter_ref[peer : peer + 1]


def plan(me, source, target, score, rows, peers, cap, tokens):
    count = source.shape[0] * source.shape[2] + target.shape[0] * target.shape[2]
    micro, _, spots = score[0].shape
    letter = -(-cap // 128) * 128 + 2 * micro * spots + 128
    shapes = [
        ((2, peers // 2 * cap), jnp.int32),
        ((count, 1), jnp.float32),
        ((peers // 2, letter), jnp.int32),
        ((peers // 2, letter), jnp.int32),
        ((micro, spots), jnp.int32),
    ]
    return pl.pallas_call(
        functools.partial(plan_kernel, rows, peers, cap, tokens),
        out_shape=[jax.ShapeDtypeStruct(*shape) for shape in shapes],
        in_specs=[smem] + [vmem] * 5,
        out_specs=[vmem] * len(shapes),
        scratch_shapes=[pltpu.VMEM((peers, letter), jnp.int32)],
        compiler_params=LIMIT,
        name="plan",
        cost_estimate=cost(4),
    )(me, source, target, *score)


def expand_kernel(sizes, slots_ref, column_ref, *refs):
    far_refs, near_ref, out_refs = refs[: -1 - len(sizes)], refs[-1 - len(sizes)], refs[-len(sizes) :]
    slots = slots_ref[...].astype(jnp.float32)
    rows = (jnp.concatenate([ref[0] for ref in far_refs], axis=0), near_ref[...])
    blocks, base = [], 0
    for out in out_refs:
        blocks += [(out, start, base + start) for start in range(0, out.shape[0], 256)]
        base = base + out.shape[0]
    picks = {}

    def match(step):
        column = column_ref[blocks[step][2] : blocks[step][2] + 256]
        picks[step] = [
            jnp.where(column == slots[i : i + 1], 1.0, 0.0).astype(jnp.bfloat16) for i in range(2)
        ]

    def fill(step):
        first, second = [dot(pick, rows[i]) for i, pick in enumerate(picks.pop(step))]
        out, start, _ = blocks[step]
        out[start : start + 256] = (first + second).astype(jnp.bfloat16)

    staged(len(blocks), (0, match), (1, fill))


def expand(slots, column, far, near, sizes):
    width = near.shape[1]
    return pl.pallas_call(
        functools.partial(expand_kernel, sizes),
        out_shape=[jax.ShapeDtypeStruct((size, width), jnp.bfloat16) for size in sizes],
        in_specs=[vmem] * (3 + len(far)),
        out_specs=[vmem] * len(sizes),
        compiler_params=LIMIT,
        name="expand",
        cost_estimate=cost(3.8),
    )(slots, column, *far, near)


def ask(near, other):
    count = near.shape[0]
    pairs = jnp.stack([near, swap(other, "dp", 1)], axis=1)
    far = [pairs[:1]] + [swap(pairs[i : i + 1], "dp", 2 * i) for i in range(1, count)]
    return jnp.concatenate(far).reshape(2 * count, -1)


def send_rows(slots, column, found, sizes, between):
    count = found.shape[0]
    far = [found[0]] + [swap(found[i], "dp", 2 * i) for i in range(1, count)]
    other = jnp.concatenate([part[1] for part in far])
    near = swap(after(other, *between), "dp", 1)
    return expand(slots, column, far, near, sizes)


def every_row(ids, table, rows):
    size = lax.axis_size("dp")
    me = lax.axis_index("dp")

    def step(i, carry):
        shard, filled = carry
        local = ids - (me + i) % size * rows
        here = (local >= 0) & (local < rows)
        found = jnp.take(shard, jnp.clip(local, 0, rows - 1), axis=0)
        shard = lax.ppermute(shard, "dp", [((j + 1) % size, j) for j in range(size)])
        return shard, jnp.where(here[:, None], found, filled)

    empty = jnp.zeros((ids.shape[0], table.shape[1]), table.dtype)
    return lax.fori_loop(0, size, step, (table, empty))[1]


def embed_rows(slots, column, found, cap, most, source, target, table, between):
    sizes = [source.size, target.size]
    result = tuple(send_rows(slots, column, found, sizes, between))

    def long_way(carry):
        ids = jnp.concatenate([source.reshape(-1), target.reshape(-1)])
        filled = every_row(ids, table, table.shape[0])
        return (jnp.zeros_like(carry[0]), (filled[: sizes[0]], filled[sizes[0] :]))

    return lax.while_loop(lambda carry: carry[0] > cap, long_way, (most, result))[1]


def gather_all(values):
    far = [values] + [swap(values, "dp", s) for s in range(2, lax.axis_size("dp"), 2)]
    return far, swap(jnp.stack(far), "dp", 1)


def add_home(own, other):
    pair = (own.astype(jnp.float32) + swap(other, "dp", 1).astype(jnp.float32)).astype(own.dtype)
    return [pair[0]] + [swap(pair[i], "dp", 2 * i) for i in range(1, pair.shape[0])]


def table_kernel(rows, table_ref, up_ref, padded_ref, weight_ref):
    block = table_ref.shape[0]
    place = lax.broadcasted_iota(jnp.int32, (block, 1), 0) + pl.program_id(0) * block
    table = jnp.where(place < rows, table_ref[...], jnp.bfloat16(0))
    padded_ref[...] = table
    lifted = dot_t(table, up_ref[...]) * (D ** (-0.5) * LOG2E)
    high = lifted.astype(jnp.bfloat16)
    weight_ref[:, :SIDE] = high
    weight_ref[:, SIDE:] = (lifted - high.astype(jnp.float32)).astype(jnp.bfloat16)


VOCAB_BLOCK = 512
TILE = 512
SCORE_TILE = 256


def table_parts(table, up_b):
    rows, width = table.shape
    padded = -(-rows // VOCAB_BLOCK) * VOCAB_BLOCK
    return pl.pallas_call(
        functools.partial(table_kernel, rows),
        out_shape=[
            jax.ShapeDtypeStruct((padded, width), jnp.bfloat16),
            jax.ShapeDtypeStruct((padded, 2 * SIDE), jnp.bfloat16),
        ],
        grid=(padded // VOCAB_BLOCK,),
        in_specs=[
            pl.BlockSpec((VOCAB_BLOCK, width), lambda i: (i, 0)),
            pl.BlockSpec((SIDE, width), lambda i: (0, 0)),
        ],
        out_specs=[
            pl.BlockSpec((VOCAB_BLOCK, width), lambda i: (i, 0)),
            pl.BlockSpec((VOCAB_BLOCK, 2 * SIDE), lambda i: (i, 0)),
        ],
        compiler_params=LIMIT,
        name="table_parts",
        cost_estimate=cost(5),
    )(table, up_b)


def goals_kernel(spots, micro, me_ref, letter_ref, table_ref, out_ref, where_ref, tall_ref, sum_ref, sem):
    peers, length = letter_ref.shape
    entry_at = length - 128 - 2 * micro * spots
    where_ref[0] = me_ref[0]
    first = jnp.int32(0)
    for device in range(peers):
        for index in range(micro):
            where_ref[2 + device * micro + index] = first
            first = first + letter_ref[me_ref[0] ^ device, length - 128 + 1 + index]
    where_ref[1] = first
    tiles = (first + TILE - 1) // TILE
    for start in range(0, table_ref.shape[0], VOCAB_BLOCK):
        tall_ref[start : start + VOCAB_BLOCK] = table_ref[start : start + VOCAB_BLOCK].astype(jnp.float32)

    def clear(i, carry):
        sum_ref[pl.ds(pl.multiple_of(i * TILE, TILE), TILE)] = jnp.zeros((TILE, sum_ref.shape[1]), jnp.float32)
        return carry

    lax.fori_loop(0, tiles, clear, 0)
    for peer in range(peers):
        base = 2 + (peer ^ where_ref[0]) * micro

        def add(j, carry):
            entry = letter_ref[peer, entry_at + j]
            slot = entry // 65536
            local = entry - slot * 65536
            row = slot + where_ref[base]
            for index in range(1, micro):
                row = jnp.where(slot >= index * spots, slot - index * spots + where_ref[base + index], row)
            sum_ref[pl.ds(row, 1)] = sum_ref[pl.ds(row, 1)] + tall_ref[pl.ds(local, 1)]
            return carry

        lax.fori_loop(0, letter_ref[peer, length - 128], add, 0)

    def send(i, carry):
        at = pl.ds(pl.multiple_of(i * TILE, TILE), TILE)
        copy = pltpu.make_async_copy(sum_ref.at[at], out_ref.at[at], sem)
        copy.start()
        copy.wait()
        return carry

    lax.fori_loop(0, tiles, send, 0)


def goal_rows(me, letters, table_pad, micro, spots):
    total = letters.shape[0] * micro * spots
    padded, width = table_pad.shape
    return pl.pallas_call(
        functools.partial(goals_kernel, spots, micro),
        out_shape=[
            jax.ShapeDtypeStruct((total, width), jnp.float32),
            jax.ShapeDtypeStruct((2 + letters.shape[0] * micro,), jnp.int32),
        ],
        in_specs=[smem, smem, vmem],
        out_specs=[hbm, smem],
        scratch_shapes=[
            pltpu.VMEM((padded, width), jnp.float32),
            pltpu.VMEM((total, width), jnp.float32),
            pltpu.SemaphoreType.DMA,
        ],
        compiler_params=LIMIT,
        name="goals",
        cost_estimate=cost(9),
    )(me, letters, table_pad)


def softmax_kernel(rows, where_ref, *refs):
    far_refs = refs[:-9]
    near_ref, letter_ref, weight_ref, table_ref, mix_ref, stats_ref, packed_ref, all_ref, gathered_ref = refs[-9:]
    step = pl.program_id(0)
    peers, micro, _, spots = gathered_ref.shape
    tiles = (where_ref[1] + SCORE_TILE - 1) // SCORE_TILE
    count_at = letter_ref.shape[1] - 128 - micro * spots

    @pl.when(step == 0)
    def _():
        def clear(i, carry):
            all_ref[pl.ds(pl.multiple_of(i * SCORE_TILE, SCORE_TILE), SCORE_TILE)] = jnp.zeros((SCORE_TILE, 128), jnp.float32)
            return carry

        lax.fori_loop(0, tiles, clear, 0)
        for i, far_ref in enumerate(far_refs):
            gathered_ref[2 * i] = far_ref[...]
            gathered_ref[2 * i + 1] = near_ref[i]
        for device in range(peers):
            for index in range(micro):
                peer = where_ref[0] ^ device
                block = jnp.concatenate(
                    [
                        gathered_ref[peer, index].astype(jnp.float32),
                        letter_ref[
                            pl.ds(peer, 1), count_at + index * spots : count_at + (index + 1) * spots
                        ].astype(jnp.float32),
                        jnp.zeros((SIDE - 1, spots), jnp.float32),
                    ],
                    axis=0,
                )
                all_ref[pl.ds(where_ref[2 + device * micro + index], spots)] = block.T

    @pl.when(step < tiles)
    def _():
        mine = all_ref[pl.ds(pl.multiple_of(step * SCORE_TILE, SCORE_TILE), SCORE_TILE)]
        packed_ref[...] = mine
        picked = jnp.concatenate([mine[:, :SIDE], mine[:, :SIDE]], axis=1).astype(jnp.bfloat16)
        padded = weight_ref.shape[0]
        chunk = min(1024, padded)
        logits, shares = {}, {}
        kept = {"peak": None}

        def score(part):
            start = part * chunk
            values = dot_t(picked, weight_ref[start : start + chunk])
            if start + chunk > rows:
                place = lax.broadcasted_iota(jnp.int32, (1, chunk), 1)
                values = jnp.where(place < rows - start, values, -jnp.inf)
            logits[part] = values

        def weigh(part):
            values = logits.pop(part)
            above = jnp.max(values, axis=1, keepdims=True)
            fade = None
            if part > 0:
                above = jnp.maximum(kept["peak"], above)
                fade = jnp.exp2(kept["peak"] - above)
            share = jnp.exp2(values - above)
            amount = jnp.sum(share, axis=1, keepdims=True)
            kept["total"] = amount if fade is None else kept["total"] * fade + amount
            kept["peak"] = above
            shares[part] = (share.astype(jnp.bfloat16), fade)

        def add(part):
            share, fade = shares.pop(part)
            piece = dot(share, table_ref[part * chunk : (part + 1) * chunk])
            kept["mix"] = piece if fade is None else kept["mix"] * fade + piece

        staged(padded // chunk, (0, score), (1, weigh), (2, add))
        peak, total, mix = kept["peak"], kept["total"], kept["mix"]
        mix_ref[...] = mix
        lane = lax.broadcasted_iota(jnp.int32, (SCORE_TILE, 128), 1)
        stats_ref[...] = jnp.where(lane == 0, peak, jnp.where(lane == 1, total, 0.0)).T[:8]


def in_use(tile, i, where):
    return jnp.minimum(i, (where[1] + tile - 1) // tile - 1)


def softmax_part(where, far, near, letters, weight, table_pad, rows):
    micro, side_width, spots = far[0].shape
    peers = 2 * len(far)
    padded, width = table_pad.shape
    total = peers * micro * spots
    return pl.pallas_call(
        functools.partial(softmax_kernel, rows),
        out_shape=[
            jax.ShapeDtypeStruct((total, width), jnp.float32),
            jax.ShapeDtypeStruct((8, total), jnp.float32),
            jax.ShapeDtypeStruct((total, 128), jnp.float32),
        ],
        grid_spec=pltpu.PrefetchScalarGridSpec(
            num_scalar_prefetch=1,
            grid=(total // SCORE_TILE,),
            in_specs=[
                *[pl.BlockSpec((micro, side_width, spots), lambda i, w: (0, 0, 0))] * len(far),
                pl.BlockSpec((len(far), micro, side_width, spots), lambda i, w: (0, 0, 0, 0)),
                pl.BlockSpec(letters.shape, lambda i, w: (0, 0)),
                pl.BlockSpec((padded, 2 * SIDE), lambda i, w: (0, 0)),
                pl.BlockSpec((padded, width), lambda i, w: (0, 0)),
            ],
            out_specs=[
                pl.BlockSpec((SCORE_TILE, width), lambda i, w: (in_use(SCORE_TILE, i, w), 0)),
                pl.BlockSpec((8, SCORE_TILE), lambda i, w: (0, in_use(SCORE_TILE, i, w))),
                pl.BlockSpec((SCORE_TILE, 128), lambda i, w: (in_use(SCORE_TILE, i, w), 0)),
            ],
            scratch_shapes=[
                pltpu.VMEM((total + spots, 128), jnp.float32),
                pltpu.VMEM((peers, micro, side_width, spots), jnp.bfloat16),
            ],
        ),
        compiler_params=LIMIT,
        name="softmax_part",
        cost_estimate=cost(22),
    )(where, *far, near, letters, weight, table_pad)


def finish_kernel(micro, where_ref, *refs):
    far_refs = refs[:-11]
    near_ref, mix_ref, goal_ref, packed_ref, up_ref, own_ref, other_ref, up_grad_ref, loss_ref, all_ref, top_ref = refs[-11:]
    step = pl.program_id(0)
    blocks, _, spots = top_ref.shape
    peers = blocks // micro
    tiles = (where_ref[1] + TILE - 1) // TILE

    @pl.when(step == 0)
    def _():
        up_grad_ref[...] = jnp.zeros_like(up_grad_ref)
        loss_ref[...] = jnp.zeros_like(loss_ref)
        all_ref[...] = jnp.zeros_like(all_ref)

    @pl.when(step < tiles)
    def _():
        stats = [(ref[...], near_ref[i]) for i, ref in enumerate(far_refs)]
        stats = [part for pair in stats for part in pair]
        peaks = [part[0:1] for part in stats]
        peak = functools.reduce(jnp.maximum, peaks)
        total = tree_sum([part[1:2] * jnp.exp2(part[0:1] - peak) for part in stats])
        lse = peak + jnp.log2(total)
        rows = jnp.concatenate([jnp.exp2(peaks[0] - lse), lse, jnp.zeros((6, TILE), jnp.float32)], axis=0).T
        heads, lifts, losses = {}, {}, []
        half = TILE // 2

        def valid(part):
            place = lax.broadcasted_iota(jnp.int32, (half, 1), 0) + (step * TILE + part * half)
            return place < where_ref[1]

        def span(part):
            return slice(part * half, (part + 1) * half)

        def picked(part):
            return jnp.where(valid(part), packed_ref[span(part), :SIDE], 0.0).astype(jnp.bfloat16)

        def lift(part):
            heads[part] = dot(picked(part), up_ref[...])

        def scale(part):
            at, here = span(part), valid(part)
            goal = goal_ref[at]
            times = packed_ref[at, SIDE : SIDE + 1]
            lifted = (mix_ref[at] * (rows[at, :1] * times) - goal) * D ** (-0.5)
            lifts[part] = jnp.where(here, lifted, 0.0).astype(jnp.bfloat16)
            aim = jnp.sum(heads.pop(part) * goal, axis=1, keepdims=True) * D ** (-0.5)
            every = jnp.where(where_ref[0] == 0, times * rows[at, 1:2] * (1.0 / LOG2E), 0.0)
            losses.append(jnp.sum(jnp.where(here, every - aim, 0.0), axis=0, keepdims=True))

        def lower(part):
            lifted = lifts.pop(part)
            at = pl.ds(pl.multiple_of(step * TILE + part * half, half), half)
            all_ref[at, :SIDE] = dot_t(lifted, up_ref[...])
            up_grad_ref[...] += dot_l(picked(part), lifted)

        staged(2, (0, lift), (1, scale), (2, lower))
        loss_ref[...] += jnp.broadcast_to(losses[0] + losses[1], loss_ref.shape)

    @pl.when(step == pl.num_programs(0) - 1)
    def _():
        for device in range(peers):
            for index in range(micro):
                block = all_ref[pl.ds(where_ref[2 + device * micro + index], spots)]
                top_ref[(where_ref[0] ^ device) * micro + index] = block.T[:SIDE].astype(jnp.bfloat16)
        for i in range(peers // 2):
            own_ref[i] = top_ref[2 * i * micro : (2 * i + 1) * micro]
            other_ref[i] = top_ref[(2 * i + 1) * micro : (2 * i + 2) * micro]


def head_finish(where, far, near, mix, goals, packed, up_b, micro, spots):
    peers = 2 * len(far)
    total, width = mix.shape
    return pl.pallas_call(
        functools.partial(finish_kernel, micro),
        out_shape=[
            *[jax.ShapeDtypeStruct((len(far), micro, SIDE, spots), jnp.bfloat16)] * 2,
            jax.ShapeDtypeStruct((SIDE, width), jnp.float32),
            jax.ShapeDtypeStruct((8, 128), jnp.float32),
        ],
        grid_spec=pltpu.PrefetchScalarGridSpec(
            num_scalar_prefetch=1,
            grid=(total // TILE,),
            in_specs=[
                *[pl.BlockSpec((2, TILE), lambda i, w: (0, in_use(TILE, i, w)))] * len(far),
                pl.BlockSpec((len(far), 2, TILE), lambda i, w: (0, 0, in_use(TILE, i, w))),
                pl.BlockSpec((TILE, width), lambda i, w: (in_use(TILE, i, w), 0)),
                pl.BlockSpec((TILE, width), lambda i, w: (in_use(TILE, i, w), 0)),
                pl.BlockSpec((TILE, 128), lambda i, w: (in_use(TILE, i, w), 0)),
                pl.BlockSpec((SIDE, width), lambda i, w: (0, 0)),
            ],
            out_specs=[
                *[pl.BlockSpec((len(far), micro, SIDE, spots), lambda i, w: (0, 0, 0, 0))] * 2,
                pl.BlockSpec((SIDE, width), lambda i, w: (0, 0)),
                pl.BlockSpec((8, 128), lambda i, w: (0, 0)),
            ],
            scratch_shapes=[
                pltpu.VMEM((total + spots, 128), jnp.float32),
                pltpu.VMEM((peers * micro, SIDE, spots), jnp.bfloat16),
            ],
        ),
        compiler_params=LIMIT,
        name="head_finish",
        cost_estimate=cost(6),
    )(where, *far, near, mix, goals, packed, up_b)


def after(values, *others):
    return lax.optimization_barrier((values, others))[0]


def pair_lanes(even, odd):
    return jnp.concatenate([even, odd], axis=1)


def flatten_kernel(me_ref, loss_ref, down_ref, in_ref, in_rest_ref, attn_out_ref, ffn_in_ref, ffn_out_ref, up_ref, small_ref, mine_ref, other_ref, turn_ref, out_ref):
    at = 0
    for i in range(4):
        turn_ref[...] = down_ref[i].T
        out_ref[at : at + 256] = pair_lanes(
            turn_ref[pl.ds(0, 256, stride=2)], turn_ref[pl.ds(1, 256, stride=2)]
        )
        at += 256
    half = SIDE // 2
    for i in range(3):
        even = in_ref.at[i][pl.ds(0, half, stride=2)]
        odd = in_ref.at[i][pl.ds(1, half, stride=2)]
        even_rest = in_rest_ref.at[i][pl.ds(0, half, stride=2)]
        odd_rest = in_rest_ref.at[i][pl.ds(1, half, stride=2)]
        out_ref[pl.ds(at, half, stride=3)] = even
        out_ref[pl.ds(at + 1, half, stride=3)] = pair_lanes(even_rest, odd[:, :SIDE])
        out_ref[pl.ds(at + 2, half, stride=3)] = pair_lanes(odd[:, SIDE:], odd_rest)
        at += 3 * half
    for i in range(3):
        out_ref[at : at + half] = pair_lanes(
            attn_out_ref.at[i][pl.ds(0, half, stride=2)], attn_out_ref.at[i][pl.ds(1, half, stride=2)]
        )
        at += half
    for i in range(2):
        for j in range(2):
            out_ref[pl.ds(at + j, SIDE, stride=2)] = ffn_in_ref[i, :, 128 * j : 128 * j + 128]
        at += 2 * SIDE
    for i in range(2):
        out_ref[at : at + 128] = pair_lanes(
            ffn_out_ref.at[i][pl.ds(0, 128, stride=2)], ffn_out_ref.at[i][pl.ds(1, 128, stride=2)]
        )
        at += 128
    for j in range(4):
        out_ref[pl.ds(at + j, SIDE, stride=4)] = up_ref[:, 128 * j : 128 * j + 128]
    at += 4 * SIDE
    turn_ref[:128] = small_ref[...].T
    out_ref[at : at + 8] = pair_lanes(
        turn_ref[pl.ds(0, 8, stride=2)], turn_ref[pl.ds(1, 8, stride=2)]
    )
    at += 8
    out_ref[at:] = jnp.zeros((out_ref.shape[0] - at, 128), jnp.float32)
    lane = lax.broadcasted_iota(jnp.int32, (8, 128), 1) - 3 * me_ref[0]
    loss = loss_ref[...]
    one = rounded(loss)
    two = rounded(loss - one)
    three = rounded(loss - one - two)
    loss = jnp.where(lane == 0, one, jnp.where(lane == 1, two, jnp.where(lane == 2, three, 0.0)))
    out_ref[LOSS_ROW : LOSS_ROW + 8] = loss
    half = mine_ref.shape[0]
    core = me_ref[0] % 2
    mine_ref[...] = out_ref[pl.ds(pl.multiple_of(core * half, 8), half)]
    other_ref[...] = out_ref[pl.ds(pl.multiple_of((1 - core) * half, 8), half)]


FLAT_ROWS = 2208
LOSS_ROW = 2192


def flatten(me, loss, pieces):
    return pl.pallas_call(
        flatten_kernel,
        out_shape=[jax.ShapeDtypeStruct((FLAT_ROWS // 2, 128), jnp.float32)] * 2,
        in_specs=[smem] + [vmem] * 9,
        out_specs=[vmem] * 2,
        scratch_shapes=[
            pltpu.VMEM((512, 64), jnp.float32),
            pltpu.VMEM((FLAT_ROWS, 128), jnp.float32),
        ],
        compiler_params=LIMIT,
        name="flatten",
        cost_estimate=cost(4),
    )(me, loss, *pieces)


MAIN_ROWS = 2176


def rows_of(ref):
    main = 128 * MAIN_ROWS
    one = len(ref.shape) == 2
    load = (lambda a, b: ref[:, a:b]) if one else (lambda a, b: ref[a:b])
    rest = load(main, main + 512).reshape(4, 128)
    last = load(main + 512, main + 576).reshape(1, 64)
    return load(0, main).reshape(MAIN_ROWS, 128), jnp.concatenate(
        [rest, jnp.concatenate([last, jnp.zeros((1, 64), jnp.float32)], axis=1)], axis=0
    )


def put_rows(ref, main_values, rest_values):
    main = 128 * MAIN_ROWS
    if len(ref.shape) == 2:
        ref[:, :main] = main_values.reshape(1, main)
        ref[:, main : main + 512] = rest_values[:4].reshape(1, 512)
        ref[:, main + 512 : main + 576] = rest_values[4:5, :64]
    else:
        ref[:main] = main_values.reshape(main)
        ref[main : main + 512] = rest_values[:4].reshape(512)
        ref[main + 512 : main + 576] = rest_values[4:5, :64].reshape(64)


def stepped(first, second, inner, part):
    new_first = beta_first * first + (1.0 - beta_first) * part
    new_second = beta_second * second + (1.0 - beta_second) * part * part
    fixed_one = new_first / (1.0 - beta_first**STEP)
    fixed_two = new_second / (1.0 - beta_second**STEP)
    new_inner = inner - learn_rate * (
        fixed_one / (jnp.sqrt(fixed_two) + adam_eps) + decay_rate * inner
    )
    return new_first, new_second, new_inner


def gap_kernel(count_at, core_ref, letter_ref, mine_ref, other_ref, first_ref, second_ref, inner_ref, anchor_ref, gap_ref, loss_ref, count_ref, norm_ref, factor_ref):
    half = mine_ref.shape[0]
    core = core_ref[0]
    count = jnp.sum(letter_ref[:, count_at : letter_ref.shape[1] - 128].astype(jnp.float32))
    count_ref[0] = count
    loss_at = LOSS_ROW - half
    mine, other = mine_ref[...], other_ref[...]
    line = lax.broadcasted_iota(jnp.int32, (half, 1), 0)
    lossy = (line >= loss_at) & (line < loss_at + 8)
    late = jnp.where(core == 0, other_ref[loss_at : loss_at + 1], mine_ref[loss_at : loss_at + 1])
    loss_ref[0] = jnp.sum(late)
    mine = jnp.where(lossy & (core == 1), 0.0, mine)
    other = jnp.where(lossy & (core == 0), 0.0, other)
    low, high = jnp.where(core == 0, mine, other), jnp.where(core == 0, other, mine)
    scale = 1.0 / jnp.full((1, 1), count)
    low, high = low * scale, high * scale
    squares = jnp.sum(low * low, axis=0, keepdims=True) + jnp.sum(high * high, axis=0, keepdims=True)
    norm = jnp.sqrt(jnp.sum(squares, axis=1, keepdims=True))
    norm_ref[0] = jnp.sum(norm)
    clip = jnp.minimum(1.0, clip_norm / norm)
    factor_ref[...] = jnp.broadcast_to(jnp.where(lax.broadcasted_iota(jnp.int32, (8, 128), 1) == 0, scale, clip), (8, 128))
    main = 128 * half
    refs = (first_ref, second_ref, inner_ref)

    @pl.when(core == 0)
    def _():
        values = [ref[:, :main].reshape(half, 128) for ref in refs]
        new_inner = stepped(*values, low * clip)[2]
        gap_ref[...] = (anchor_ref[:main].reshape(half, 128) - new_inner).astype(jnp.bfloat16)

    @pl.when(core == 1)
    def _():
        own = MAIN_ROWS - half
        end = 128 * MAIN_ROWS
        part = high * clip
        values = [ref[:, main:end].reshape(own, 128) for ref in refs]
        new_inner = stepped(*values, part[:own])[2]
        gap_ref[:own] = (anchor_ref[main:end].reshape(own, 128) - new_inner).astype(jnp.bfloat16)
        rests = [rest_of(ref) for ref in refs]
        new_inner = stepped(*rests, part[own : own + 8])[2]
        gap_ref[own : own + 8] = (rest_of(anchor_ref) - new_inner).astype(jnp.bfloat16)
        gap_ref[own + 8 :] = jnp.zeros((half - own - 8, 128), jnp.bfloat16)


def rest_of(ref):
    main = 128 * MAIN_ROWS
    load = (lambda a, b: ref[:, a:b]) if len(ref.shape) == 2 else (lambda a, b: ref[a:b])
    last = load(main + 512, main + 576).reshape(1, 64)
    return jnp.concatenate(
        [
            load(main, main + 512).reshape(4, 128),
            jnp.concatenate([last, jnp.zeros((1, 64), jnp.float32)], axis=1),
            jnp.zeros((3, 128), jnp.float32),
        ],
        axis=0,
    )


def gap_part(core, letters, count_at, mine, other, first, second, inner, anchor):
    return pl.pallas_call(
        functools.partial(gap_kernel, count_at),
        out_shape=[
            jax.ShapeDtypeStruct(mine.shape, jnp.bfloat16),
            *[jax.ShapeDtypeStruct((1,), jnp.float32)] * 3,
            jax.ShapeDtypeStruct((8, 128), jnp.float32),
        ],
        in_specs=[smem] + [vmem] * 7,
        out_specs=[vmem] + [smem] * 3 + [vmem],
        compiler_params=LIMIT,
        name="gap",
        cost_estimate=cost(4),
    )(core, letters, mine, other, first, second, inner, anchor)


def adam_kernel(core_ref, factor_ref, mine_ref, other_ref, first_ref, second_ref, inner_ref, new_first_ref, new_second_ref, new_inner_ref, grad_ref):
    half = mine_ref.shape[0]
    core = core_ref[0]
    grad_ref[pl.ds(pl.multiple_of(core * half, 8), half)] = mine_ref[...]
    grad_ref[pl.ds(pl.multiple_of((1 - core) * half, 8), half)] = other_ref[...]
    scale, clip = factor_ref[0:1, 0:1], factor_ref[0:1, 1:2]
    spans = ((0, MAIN_ROWS), (MAIN_ROWS, MAIN_ROWS + 5))
    news = []
    for span, first, second, inner in zip(
        spans, rows_of(first_ref), rows_of(second_ref), rows_of(inner_ref)
    ):
        news.append(stepped(first, second, inner, grad_ref[span[0] : span[1]] * scale * clip))
    for ref, main, rest in zip((new_first_ref, new_second_ref, new_inner_ref), news[0], news[1]):
        put_rows(ref, main, rest)


def adam(core, factor, mine, other, first, second, inner):
    return pl.pallas_call(
        adam_kernel,
        out_shape=[jax.ShapeDtypeStruct(first.shape, jnp.float32)] * 3,
        in_specs=[smem] + [vmem] * 6,
        out_specs=[vmem] * 3,
        scratch_shapes=[pltpu.VMEM((FLAT_ROWS, 128), jnp.float32)],
        compiler_params=LIMIT,
        name="adam",
        cost_estimate=cost(6),
    )(core, factor, mine, other, first, second, inner)


def outer_kernel(core_ref, mine_ref, other_ref, anchor_ref, momentum_ref, delta_ref, new_momentum_ref, new_anchor_ref, full_ref):
    half = mine_ref.shape[0]
    core = core_ref[0]
    full_ref[pl.ds(pl.multiple_of(core * half, 8), half)] = mine_ref[...]
    full_ref[pl.ds(pl.multiple_of((1 - core) * half, 8), half)] = other_ref[...]
    news = []
    for span, anchor, momentum in zip(
        ((0, MAIN_ROWS), (MAIN_ROWS, MAIN_ROWS + 5)), rows_of(anchor_ref), rows_of(momentum_ref)
    ):
        delta = full_ref[span[0] : span[1]]
        new_momentum = outer_beta * momentum + delta
        news.append((delta, new_momentum, anchor - outer_rate * (delta + outer_beta * new_momentum)))
    for ref, main, rest in zip((delta_ref, new_momentum_ref, new_anchor_ref), news[0], news[1]):
        put_rows(ref, main, rest)


def outer(core, mine, other, anchor, momentum):
    flat = jax.ShapeDtypeStruct(anchor.shape, jnp.float32)
    return pl.pallas_call(
        outer_kernel,
        out_shape=[flat] * 3,
        in_specs=[smem] + [vmem] * 4,
        out_specs=[vmem] * 3,
        scratch_shapes=[pltpu.VMEM((FLAT_ROWS, 128), jnp.float32)],
        compiler_params=LIMIT,
        name="outer",
        cost_estimate=cost(5),
    )(core, mine, other, anchor, momentum)


def unpack_kernel(flat_ref, down_ref, in_t_ref, out_t_ref, ffn_in_t_ref, ffn_out_t_ref, in_ref, out_ref, ffn_in_ref, ffn_out_ref, up_ref, small_ref, rows_ref, tall_ref):
    main, rest = rows_of(flat_ref)
    rows_ref[:MAIN_ROWS] = main
    rows_ref[MAIN_ROWS : MAIN_ROWS + 8] = jnp.concatenate([rest, jnp.zeros((3, 128), jnp.float32)], axis=0)

    def natural(at, count):
        packed = rows_ref[at : at + count // 2]
        tall_ref[pl.ds(0, count // 2, stride=2)] = packed[:, :SIDE]
        tall_ref[pl.ds(1, count // 2, stride=2)] = packed[:, SIDE:]
        return tall_ref[:count]

    at = 0
    for i in range(4):
        down_ref[i] = natural(at, 512).T.astype(jnp.bfloat16)
        at += 256
    half = SIDE // 2
    for i in range(3):
        one, two, three = [rows_ref[pl.ds(at + j, half, stride=3)] for j in range(3)]
        tall_ref[pl.ds(0, half, stride=2)] = one[:, :SIDE]
        tall_ref[pl.ds(1, half, stride=2)] = two[:, SIDE:]
        tall_ref[pl.ds(64, half, stride=2)] = one[:, SIDE:]
        tall_ref[pl.ds(65, half, stride=2)] = three[:, :SIDE]
        tall_ref[pl.ds(128, half, stride=2)] = two[:, :SIDE]
        tall_ref[pl.ds(129, half, stride=2)] = three[:, SIDE:]
        columns = [tall_ref[64 * j : 64 * j + 64] for j in range(3)]
        in_ref[i] = jnp.concatenate(columns, axis=1).astype(jnp.bfloat16)
        in_t_ref[i] = jnp.concatenate([column.T for column in columns], axis=0).astype(jnp.bfloat16)
        at += 3 * half
    for i in range(3):
        square = natural(at, SIDE)
        out_ref[i] = square.astype(jnp.bfloat16)
        out_t_ref[i] = square.T.astype(jnp.bfloat16)
        at += half
    for i in range(2):
        wide = jnp.concatenate([rows_ref[pl.ds(at + j, SIDE, stride=2)] for j in range(2)], axis=1)
        ffn_in_ref[i] = wide.astype(jnp.bfloat16)
        ffn_in_t_ref[i] = wide.T.astype(jnp.bfloat16)
        at += 2 * SIDE
    for i in range(2):
        tall = natural(at, 256)
        ffn_out_ref[i] = tall.astype(jnp.bfloat16)
        ffn_out_t_ref[i] = tall.T.astype(jnp.bfloat16)
        at += 128
    up_ref[...] = jnp.concatenate(
        [rows_ref[pl.ds(at + j, SIDE, stride=4)] for j in range(4)], axis=1
    ).astype(jnp.bfloat16)
    at += 4 * SIDE
    tall_ref[:128] = jnp.zeros((128, SIDE), jnp.float32)
    tall = natural(at, 16)
    tall_ref[16:128] = jnp.zeros((112, SIDE), jnp.float32)
    small_ref[...] = tall_ref[:128].T


def unpack_weights(flat):
    bf16 = jnp.bfloat16
    shapes = [
        (4, SIDE, D),
        (3, 3 * SIDE, SIDE),
        (3, SIDE, SIDE),
        (2, SIDE_FF, SIDE),
        (2, SIDE, SIDE_FF),
        (3, SIDE, 3 * SIDE),
        (3, SIDE, SIDE),
        (2, SIDE, SIDE_FF),
        (2, SIDE_FF, SIDE),
        (SIDE, D),
    ]
    return pl.pallas_call(
        unpack_kernel,
        out_shape=[jax.ShapeDtypeStruct(shape, bf16) for shape in shapes]
        + [jax.ShapeDtypeStruct((SIDE, 128), jnp.float32)],
        in_specs=[vmem],
        out_specs=[vmem] * 11,
        scratch_shapes=[
            pltpu.VMEM((MAIN_ROWS + 8, 128), jnp.float32),
            pltpu.VMEM((512, SIDE), jnp.float32),
        ],
        compiler_params=LIMIT,
        name="unpack",
        cost_estimate=cost(8),
    )(flat)


def per_device(
    source_ids,
    target_inputs,
    lengths,
    positions,
    target_ids,
    target_mask,
    table,
    backbone_attn,
    backbone_ffn_in,
    backbone_ffn_out,
    backbone_gains,
    inner_weights,
    first_moment,
    second_moment,
    anchor,
    outer_momentum,
):
    micro = source_ids.shape[0]
    src_tokens = source_ids.shape[2]
    tgt_tokens = target_inputs.shape[2]
    size = lax.axis_size("dp")
    me = lax.axis_index("dp")
    core = me & 1
    rows = table.shape[0]
    score = [positions, target_ids, target_mask]
    spots = positions.shape[2]
    ids_count = source_ids.size + target_inputs.size
    cap = -(-(ids_count * 5 // (size * 6)) // 16) * 16
    slots, column, near, other, scored = plan(
        me[None], source_ids, target_inputs, score, rows, size, cap, tgt_tokens
    )
    asked = ask(near, other)
    found = jnp.take(table, asked[:, :cap].reshape(-1), axis=0, mode="clip")
    most = functools.reduce(jnp.maximum, gather_peers(after(asked, found)[:, -128:], "grp"))
    weights = unpack_weights(after(inner_weights, found, most))
    table_pad, weight = table_parts(after(table, found, most), weights[9])
    most = jnp.max(most[:, 1 + micro])
    goals, where = goal_rows(after(me[None], most), asked, table_pad, micro, spots)
    embed_src, embed_tgt = embed_rows(
        slots,
        column,
        found.reshape(size // 2, 2, cap, -1),
        cap,
        most,
        source_ids,
        target_inputs,
        table,
        (goals, weight, weights[0]),
    )
    down_t, in_t, out_t, ffn_in_t, ffn_out_t, attn_in, attn_out, ffn_in, ffn_out, up_b, small = weights
    ahead = [down_t, in_t, out_t, ffn_in_t, ffn_out_t, small]
    behind = [in_t, ffn_in_t, attn_in, attn_out, ffn_in, ffn_out, small]
    lens = lengths[:, 0]
    encoded = encode(lens, embed_src, backbone_attn, backbone_ffn_in, backbone_ffn_out, backbone_gains)
    decoded = decode(lens, embed_tgt, encoded, backbone_attn, backbone_ffn_in, backbone_ffn_out, backbone_gains)
    picked, *kept = side(lens, embed_src, encoded, embed_tgt, decoded, scored, ahead)
    far, near = gather_all(picked)
    mix, stats, packed = softmax_part(where, far, near, asked, weight, table_pad, rows)
    far, near = gather_all(stats[:2])
    own, other, grad_up, loss_part = head_finish(
        where, far, near, mix, goals, packed, up_b, micro, spots
    )
    tops = add_home(own, other)
    grads = side_back(lens, embed_src, encoded, embed_tgt, decoded, scored, behind, kept, tops)
    mine, other = flatten(me[None], loss_part, [*grads[:6], grad_up, grads[6]])
    sent = (mine + swap(other, "dp", 1)).astype(jnp.bfloat16)
    terms = [sent] + [swap(sent, "dp", s) for s in range(2, size, 2)]
    mine = tree_sum([term.astype(jnp.float32) for term in terms])
    other = swap(mine, "dp", 1)
    gap, loss_total, count_total, norm, factor = gap_part(
        core[None], asked, asked.shape[1] - 128 - micro * spots, mine, other, first_moment, second_moment, inner_weights, anchor
    )
    new_first, new_second, new_inner = adam(
        core[None], factor, mine, other, first_moment, second_moment, inner_weights
    )
    terms = gather_peers(gap, "grp")
    mine = tree_sum([term.astype(jnp.float32) for term in terms]) / lax.axis_size("grp")
    other = swap(after(mine, new_first), "dp", 1)
    delta, momentum, new_anchor = outer(core[None], mine, other, anchor, outer_momentum)
    return (
        loss_total,
        count_total,
        norm,
        new_first,
        new_second,
        new_inner,
        delta,
        momentum,
        new_anchor,
    )


def solution(mesh):
    return jax.shard_map(
        per_device,
        mesh=mesh,
        in_specs=(
            P(None, ("grp", "dp"), None),
            P(None, ("grp", "dp"), None),
            P(None, ("grp", "dp"), None),
            P(None, ("grp", "dp"), None),
            P(None, ("grp", "dp"), None),
            P(None, ("grp", "dp"), None),
            P("dp", None),
            P(),
            P(),
            P(),
            P(),
            P("grp", None),
            P("grp", None),
            P("grp", None),
            P(),
            P(),
        ),
        out_specs=(
            P("grp"),
            P("grp"),
            P("grp"),
            P("grp", None),
            P("grp", None),
            P("grp", None),
            P(),
            P(),
            P(),
        ),
        check_vma=False,
    )
```
